32 devices in a mesh: dp: 4 (over y, core), cls: 8 (over z, x).
Axes of the slice: x: 2, y: 2, z: 4, core: 2. Of those that a mesh axis runs over, the one named last changes fastest.
Arguments:
- embeddings: bfloat16 [32768, 512], P(('dp', 'cls'))
- proxies: bfloat16 [24576, 512], P('cls')
- hard_tiles: int32 [256, 8], P(('dp', 'cls')), may hold values from 0 to 191, as said below
- tile_count: int32 [256], P(('dp', 'cls')), may hold values from 5 to 8
- labels: int32 [32768], P(('dp', 'cls')), may hold values from 0 to 24575, as said below
Outputs:
- row_loss: float32 [32768], P(('dp', 'cls'))
- embed_grad: bfloat16 [32768, 512], P(('dp', 'cls'))
- proxy_grad: float32 [24576, 512], P('cls', 'dp')
The draws below stay inside these ranges and needn't reach their ends.
Inputs may be any that keep to these rules, and one draw needn't show every extreme that they name: `hard_tiles`: tile t is stored on class shard t // 24. Among the 8 x 8 list entries of one device's blocks (all entries, used or not), every one of the class shards is named exactly 8 times; the entries of one block name different tiles. Only the first tile_count entries of a block's list are used. `labels`: A row's positive class lies in the first tile of its block's list.
All inputs are finite; a program needn't handle non-finite values.
Results may differ from the reference program's by a relative error of at most 0.0098.
Values may be sent and summed in bfloat16 or wider, within the bound.
No kernel may reach another device: no remote copies, remote signals or barrier semaphores. Data moves between devices by JAX's collectives and lax.ppermute only.
A program may use at most 128 MiB of HBM per device.

```python
import jax
import jax.numpy as jnp
import numpy as np
from jax import lax

D = 512
TILE = 128
BR = 128
K = 8
K_MIN = 5
BLK_DEV = 8
TILE_DEV = 24
CAP = 8
BLOCKS = 256
ROWS = 32768
CLASSES = 24576
N_CLS = 8


def request_plan(key):
    devices_all = BLOCKS // BLK_DEV
    pair_count = BLK_DEV * K
    subkeys = jax.random.split(jax.random.fold_in(key, 101), 4)
    counter = jnp.arange(pair_count, dtype=jnp.int32)
    owner_of = counter // CAP
    noise_bits = jax.random.randint(subkeys[0], (devices_all, pair_count), 0, 1 << 20)
    chosen = jax.random.randint(subkeys[1], (devices_all, 1), 0, N_CLS)
    scores = noise_bits * pair_count + counter[None, :]
    scores = jnp.where(owner_of[None, :] == chosen, scores - (1 << 30), scores)
    ranking = jnp.argsort(scores, axis=1, stable=True).astype(jnp.int32)
    static_index = np.arange(pair_count)
    position_key = np.where(static_index % K < K_MIN, 0, 1) * pair_count + static_index
    positions = np.argsort(position_key, kind='stable')
    placed = jnp.zeros((devices_all, pair_count), jnp.int32).at[:, positions].set(ranking)
    owner_at = placed // CAP
    copy_at = placed % CAP
    base_tile = jax.random.randint(subkeys[2], (devices_all, BLK_DEV * N_CLS), 0, TILE_DEV)
    block_at = counter // K
    base_at = jnp.take_along_axis(base_tile, block_at[None, :] * N_CLS + owner_at, axis=1)
    tile_ids = owner_at * TILE_DEV + (base_at + copy_at) % TILE_DEV
    hard_list = tile_ids.reshape(BLOCKS, K).astype(jnp.int32)
    offsets = jax.random.randint(subkeys[3], (BLOCKS, BR), 0, TILE)
    labels = (hard_list[:, 0:1] * TILE + offsets).reshape(ROWS).astype(jnp.int32)
    return (hard_list, labels)


def proxy_table(key):
    proxy_rows = jax.random.normal(jax.random.fold_in(key, 202), (CLASSES, D), jnp.float32) * 0.5
    return proxy_rows


def draw_hard_tiles(key, part):
    hard_list, labels = request_plan(key)
    return hard_list


def draw_labels(key, part):
    hard_list, labels = request_plan(key)
    return labels


def draw_proxies(key, part):
    return proxy_table(key).astype(jnp.bfloat16)


def draw_embeddings(key, part):
    noise_rows = jax.random.normal(jax.random.fold_in(key, 204), (ROWS, D), jnp.float32)
    result = noise_rows
    return result.astype(jnp.bfloat16)


def set_ends(values, key, smallest, largest):
    place = [jax.random.randint(jax.random.fold_in(key, axis), (), 0, length) for axis, length in enumerate(values.shape)]
    main_axis = values.shape.index(max(values.shape))
    beside = place[:main_axis] + [(place[main_axis] + 1) % values.shape[main_axis]] + place[main_axis + 1:]
    return values.at[tuple(place)].set(smallest).at[tuple(beside)].set(largest)


def setup_inputs(seed: int = 0) -> dict:
    seeds = jax.random.split(jax.random.key(seed), 6)
    return {
        "embeddings": draw_embeddings(jax.random.fold_in(seeds[5], 71), 0),
        "proxies": draw_proxies(jax.random.fold_in(seeds[5], 71), 0),
        "hard_tiles": draw_hard_tiles(jax.random.fold_in(seeds[5], 71), 0),
        "tile_count": set_ends(jax.random.randint(seeds[3], (BLOCKS,), K_MIN, K + 1), jax.random.fold_in(seeds[3], 1), K_MIN, K).astype(jnp.int32),
        "labels": draw_labels(jax.random.fold_in(seeds[5], 71), 0),
    }


logit_scale = 4.0
epsilon = 1e-06

def reference(embeddings, proxies, hard_tiles, tile_count, labels):
    emb_exact = embeddings.astype(jnp.float32)
    inverse_norm = lax.rsqrt(lax.optimization_barrier(jnp.sum(emb_exact * emb_exact, axis=1, keepdims=True)) + epsilon)
    unit_exact = emb_exact * inverse_norm
    unit_rows = unit_exact.astype(jnp.bfloat16)
    tile_table = proxies.reshape(-1, TILE, D)
    columns = jnp.arange(TILE, dtype=jnp.int32)
    entries = jnp.arange(K, dtype=jnp.int32)

    def per_block(accumulated, inputs):
        unit_block, exact_block, norm_block, tile_list, count_one, label_block = inputs
        candidates = tile_table[tile_list].astype(jnp.float32)
        unit_wide = unit_block.astype(jnp.float32)
        logits = logit_scale * jnp.einsum('rd,kcd->rkc', unit_wide, candidates)
        valid_entry = (entries < count_one)[None, :, None]
        masked = jnp.where(valid_entry, logits, -1e+30)
        peak_row = lax.optimization_barrier(jnp.max(masked, axis=(1, 2)))
        total_row = lax.optimization_barrier(jnp.sum(jnp.exp(masked - peak_row[:, None, None]), axis=(1, 2)))
        log_total = peak_row + jnp.log(total_row)
        position = label_block - tile_list[0] * TILE
        positive_hit = ((entries == 0)[None, :, None] & (columns[None, None, :] == position[:, None, None])).astype(jnp.float32)
        positive = lax.optimization_barrier(jnp.sum(logits * positive_hit, axis=(1, 2)))
        probabilities = jnp.exp(masked - log_total[:, None, None])
        dscore = (logit_scale * (probabilities - positive_hit)).astype(jnp.bfloat16)
        dscore = lax.optimization_barrier(dscore)
        score_wide = dscore.astype(jnp.float32)
        tile_terms = jnp.einsum('rkc,kcd->rkd', score_wide, candidates).astype(jnp.bfloat16)
        tile_terms = lax.optimization_barrier(tile_terms)
        grad_unit = lax.optimization_barrier(jnp.sum(tile_terms.astype(jnp.float32), axis=1))
        radial = lax.optimization_barrier(jnp.sum(exact_block * grad_unit, axis=1, keepdims=True))
        grad_rows = ((grad_unit - exact_block * radial) * norm_block).astype(jnp.bfloat16)
        tile_grads = jnp.einsum('rkc,rd->kcd', score_wide, unit_wide)
        accumulated = accumulated.at[tile_list].add(tile_grads)
        return (accumulated, (log_total - positive, grad_rows))
    zero_grads = jnp.zeros((tile_table.shape[0], TILE, D), jnp.float32)
    inputs = (unit_rows.reshape(-1, BR, D), unit_exact.reshape(-1, BR, D), inverse_norm.reshape(-1, BR, 1), hard_tiles, tile_count, labels.reshape(-1, BR))
    accumulated, outputs = lax.scan(per_block, zero_grads, inputs)
    losses, row_grads = outputs
    return (losses.reshape(-1), row_grads.reshape(-1, D), accumulated.reshape(-1, D))
```

```python
import functools

import jax
import jax.numpy as jnp
from jax import lax
from jax.experimental import pallas as pl
from jax.experimental.pallas import tpu as pltpu
from jax.sharding import PartitionSpec as P

D = 512
TILE = 128
BR = 128
K = 8
PAIRS_PER_STEP = 4
FIELD = 128
VMEM_BYTES = 60 * 1024 * 1024

logit_scale = 4.0
epsilon = 1e-06
unused_logit = -1e30


def transposed_logits(tile, rows):
    return logit_scale * lax.dot_general(
        tile, rows, (((1,), (1,)), ((), ())), preferred_element_type=jnp.float32
    )


def decode(code):
    return code // (2 * FIELD), (code // 2) % FIELD, (code % 2) == 1


def score_kernel(blocks, tiles, codes_ref, count_ref, rows_ref, table_ref, hit_ref, stats_ref, lse_ref, pos_ref):
    lse_ref[...] = jnp.full(lse_ref.shape, unused_logit, jnp.float32)
    pos_ref[...] = jnp.zeros(pos_ref.shape, jnp.float32)
    class_at = lax.broadcasted_iota(jnp.int32, (TILE, BR), 0)

    def step(index, carry):
        held = []
        for lane in range(PAIRS_PER_STEP):
            block, tile, first = decode(codes_ref[index * PAIRS_PER_STEP + lane])
            source = jnp.minimum(block, blocks - 1)
            logits = transposed_logits(
                table_ref[jnp.minimum(tile, tiles - 1)], rows_ref[source]
            )
            peak = jnp.max(logits, axis=0, keepdims=True)
            total = jnp.sum(jnp.exp(logits - peak), axis=0, keepdims=True)
            hit = class_at == hit_ref[pl.ds(source, 1), :]
            positive = jnp.sum(jnp.where(hit, logits, 0.0), axis=0, keepdims=True)
            held.append((block, peak + jnp.log(total), jnp.where(first, positive, 0.0)))
        for block, lse, positive in held:
            before = lse_ref[pl.ds(block, 1), :]
            top = jnp.maximum(before, lse)
            lse_ref[pl.ds(block, 1), :] = top + jnp.log(
                jnp.exp(before - top) + jnp.exp(lse - top)
            )
            pos_ref[pl.ds(block, 1), :] += positive
        return carry

    lax.fori_loop(0, pl.cdiv(count_ref[0], PAIRS_PER_STEP), step, 0)
    stats_ref[0] = lse_ref[:blocks, :]
    stats_ref[1] = pos_ref[:blocks, :]


def grad_kernel(
    blocks, tiles, has_carry, last, split,
    codes_ref, count_ref, rows_ref, table_ref, hit_ref, stats_ref, *refs,
):
    if has_carry:
        carry_ref, grad_ref, share_ref, loss_ref, total_ref, rows_acc, tiles_acc = refs
        tiles_acc[:tiles] = carry_ref[...]
    else:
        grad_ref, share_ref, loss_ref, total_ref, rows_acc, tiles_acc = refs
        tiles_acc[...] = jnp.zeros(tiles_acc.shape, jnp.float32)
    rows_acc[...] = jnp.zeros(rows_acc.shape, jnp.float32)
    lse = stats_ref[:, 0]
    top = jnp.max(lse, axis=0)
    total = top + jnp.log(jnp.sum(jnp.exp(lse - top[None]), axis=0))
    total_ref[:blocks, :] = total
    total_ref[blocks:, :] = jnp.zeros((8, BR), jnp.float32)
    loss_ref[...] = total - jnp.sum(stats_ref[:, 1], axis=0)
    class_at = lax.broadcasted_iota(jnp.int32, (TILE, BR), 0)

    def step(index, carry):
        held = []
        for lane in range(PAIRS_PER_STEP):
            block, tile, first = decode(codes_ref[index * PAIRS_PER_STEP + lane])
            source = jnp.minimum(block, blocks - 1)
            table_at = jnp.minimum(tile, tiles - 1)
            logits = transposed_logits(table_ref[table_at], rows_ref[source])
            share = jnp.exp(logits - total_ref[pl.ds(source, 1), :])
            wanted = jnp.where(first, hit_ref[pl.ds(source, 1), :], -1)
            hit = (class_at == wanted).astype(jnp.float32)
            score = (logit_scale * (share - hit)).astype(jnp.bfloat16)
            held.append((block, tile, source, table_at, score))
        for block, tile, source, table_at, score in held:
            rows_acc[block] += lax.dot_general(
                score, table_ref[table_at], (((0,), (0,)), ((), ())),
                preferred_element_type=jnp.float32,
            )
            tiles_acc[tile] += jnp.dot(
                score, rows_ref[source], preferred_element_type=jnp.float32
            )
        return carry

    lax.fori_loop(0, pl.cdiv(count_ref[0], PAIRS_PER_STEP), step, 0)
    grad_ref[...] = rows_acc[:blocks].astype(grad_ref.dtype)
    if not last:
        share_ref[...] = tiles_acc[:tiles]
    elif split:
        width = D // split
        for part in range(split):
            share_ref[part] = tiles_acc[:tiles, :, part * width:(part + 1) * width].astype(
                share_ref.dtype
            )
    else:
        share_ref[...] = tiles_acc[:tiles].astype(share_ref.dtype)


SMEM = pl.BlockSpec(memory_space=pltpu.SMEM)
VMEM = pl.BlockSpec(memory_space=pltpu.VMEM)


def score(codes, count, rows, table, hit):
    blocks, tiles = rows.shape[0], table.shape[0]
    return pl.pallas_call(
        functools.partial(score_kernel, blocks, tiles),
        out_shape=jax.ShapeDtypeStruct((2, blocks, BR), jnp.float32),
        in_specs=[SMEM, SMEM, VMEM, VMEM, VMEM],
        out_specs=VMEM,
        scratch_shapes=[
            pltpu.VMEM((blocks + 8, BR), jnp.float32),
            pltpu.VMEM((blocks + 8, BR), jnp.float32),
        ],
        compiler_params=pltpu.CompilerParams(vmem_limit_bytes=VMEM_BYTES),
    )(codes, count, rows, table, hit)


def grads(codes, count, rows, table, hit, stats, carry, last, split):
    blocks, tiles = rows.shape[0], table.shape[0]
    if not last:
        share = jax.ShapeDtypeStruct((tiles, TILE, D), jnp.float32)
    elif split:
        share = jax.ShapeDtypeStruct((split, tiles, TILE, D // split), jnp.bfloat16)
    else:
        share = jax.ShapeDtypeStruct((tiles, TILE, D), jnp.bfloat16)
    has_carry = carry is not None
    operands = (codes, count, rows, table, hit, stats) + ((carry,) if has_carry else ())
    return pl.pallas_call(
        functools.partial(grad_kernel, blocks, tiles, has_carry, last, split),
        out_shape=(
            jax.ShapeDtypeStruct((blocks, BR, D), jnp.bfloat16),
            share,
            jax.ShapeDtypeStruct((blocks, BR), jnp.float32),
        ),
        in_specs=[SMEM, SMEM] + [VMEM] * (len(operands) - 2),
        out_specs=(VMEM, VMEM, VMEM),
        scratch_shapes=[
            pltpu.VMEM((blocks + 8, BR), jnp.float32),
            pltpu.VMEM((blocks + 1, BR, D), jnp.float32),
            pltpu.VMEM((tiles + 1, TILE, D), jnp.float32),
        ],
        compiler_params=pltpu.CompilerParams(vmem_limit_bytes=VMEM_BYTES),
    )(*operands)


def per_device(nx, chunks, embeddings, proxies, hard_tiles, tile_count, labels):
    groups = lax.axis_size("cls")
    dp = lax.axis_size("dp")
    nz = groups // nx
    blocks = hard_tiles.shape[0]
    shard_tiles = proxies.shape[0] // TILE
    me = lax.axis_index("cls")
    z_groups = [[z * nx + x for z in range(nz)] for x in range(nx)]
    x_groups = [[z * nx + x for x in range(nx)] for z in range(nz)]
    place = me // nx

    emb_exact = embeddings.astype(jnp.float32)
    inverse_norm = lax.rsqrt(jnp.sum(emb_exact * emb_exact, axis=1, keepdims=True) + epsilon)
    unit_exact = emb_exact * inverse_norm
    unit_blocks = unit_exact.astype(jnp.bfloat16).reshape(blocks, BR, D)

    position = labels.reshape(blocks, BR) - hard_tiles[:, 0:1] * TILE
    entries = jnp.arange(K, dtype=jnp.int32)
    used = jnp.where(entries[None, :] < tile_count[:, None], hard_tiles, -1)
    lists = lax.all_gather(
        jnp.concatenate([used, position], axis=1), "cls", axis_index_groups=z_groups
    )

    table = proxies.reshape(shard_tiles, TILE, D)
    if nx > 1:
        table = lax.all_gather(table, "cls", axis_index_groups=x_groups, tiled=True)
    tiles = nx * shard_tiles

    per_chunk = blocks // chunks
    held = nz * per_chunk
    room = min(held * K, nz * (blocks * K // groups) * nx)
    room = -(-room // PAIRS_PER_STEP) * PAIRS_PER_STEP
    split = dp if (D // dp) % 128 == 0 else 0
    padding = (held * FIELD + tiles) * 2

    losses, row_grads, carry = [], [], None
    for chunk in range(chunks):
        here = slice(chunk * per_chunk, (chunk + 1) * per_chunk)
        rows = lax.all_gather(unit_blocks[here], "cls", axis_index_groups=z_groups, tiled=True)
        chunk_lists = lists[:, here].reshape(held, K + BR)
        hit = chunk_lists[:, K:]
        entry = chunk_lists[:, :K].reshape(-1)
        local = entry - place * tiles
        mine = (entry >= 0) & (local >= 0) & (local < tiles)
        counter = jnp.arange(held * K, dtype=jnp.int32)
        code = ((counter // K) * FIELD + local) * 2 + (counter % K == 0)
        rank = jnp.sum(
            jnp.where(mine[None, :] & (counter[None, :] < counter[:, None]), 1, 0), axis=1
        ).astype(jnp.int32)
        slots = jnp.arange(room, dtype=jnp.int32)
        chosen = mine[None, :] & (rank[None, :] == slots[:, None])
        codes = padding + jnp.sum(jnp.where(chosen, code[None, :] - padding, 0), axis=1).astype(jnp.int32)
        count = jnp.sum(mine.astype(jnp.int32)).reshape(1)

        stats = score(codes, count, rows, table, hit)
        stats = lax.all_gather(stats, "cls", axis_index_groups=z_groups)
        last = chunk == chunks - 1
        partial, carry, loss = grads(codes, count, rows, table, hit, stats, carry, last, split)
        partial = partial.reshape(nz, per_chunk * BR, D)
        row_grads.append(
            lax.psum_scatter(partial, "cls", scatter_dimension=0, axis_index_groups=z_groups)
        )
        losses.append(lax.dynamic_slice_in_dim(loss, place * per_chunk, per_chunk, axis=0))

    if split:
        share = lax.psum_scatter(carry, "dp", scatter_dimension=0)
        share = share.reshape(tiles * TILE, D // dp)
    else:
        share = lax.psum_scatter(
            carry.reshape(tiles * TILE, D), "dp", scatter_dimension=1, tiled=True
        )
    if nx > 1:
        share = lax.psum_scatter(
            share, "cls", scatter_dimension=0, axis_index_groups=x_groups, tiled=True
        )
    proxy_grad = share.astype(jnp.float32)

    row_loss = jnp.concatenate(losses, axis=0).reshape(-1)
    grad_flat = jnp.concatenate(row_grads, axis=0).astype(jnp.float32)
    radial = jnp.sum(unit_exact * grad_flat, axis=1, keepdims=True)
    embed_grad = ((grad_flat - unit_exact * radial) * inverse_norm).astype(jnp.bfloat16)
    return (row_loss, embed_grad, proxy_grad)


def solution(mesh):
    placed = (
        P(("dp", "cls"), None),
        P("cls", None),
        P(("dp", "cls"), None),
        P(("dp", "cls")),
        P(("dp", "cls")),
    )
    nx = 1
    chunks = max(1, mesh.shape["cls"] // nx // 8)
    return jax.shard_map(
        functools.partial(per_device, nx, chunks),
        mesh=mesh,
        in_specs=placed,
        out_specs=(P(("dp", "cls")), P(("dp", "cls"), None), P("cls", "dp")),
        check_vma=False,
    )
```

```python
import functools

import jax
import jax.numpy as jnp
from jax import lax
from jax.experimental import pallas as pl
from jax.experimental.pallas import tpu as pltpu
from jax.sharding import PartitionSpec as P

D = 512
TILE = 128
BR = 128
K = 8
PAIRS_PER_STEP = 4
FIELD = 128
VMEM_BYTES = 60 * 1024 * 1024

logit_scale = 4.0
epsilon = 1e-06
unused_logit = -1e30

SMEM = pl.BlockSpec(memory_space=pltpu.SMEM)
VMEM = pl.BlockSpec(memory_space=pltpu.VMEM)
ANY = pl.BlockSpec(memory_space=pl.ANY)


class Line:
    def __init__(self, places, blocks, pieces):
        self.places, self.blocks, self.pieces = places, blocks, pieces

    def spans(self, place):
        if self.pieces == 1:
            return [(None, 0)]
        spans = [(None, place * self.blocks)]
        for step in range(1, self.places):
            spans.append((place >= step, (place - step) * self.blocks))
        for step in range(1, self.places):
            spans.append((place + step < self.places, (place + step) * self.blocks))
        return spans


def run_copies(jobs, sems):
    copies = []
    for index, (needed, source, target) in enumerate(jobs):
        copy = pltpu.make_async_copy(source, target, sems.at[index])
        copies.append((needed, copy))
        if needed is None:
            copy.start()
        else:
            pl.when(needed)(copy.start)

    def finish():
        for needed, copy in copies:
            if needed is None:
                copy.wait()
            else:
                pl.when(needed)(copy.wait)

    return finish


def load_operands(line, place, core, row_refs, table_refs, rows_ref, table_ref, sems):
    size = row_refs[0].shape[0]
    jobs = [
        (needed, ref, rows_ref.at[pl.ds(start, size)])
        for ref, (needed, start) in zip(row_refs, line.spans(place))
    ]
    jobs.append((None, table_refs[0], table_ref.at[pl.ds(0, table_refs[0].shape[0])]))
    if len(table_refs) > 1:
        half = table_refs[1].shape[0]
        jobs.append((None, table_refs[1], table_ref.at[pl.ds((2 + core) * half, half)]))
        jobs.append((None, table_refs[2], table_ref.at[pl.ds((3 - core) * half, half)]))
    return run_copies(jobs, sems)


def transposed_logits(tile, rows):
    return logit_scale * lax.dot_general(
        tile, rows, (((1,), (1,)), ((), ())), preferred_element_type=jnp.float32
    )


def decode(code):
    return code // (2 * FIELD), (code // 2) % FIELD, (code % 2) == 1


def score_kernel(line, n_tables, blocks, tiles, codes_ref, meta_ref, hit_ref, *refs):
    row_refs, refs = refs[:line.pieces], refs[line.pieces:]
    table_refs, refs = refs[:n_tables], refs[n_tables:]
    stats_ref, rows_ref, table_ref, lse_ref, pos_ref, sems = refs
    finish = load_operands(
        line, meta_ref[1], meta_ref[2] % 2, row_refs, table_refs, rows_ref, table_ref, sems
    )
    lse_ref[...] = jnp.full(lse_ref.shape, unused_logit, jnp.float32)
    pos_ref[...] = jnp.zeros(pos_ref.shape, jnp.float32)
    class_at = lax.broadcasted_iota(jnp.int32, (TILE, BR), 0)
    finish()

    def step(index, carry):
        held = []
        for lane in range(PAIRS_PER_STEP):
            block, tile, first = decode(codes_ref[index * PAIRS_PER_STEP + lane])
            source = jnp.minimum(block, blocks - 1)
            logits = transposed_logits(
                table_ref[jnp.minimum(tile, tiles - 1)], rows_ref[source]
            )
            peak = jnp.max(logits, axis=0, keepdims=True)
            total = jnp.sum(jnp.exp(logits - peak), axis=0, keepdims=True)
            hit = class_at == hit_ref[pl.ds(source, 1), :]
            positive = jnp.sum(jnp.where(hit, logits, 0.0), axis=0, keepdims=True)
            held.append((block, peak + jnp.log(total), jnp.where(first, positive, 0.0)))
        for block, lse, positive in held:
            before = lse_ref[pl.ds(block, 1), :]
            top = jnp.maximum(before, lse)
            lse_ref[pl.ds(block, 1), :] = top + jnp.log(
                jnp.exp(before - top) + jnp.exp(lse - top)
            )
            pos_ref[pl.ds(block, 1), :] += positive
        return carry

    lax.fori_loop(0, pl.cdiv(meta_ref[0], PAIRS_PER_STEP), step, 0)
    stats_ref[0] = lse_ref[:blocks, :]
    stats_ref[1] = pos_ref[:blocks, :]


def grad_kernel(
    line, n_tables, n_stats, blocks, tiles, has_carry, n_shares,
    codes_ref, meta_ref, hit_ref, *refs,
):
    stat_refs, refs = refs[:n_stats], refs[n_stats:]
    row_refs, refs = refs[:line.pieces], refs[line.pieces:]
    table_refs, refs = refs[:n_tables], refs[n_tables:]
    carry_refs, refs = refs[:has_carry], refs[has_carry:]
    grad_refs, refs = refs[:line.pieces], refs[line.pieces:]
    share_refs, refs = refs[:n_shares], refs[n_shares:]
    loss_ref, rows_ref, table_ref, total_ref, rows_acc, tiles_acc, out_ref, sems, sem = refs
    place, lane_part = meta_ref[1], meta_ref[2]
    finish = load_operands(
        line, place, lane_part % 2, row_refs, table_refs, rows_ref, table_ref, sems
    )
    if has_carry:
        carried = pltpu.make_async_copy(carry_refs[0], tiles_acc.at[pl.ds(0, tiles)], sem)
        carried.start()
    else:
        tiles_acc[...] = jnp.zeros(tiles_acc.shape, jnp.float32)
    rows_acc[...] = jnp.zeros(rows_acc.shape, jnp.float32)
    lse = [ref[0] for ref in stat_refs]
    top = functools.reduce(jnp.maximum, lse)
    total = top + jnp.log(sum(jnp.exp(part - top) for part in lse))
    total_ref[...] = total
    loss_ref[...] = total - sum(ref[1] for ref in stat_refs)
    class_at = lax.broadcasted_iota(jnp.int32, (TILE, BR), 0)
    finish()
    if has_carry:
        carried.wait()

    def step(index, carry):
        held = []
        for lane in range(PAIRS_PER_STEP):
            block, tile, first = decode(codes_ref[index * PAIRS_PER_STEP + lane])
            source = jnp.minimum(block, blocks - 1)
            table_at = jnp.minimum(tile, tiles - 1)
            logits = transposed_logits(table_ref[table_at], rows_ref[source])
            share = jnp.exp(logits - total_ref[pl.ds(source, 1), :])
            wanted = jnp.where(first, hit_ref[pl.ds(source, 1), :], -1)
            hit = (class_at == wanted).astype(jnp.float32)
            score = (logit_scale * (share - hit)).astype(jnp.bfloat16)
            held.append((block, tile, source, table_at, score))
        for block, tile, source, table_at, score in held:
            rows_acc[block] += lax.dot_general(
                score, table_ref[table_at], (((0,), (0,)), ((), ())),
                preferred_element_type=jnp.float32,
            )
            tiles_acc[tile] += jnp.dot(
                score, rows_ref[source], preferred_element_type=jnp.float32
            )
        return carry

    lax.fori_loop(0, pl.cdiv(meta_ref[0], PAIRS_PER_STEP), step, 0)
    out_ref[...] = rows_acc[:blocks].astype(out_ref.dtype)
    size = grad_refs[0].shape[0]
    stored = run_copies(
        [
            (needed, out_ref.at[pl.ds(start, size)], ref)
            for ref, (needed, start) in zip(grad_refs, line.spans(place))
        ],
        sems,
    )
    if share_refs[0].dtype == jnp.float32:
        kept = pltpu.make_async_copy(tiles_acc.at[pl.ds(0, tiles)], share_refs[0], sem)
        kept.start()
        kept.wait()
    elif n_shares == 1:
        share_refs[0][...] = tiles_acc[:tiles].astype(jnp.bfloat16)
    else:
        shard, width = share_refs[0].shape[2], share_refs[0].shape[-1]
        for core, ref in enumerate(share_refs):
            for y in range(ref.shape[1]):
                start = pl.multiple_of(((2 * y + core) ^ lane_part) * width, width)
                for x in range(ref.shape[0]):
                    ref[x, y] = tiles_acc[
                        pl.ds(x * shard, shard), :, pl.ds(start, width)
                    ].astype(jnp.bfloat16)
    stored()


def score(line, blocks, codes, meta, hit, rows, tables):
    tiles = sum(table.shape[0] for table in tables)
    return pl.pallas_call(
        functools.partial(score_kernel, line, len(tables), blocks, tiles),
        out_shape=jax.ShapeDtypeStruct((2, blocks, BR), jnp.float32),
        in_specs=[SMEM, SMEM, VMEM] + [ANY] * (len(rows) + len(tables)),
        out_specs=VMEM,
        scratch_shapes=[
            pltpu.VMEM((blocks, BR, D), jnp.bfloat16),
            pltpu.VMEM((tiles, TILE, D), jnp.bfloat16),
            pltpu.VMEM((blocks + 8, BR), jnp.float32),
            pltpu.VMEM((blocks + 8, BR), jnp.float32),
            pltpu.SemaphoreType.DMA((len(rows) + len(tables),)),
        ],
        compiler_params=pltpu.CompilerParams(vmem_limit_bytes=VMEM_BYTES),
    )(codes, meta, hit, *rows, *tables)


def grads(line, blocks, codes, meta, hit, stats, rows, tables, carry, shares, shares_spec):
    tiles = sum(table.shape[0] for table in tables)
    carries = () if carry is None else (carry,)
    operands = (codes, meta, hit, *stats, *rows, *tables, *carries)
    outs = pl.pallas_call(
        functools.partial(
            grad_kernel, line, len(tables), len(stats), blocks, tiles, len(carries), len(shares)
        ),
        out_shape=(
            *(jax.ShapeDtypeStruct(part.shape, jnp.bfloat16) for part in rows),
            *shares,
            jax.ShapeDtypeStruct((blocks, BR), jnp.float32),
        ),
        in_specs=[SMEM, SMEM] + [VMEM] * (1 + len(stats))
        + [ANY] * (len(rows) + len(tables) + len(carries)),
        out_specs=(*[ANY] * len(rows), *[shares_spec] * len(shares), VMEM),
        scratch_shapes=[
            pltpu.VMEM((blocks, BR, D), jnp.bfloat16),
            pltpu.VMEM((tiles, TILE, D), jnp.bfloat16),
            pltpu.VMEM((blocks, BR), jnp.float32),
            pltpu.VMEM((blocks + 1, BR, D), jnp.float32),
            pltpu.VMEM((tiles + 1, TILE, D), jnp.float32),
            pltpu.VMEM((blocks, BR, D), jnp.bfloat16),
            pltpu.SemaphoreType.DMA((len(rows) + len(tables),)),
            pltpu.SemaphoreType.DMA,
        ],
        compiler_params=pltpu.CompilerParams(vmem_limit_bytes=VMEM_BYTES),
    )(*operands)
    return list(outs[:len(rows)]), list(outs[len(rows):-1]), outs[-1]


def add(first, second):
    return (first.astype(jnp.float32) + second.astype(jnp.float32)).astype(jnp.bfloat16)


class Neighbours:
    def __init__(self, nx, nz, dp):
        self.nx, self.nz, self.dp = nx, nz, dp

    def along_z(self, value, shift, lowest, highest):
        pairs = [
            (z * self.nx + x, (z + shift) * self.nx + x)
            for z in range(lowest, highest) for x in range(self.nx)
        ]
        return lax.ppermute(value, "cls", pairs)

    def around_z(self, value, shift):
        pairs = [
            (z * self.nx + x, (z + shift) % self.nz * self.nx + x)
            for z in range(self.nz) for x in range(self.nx)
        ]
        return lax.ppermute(value, "cls", pairs)

    def over_x(self, value):
        return lax.ppermute(value, "cls", [(c, c ^ 1) for c in range(self.nx * self.nz)])

    def over_y(self, value):
        return lax.ppermute(value, "dp", [(d, d ^ 2) for d in range(self.dp)])

    def over_core(self, value):
        return lax.ppermute(value, "dp", [(d, d ^ 1) for d in range(self.dp)])

    def gather_lists(self, lists, place):
        turned = [lists] + [self.around_z(lists, shift) for shift in range(1, self.nz)]
        twice = jnp.stack((turned[::-1] * 2)[:2 * self.nz - 1])
        return lax.dynamic_slice_in_dim(twice, self.nz - 1 - place, self.nz, axis=0)

    def gather_rows(self, rows):
        from_left, from_right = [rows], [rows]
        for step in range(1, self.nz):
            from_left.append(self.along_z(from_left[-1], 1, step - 1, self.nz - 1))
            from_right.append(self.along_z(from_right[-1], -1, 1, self.nz + 1 - step))
        return from_left + from_right[1:]

    def gather_stats(self, stats):
        return [stats] + [self.around_z(stats, shift) for shift in range(1, self.nz)]

    def gather_tables(self, table, core):
        half = table.shape[0] // 2
        sent = lax.dynamic_slice_in_dim(table, core * half, half, axis=0)
        mine = self.over_x(sent)
        return [table, mine, self.over_core(mine)]

    def sum_rows(self, parts):
        own, lefts, rights = parts[0], parts[1:self.nz], parts[self.nz:]
        going_right = going_left = None
        for step in range(self.nz - 1, 0, -1):
            right, left = rights[step - 1], lefts[step - 1]
            if going_right is not None:
                right, left = add(right, going_right), add(left, going_left)
            going_right = self.along_z(right, 1, 0, self.nz - step)
            going_left = self.along_z(left, -1, step, self.nz)
        return own.astype(jnp.float32) + going_right.astype(jnp.float32) + going_left.astype(jnp.float32)

    def sum_shares(self, kept, sent):
        got = self.over_core(sent)
        half = kept.shape[2] // 2
        x_sent = add(kept[1, :, :half], got[1, :, :half])
        y_sent = add(kept[:, 1, half:], got[:, 1, half:])
        x_got, y_got = self.over_x(x_sent), self.over_y(y_sent)
        x_kept = [add(add(kept[0, y, :half], got[0, y, :half]), x_got[y]) for y in range(2)]
        y_kept = [add(add(kept[x, 0, half:], got[x, 0, half:]), y_got[x]) for x in range(2)]
        low = x_kept[0].astype(jnp.float32) + self.over_y(x_kept[1]).astype(jnp.float32)
        high = y_kept[0].astype(jnp.float32) + self.over_x(y_kept[1]).astype(jnp.float32)
        return jnp.concatenate([low, high], axis=0)


class Groups:
    def __init__(self, nz, dp):
        self.nx, self.nz, self.dp = 1, nz, dp

    def gather_lists(self, lists, place):
        return lax.all_gather(lists, "cls")

    def gather_rows(self, rows):
        return [lax.all_gather(rows, "cls", tiled=True)]

    def gather_stats(self, stats):
        return list(lax.all_gather(stats, "cls"))

    def gather_tables(self, table, core):
        return [table]

    def sum_rows(self, parts):
        return lax.psum_scatter(
            parts[0], "cls", scatter_dimension=0, tiled=True
        ).astype(jnp.float32)

    def sum_shares(self, share):
        return lax.psum_scatter(
            share, "dp", scatter_dimension=2, tiled=True
        ).astype(jnp.float32)


def per_device(moves, chunks, embeddings, proxies, hard_tiles, tile_count, labels):
    nx, nz, dp = moves.nx, moves.nz, moves.dp
    blocks = hard_tiles.shape[0]
    shard_tiles = proxies.shape[0] // TILE
    tiles = nx * shard_tiles
    me, part = lax.axis_index("cls"), lax.axis_index("dp")
    place, column = me // nx, me % nx

    emb_exact = embeddings.astype(jnp.float32)
    inverse_norm = lax.rsqrt(jnp.sum(emb_exact * emb_exact, axis=1, keepdims=True) + epsilon)
    unit_exact = emb_exact * inverse_norm
    unit_blocks = unit_exact.astype(jnp.bfloat16).reshape(blocks, BR, D)

    position = labels.reshape(blocks, BR) - hard_tiles[:, 0:1] * TILE
    entries = jnp.arange(K, dtype=jnp.int32)
    used = jnp.where(entries[None, :] < tile_count[:, None], hard_tiles, -1)
    lists = moves.gather_lists(jnp.concatenate([used, position], axis=1), place)
    tables = moves.gather_tables(proxies.reshape(shard_tiles, TILE, D), part % 2)

    per_chunk = blocks // chunks
    held = nz * per_chunk
    room = min(held * K, nz * (blocks * K // (nx * nz)) * nx)
    room = -(-room // PAIRS_PER_STEP) * PAIRS_PER_STEP
    padding = (held * FIELD + tiles) * 2

    losses, row_grads, carry = [], [], None
    for chunk in range(chunks):
        here = slice(chunk * per_chunk, (chunk + 1) * per_chunk)
        rows = moves.gather_rows(unit_blocks[here])
        line = Line(nz, per_chunk, len(rows))
        chunk_lists = lists[:, here].reshape(held, K + BR)
        hit = chunk_lists[:, K:]
        entry = chunk_lists[:, :K].reshape(-1)
        owner = entry // shard_tiles
        mine = (entry >= 0) & (owner // nx == place)
        local = jnp.where(owner % nx == column, 0, shard_tiles) + entry % shard_tiles
        counter = jnp.arange(held * K, dtype=jnp.int32)
        code = ((counter // K) * FIELD + local) * 2 + (counter % K == 0)
        rank = jnp.sum(
            jnp.where(mine[None, :] & (counter[None, :] < counter[:, None]), 1, 0), axis=1
        ).astype(jnp.int32)
        slots = jnp.arange(room, dtype=jnp.int32)
        chosen = mine[None, :] & (rank[None, :] == slots[:, None])
        codes = padding + jnp.sum(
            jnp.where(chosen, code[None, :] - padding, 0), axis=1
        ).astype(jnp.int32)
        meta = jnp.stack([jnp.sum(mine.astype(jnp.int32)), place, part]).astype(jnp.int32)

        stats = moves.gather_stats(score(line, held, codes, meta, hit, rows, tables))
        if chunk < chunks - 1:
            shares = [jax.ShapeDtypeStruct((tiles, TILE, D), jnp.float32)]
            shares_spec = ANY
        elif nx == 1:
            shares = [jax.ShapeDtypeStruct((tiles, TILE, D), jnp.bfloat16)]
            shares_spec = VMEM
        else:
            split = (nx, dp // 2, shard_tiles, TILE, D // dp)
            shares = [jax.ShapeDtypeStruct(split, jnp.bfloat16)] * 2
            shares_spec = VMEM
        partial, share, loss = grads(
            line, held, codes, meta, hit, stats, rows, tables, carry, shares, shares_spec
        )
        carry = share[0]
        row_grads.append(moves.sum_rows(partial))
        losses.append(lax.dynamic_slice_in_dim(loss, place * per_chunk, per_chunk, axis=0))

    proxy_grad = moves.sum_shares(*share).reshape(shard_tiles * TILE, D // dp)
    row_loss = jnp.concatenate(losses, axis=0).reshape(-1)
    grad_flat = jnp.concatenate(row_grads, axis=0).reshape(blocks * BR, D)
    radial = jnp.sum(unit_exact * grad_flat, axis=1, keepdims=True)
    embed_grad = ((grad_flat - unit_exact * radial) * inverse_norm).astype(jnp.bfloat16)
    return (row_loss, embed_grad, proxy_grad)


def solution(mesh):
    placed = (
        P(("dp", "cls"), None),
        P("cls", None),
        P(("dp", "cls"), None),
        P(("dp", "cls")),
        P(("dp", "cls")),
    )
    dp, groups = mesh.shape["dp"], mesh.shape["cls"]
    if (dp, groups) == (4, 8):
        moves, chunks = Neighbours(2, groups // 2, dp), 2
    else:
        moves, chunks = Groups(groups, dp), max(1, groups // 8)
    return jax.shard_map(
        functools.partial(per_device, moves, chunks),
        mesh=mesh,
        in_specs=placed,
        out_specs=(P(("dp", "cls")), P(("dp", "cls"), None), P("cls", "dp")),
        check_vma=False,
    )
```

```python
import functools

import jax
import jax.numpy as jnp
from jax import lax
from jax.experimental import pallas as pl
from jax.experimental.pallas import tpu as pltpu
from jax.sharding import PartitionSpec as P

D = 512
TILE = 128
BR = 128
K = 8
PAIRS_PER_STEP = 4
FIELD = 128
VMEM_BYTES = 60 * 1024 * 1024

logit_scale = 4.0
epsilon = 1e-06
unused_logit = -1e30

SMEM = pl.BlockSpec(memory_space=pltpu.SMEM)
VMEM = pl.BlockSpec(memory_space=pltpu.VMEM)
ANY = pl.BlockSpec(memory_space=pl.ANY)


class Line:
    def __init__(self, places, blocks, pieces):
        self.places, self.blocks, self.pieces = places, blocks, pieces

    def spans(self, place):
        if self.pieces == 1:
            return [(None, 0)]
        spans = [(None, place * self.blocks)]
        for step in range(1, self.places):
            spans.append((place >= step, (place - step) * self.blocks))
        for step in range(1, self.places):
            spans.append((place + step < self.places, (place + step) * self.blocks))
        return spans


def run_copies(jobs, sems):
    copies = []
    for index, (needed, source, target) in enumerate(jobs):
        copy = pltpu.make_async_copy(source, target, sems.at[index])
        copies.append((needed, copy))
        if needed is None:
            copy.start()
        else:
            pl.when(needed)(copy.start)

    def finish():
        for needed, copy in copies:
            if needed is None:
                copy.wait()
            else:
                pl.when(needed)(copy.wait)

    return finish


def load_operands(line, place, core, row_refs, table_refs, rows_ref, table_ref, sems):
    size = row_refs[0].shape[0]
    jobs = [
        (needed, ref, rows_ref.at[pl.ds(start, size)])
        for ref, (needed, start) in zip(row_refs, line.spans(place))
    ]
    jobs.append((None, table_refs[0], table_ref.at[pl.ds(0, table_refs[0].shape[0])]))
    if len(table_refs) > 1:
        half = table_refs[1].shape[0]
        jobs.append((None, table_refs[1], table_ref.at[pl.ds((2 + core) * half, half)]))
        jobs.append((None, table_refs[2], table_ref.at[pl.ds((3 - core) * half, half)]))
    return run_copies(jobs, sems)


def transposed_logits(tile, rows):
    return logit_scale * lax.dot_general(
        tile, rows, (((1,), (1,)), ((), ())), preferred_element_type=jnp.float32
    )


def decode(code):
    return code // (2 * FIELD), (code // 2) % FIELD, (code % 2) == 1


def score_kernel(line, n_tables, blocks, tiles, codes_ref, meta_ref, hit_ref, *refs):
    row_refs, refs = refs[:line.pieces], refs[line.pieces:]
    table_refs, refs = refs[:n_tables], refs[n_tables:]
    stats_ref, rows_ref, table_ref, lse_ref, pos_ref, sems = refs
    finish = load_operands(
        line, meta_ref[1], meta_ref[2] % 2, row_refs, table_refs, rows_ref, table_ref, sems
    )
    lse_ref[...] = jnp.full(lse_ref.shape, unused_logit, jnp.float32)
    pos_ref[...] = jnp.zeros(pos_ref.shape, jnp.float32)
    class_at = lax.broadcasted_iota(jnp.int32, (TILE, BR), 0)
    finish()

    def step(index, carry):
        held = []
        for lane in range(PAIRS_PER_STEP):
            block, tile, first = decode(codes_ref[index * PAIRS_PER_STEP + lane])
            source = jnp.minimum(block, blocks - 1)
            logits = transposed_logits(
                table_ref[jnp.minimum(tile, tiles - 1)], rows_ref[source]
            )
            peak = jnp.max(logits, axis=0, keepdims=True)
            total = jnp.sum(jnp.exp(logits - peak), axis=0, keepdims=True)
            hit = class_at == hit_ref[pl.ds(source, 1), :]
            positive = jnp.sum(jnp.where(hit, logits, 0.0), axis=0, keepdims=True)
            held.append((block, peak + jnp.log(total), jnp.where(first, positive, 0.0)))
        for block, lse, positive in held:
            before = lse_ref[pl.ds(block, 1), :]
            top = jnp.maximum(before, lse)
            lse_ref[pl.ds(block, 1), :] = top + jnp.log(
                jnp.exp(before - top) + jnp.exp(lse - top)
            )
            pos_ref[pl.ds(block, 1), :] += positive
        return carry

    lax.fori_loop(0, pl.cdiv(meta_ref[0], PAIRS_PER_STEP), step, 0)
    stats_ref[0] = lse_ref[:blocks, :]
    stats_ref[1] = pos_ref[:blocks, :]


def grad_kernel(
    line, n_tables, n_stats, blocks, tiles, has_carry, n_shares,
    codes_ref, meta_ref, hit_ref, *refs,
):
    stat_refs, refs = refs[:n_stats], refs[n_stats:]
    row_refs, refs = refs[:line.pieces], refs[line.pieces:]
    table_refs, refs = refs[:n_tables], refs[n_tables:]
    carry_refs, refs = refs[:has_carry], refs[has_carry:]
    grad_refs, refs = refs[:line.pieces], refs[line.pieces:]
    share_refs, refs = refs[:n_shares], refs[n_shares:]
    loss_ref, rows_ref, table_ref, total_ref, rows_acc, tiles_acc, out_ref, sems, sem = refs
    place, lane_part = meta_ref[1], meta_ref[2]
    finish = load_operands(
        line, place, lane_part % 2, row_refs, table_refs, rows_ref, table_ref, sems
    )
    if has_carry:
        carried = pltpu.make_async_copy(carry_refs[0], tiles_acc.at[pl.ds(0, tiles)], sem)
        carried.start()
    else:
        tiles_acc[...] = jnp.zeros(tiles_acc.shape, jnp.float32)
    rows_acc[...] = jnp.zeros(rows_acc.shape, jnp.float32)
    lse = [ref[0] for ref in stat_refs]
    top = functools.reduce(jnp.maximum, lse)
    total = top + jnp.log(sum(jnp.exp(part - top) for part in lse))
    total_ref[...] = total
    loss_ref[...] = total - sum(ref[1] for ref in stat_refs)
    class_at = lax.broadcasted_iota(jnp.int32, (TILE, BR), 0)
    finish()
    if has_carry:
        carried.wait()

    def step(index, carry):
        held = []
        for lane in range(PAIRS_PER_STEP):
            block, tile, first = decode(codes_ref[index * PAIRS_PER_STEP + lane])
            source = jnp.minimum(block, blocks - 1)
            table_at = jnp.minimum(tile, tiles - 1)
            logits = transposed_logits(table_ref[table_at], rows_ref[source])
            share = jnp.exp(logits - total_ref[pl.ds(source, 1), :])
            wanted = jnp.where(first, hit_ref[pl.ds(source, 1), :], -1)
            hit = (class_at == wanted).astype(jnp.float32)
            score = (logit_scale * (share - hit)).astype(jnp.bfloat16)
            held.append((block, tile, source, table_at, score))
        for block, tile, source, table_at, score in held:
            rows_acc[block] += lax.dot_general(
                score, table_ref[table_at], (((0,), (0,)), ((), ())),
                preferred_element_type=jnp.float32,
            )
            tiles_acc[tile] += jnp.dot(
                score, rows_ref[source], preferred_element_type=jnp.float32
            )
        return carry

    lax.fori_loop(0, pl.cdiv(meta_ref[0], PAIRS_PER_STEP), step, 0)
    out_ref[...] = rows_acc[:blocks].astype(out_ref.dtype)
    size = grad_refs[0].shape[0]
    stored = run_copies(
        [
            (needed, out_ref.at[pl.ds(start, size)], ref)
            for ref, (needed, start) in zip(grad_refs, line.spans(place))
        ],
        sems,
    )
    if share_refs[0].dtype == jnp.float32:
        kept = pltpu.make_async_copy(tiles_acc.at[pl.ds(0, tiles)], share_refs[0], sem)
        kept.start()
        kept.wait()
    elif n_shares == 1:
        share_refs[0][...] = tiles_acc[:tiles].astype(jnp.bfloat16)
    else:
        shard, width = share_refs[0].shape[2], share_refs[0].shape[-1]
        for core, ref in enumerate(share_refs):
            for y in range(ref.shape[1]):
                start = pl.multiple_of(((2 * y + core) ^ lane_part) * width, width)
                for x in range(ref.shape[0]):
                    ref[x, y] = tiles_acc[
                        pl.ds(x * shard, shard), :, pl.ds(start, width)
                    ].astype(jnp.bfloat16)
    stored()


def kernel_cost(blocks):
    return pl.CostEstimate(flops=blocks * BR * D, bytes_accessed=blocks * BR * D, transcendentals=0)


def score(line, blocks, codes, meta, hit, rows, tables):
    tiles = sum(table.shape[0] for table in tables)
    return pl.pallas_call(
        functools.partial(score_kernel, line, len(tables), blocks, tiles),
        out_shape=jax.ShapeDtypeStruct((2, blocks, BR), jnp.float32),
        in_specs=[SMEM, SMEM, VMEM] + [ANY] * (len(rows) + len(tables)),
        out_specs=VMEM,
        scratch_shapes=[
            pltpu.VMEM((blocks, BR, D), jnp.bfloat16),
            pltpu.VMEM((tiles, TILE, D), jnp.bfloat16),
            pltpu.VMEM((blocks + 8, BR), jnp.float32),
            pltpu.VMEM((blocks + 8, BR), jnp.float32),
            pltpu.SemaphoreType.DMA((len(rows) + len(tables),)),
        ],
        cost_estimate=kernel_cost(blocks),
        compiler_params=pltpu.CompilerParams(vmem_limit_bytes=VMEM_BYTES),
    )(codes, meta, hit, *rows, *tables)


def grads(line, blocks, codes, meta, hit, stats, rows, tables, carry, shares, shares_spec):
    tiles = sum(table.shape[0] for table in tables)
    carries = () if carry is None else (carry,)
    operands = (codes, meta, hit, *stats, *rows, *tables, *carries)
    outs = pl.pallas_call(
        functools.partial(
            grad_kernel, line, len(tables), len(stats), blocks, tiles, len(carries), len(shares)
        ),
        out_shape=(
            *(jax.ShapeDtypeStruct(part.shape, jnp.bfloat16) for part in rows),
            *shares,
            jax.ShapeDtypeStruct((blocks, BR), jnp.float32),
        ),
        in_specs=[SMEM, SMEM] + [VMEM] * (1 + len(stats))
        + [ANY] * (len(rows) + len(tables) + len(carries)),
        out_specs=(*[ANY] * len(rows), *[shares_spec] * len(shares), VMEM),
        scratch_shapes=[
            pltpu.VMEM((blocks, BR, D), jnp.bfloat16),
            pltpu.VMEM((tiles, TILE, D), jnp.bfloat16),
            pltpu.VMEM((blocks, BR), jnp.float32),
            pltpu.VMEM((blocks + 1, BR, D), jnp.float32),
            pltpu.VMEM((tiles + 1, TILE, D), jnp.float32),
            pltpu.VMEM((blocks, BR, D), jnp.bfloat16),
            pltpu.SemaphoreType.DMA((len(rows) + len(tables),)),
            pltpu.SemaphoreType.DMA,
        ],
        cost_estimate=kernel_cost(blocks),
        compiler_params=pltpu.CompilerParams(vmem_limit_bytes=VMEM_BYTES),
    )(*operands)
    return list(outs[:len(rows)]), list(outs[len(rows):-1]), outs[-1]


def add(first, second):
    return (first.astype(jnp.float32) + second.astype(jnp.float32)).astype(jnp.bfloat16)


class Neighbours:
    def __init__(self, nx, nz, dp):
        self.nx, self.nz, self.dp = nx, nz, dp

    def around_z(self, value, shift):
        pairs = [
            (z * self.nx + x, (z + shift) % self.nz * self.nx + x)
            for z in range(self.nz) for x in range(self.nx)
        ]
        return lax.ppermute(value, "cls", pairs)

    def over_x(self, value):
        return lax.ppermute(value, "cls", [(c, c ^ 1) for c in range(self.nx * self.nz)])

    def over_y(self, value):
        return lax.ppermute(value, "dp", [(d, d ^ 2) for d in range(self.dp)])

    def over_core(self, value):
        return lax.ppermute(value, "dp", [(d, d ^ 1) for d in range(self.dp)])

    def gather_lists(self, lists, place):
        turned = [lists] + [self.around_z(lists, shift) for shift in range(1, self.nz)]
        twice = jnp.stack((turned[::-1] * 2)[:2 * self.nz - 1])
        return lax.dynamic_slice_in_dim(twice, self.nz - 1 - place, self.nz, axis=0)

    def z_groups(self):
        return [[z * self.nx + x for z in range(self.nz)] for x in range(self.nx)]

    def gather_rows(self, rows):
        return [lax.all_gather(rows, "cls", axis_index_groups=self.z_groups(), tiled=True)]

    def gather_stats(self, stats):
        return [stats] + [self.around_z(stats, shift) for shift in range(1, self.nz)]

    def gather_tables(self, table, core):
        half = table.shape[0] // 2
        sent = lax.dynamic_slice_in_dim(table, core * half, half, axis=0)
        mine = self.over_x(sent)
        return [table, mine, self.over_core(mine)]

    def sum_rows(self, parts):
        return lax.psum_scatter(
            parts[0], "cls", scatter_dimension=0, axis_index_groups=self.z_groups(), tiled=True
        ).astype(jnp.float32)

    def sum_shares(self, kept, sent):
        got = self.over_core(sent)
        half = kept.shape[2] // 2
        x_sent = add(kept[1, :, :half], got[1, :, :half])
        y_sent = add(kept[:, 1, half:], got[:, 1, half:])
        x_got, y_got = self.over_x(x_sent), self.over_y(y_sent)
        x_kept = [add(add(kept[0, y, :half], got[0, y, :half]), x_got[y]) for y in range(2)]
        y_kept = [add(add(kept[x, 0, half:], got[x, 0, half:]), y_got[x]) for x in range(2)]
        low = x_kept[0].astype(jnp.float32) + self.over_y(x_kept[1]).astype(jnp.float32)
        high = y_kept[0].astype(jnp.float32) + self.over_x(y_kept[1]).astype(jnp.float32)
        return jnp.concatenate([low, high], axis=0)


class Groups:
    def __init__(self, nz, dp):
        self.nx, self.nz, self.dp = 1, nz, dp

    def gather_lists(self, lists, place):
        return lax.all_gather(lists, "cls")

    def gather_rows(self, rows):
        return [lax.all_gather(rows, "cls", tiled=True)]

    def gather_stats(self, stats):
        return list(lax.all_gather(stats, "cls"))

    def gather_tables(self, table, core):
        return [table]

    def sum_rows(self, parts):
        return lax.psum_scatter(
            parts[0], "cls", scatter_dimension=0, tiled=True
        ).astype(jnp.float32)

    def sum_shares(self, share):
        return lax.psum_scatter(
            share, "dp", scatter_dimension=2, tiled=True
        ).astype(jnp.float32)


def per_device(moves, chunks, embeddings, proxies, hard_tiles, tile_count, labels):
    nx, nz, dp = moves.nx, moves.nz, moves.dp
    blocks = hard_tiles.shape[0]
    shard_tiles = proxies.shape[0] // TILE
    tiles = nx * shard_tiles
    me, part = lax.axis_index("cls"), lax.axis_index("dp")
    place, column = me // nx, me % nx

    emb_exact = embeddings.astype(jnp.float32)
    inverse_norm = lax.rsqrt(jnp.sum(emb_exact * emb_exact, axis=1, keepdims=True) + epsilon)
    unit_exact = emb_exact * inverse_norm
    unit_blocks = unit_exact.astype(jnp.bfloat16).reshape(blocks, BR, D)

    position = labels.reshape(blocks, BR) - hard_tiles[:, 0:1] * TILE
    entries = jnp.arange(K, dtype=jnp.int32)
    used = jnp.where(entries[None, :] < tile_count[:, None], hard_tiles, -1)
    lists = moves.gather_lists(jnp.concatenate([used, position], axis=1), place)
    tables = moves.gather_tables(proxies.reshape(shard_tiles, TILE, D), part % 2)

    per_chunk = blocks // chunks
    held = nz * per_chunk
    room = min(held * K, nz * (blocks * K // (nx * nz)) * nx)
    room = -(-room // PAIRS_PER_STEP) * PAIRS_PER_STEP
    padding = (held * FIELD + tiles) * 2

    gathered = [
        moves.gather_rows(unit_blocks[chunk * per_chunk:(chunk + 1) * per_chunk])
        for chunk in range(chunks)
    ]
    losses, row_grads, carry, partial = [], [], None, None
    for chunk in range(chunks):
        here = slice(chunk * per_chunk, (chunk + 1) * per_chunk)
        rows = gathered[chunk]
        if chunk:
            rows, partial = lax.optimization_barrier((rows, partial))
            row_grads.append(moves.sum_rows(partial))
        line = Line(nz, per_chunk, len(rows))
        chunk_lists = lists[:, here].reshape(held, K + BR)
        hit = chunk_lists[:, K:]
        entry = chunk_lists[:, :K].reshape(-1)
        owner = entry // shard_tiles
        mine = (entry >= 0) & (owner // nx == place)
        local = jnp.where(owner % nx == column, 0, shard_tiles) + entry % shard_tiles
        counter = jnp.arange(held * K, dtype=jnp.int32)
        code = ((counter // K) * FIELD + local) * 2 + (counter % K == 0)
        rank = jnp.sum(
            jnp.where(mine[None, :] & (counter[None, :] < counter[:, None]), 1, 0), axis=1
        ).astype(jnp.int32)
        slots = jnp.arange(room, dtype=jnp.int32)
        chosen = mine[None, :] & (rank[None, :] == slots[:, None])
        codes = padding + jnp.sum(
            jnp.where(chosen, code[None, :] - padding, 0), axis=1
        ).astype(jnp.int32)
        meta = jnp.stack([jnp.sum(mine.astype(jnp.int32)), place, part]).astype(jnp.int32)

        stats = moves.gather_stats(score(line, held, codes, meta, hit, rows, tables))
        if chunk < chunks - 1:
            shares = [jax.ShapeDtypeStruct((tiles, TILE, D), jnp.float32)]
            shares_spec = ANY
        elif nx == 1:
            shares = [jax.ShapeDtypeStruct((tiles, TILE, D), jnp.bfloat16)]
            shares_spec = VMEM
        else:
            split = (nx, dp // 2, shard_tiles, TILE, D // dp)
            shares = [jax.ShapeDtypeStruct(split, jnp.bfloat16)] * 2
            shares_spec = VMEM
        partial, share, loss = grads(
            line, held, codes, meta, hit, stats, rows, tables, carry, shares, shares_spec
        )
        carry = share[0]
        losses.append(lax.dynamic_slice_in_dim(loss, place * per_chunk, per_chunk, axis=0))

    if row_grads:
        partial, row_grads[-1] = lax.optimization_barrier((partial, row_grads[-1]))
    row_grads.append(moves.sum_rows(partial))
    proxy_grad = moves.sum_shares(*share).reshape(shard_tiles * TILE, D // dp)
    row_loss = jnp.concatenate(losses, axis=0).reshape(-1)
    grad_flat = jnp.concatenate(row_grads, axis=0).reshape(blocks * BR, D)
    radial = jnp.sum(unit_exact * grad_flat, axis=1, keepdims=True)
    embed_grad = ((grad_flat - unit_exact * radial) * inverse_norm).astype(jnp.bfloat16)
    return (row_loss, embed_grad, proxy_grad)


def solution(mesh):
    placed = (
        P(("dp", "cls"), None),
        P("cls", None),
        P(("dp", "cls"), None),
        P(("dp", "cls")),
        P(("dp", "cls")),
    )
    dp, groups = mesh.shape["dp"], mesh.shape["cls"]
    if (dp, groups) == (4, 8):
        moves, chunks = Neighbours(2, groups // 2, dp), 2
    else:
        moves, chunks = Groups(groups, dp), max(1, groups // 8)
    return jax.shard_map(
        functools.partial(per_device, moves, chunks),
        mesh=mesh,
        in_specs=placed,
        out_specs=(P(("dp", "cls")), P(("dp", "cls"), None), P("cls", "dp")),
        check_vma=False,
    )
```

```python
import functools

import jax
import jax.numpy as jnp
from jax import lax
from jax.experimental import pallas as pl
from jax.experimental.pallas import tpu as pltpu
from jax.sharding import PartitionSpec as P

D = 512
TILE = 128
BR = 128
K = 8
PAIRS_PER_STEP = 4
FIELD = 128
VMEM_BYTES = 60 * 1024 * 1024

logit_scale = 4.0
epsilon = 1e-06
unused_logit = -1e30

SMEM = pl.BlockSpec(memory_space=pltpu.SMEM)
VMEM = pl.BlockSpec(memory_space=pltpu.VMEM)
ANY = pl.BlockSpec(memory_space=pl.ANY)


def spans(meta_ref, blocks, pieces):
    if pieces == 1:
        return [0]
    return [meta_ref[2 + piece] * blocks for piece in range(pieces)]


def run_copies(jobs, sems, first=0):
    copies = [
        pltpu.make_async_copy(source, target, sems.at[first + index])
        for index, (source, target) in enumerate(jobs)
    ]
    for copy in copies:
        copy.start()
    return copies


def row_jobs(meta_ref, row_refs, rows_ref):
    size = row_refs[0].shape[0]
    return [
        (ref, rows_ref.at[pl.ds(start, size)])
        for ref, start in zip(row_refs, spans(meta_ref, size, len(row_refs)))
    ]


def table_jobs(meta_ref, table_refs, table_ref):
    core = meta_ref[1] % 2
    jobs = [(table_refs[0], table_ref.at[pl.ds(0, table_refs[0].shape[0])])]
    if len(table_refs) > 1:
        half = table_refs[1].shape[0]
        jobs.append((table_refs[1], table_ref.at[pl.ds((2 + core) * half, half)]))
        jobs.append((table_refs[2], table_ref.at[pl.ds((3 - core) * half, half)]))
    return jobs


def transposed_logits(tile, rows):
    return logit_scale * lax.dot_general(
        tile, rows, (((1,), (1,)), ((), ())), preferred_element_type=jnp.float32
    )


def decode(code):
    return code // (2 * FIELD), (code // 2) % FIELD, (code % 2) == 1


def score_kernel(n_rows, n_tables, blocks, tiles, codes_ref, meta_ref, hit_ref, *refs):
    row_refs, refs = refs[:n_rows], refs[n_rows:]
    table_refs, refs = refs[:n_tables], refs[n_tables:]
    stats_ref, rows_ref, table_ref, lse_ref, pos_ref, sems = refs
    copies = run_copies(
        row_jobs(meta_ref, row_refs, rows_ref) + table_jobs(meta_ref, table_refs, table_ref), sems
    )
    lse_ref[...] = jnp.full(lse_ref.shape, unused_logit, jnp.float32)
    pos_ref[...] = jnp.zeros(pos_ref.shape, jnp.float32)
    class_at = lax.broadcasted_iota(jnp.int32, (TILE, BR), 0)
    for copy in copies:
        copy.wait()

    def step(index, carry):
        held = []
        for lane in range(PAIRS_PER_STEP):
            block, tile, first = decode(codes_ref[index * PAIRS_PER_STEP + lane])
            source = jnp.minimum(block, blocks - 1)
            logits = transposed_logits(
                table_ref[jnp.minimum(tile, tiles - 1)], rows_ref[source]
            )
            peak = jnp.max(logits, axis=0, keepdims=True)
            total = jnp.sum(jnp.exp(logits - peak), axis=0, keepdims=True)
            hit = class_at == hit_ref[pl.ds(source, 1), :]
            positive = jnp.sum(jnp.where(hit, logits, 0.0), axis=0, keepdims=True)
            held.append((block, peak + jnp.log(total), jnp.where(first, positive, 0.0)))
        for block, lse, positive in held:
            before = lse_ref[pl.ds(block, 1), :]
            top = jnp.maximum(before, lse)
            lse_ref[pl.ds(block, 1), :] = top + jnp.log(
                jnp.exp(before - top) + jnp.exp(lse - top)
            )
            pos_ref[pl.ds(block, 1), :] += positive
        return carry

    lax.fori_loop(0, pl.cdiv(meta_ref[0], PAIRS_PER_STEP), step, 0)
    stats_ref[0] = lse_ref[:blocks, :]
    stats_ref[1] = pos_ref[:blocks, :]


def grad_kernel(
    n_rows, n_tables, n_stats, blocks, tiles, codes_ref, meta_ref, hit_ref, *refs
):
    stat_refs, refs = refs[:n_stats], refs[n_stats:]
    row_refs, refs = refs[:n_rows], refs[n_rows:]
    table_refs, refs = refs[:n_tables], refs[n_tables:]
    grad_refs, refs = refs[:n_rows], refs[n_rows:]
    scores_ref, loss_ref, rows_ref, table_ref, total_ref, rows_acc, out_ref, sems = refs
    copies = run_copies(
        row_jobs(meta_ref, row_refs, rows_ref) + table_jobs(meta_ref, table_refs, table_ref), sems
    )
    rows_acc[...] = jnp.zeros(rows_acc.shape, jnp.float32)
    lse = [ref[0] for ref in stat_refs]
    top = functools.reduce(jnp.maximum, lse)
    total = top + jnp.log(sum(jnp.exp(part - top) for part in lse))
    total_ref[...] = total
    loss_ref[...] = total - sum(ref[1] for ref in stat_refs)
    class_at = lax.broadcasted_iota(jnp.int32, (TILE, BR), 0)
    for copy in copies:
        copy.wait()

    def step(index, carry):
        held = []
        for lane in range(PAIRS_PER_STEP):
            pair = index * PAIRS_PER_STEP + lane
            block, tile, first = decode(codes_ref[pair])
            source = jnp.minimum(block, blocks - 1)
            table_at = jnp.minimum(tile, tiles - 1)
            logits = transposed_logits(table_ref[table_at], rows_ref[source])
            share = jnp.exp(logits - total_ref[pl.ds(source, 1), :])
            wanted = jnp.where(first, hit_ref[pl.ds(source, 1), :], -1)
            hit = (class_at == wanted).astype(jnp.float32)
            score = (logit_scale * (share - hit)).astype(jnp.bfloat16)
            scores_ref[pair] = score
            held.append((block, table_at, score))
        for block, table_at, score in held:
            rows_acc[block] += lax.dot_general(
                score, table_ref[table_at], (((0,), (0,)), ((), ())),
                preferred_element_type=jnp.float32,
            )
        return carry

    lax.fori_loop(0, pl.cdiv(meta_ref[0], PAIRS_PER_STEP), step, 0)
    out_ref[...] = rows_acc[:blocks].astype(out_ref.dtype)
    size = grad_refs[0].shape[0]
    stored = run_copies(
        [
            (out_ref.at[pl.ds(start, size)], ref)
            for ref, start in zip(grad_refs, spans(meta_ref, size, n_rows))
        ],
        sems,
    )
    for copy in stored:
        copy.wait()


def share_kernel(counts, tiles, *refs):
    chunks = len(counts)
    codes_refs, refs = refs[:chunks], refs[chunks:]
    meta_refs, refs = refs[:chunks], refs[chunks:]
    scores_refs, refs = refs[:chunks], refs[chunks:]
    row_refs = []
    for n_rows, _ in counts:
        row_refs.append(refs[:n_rows])
        refs = refs[n_rows:]
    n_shares = len(refs) - 2 - 2 * chunks
    share_refs, refs = refs[:n_shares], refs[n_shares:]
    rows_refs, refs = refs[:chunks], refs[chunks:]
    held_refs, (tiles_acc, sems) = refs[:chunks], refs[chunks:]
    copies, used = [], 0
    for chunk in range(chunks):
        jobs = row_jobs(meta_refs[chunk], row_refs[chunk], rows_refs[chunk])
        jobs.append((scores_refs[chunk], held_refs[chunk]))
        copies.append(run_copies(jobs, sems, used))
        used += len(jobs)
    tiles_acc[...] = jnp.zeros(tiles_acc.shape, jnp.float32)
    for chunk, (_, blocks) in enumerate(counts):
        for copy in copies[chunk]:
            copy.wait()

        def step(index, carry, chunk=chunk, blocks=blocks):
            for lane in range(PAIRS_PER_STEP):
                pair = index * PAIRS_PER_STEP + lane
                block, tile, first = decode(codes_refs[chunk][pair])
                tiles_acc[tile] += jnp.dot(
                    held_refs[chunk][pair],
                    rows_refs[chunk][jnp.minimum(block, blocks - 1)],
                    preferred_element_type=jnp.float32,
                )
            return carry

        lax.fori_loop(0, pl.cdiv(meta_refs[chunk][0], PAIRS_PER_STEP), step, 0)
    if n_shares == 1:
        share_refs[0][...] = tiles_acc[:tiles].astype(jnp.bfloat16)
    else:
        part = meta_refs[0][1]
        shard, width = share_refs[0].shape[2], share_refs[0].shape[-1]
        for core, ref in enumerate(share_refs):
            for y in range(ref.shape[1]):
                start = pl.multiple_of(((2 * y + core) ^ part) * width, width)
                for x in range(ref.shape[0]):
                    ref[x, y] = tiles_acc[
                        pl.ds(x * shard, shard), :, pl.ds(start, width)
                    ].astype(jnp.bfloat16)


def kernel_cost(blocks):
    return pl.CostEstimate(flops=blocks * BR * D, bytes_accessed=blocks * BR * D, transcendentals=0)


def score(blocks, codes, meta, hit, rows, tables):
    tiles = sum(table.shape[0] for table in tables)
    return pl.pallas_call(
        functools.partial(score_kernel, len(rows), len(tables), blocks, tiles),
        out_shape=jax.ShapeDtypeStruct((2, blocks, BR), jnp.float32),
        in_specs=[SMEM, SMEM, VMEM] + [ANY] * (len(rows) + len(tables)),
        out_specs=VMEM,
        scratch_shapes=[
            pltpu.VMEM((blocks, BR, D), jnp.bfloat16),
            pltpu.VMEM((tiles, TILE, D), jnp.bfloat16),
            pltpu.VMEM((blocks + 8, BR), jnp.float32),
            pltpu.VMEM((blocks + 8, BR), jnp.float32),
            pltpu.SemaphoreType.DMA((len(rows) + len(tables),)),
        ],
        cost_estimate=kernel_cost(blocks),
        compiler_params=pltpu.CompilerParams(vmem_limit_bytes=VMEM_BYTES),
    )(codes, meta, hit, *rows, *tables)


def grads(blocks, codes, meta, hit, stats, rows, tables):
    tiles = sum(table.shape[0] for table in tables)
    outs = pl.pallas_call(
        functools.partial(grad_kernel, len(rows), len(tables), len(stats), blocks, tiles),
        out_shape=(
            *(jax.ShapeDtypeStruct(part.shape, jnp.bfloat16) for part in rows),
            jax.ShapeDtypeStruct((codes.shape[0], TILE, BR), jnp.bfloat16),
            jax.ShapeDtypeStruct((blocks, BR), jnp.float32),
        ),
        in_specs=[SMEM, SMEM] + [VMEM] * (1 + len(stats)) + [ANY] * (len(rows) + len(tables)),
        out_specs=(*[ANY] * len(rows), VMEM, VMEM),
        scratch_shapes=[
            pltpu.VMEM((blocks, BR, D), jnp.bfloat16),
            pltpu.VMEM((tiles, TILE, D), jnp.bfloat16),
            pltpu.VMEM((blocks, BR), jnp.float32),
            pltpu.VMEM((blocks + 1, BR, D), jnp.float32),
            pltpu.VMEM((blocks, BR, D), jnp.bfloat16),
            pltpu.SemaphoreType.DMA((len(rows) + len(tables),)),
        ],
        cost_estimate=kernel_cost(blocks),
        compiler_params=pltpu.CompilerParams(vmem_limit_bytes=VMEM_BYTES),
    )(codes, meta, hit, *stats, *rows, *tables)
    return list(outs[:len(rows)]), outs[len(rows)], outs[-1]


def proxy_shares(codes, metas, scores, rows, tiles, shapes):
    counts = [(len(parts), sum(part.shape[0] for part in parts)) for parts in rows]
    n_rows = sum(count for count, _ in counts)
    return pl.pallas_call(
        functools.partial(share_kernel, counts, tiles),
        out_shape=tuple(jax.ShapeDtypeStruct(shape, jnp.bfloat16) for shape in shapes),
        in_specs=[SMEM] * (2 * len(rows)) + [ANY] * (len(rows) + n_rows),
        out_specs=(VMEM,) * len(shapes),
        scratch_shapes=[
            *(pltpu.VMEM((blocks, BR, D), jnp.bfloat16) for _, blocks in counts),
            *(pltpu.VMEM(score.shape, jnp.bfloat16) for score in scores),
            pltpu.VMEM((tiles + 1, TILE, D), jnp.float32),
            pltpu.SemaphoreType.DMA((len(rows) + n_rows,)),
        ],
        cost_estimate=kernel_cost(sum(blocks for _, blocks in counts)),
        compiler_params=pltpu.CompilerParams(vmem_limit_bytes=VMEM_BYTES),
    )(*codes, *metas, *scores, *[part for parts in rows for part in parts])


def add(first, second):
    return (first.astype(jnp.float32) + second.astype(jnp.float32)).astype(jnp.bfloat16)


class GroupSum:
    def __init__(self, groups, part):
        self.groups, self.part = groups, part

    def step(self, others):
        return others

    def finish(self):
        return lax.psum_scatter(
            self.part, "cls", scatter_dimension=0, axis_index_groups=self.groups, tiled=True
        ).astype(jnp.float32)


class RingSum:
    def __init__(self, moves, parts):
        self.moves, self.own, self.left = moves, parts[0], parts[2:]
        self.moving = moves.to_next(parts[1])

    def step(self, others):
        if self.left:
            self.moving, others = lax.optimization_barrier((self.moving, others))
            self.moving = self.moves.to_next(add(self.moving, self.left.pop(0)))
        return others

    def finish(self):
        while self.left:
            self.step(())
        return self.own.astype(jnp.float32) + self.moving.astype(jnp.float32)


class Neighbours:
    def __init__(self, nx, nz, dp):
        self.nx, self.nz, self.dp = nx, nz, dp
        evens = list(range(0, nz, 2))
        self.ring = [0] + list(range(1, nz, 2)) + evens[:0:-1]
        self.z_groups = [[z * nx + x for z in range(nz)] for x in range(nx)]

    def around_z(self, value, shift):
        pairs = [
            (z * self.nx + x, (z + shift) % self.nz * self.nx + x)
            for z in range(self.nz) for x in range(self.nx)
        ]
        return lax.ppermute(value, "cls", pairs)

    def to_next(self, value):
        pairs = [
            (z * self.nx + x, self.ring[(at + 1) % self.nz] * self.nx + x)
            for at, z in enumerate(self.ring) for x in range(self.nx)
        ]
        return lax.ppermute(value, "cls", pairs)

    def over_x(self, value):
        return lax.ppermute(value, "cls", [(c, c ^ 1) for c in range(self.nx * self.nz)])

    def over_y(self, value):
        return lax.ppermute(value, "dp", [(d, d ^ 2) for d in range(self.dp)])

    def over_core(self, value):
        return lax.ppermute(value, "dp", [(d, d ^ 1) for d in range(self.dp)])

    def sources(self, place):
        where = [0] * self.nz
        for at, z in enumerate(self.ring):
            where[z] = at
        table = [
            [self.ring[(where[z] - step) % self.nz] for step in range(self.nz)]
            for z in range(self.nz)
        ]
        return jnp.asarray(table, jnp.int32)[place]

    def gather_lists(self, lists, place):
        turned = [lists] + [self.around_z(lists, shift) for shift in range(1, self.nz)]
        twice = jnp.stack((turned[::-1] * 2)[:2 * self.nz - 1])
        return lax.dynamic_slice_in_dim(twice, self.nz - 1 - place, self.nz, axis=0)

    def gather_rows(self, rows, by_ring):
        if not by_ring:
            return [lax.all_gather(rows, "cls", axis_index_groups=self.z_groups, tiled=True)]
        pieces = [rows]
        for _ in range(1, self.nz):
            pieces.append(self.to_next(pieces[-1]))
        return pieces

    def gather_stats(self, stats):
        return [stats] + [self.around_z(stats, shift) for shift in range(1, self.nz)]

    def gather_tables(self, table, core):
        half = table.shape[0] // 2
        sent = lax.dynamic_slice_in_dim(table, core * half, half, axis=0)
        mine = self.over_x(sent)
        return [table, mine, self.over_core(mine)]

    def sum_rows(self, parts):
        return RingSum(self, parts) if len(parts) > 1 else GroupSum(self.z_groups, parts[0])

    def share_shapes(self, shard_tiles):
        return [(self.nx, self.dp // 2, shard_tiles, TILE, D // self.dp)] * 2

    def sum_shares(self, kept, sent):
        got = self.over_core(sent)
        half = kept.shape[2] // 2
        x_sent = add(kept[1, :, :half], got[1, :, :half])
        y_sent = add(kept[:, 1, half:], got[:, 1, half:])
        x_got, y_got = lax.optimization_barrier((self.over_x(x_sent), self.over_y(y_sent)))
        x_kept = [add(add(kept[0, y, :half], got[0, y, :half]), x_got[y]) for y in range(2)]
        y_kept = [add(add(kept[x, 0, half:], got[x, 0, half:]), y_got[x]) for x in range(2)]
        low, high = lax.optimization_barrier((self.over_y(x_kept[1]), self.over_x(y_kept[1])))
        low = x_kept[0].astype(jnp.float32) + low.astype(jnp.float32)
        high = y_kept[0].astype(jnp.float32) + high.astype(jnp.float32)
        return jnp.concatenate([low, high], axis=0)


class Groups:
    def __init__(self, nz, dp):
        self.nx, self.nz, self.dp = 1, nz, dp

    def sources(self, place):
        return place[None]

    def gather_lists(self, lists, place):
        return lax.all_gather(lists, "cls")

    def gather_rows(self, rows, by_ring):
        return [lax.all_gather(rows, "cls", tiled=True)]

    def gather_stats(self, stats):
        return list(lax.all_gather(stats, "cls"))

    def gather_tables(self, table, core):
        return [table]

    def sum_rows(self, parts):
        return GroupSum(None, parts[0])

    def share_shapes(self, shard_tiles):
        return [(shard_tiles, TILE, D)]

    def sum_shares(self, share):
        return lax.psum_scatter(
            share, "dp", scatter_dimension=2, tiled=True
        ).astype(jnp.float32)


def pair_codes(lists, shard_tiles, nx, place, column, room):
    entry = lists[:, :K].reshape(-1)
    owner = entry // shard_tiles
    mine = (entry >= 0) & (owner // nx == place)
    local = jnp.where(owner % nx == column, 0, shard_tiles) + entry % shard_tiles
    counter = jnp.arange(entry.shape[0], dtype=jnp.int32)
    code = ((counter // K) * FIELD + local) * 2 + (counter % K == 0)
    rank = jnp.sum(
        jnp.where(mine[None, :] & (counter[None, :] < counter[:, None]), 1, 0), axis=1
    ).astype(jnp.int32)
    slots = jnp.arange(room, dtype=jnp.int32)
    chosen = mine[None, :] & (rank[None, :] == slots[:, None])
    padding = (lists.shape[0] * FIELD + nx * shard_tiles) * 2
    codes = padding + jnp.sum(jnp.where(chosen, code[None, :] - padding, 0), axis=1)
    return codes.astype(jnp.int32), jnp.sum(mine.astype(jnp.int32))


def per_device(moves, sizes, embeddings, proxies, hard_tiles, tile_count, labels):
    nx, nz, dp = moves.nx, moves.nz, moves.dp
    blocks = hard_tiles.shape[0]
    shard_tiles = proxies.shape[0] // TILE
    me, part = lax.axis_index("cls"), lax.axis_index("dp")
    place, column = me // nx, me % nx

    emb_exact = embeddings.astype(jnp.float32)
    inverse_norm = lax.rsqrt(jnp.sum(emb_exact * emb_exact, axis=1, keepdims=True) + epsilon)
    unit_exact = emb_exact * inverse_norm
    unit_blocks = unit_exact.astype(jnp.bfloat16).reshape(blocks, BR, D)

    position = labels.reshape(blocks, BR) - hard_tiles[:, 0:1] * TILE
    entries = jnp.arange(K, dtype=jnp.int32)
    used = jnp.where(entries[None, :] < tile_count[:, None], hard_tiles, -1)
    lists = moves.gather_lists(jnp.concatenate([used, position], axis=1), place)
    tables = moves.gather_tables(proxies.reshape(shard_tiles, TILE, D), part % 2)
    sources = moves.sources(place)

    starts = [sum(sizes[:chunk]) for chunk in range(len(sizes))]
    spots = [slice(start, start + size) for start, size in zip(starts, sizes)]
    gathered = [
        moves.gather_rows(unit_blocks[spot], by_ring=chunk == 0) for chunk, spot in enumerate(spots)
    ]
    losses, row_grads, codes, metas, scores, partial = [], [], [], [], [], None
    for chunk, (spot, size) in enumerate(zip(spots, sizes)):
        held = nz * size
        room = min(held * K, nz * (blocks * K // (nx * nz)) * nx)
        room = -(-room // PAIRS_PER_STEP) * PAIRS_PER_STEP
        chunk_lists = lists[:, spot].reshape(held, K + BR)
        hit = chunk_lists[:, K:]
        code, count = pair_codes(chunk_lists, shard_tiles, nx, place, column, room)
        meta = jnp.concatenate([jnp.stack([count, part]), sources]).astype(jnp.int32)
        if chunk:
            row_grads.append(moves.sum_rows(partial))
            gathered[chunk], _ = lax.optimization_barrier((gathered[chunk], partial))
        rows = gathered[chunk]
        stats = moves.gather_stats(score(held, code, meta, hit, rows, tables))
        if chunk:
            stats = row_grads[-1].step(stats)
        partial, dscore, loss = grads(held, code, meta, hit, stats, rows, tables)
        codes.append(code)
        metas.append(meta)
        scores.append(dscore)
        losses.append(lax.dynamic_slice_in_dim(loss, place * size, size, axis=0))

    if row_grads:
        scores = row_grads[-1].step(scores)
    shares = proxy_shares(
        codes, metas, scores, gathered, nx * shard_tiles, moves.share_shapes(shard_tiles)
    )
    row_grads.append(moves.sum_rows(partial))
    proxy_grad = moves.sum_shares(*shares).reshape(shard_tiles * TILE, D // dp)
    row_loss = jnp.concatenate(losses, axis=0).reshape(-1)
    grad_flat = jnp.concatenate([total.finish() for total in row_grads], axis=0).reshape(blocks * BR, D)
    radial = jnp.sum(unit_exact * grad_flat, axis=1, keepdims=True)
    embed_grad = ((grad_flat - unit_exact * radial) * inverse_norm).astype(jnp.bfloat16)
    return (row_loss, embed_grad, proxy_grad)


def solution(mesh):
    placed = (
        P(("dp", "cls"), None),
        P("cls", None),
        P(("dp", "cls"), None),
        P(("dp", "cls")),
        P(("dp", "cls")),
    )
    dp, groups = mesh.shape["dp"], mesh.shape["cls"]
    if (dp, groups) == (4, 8):
        moves, sizes = Neighbours(2, groups // 2, dp), [4, 4]
    else:
        chunks = max(1, groups // 8)
        moves, sizes = Groups(groups, dp), [8 // chunks] * chunks
    return jax.shard_map(
        functools.partial(per_device, moves, sizes),
        mesh=mesh,
        in_specs=placed,
        out_specs=(P(("dp", "cls")), P(("dp", "cls"), None), P("cls", "dp")),
        check_vma=False,
    )
```

```python
import functools

import jax
import jax.numpy as jnp
from jax import lax
from jax.experimental import pallas as pl
from jax.experimental.pallas import tpu as pltpu
from jax.sharding import PartitionSpec as P

D = 512
TILE = 128
BR = 128
K = 8
PAIRS_PER_STEP = 4
FIELD = 128
PIECES = 4
VMEM_BYTES = 60 * 1024 * 1024

logit_scale = 4.0
epsilon = 1e-06
unused_logit = -1e30

SMEM = pl.BlockSpec(memory_space=pltpu.SMEM)
VMEM = pl.BlockSpec(memory_space=pltpu.VMEM)
ANY = pl.BlockSpec(memory_space=pl.ANY)


def run_copies(jobs, sems, first=0):
    copies = [
        pltpu.make_async_copy(source, target, sems.at[first + index])
        for index, (source, target) in enumerate(jobs)
    ]
    for copy in copies:
        copy.start()
    return copies


def row_jobs(row_refs, rows_ref):
    size = row_refs[0].shape[0]
    return [
        (ref, rows_ref.at[pl.ds(piece * size, size)]) for piece, ref in enumerate(row_refs)
    ]


def aligned(refs, row):
    parts = [ref[row] for ref in refs]
    if len(refs) != PIECES:
        return parts
    size = parts[0].shape[0] // PIECES
    return [
        jnp.concatenate(
            [part[(piece ^ away) * size:((piece ^ away) + 1) * size] for piece in range(PIECES)]
        )
        for away, part in enumerate(parts)
    ]


def table_jobs(meta_ref, table_refs, table_ref):
    core = meta_ref[1] % 2
    jobs = [(table_refs[0], table_ref.at[pl.ds(0, table_refs[0].shape[0])])]
    if len(table_refs) > 1:
        half = table_refs[1].shape[0]
        jobs.append((table_refs[1], table_ref.at[pl.ds((2 + core) * half, half)]))
        jobs.append((table_refs[2], table_ref.at[pl.ds((3 - core) * half, half)]))
    return jobs


def transposed_logits(tile, rows):
    return logit_scale * lax.dot_general(
        tile, rows, (((1,), (1,)), ((), ())), preferred_element_type=jnp.float32
    )


def decode(code):
    return code // (2 * FIELD), (code // 2) % FIELD, (code % 2) == 1


def score_kernel(n_rows, n_tables, blocks, tiles, codes_ref, meta_ref, hit_ref, *refs):
    row_refs, refs = refs[:n_rows], refs[n_rows:]
    table_refs, refs = refs[:n_tables], refs[n_tables:]
    stats_ref, rows_ref, table_ref, lse_ref, pos_ref, sems = refs
    copies = run_copies(
        row_jobs(row_refs, rows_ref) + table_jobs(meta_ref, table_refs, table_ref), sems
    )
    lse_ref[...] = jnp.full(lse_ref.shape, unused_logit, jnp.float32)
    pos_ref[...] = jnp.zeros(pos_ref.shape, jnp.float32)
    class_at = lax.broadcasted_iota(jnp.int32, (TILE, BR), 0)
    for copy in copies:
        copy.wait()

    def step(index, carry):
        held = []
        for lane in range(PAIRS_PER_STEP):
            block, tile, first = decode(codes_ref[index * PAIRS_PER_STEP + lane])
            source = jnp.minimum(block, blocks - 1)
            logits = transposed_logits(
                table_ref[jnp.minimum(tile, tiles - 1)], rows_ref[source]
            )
            peak = jnp.max(logits, axis=0, keepdims=True)
            total = jnp.sum(jnp.exp(logits - peak), axis=0, keepdims=True)
            hit = class_at == hit_ref[pl.ds(source, 1), :]
            positive = jnp.sum(jnp.where(hit, logits, 0.0), axis=0, keepdims=True)
            held.append((block, peak + jnp.log(total), jnp.where(first, positive, 0.0)))
        for block, lse, positive in held:
            before = lse_ref[pl.ds(block, 1), :]
            top = jnp.maximum(before, lse)
            lse_ref[pl.ds(block, 1), :] = top + jnp.log(
                jnp.exp(before - top) + jnp.exp(lse - top)
            )
            pos_ref[pl.ds(block, 1), :] += positive
        return carry

    lax.fori_loop(0, pl.cdiv(meta_ref[0], PAIRS_PER_STEP), step, 0)
    stats_ref[0] = lse_ref[:blocks, :]
    stats_ref[1] = pos_ref[:blocks, :]


def make_totals(stat_refs, total_ref, loss_ref):
    lse = aligned(stat_refs, 0)
    top = functools.reduce(jnp.maximum, lse)
    total = top + jnp.log(sum(jnp.exp(part - top) for part in lse))
    total_ref[...] = total
    loss_ref[...] = total - sum(aligned(stat_refs, 1))


def pair_score(code, blocks, tiles, rows_ref, table_ref, hit_ref, total_ref, class_at):
    block, tile, first = decode(code)
    source = jnp.minimum(block, blocks - 1)
    table_at = jnp.minimum(tile, tiles - 1)
    logits = transposed_logits(table_ref[table_at], rows_ref[source])
    share = jnp.exp(logits - total_ref[pl.ds(source, 1), :])
    wanted = jnp.where(first, hit_ref[pl.ds(source, 1), :], -1)
    hit = (class_at == wanted).astype(jnp.float32)
    return (logit_scale * (share - hit)).astype(jnp.bfloat16)


def row_terms(score, tile):
    return lax.dot_general(
        score, tile, (((0,), (0,)), ((), ())), preferred_element_type=jnp.float32
    )


def grad_kernel(
    n_rows, n_tables, n_stats, blocks, tiles, codes_ref, meta_ref, hit_ref, *refs
):
    stat_refs, refs = refs[:n_stats], refs[n_stats:]
    row_refs, refs = refs[:n_rows], refs[n_rows:]
    table_refs, refs = refs[:n_tables], refs[n_tables:]
    grad_refs, refs = refs[:n_rows], refs[n_rows:]
    scores_ref, loss_ref, rows_ref, table_ref, total_ref, rows_acc, out_ref, sems = refs
    copies = run_copies(
        row_jobs(row_refs, rows_ref) + table_jobs(meta_ref, table_refs, table_ref), sems
    )
    rows_acc[...] = jnp.zeros(rows_acc.shape, jnp.float32)
    make_totals(stat_refs, total_ref, loss_ref)
    class_at = lax.broadcasted_iota(jnp.int32, (TILE, BR), 0)
    for copy in copies:
        copy.wait()

    def step(index, carry):
        held = []
        for lane in range(PAIRS_PER_STEP):
            pair = index * PAIRS_PER_STEP + lane
            score = pair_score(
                codes_ref[pair], blocks, tiles, rows_ref, table_ref, hit_ref, total_ref, class_at
            )
            scores_ref[pair] = score
            held.append(score)
        for lane, score in enumerate(held):
            block, tile, _ = decode(codes_ref[index * PAIRS_PER_STEP + lane])
            rows_acc[block] += row_terms(score, table_ref[jnp.minimum(tile, tiles - 1)])
        return carry

    lax.fori_loop(0, pl.cdiv(meta_ref[0], PAIRS_PER_STEP), step, 0)
    out_ref[...] = rows_acc[:blocks].astype(out_ref.dtype)
    size = grad_refs[0].shape[0]
    stored = run_copies(
        [
            (out_ref.at[pl.ds(piece * size, size)], ref)
            for piece, ref in enumerate(grad_refs)
        ],
        sems,
    )
    for copy in stored:
        copy.wait()


def late_grad_kernel(n_rows, n_tables, blocks, tiles, codes_ref, meta_ref, scores_ref, *refs):
    table_refs, refs = refs[:n_tables], refs[n_tables:]
    grad_refs, refs = refs[:n_rows], refs[n_rows:]
    held_ref, table_ref, rows_acc, out_ref, sems = refs
    copies = run_copies([(scores_ref, held_ref)] + table_jobs(meta_ref, table_refs, table_ref), sems)
    rows_acc[...] = jnp.zeros(rows_acc.shape, jnp.float32)
    for copy in copies:
        copy.wait()

    def step(index, carry):
        for lane in range(PAIRS_PER_STEP):
            pair = index * PAIRS_PER_STEP + lane
            block, tile, _ = decode(codes_ref[pair])
            rows_acc[block] += row_terms(held_ref[pair], table_ref[jnp.minimum(tile, tiles - 1)])
        return carry

    lax.fori_loop(0, pl.cdiv(meta_ref[0], PAIRS_PER_STEP), step, 0)
    out_ref[...] = rows_acc[:blocks].astype(out_ref.dtype)
    size = grad_refs[0].shape[0]
    stored = run_copies(
        [
            (out_ref.at[pl.ds(piece * size, size)], ref)
            for piece, ref in enumerate(grad_refs)
        ],
        sems,
    )
    for copy in stored:
        copy.wait()


def share_kernel(counts, n_stats, n_tables, tiles, *refs):
    chunks = len(counts)
    codes_refs, refs = refs[:chunks], refs[chunks:]
    meta_refs, refs = refs[:chunks], refs[chunks:]
    hit_ref, refs = refs[0], refs[1:]
    stat_refs, refs = refs[:n_stats], refs[n_stats:]
    scores_refs, refs = refs[:chunks - 1], refs[chunks - 1:]
    row_refs = []
    for n_rows, _ in counts:
        row_refs.append(refs[:n_rows])
        refs = refs[n_rows:]
    table_refs, refs = refs[:n_tables], refs[n_tables:]
    n_shares = len(refs) - 6 - 2 * chunks + 1
    share_refs, refs = refs[:n_shares], refs[n_shares:]
    (last_ref, loss_ref), refs = refs[:2], refs[2:]
    rows_refs, refs = refs[:chunks], refs[chunks:]
    held_refs, refs = refs[:chunks - 1], refs[chunks - 1:]
    table_ref, total_ref, tiles_acc, sems = refs
    copies, used = [], 0
    for chunk in range(chunks):
        jobs = row_jobs(row_refs[chunk], rows_refs[chunk])
        if chunk < chunks - 1:
            jobs.append((scores_refs[chunk], held_refs[chunk]))
        else:
            jobs += table_jobs(meta_refs[0], table_refs, table_ref)
        copies.append(run_copies(jobs, sems, used))
        used += len(jobs)
    tiles_acc[...] = jnp.zeros(tiles_acc.shape, jnp.float32)
    make_totals(stat_refs, total_ref, loss_ref)
    class_at = lax.broadcasted_iota(jnp.int32, (TILE, BR), 0)
    for chunk, (_, blocks) in enumerate(counts):
        for copy in copies[chunk]:
            copy.wait()

        def step(index, carry, chunk=chunk, blocks=blocks):
            held = []
            for lane in range(PAIRS_PER_STEP):
                pair = index * PAIRS_PER_STEP + lane
                if chunk < chunks - 1:
                    held.append(held_refs[chunk][pair])
                else:
                    score = pair_score(
                        codes_refs[chunk][pair], blocks, tiles, rows_refs[chunk], table_ref,
                        hit_ref, total_ref, class_at,
                    )
                    last_ref[pair] = score
                    held.append(score)
            for lane, score in enumerate(held):
                block, tile, _ = decode(codes_refs[chunk][index * PAIRS_PER_STEP + lane])
                tiles_acc[tile] += jnp.dot(
                    score, rows_refs[chunk][jnp.minimum(block, blocks - 1)],
                    preferred_element_type=jnp.float32,
                )
            return carry

        lax.fori_loop(0, pl.cdiv(meta_refs[chunk][0], PAIRS_PER_STEP), step, 0)
    if n_shares == 1:
        share_refs[0][...] = tiles_acc[:tiles].astype(jnp.bfloat16)
    else:
        part = meta_refs[0][1]
        shard, width = share_refs[0].shape[2], share_refs[0].shape[-1]
        for core, ref in enumerate(share_refs):
            for y in range(ref.shape[1]):
                start = pl.multiple_of(((2 * y + core) ^ part) * width, width)
                for x in range(ref.shape[0]):
                    ref[x, y] = tiles_acc[
                        pl.ds(x * shard, shard), :, pl.ds(start, width)
                    ].astype(jnp.bfloat16)


def kernel_cost(blocks):
    return pl.CostEstimate(flops=blocks * BR * D, bytes_accessed=blocks * BR * D, transcendentals=0)


def score(blocks, codes, meta, hit, rows, tables):
    tiles = sum(table.shape[0] for table in tables)
    return pl.pallas_call(
        functools.partial(score_kernel, len(rows), len(tables), blocks, tiles),
        out_shape=jax.ShapeDtypeStruct((2, blocks, BR), jnp.float32),
        in_specs=[SMEM, SMEM, VMEM] + [ANY] * (len(rows) + len(tables)),
        out_specs=VMEM,
        scratch_shapes=[
            pltpu.VMEM((blocks, BR, D), jnp.bfloat16),
            pltpu.VMEM((tiles, TILE, D), jnp.bfloat16),
            pltpu.VMEM((blocks + 8, BR), jnp.float32),
            pltpu.VMEM((blocks + 8, BR), jnp.float32),
            pltpu.SemaphoreType.DMA((len(rows) + len(tables),)),
        ],
        cost_estimate=kernel_cost(blocks),
        compiler_params=pltpu.CompilerParams(vmem_limit_bytes=VMEM_BYTES),
    )(codes, meta, hit, *rows, *tables)


def grads(blocks, codes, meta, hit, stats, rows, tables):
    tiles = sum(table.shape[0] for table in tables)
    outs = pl.pallas_call(
        functools.partial(grad_kernel, len(rows), len(tables), len(stats), blocks, tiles),
        out_shape=(
            *(jax.ShapeDtypeStruct(part.shape, jnp.bfloat16) for part in rows),
            jax.ShapeDtypeStruct((codes.shape[0], TILE, BR), jnp.bfloat16),
            jax.ShapeDtypeStruct((blocks, BR), jnp.float32),
        ),
        in_specs=[SMEM, SMEM] + [VMEM] * (1 + len(stats)) + [ANY] * (len(rows) + len(tables)),
        out_specs=(*[ANY] * len(rows), VMEM, VMEM),
        scratch_shapes=[
            pltpu.VMEM((blocks, BR, D), jnp.bfloat16),
            pltpu.VMEM((tiles, TILE, D), jnp.bfloat16),
            pltpu.VMEM((blocks, BR), jnp.float32),
            pltpu.VMEM((blocks + 1, BR, D), jnp.float32),
            pltpu.VMEM((blocks, BR, D), jnp.bfloat16),
            pltpu.SemaphoreType.DMA((len(rows) + len(tables),)),
        ],
        cost_estimate=kernel_cost(blocks),
        compiler_params=pltpu.CompilerParams(vmem_limit_bytes=VMEM_BYTES),
    )(codes, meta, hit, *stats, *rows, *tables)
    return list(outs[:len(rows)]), outs[len(rows)], outs[-1]


def late_grads(blocks, code, meta, scores, shapes, tables):
    tiles = sum(table.shape[0] for table in tables)
    return list(pl.pallas_call(
        functools.partial(late_grad_kernel, len(shapes), len(tables), blocks, tiles),
        out_shape=tuple(jax.ShapeDtypeStruct(shape, jnp.bfloat16) for shape in shapes),
        in_specs=[SMEM, SMEM] + [ANY] * (1 + len(tables)),
        out_specs=(ANY,) * len(shapes),
        scratch_shapes=[
            pltpu.VMEM(scores.shape, jnp.bfloat16),
            pltpu.VMEM((tiles, TILE, D), jnp.bfloat16),
            pltpu.VMEM((blocks + 1, BR, D), jnp.float32),
            pltpu.VMEM((blocks, BR, D), jnp.bfloat16),
            pltpu.SemaphoreType.DMA((len(shapes) + len(tables) + 1,)),
        ],
        cost_estimate=kernel_cost(blocks),
        compiler_params=pltpu.CompilerParams(vmem_limit_bytes=VMEM_BYTES),
    )(code, meta, scores, *tables))


def proxy_shares(codes, metas, hit, stats, scores, rows, tables, shapes):
    counts = [(len(parts), sum(part.shape[0] for part in parts)) for parts in rows]
    n_rows = sum(count for count, _ in counts)
    tiles = sum(table.shape[0] for table in tables)
    chunks, blocks = len(counts), counts[-1][1]
    n_copies = chunks - 1 + n_rows + len(tables)
    outs = pl.pallas_call(
        functools.partial(share_kernel, counts, len(stats), len(tables), tiles),
        out_shape=(
            *(jax.ShapeDtypeStruct(shape, jnp.bfloat16) for shape in shapes),
            jax.ShapeDtypeStruct((codes[-1].shape[0], TILE, BR), jnp.bfloat16),
            jax.ShapeDtypeStruct((blocks, BR), jnp.float32),
        ),
        in_specs=[SMEM] * (2 * chunks) + [VMEM] * (1 + len(stats)) + [ANY] * n_copies,
        out_specs=(VMEM,) * (len(shapes) + 2),
        scratch_shapes=[
            *(pltpu.VMEM((held, BR, D), jnp.bfloat16) for _, held in counts),
            *(pltpu.VMEM(score.shape, jnp.bfloat16) for score in scores),
            pltpu.VMEM((tiles, TILE, D), jnp.bfloat16),
            pltpu.VMEM((blocks, BR), jnp.float32),
            pltpu.VMEM((tiles + 1, TILE, D), jnp.float32),
            pltpu.SemaphoreType.DMA((n_copies,)),
        ],
        cost_estimate=kernel_cost(sum(held for _, held in counts)),
        compiler_params=pltpu.CompilerParams(vmem_limit_bytes=VMEM_BYTES),
    )(*codes, *metas, hit, *stats, *scores, *[part for parts in rows for part in parts], *tables)
    return list(outs[:-2]), outs[-2], outs[-1]


def add(first, second):
    return (first.astype(jnp.float32) + second.astype(jnp.float32)).astype(jnp.bfloat16)


class GroupSum:
    def __init__(self, part):
        self.part = part

    def step(self, others):
        return others

    def finish(self):
        return lax.psum_scatter(
            self.part, "cls", scatter_dimension=0, tiled=True
        ).astype(jnp.float32)


class PairSum:
    def __init__(self, moves, parts):
        self.moves, self.parts, self.far = moves, parts, None
        self.passed = moves.over_z(parts[3], 1)
        self.near = moves.over_z(parts[1], 1)

    def step(self, others):
        self.passed, self.near, others = lax.optimization_barrier((self.passed, self.near, others))
        self.far = self.moves.over_z(add(self.passed, self.parts[2]), 2)
        return others

    def hold(self, others):
        self.far, others = lax.optimization_barrier((self.far, others))
        return others

    def finish(self):
        if self.far is None:
            self.far = self.moves.over_z(add(self.passed, self.parts[2]), 2)
        return sum(part.astype(jnp.float32) for part in (self.parts[0], self.near, self.far))


class Neighbours:
    def __init__(self, nx, dp):
        self.nx, self.nz, self.dp = nx, PIECES, dp

    def over_z(self, value, away):
        pairs = [
            (z * self.nx + x, (z ^ away) * self.nx + x)
            for z in range(self.nz) for x in range(self.nx)
        ]
        return lax.ppermute(value, "cls", pairs)

    def over_x(self, value):
        return lax.ppermute(value, "cls", [(c, c ^ 1) for c in range(self.nx * self.nz)])

    def over_y(self, value):
        return lax.ppermute(value, "dp", [(d, d ^ 2) for d in range(self.dp)])

    def over_core(self, value):
        return lax.ppermute(value, "dp", [(d, d ^ 1) for d in range(self.dp)])

    def all_over_z(self, value):
        return [value] + [self.over_z(value, away) for away in range(1, self.nz)]

    def gather(self, chunks, lists, table, core):
        half = table.shape[0] // 2
        sent = lax.dynamic_slice_in_dim(table, core * half, half, axis=0)
        from_x = self.over_x(sent)
        gathered, before = [], None
        for rows in chunks:
            if before is not None:
                rows, before = lax.optimization_barrier((rows, before))
            far, near = self.over_z(rows, 2), self.over_z(rows, 1)
            if before is None:
                far, lists = lax.optimization_barrier((far, lists))
                passed = self.over_z(far, 1)
                lists = self.all_over_z(lists)
                from_x, passed = lax.optimization_barrier((from_x, passed))
                from_core = self.over_core(from_x)
            else:
                passed = self.over_z(far, 1)
            before = (near, passed)
            gathered.append([rows, near, far, passed])
        return gathered, jnp.stack(lists), [table, from_x, from_core]

    def gather_stats(self, stats):
        return self.all_over_z(stats)

    def sum_rows(self, parts):
        return PairSum(self, parts)

    def own(self, loss, place, size):
        return loss[:size]

    def share_shapes(self, shard_tiles):
        return [(self.nx, self.dp // 2, shard_tiles, TILE, D // self.dp)] * 2

    def sum_shares(self, shares, pending):
        kept, sent = shares
        got = self.over_core(sent)
        for total in pending:
            got = total.hold(got)
        half = kept.shape[2] // 2
        x_sent = add(kept[1, :, :half], got[1, :, :half])
        y_sent = add(kept[:, 1, half:], got[:, 1, half:])
        x_got, y_got = lax.optimization_barrier((self.over_x(x_sent), self.over_y(y_sent)))
        x_kept = [add(add(kept[0, y, :half], got[0, y, :half]), x_got[y]) for y in range(2)]
        y_kept = [add(add(kept[x, 0, half:], got[x, 0, half:]), y_got[x]) for x in range(2)]
        low, high = lax.optimization_barrier((self.over_y(x_kept[1]), self.over_x(y_kept[1])))
        low = x_kept[0].astype(jnp.float32) + low.astype(jnp.float32)
        high = y_kept[0].astype(jnp.float32) + high.astype(jnp.float32)
        return jnp.concatenate([low, high], axis=0)


class Groups:
    def __init__(self, nz, dp):
        self.nx, self.nz, self.dp = 1, nz, dp

    def gather(self, chunks, lists, table, core):
        gathered = [[lax.all_gather(rows, "cls", tiled=True)] for rows in chunks]
        return gathered, lax.all_gather(lists, "cls"), [table]

    def gather_stats(self, stats):
        return list(lax.all_gather(stats, "cls"))

    def sum_rows(self, parts):
        return GroupSum(parts[0])

    def own(self, loss, place, size):
        return lax.dynamic_slice_in_dim(loss, place * size, size, axis=0)

    def share_shapes(self, shard_tiles):
        return [(shard_tiles, TILE, D)]

    def sum_shares(self, shares, pending):
        return lax.psum_scatter(
            shares[0], "dp", scatter_dimension=2, tiled=True
        ).astype(jnp.float32)


def pair_codes(lists, shard_tiles, nx, place, column, room):
    entry = lists[:, :K].reshape(-1)
    owner = entry // shard_tiles
    mine = (entry >= 0) & (owner // nx == place)
    local = jnp.where(owner % nx == column, 0, shard_tiles) + entry % shard_tiles
    counter = jnp.arange(entry.shape[0], dtype=jnp.int32)
    code = ((counter // K) * FIELD + local) * 2 + (counter % K == 0)
    rank = jnp.sum(
        jnp.where(mine[None, :] & (counter[None, :] < counter[:, None]), 1, 0), axis=1
    ).astype(jnp.int32)
    slots = jnp.arange(room, dtype=jnp.int32)
    chosen = mine[None, :] & (rank[None, :] == slots[:, None])
    padding = (lists.shape[0] * FIELD + nx * shard_tiles) * 2
    codes = padding + jnp.sum(jnp.where(chosen, code[None, :] - padding, 0), axis=1)
    return codes.astype(jnp.int32), jnp.sum(mine.astype(jnp.int32))


def per_device(moves, sizes, embeddings, proxies, hard_tiles, tile_count, labels):
    nx, nz, dp = moves.nx, moves.nz, moves.dp
    blocks = hard_tiles.shape[0]
    shard_tiles = proxies.shape[0] // TILE
    me, part = lax.axis_index("cls"), lax.axis_index("dp")
    place, column = me // nx, me % nx

    emb_exact = embeddings.astype(jnp.float32)
    inverse_norm = lax.rsqrt(jnp.sum(emb_exact * emb_exact, axis=1, keepdims=True) + epsilon)
    unit_exact = emb_exact * inverse_norm
    unit_blocks = unit_exact.astype(jnp.bfloat16).reshape(blocks, BR, D)

    position = labels.reshape(blocks, BR) - hard_tiles[:, 0:1] * TILE
    entries = jnp.arange(K, dtype=jnp.int32)
    used = jnp.where(entries[None, :] < tile_count[:, None], hard_tiles, -1)
    starts = [sum(sizes[:chunk]) for chunk in range(len(sizes))]
    spots = [slice(start, start + size) for start, size in zip(starts, sizes)]
    gathered, lists, tables = moves.gather(
        [unit_blocks[spot] for spot in spots],
        jnp.concatenate([used, position], axis=1),
        proxies.reshape(shard_tiles, TILE, D),
        part % 2,
    )
    losses, row_grads, codes, metas, scores, partial = [], [], [], [], [], None
    for chunk, (spot, size) in enumerate(zip(spots, sizes)):
        held = nz * size
        room = min(held * K, nz * (blocks * K // (nx * nz)) * nx)
        room = -(-room // PAIRS_PER_STEP) * PAIRS_PER_STEP
        chunk_lists = lists[:, spot].reshape(held, K + BR)
        hit = chunk_lists[:, K:]
        code, count = pair_codes(chunk_lists, shard_tiles, nx, place, column, room)
        meta = jnp.stack([count, part]).astype(jnp.int32)
        if chunk:
            row_grads.append(moves.sum_rows(partial))
            gathered[chunk], _ = lax.optimization_barrier((gathered[chunk], partial))
        rows = gathered[chunk]
        stats = moves.gather_stats(score(held, code, meta, hit, rows, tables))
        if chunk:
            stats = row_grads[-1].step(stats)
        elif len(sizes) > 1 and len(rows) > 1:
            stats, gathered[1][2] = lax.optimization_barrier((stats, gathered[1][2]))
        codes.append(code)
        metas.append(meta)
        if chunk < len(sizes) - 1:
            partial, dscore, loss = grads(held, code, meta, hit, stats, rows, tables)
            scores.append(dscore)
        else:
            shares, dscore, loss = proxy_shares(
                codes, metas, hit, stats, scores, gathered, tables, moves.share_shapes(shard_tiles)
            )
            partial = late_grads(held, code, meta, dscore, [part.shape for part in rows], tables)
        losses.append(moves.own(loss, place, size))
    row_grads.append(moves.sum_rows(partial))

    proxy_grad = moves.sum_shares(shares, row_grads[:-1]).reshape(shard_tiles * TILE, D // dp)
    row_loss = jnp.concatenate(losses, axis=0).reshape(-1)
    grad_flat = jnp.concatenate([total.finish() for total in row_grads], axis=0).reshape(blocks * BR, D)
    radial = jnp.sum(unit_exact * grad_flat, axis=1, keepdims=True)
    embed_grad = ((grad_flat - unit_exact * radial) * inverse_norm).astype(jnp.bfloat16)
    return (row_loss, embed_grad, proxy_grad)


def solution(mesh):
    placed = (
        P(("dp", "cls"), None),
        P("cls", None),
        P(("dp", "cls"), None),
        P(("dp", "cls")),
        P(("dp", "cls")),
    )
    dp, groups = mesh.shape["dp"], mesh.shape["cls"]
    if (dp, groups) == (4, 2 * PIECES):
        moves, sizes = Neighbours(2, dp), [4, 4]
    else:
        chunks = max(1, groups // 8)
        moves, sizes = Groups(groups, dp), [8 // chunks] * chunks
    return jax.shard_map(
        functools.partial(per_device, moves, sizes),
        mesh=mesh,
        in_specs=placed,
        out_specs=(P(("dp", "cls")), P(("dp", "cls"), None), P("cls", "dp")),
        check_vma=False,
    )
```

```python
import functools

import jax
import jax.numpy as jnp
from jax import lax
from jax.experimental import pallas as pl
from jax.experimental.pallas import tpu as pltpu
from jax.sharding import PartitionSpec as P

D = 512
TILE = 128
BR = 128
K = 8
PAIRS_PER_STEP = 4
FIELD = 128
PIECES = 4
VMEM_BYTES = 60 * 1024 * 1024

logit_scale = 4.0
epsilon = 1e-06
unused_logit = -1e30

SMEM = pl.BlockSpec(memory_space=pltpu.SMEM)
VMEM = pl.BlockSpec(memory_space=pltpu.VMEM)
ANY = pl.BlockSpec(memory_space=pl.ANY)


def run_copies(jobs, sems, first=0):
    copies = [
        pltpu.make_async_copy(source, target, sems.at[first + index])
        for index, (source, target) in enumerate(jobs)
    ]
    for copy in copies:
        copy.start()
    return copies


def row_places(meta_ref, refs, blocks):
    if len(refs) == 1:
        return [(refs[0], 0)]
    per_piece = blocks // PIECES
    whole = refs[0].shape[0] // PIECES
    places = [
        (refs[0].at[pl.ds(place * whole, whole)], (meta_ref[2] ^ place) * per_piece)
        for place in range(PIECES)
    ]
    return places + [(ref, piece * per_piece + whole) for piece, ref in enumerate(refs[1:])]


def row_jobs(meta_ref, refs, rows_ref):
    blocks = rows_ref.shape[0]
    return [
        (ref, rows_ref.at[pl.ds(start, ref.shape[0])])
        for ref, start in row_places(meta_ref, refs, blocks)
    ]


def copy_count(parts):
    return len(parts) if len(parts) == 1 else len(parts) - 1 + PIECES


def aligned(refs, row):
    parts = [ref[row] for ref in refs]
    if len(refs) != PIECES:
        return parts
    size = parts[0].shape[0] // PIECES
    return [
        jnp.concatenate(
            [part[(piece ^ away) * size:((piece ^ away) + 1) * size] for piece in range(PIECES)]
        )
        for away, part in enumerate(parts)
    ]


def table_jobs(meta_ref, table_refs, table_ref):
    core = meta_ref[1] % 2
    jobs = [(table_refs[0], table_ref.at[pl.ds(0, table_refs[0].shape[0])])]
    if len(table_refs) > 1:
        half = table_refs[1].shape[0]
        jobs.append((table_refs[1], table_ref.at[pl.ds((2 + core) * half, half)]))
        jobs.append((table_refs[2], table_ref.at[pl.ds((3 - core) * half, half)]))
    return jobs


def transposed_logits(tile, rows):
    return logit_scale * lax.dot_general(
        tile, rows, (((1,), (1,)), ((), ())), preferred_element_type=jnp.float32
    )


def decode(code):
    return code // (2 * FIELD), (code // 2) % FIELD, (code % 2) == 1


def score_kernel(n_rows, n_tables, blocks, tiles, codes_ref, meta_ref, hit_ref, *refs):
    row_refs, refs = refs[:n_rows], refs[n_rows:]
    table_refs, refs = refs[:n_tables], refs[n_tables:]
    stats_ref, rows_ref, table_ref, lse_ref, pos_ref, sems = refs
    copies = run_copies(
        row_jobs(meta_ref, row_refs, rows_ref) + table_jobs(meta_ref, table_refs, table_ref), sems
    )
    lse_ref[...] = jnp.full(lse_ref.shape, unused_logit, jnp.float32)
    pos_ref[...] = jnp.zeros(pos_ref.shape, jnp.float32)
    class_at = lax.broadcasted_iota(jnp.int32, (TILE, BR), 0)
    for copy in copies:
        copy.wait()

    def step(index, carry):
        held = []
        for lane in range(PAIRS_PER_STEP):
            block, tile, first = decode(codes_ref[index * PAIRS_PER_STEP + lane])
            source = jnp.minimum(block, blocks - 1)
            logits = transposed_logits(
                table_ref[jnp.minimum(tile, tiles - 1)], rows_ref[source]
            )
            peak = jnp.max(logits, axis=0, keepdims=True)
            total = jnp.sum(jnp.exp(logits - peak), axis=0, keepdims=True)
            hit = class_at == hit_ref[pl.ds(source, 1), :]
            positive = jnp.sum(jnp.where(hit, logits, 0.0), axis=0, keepdims=True)
            held.append((block, peak + jnp.log(total), jnp.where(first, positive, 0.0)))
        for block, lse, positive in held:
            before = lse_ref[pl.ds(block, 1), :]
            top = jnp.maximum(before, lse)
            lse_ref[pl.ds(block, 1), :] = top + jnp.log(
                jnp.exp(before - top) + jnp.exp(lse - top)
            )
            pos_ref[pl.ds(block, 1), :] += positive
        return carry

    lax.fori_loop(0, pl.cdiv(meta_ref[0], PAIRS_PER_STEP), step, 0)
    stats_ref[0] = lse_ref[:blocks, :]
    stats_ref[1] = pos_ref[:blocks, :]


def make_totals(stat_refs, total_ref, loss_ref):
    lse = aligned(stat_refs, 0)
    top = functools.reduce(jnp.maximum, lse)
    total = top + jnp.log(sum(jnp.exp(part - top) for part in lse))
    total_ref[...] = total
    loss_ref[...] = total - sum(aligned(stat_refs, 1))


def pair_score(code, blocks, tiles, rows_ref, table_ref, hit_ref, total_ref, class_at):
    block, tile, first = decode(code)
    source = jnp.minimum(block, blocks - 1)
    table_at = jnp.minimum(tile, tiles - 1)
    logits = transposed_logits(table_ref[table_at], rows_ref[source])
    share = jnp.exp(logits - total_ref[pl.ds(source, 1), :])
    wanted = jnp.where(first, hit_ref[pl.ds(source, 1), :], -1)
    hit = (class_at == wanted).astype(jnp.float32)
    return (logit_scale * (share - hit)).astype(jnp.bfloat16)


def row_terms(score, tile):
    return lax.dot_general(
        score, tile, (((0,), (0,)), ((), ())), preferred_element_type=jnp.float32
    )


def grad_kernel(
    n_rows, n_tables, n_stats, blocks, tiles, codes_ref, meta_ref, hit_ref, *refs
):
    stat_refs, refs = refs[:n_stats], refs[n_stats:]
    row_refs, refs = refs[:n_rows], refs[n_rows:]
    table_refs, refs = refs[:n_tables], refs[n_tables:]
    grad_refs, refs = refs[:n_rows], refs[n_rows:]
    scores_ref, loss_ref, rows_ref, table_ref, total_ref, rows_acc, out_ref, sems = refs
    copies = run_copies(
        row_jobs(meta_ref, row_refs, rows_ref) + table_jobs(meta_ref, table_refs, table_ref), sems
    )
    rows_acc[...] = jnp.zeros(rows_acc.shape, jnp.float32)
    make_totals(stat_refs, total_ref, loss_ref)
    class_at = lax.broadcasted_iota(jnp.int32, (TILE, BR), 0)
    for copy in copies:
        copy.wait()

    def step(index, carry):
        held = []
        for lane in range(PAIRS_PER_STEP):
            pair = index * PAIRS_PER_STEP + lane
            score = pair_score(
                codes_ref[pair], blocks, tiles, rows_ref, table_ref, hit_ref, total_ref, class_at
            )
            scores_ref[pair] = score
            held.append(score)
        for lane, score in enumerate(held):
            block, tile, _ = decode(codes_ref[index * PAIRS_PER_STEP + lane])
            rows_acc[block] += row_terms(score, table_ref[jnp.minimum(tile, tiles - 1)])
        return carry

    lax.fori_loop(0, pl.cdiv(meta_ref[0], PAIRS_PER_STEP), step, 0)
    out_ref[...] = rows_acc[:blocks].astype(out_ref.dtype)
    stored = run_copies(
        [
            (out_ref.at[pl.ds(start, ref.shape[0])], ref)
            for ref, start in row_places(meta_ref, grad_refs, blocks)
        ],
        sems,
    )
    for copy in stored:
        copy.wait()


def late_grad_kernel(n_rows, n_tables, blocks, tiles, codes_ref, meta_ref, scores_ref, *refs):
    table_refs, refs = refs[:n_tables], refs[n_tables:]
    grad_refs, refs = refs[:n_rows], refs[n_rows:]
    held_ref, table_ref, rows_acc, out_ref, sems = refs
    copies = run_copies([(scores_ref, held_ref)] + table_jobs(meta_ref, table_refs, table_ref), sems)
    rows_acc[...] = jnp.zeros(rows_acc.shape, jnp.float32)
    for copy in copies:
        copy.wait()

    def step(index, carry):
        for lane in range(PAIRS_PER_STEP):
            pair = index * PAIRS_PER_STEP + lane
            block, tile, _ = decode(codes_ref[pair])
            rows_acc[block] += row_terms(held_ref[pair], table_ref[jnp.minimum(tile, tiles - 1)])
        return carry

    lax.fori_loop(0, pl.cdiv(meta_ref[0], PAIRS_PER_STEP), step, 0)
    out_ref[...] = rows_acc[:blocks].astype(out_ref.dtype)
    stored = run_copies(
        [
            (out_ref.at[pl.ds(start, ref.shape[0])], ref)
            for ref, start in row_places(meta_ref, grad_refs, blocks)
        ],
        sems,
    )
    for copy in stored:
        copy.wait()


def share_kernel(counts, n_stats, n_tables, tiles, *refs):
    chunks = len(counts)
    codes_refs, refs = refs[:chunks], refs[chunks:]
    meta_refs, refs = refs[:chunks], refs[chunks:]
    hit_ref, refs = refs[0], refs[1:]
    stat_refs, refs = refs[:n_stats], refs[n_stats:]
    scores_refs, refs = refs[:chunks - 1], refs[chunks - 1:]
    row_refs = []
    for n_rows, _ in counts:
        row_refs.append(refs[:n_rows])
        refs = refs[n_rows:]
    table_refs, refs = refs[:n_tables], refs[n_tables:]
    n_shares = len(refs) - 6 - 2 * chunks + 1
    share_refs, refs = refs[:n_shares], refs[n_shares:]
    (last_ref, loss_ref), refs = refs[:2], refs[2:]
    rows_refs, refs = refs[:chunks], refs[chunks:]
    held_refs, refs = refs[:chunks - 1], refs[chunks - 1:]
    table_ref, total_ref, tiles_acc, sems = refs
    copies, used = [], 0
    for chunk in range(chunks):
        jobs = row_jobs(meta_refs[chunk], row_refs[chunk], rows_refs[chunk])
        if chunk < chunks - 1:
            jobs.append((scores_refs[chunk], held_refs[chunk]))
        else:
            jobs += table_jobs(meta_refs[0], table_refs, table_ref)
        copies.append(run_copies(jobs, sems, used))
        used += len(jobs)
    tiles_acc[...] = jnp.zeros(tiles_acc.shape, jnp.float32)
    make_totals(stat_refs, total_ref, loss_ref)
    class_at = lax.broadcasted_iota(jnp.int32, (TILE, BR), 0)
    for chunk, (_, blocks) in enumerate(counts):
        for copy in copies[chunk]:
            copy.wait()

        def step(index, carry, chunk=chunk, blocks=blocks):
            held = []
            for lane in range(PAIRS_PER_STEP):
                pair = index * PAIRS_PER_STEP + lane
                if chunk < chunks - 1:
                    held.append(held_refs[chunk][pair])
                else:
                    score = pair_score(
                        codes_refs[chunk][pair], blocks, tiles, rows_refs[chunk], table_ref,
                        hit_ref, total_ref, class_at,
                    )
                    last_ref[pair] = score
                    held.append(score)
            for lane, score in enumerate(held):
                block, tile, _ = decode(codes_refs[chunk][index * PAIRS_PER_STEP + lane])
                tiles_acc[tile] += jnp.dot(
                    score, rows_refs[chunk][jnp.minimum(block, blocks - 1)],
                    preferred_element_type=jnp.float32,
                )
            return carry

        lax.fori_loop(0, pl.cdiv(meta_refs[chunk][0], PAIRS_PER_STEP), step, 0)
    if n_shares == 1:
        share_refs[0][...] = tiles_acc[:tiles].astype(jnp.bfloat16)
    else:
        part = meta_refs[0][1]
        shard, width = share_refs[0].shape[2], share_refs[0].shape[-1]
        for core, ref in enumerate(share_refs):
            for y in range(ref.shape[1]):
                start = pl.multiple_of(((2 * y + core) ^ part) * width, width)
                for x in range(ref.shape[0]):
                    ref[x, y] = tiles_acc[
                        pl.ds(x * shard, shard), :, pl.ds(start, width)
                    ].astype(jnp.bfloat16)


def kernel_cost(blocks):
    return pl.CostEstimate(flops=blocks * BR * D, bytes_accessed=blocks * BR * D, transcendentals=0)


def score(blocks, codes, meta, hit, rows, tables):
    tiles = sum(table.shape[0] for table in tables)
    return pl.pallas_call(
        functools.partial(score_kernel, len(rows), len(tables), blocks, tiles),
        out_shape=jax.ShapeDtypeStruct((2, blocks, BR), jnp.float32),
        in_specs=[SMEM, SMEM, VMEM] + [ANY] * (len(rows) + len(tables)),
        out_specs=VMEM,
        scratch_shapes=[
            pltpu.VMEM((blocks, BR, D), jnp.bfloat16),
            pltpu.VMEM((tiles, TILE, D), jnp.bfloat16),
            pltpu.VMEM((blocks + 8, BR), jnp.float32),
            pltpu.VMEM((blocks + 8, BR), jnp.float32),
            pltpu.SemaphoreType.DMA((copy_count(rows) + len(tables),)),
        ],
        cost_estimate=kernel_cost(blocks),
        compiler_params=pltpu.CompilerParams(vmem_limit_bytes=VMEM_BYTES),
    )(codes, meta, hit, *rows, *tables)


def grads(blocks, codes, meta, hit, stats, rows, tables):
    tiles = sum(table.shape[0] for table in tables)
    outs = pl.pallas_call(
        functools.partial(grad_kernel, len(rows), len(tables), len(stats), blocks, tiles),
        out_shape=(
            *(jax.ShapeDtypeStruct(part.shape, jnp.bfloat16) for part in rows),
            jax.ShapeDtypeStruct((codes.shape[0], TILE, BR), jnp.bfloat16),
            jax.ShapeDtypeStruct((blocks, BR), jnp.float32),
        ),
        in_specs=[SMEM, SMEM] + [VMEM] * (1 + len(stats)) + [ANY] * (len(rows) + len(tables)),
        out_specs=(*[ANY] * len(rows), VMEM, VMEM),
        scratch_shapes=[
            pltpu.VMEM((blocks, BR, D), jnp.bfloat16),
            pltpu.VMEM((tiles, TILE, D), jnp.bfloat16),
            pltpu.VMEM((blocks, BR), jnp.float32),
            pltpu.VMEM((blocks + 1, BR, D), jnp.float32),
            pltpu.VMEM((blocks, BR, D), jnp.bfloat16),
            pltpu.SemaphoreType.DMA((copy_count(rows) + len(tables),)),
        ],
        cost_estimate=kernel_cost(blocks),
        compiler_params=pltpu.CompilerParams(vmem_limit_bytes=VMEM_BYTES),
    )(codes, meta, hit, *stats, *rows, *tables)
    return list(outs[:len(rows)]), outs[len(rows)], outs[-1]


def late_grads(blocks, code, meta, scores, shapes, tables):
    tiles = sum(table.shape[0] for table in tables)
    return list(pl.pallas_call(
        functools.partial(late_grad_kernel, len(shapes), len(tables), blocks, tiles),
        out_shape=tuple(jax.ShapeDtypeStruct(shape, jnp.bfloat16) for shape in shapes),
        in_specs=[SMEM, SMEM] + [ANY] * (1 + len(tables)),
        out_specs=(ANY,) * len(shapes),
        scratch_shapes=[
            pltpu.VMEM(scores.shape, jnp.bfloat16),
            pltpu.VMEM((tiles, TILE, D), jnp.bfloat16),
            pltpu.VMEM((blocks + 1, BR, D), jnp.float32),
            pltpu.VMEM((blocks, BR, D), jnp.bfloat16),
            pltpu.SemaphoreType.DMA((copy_count(shapes) + len(tables) + 1,)),
        ],
        cost_estimate=kernel_cost(blocks),
        compiler_params=pltpu.CompilerParams(vmem_limit_bytes=VMEM_BYTES),
    )(code, meta, scores, *tables))


def proxy_shares(codes, metas, hit, stats, scores, rows, tables, shapes):
    counts = [(len(parts), sum(part.shape[0] for part in parts)) for parts in rows]
    n_rows = sum(count for count, _ in counts)
    tiles = sum(table.shape[0] for table in tables)
    chunks, blocks = len(counts), counts[-1][1]
    n_inputs = chunks - 1 + n_rows + len(tables)
    n_copies = chunks - 1 + sum(copy_count(parts) for parts in rows) + len(tables)
    outs = pl.pallas_call(
        functools.partial(share_kernel, counts, len(stats), len(tables), tiles),
        out_shape=(
            *(jax.ShapeDtypeStruct(shape, jnp.bfloat16) for shape in shapes),
            jax.ShapeDtypeStruct((codes[-1].shape[0], TILE, BR), jnp.bfloat16),
            jax.ShapeDtypeStruct((blocks, BR), jnp.float32),
        ),
        in_specs=[SMEM] * (2 * chunks) + [VMEM] * (1 + len(stats)) + [ANY] * n_inputs,
        out_specs=(VMEM,) * (len(shapes) + 2),
        scratch_shapes=[
            *(pltpu.VMEM((held, BR, D), jnp.bfloat16) for _, held in counts),
            *(pltpu.VMEM(score.shape, jnp.bfloat16) for score in scores),
            pltpu.VMEM((tiles, TILE, D), jnp.bfloat16),
            pltpu.VMEM((blocks, BR), jnp.float32),
            pltpu.VMEM((tiles + 1, TILE, D), jnp.float32),
            pltpu.SemaphoreType.DMA((n_copies,)),
        ],
        cost_estimate=kernel_cost(sum(held for _, held in counts)),
        compiler_params=pltpu.CompilerParams(vmem_limit_bytes=VMEM_BYTES),
    )(*codes, *metas, hit, *stats, *scores, *[part for parts in rows for part in parts], *tables)
    return list(outs[:-2]), outs[-2], outs[-1]


def add(first, second):
    return (first.astype(jnp.float32) + second.astype(jnp.float32)).astype(jnp.bfloat16)


class GroupSum:
    def __init__(self, part):
        self.part = part

    def step(self, others):
        return others

    def finish(self):
        return lax.psum_scatter(
            self.part, "cls", scatter_dimension=0, tiled=True
        ).astype(jnp.float32)


class BothSum:
    def __init__(self, moves, parts):
        self.whole = lax.psum_scatter(
            parts[0], "cls", scatter_dimension=0, axis_index_groups=moves.z_groups, tiled=True
        )
        self.pairs = PairSum(moves, parts[1:])

    def step(self, others):
        self.whole, others = lax.optimization_barrier((self.whole, others))
        return self.pairs.step(others)

    def hold(self, others):
        return self.pairs.hold(others)

    def finish(self):
        return jnp.concatenate([self.whole.astype(jnp.float32), self.pairs.finish()])


class PairSum:
    def __init__(self, moves, parts):
        self.moves, self.parts, self.far = moves, parts, None
        self.passed = moves.over_z(parts[3], 1)
        self.near = moves.over_z(parts[1], 1)

    def step(self, others):
        self.passed, self.near, others = lax.optimization_barrier((self.passed, self.near, others))
        self.far = self.moves.over_z(add(self.passed, self.parts[2]), 2)
        return others

    def hold(self, others):
        self.far, others = lax.optimization_barrier((self.far, others))
        return others

    def finish(self):
        if self.far is None:
            self.far = self.moves.over_z(add(self.passed, self.parts[2]), 2)
        return sum(part.astype(jnp.float32) for part in (self.parts[0], self.near, self.far))


class Neighbours:
    def __init__(self, nx, dp):
        self.nx, self.nz, self.dp = nx, PIECES, dp
        self.z_groups = [[z * nx + x for z in range(PIECES)] for x in range(nx)]

    def over_z(self, value, away):
        pairs = [
            (z * self.nx + x, (z ^ away) * self.nx + x)
            for z in range(self.nz) for x in range(self.nx)
        ]
        return lax.ppermute(value, "cls", pairs)

    def over_x(self, value):
        return lax.ppermute(value, "cls", [(c, c ^ 1) for c in range(self.nx * self.nz)])

    def over_y(self, value):
        return lax.ppermute(value, "dp", [(d, d ^ 2) for d in range(self.dp)])

    def over_core(self, value):
        return lax.ppermute(value, "dp", [(d, d ^ 1) for d in range(self.dp)])

    def all_over_z(self, value):
        return [value] + [self.over_z(value, away) for away in range(1, self.nz)]

    def gather(self, chunks, lists, table, core):
        wholes = [
            lax.all_gather(
                rows[:rows.shape[0] // 2], "cls", axis_index_groups=self.z_groups, tiled=True
            )
            for rows in chunks
        ]
        half = table.shape[0] // 2
        sent = lax.dynamic_slice_in_dim(table, core * half, half, axis=0)
        from_x = self.over_x(sent)
        gathered, before = [], None
        for rows, whole in zip(chunks, wholes):
            rows = rows[rows.shape[0] // 2:]
            if before is not None:
                rows, before = lax.optimization_barrier((rows, before))
            far, near = lax.optimization_barrier((self.over_z(rows, 2), self.over_z(rows, 1)))
            if before is None:
                far, near, lists = lax.optimization_barrier((far, near, lists))
                passed = self.over_z(far, 1)
                lists = self.all_over_z(lists)
                from_x, passed = lax.optimization_barrier((from_x, passed))
                from_core = self.over_core(from_x)
            else:
                passed = self.over_z(far, 1)
            before = (near, passed)
            gathered.append([whole, rows, near, far, passed])
        return gathered, jnp.stack(lists), [table, from_x, from_core]

    def gather_stats(self, stats):
        return self.all_over_z(stats)

    def sum_rows(self, parts):
        return BothSum(self, parts)

    def own(self, loss, place, size):
        return loss[:size]

    def share_shapes(self, shard_tiles):
        return [(self.nx, self.dp // 2, shard_tiles, TILE, D // self.dp)] * 2

    def sum_shares(self, shares, pending):
        kept, sent = shares
        got = self.over_core(sent)
        for total in pending:
            got = total.hold(got)
        half = kept.shape[2] // 2
        x_sent = add(kept[1, :, :half], got[1, :, :half])
        y_sent = add(kept[:, 1, half:], got[:, 1, half:])
        x_got, y_got = lax.optimization_barrier((self.over_x(x_sent), self.over_y(y_sent)))
        x_kept = [add(add(kept[0, y, :half], got[0, y, :half]), x_got[y]) for y in range(2)]
        y_kept = [add(add(kept[x, 0, half:], got[x, 0, half:]), y_got[x]) for x in range(2)]
        low, high = lax.optimization_barrier((self.over_y(x_kept[1]), self.over_x(y_kept[1])))
        low = x_kept[0].astype(jnp.float32) + low.astype(jnp.float32)
        high = y_kept[0].astype(jnp.float32) + high.astype(jnp.float32)
        return jnp.concatenate([low, high], axis=0)


class Groups:
    def __init__(self, nz, dp):
        self.nx, self.nz, self.dp = 1, nz, dp

    def gather(self, chunks, lists, table, core):
        gathered = [[lax.all_gather(rows, "cls", tiled=True)] for rows in chunks]
        return gathered, lax.all_gather(lists, "cls"), [table]

    def gather_stats(self, stats):
        return list(lax.all_gather(stats, "cls"))

    def sum_rows(self, parts):
        return GroupSum(parts[0])

    def own(self, loss, place, size):
        return lax.dynamic_slice_in_dim(loss, place * size, size, axis=0)

    def share_shapes(self, shard_tiles):
        return [(shard_tiles, TILE, D)]

    def sum_shares(self, shares, pending):
        return lax.psum_scatter(
            shares[0], "dp", scatter_dimension=2, tiled=True
        ).astype(jnp.float32)


def pair_codes(lists, shard_tiles, nx, place, column, room):
    entry = lists[:, :K].reshape(-1)
    owner = entry // shard_tiles
    mine = (entry >= 0) & (owner // nx == place)
    local = jnp.where(owner % nx == column, 0, shard_tiles) + entry % shard_tiles
    counter = jnp.arange(entry.shape[0], dtype=jnp.int32)
    code = ((counter // K) * FIELD + local) * 2 + (counter % K == 0)
    rank = jnp.sum(
        jnp.where(mine[None, :] & (counter[None, :] < counter[:, None]), 1, 0), axis=1
    ).astype(jnp.int32)
    slots = jnp.arange(room, dtype=jnp.int32)
    chosen = mine[None, :] & (rank[None, :] == slots[:, None])
    padding = (lists.shape[0] * FIELD + nx * shard_tiles) * 2
    codes = padding + jnp.sum(jnp.where(chosen, code[None, :] - padding, 0), axis=1)
    return codes.astype(jnp.int32), jnp.sum(mine.astype(jnp.int32))


def per_device(moves, sizes, embeddings, proxies, hard_tiles, tile_count, labels):
    nx, nz, dp = moves.nx, moves.nz, moves.dp
    blocks = hard_tiles.shape[0]
    shard_tiles = proxies.shape[0] // TILE
    me, part = lax.axis_index("cls"), lax.axis_index("dp")
    place, column = me // nx, me % nx

    emb_exact = embeddings.astype(jnp.float32)
    inverse_norm = lax.rsqrt(jnp.sum(emb_exact * emb_exact, axis=1, keepdims=True) + epsilon)
    unit_exact = emb_exact * inverse_norm
    unit_blocks = unit_exact.astype(jnp.bfloat16).reshape(blocks, BR, D)

    position = labels.reshape(blocks, BR) - hard_tiles[:, 0:1] * TILE
    entries = jnp.arange(K, dtype=jnp.int32)
    used = jnp.where(entries[None, :] < tile_count[:, None], hard_tiles, -1)
    starts = [sum(sizes[:chunk]) for chunk in range(len(sizes))]
    spots = [slice(start, start + size) for start, size in zip(starts, sizes)]
    gathered, lists, tables = moves.gather(
        [unit_blocks[spot] for spot in spots],
        jnp.concatenate([used, position], axis=1),
        proxies.reshape(shard_tiles, TILE, D),
        part % 2,
    )
    losses, row_grads, codes, metas, scores, partial = [], [], [], [], [], None
    for chunk, (spot, size) in enumerate(zip(spots, sizes)):
        held = nz * size
        room = min(held * K, nz * (blocks * K // (nx * nz)) * nx)
        room = -(-room // PAIRS_PER_STEP) * PAIRS_PER_STEP
        chunk_lists = lists[:, spot].reshape(held, K + BR)
        hit = chunk_lists[:, K:]
        code, count = pair_codes(chunk_lists, shard_tiles, nx, place, column, room)
        meta = jnp.stack([count, part, place]).astype(jnp.int32)
        if chunk:
            row_grads.append(moves.sum_rows(partial))
            gathered[chunk], _ = lax.optimization_barrier((gathered[chunk], partial))
        rows = gathered[chunk]
        stats = moves.gather_stats(score(held, code, meta, hit, rows, tables))
        if chunk:
            stats = row_grads[-1].step(stats)
        elif len(sizes) > 1 and len(rows) > 1:
            stats, gathered[1][3] = lax.optimization_barrier((stats, gathered[1][3]))
        codes.append(code)
        metas.append(meta)
        if chunk < len(sizes) - 1:
            partial, dscore, loss = grads(held, code, meta, hit, stats, rows, tables)
            scores.append(dscore)
        else:
            shares, dscore, loss = proxy_shares(
                codes, metas, hit, stats, scores, gathered, tables, moves.share_shapes(shard_tiles)
            )
            partial = late_grads(held, code, meta, dscore, [part.shape for part in rows], tables)
        losses.append(moves.own(loss, place, size))
    row_grads.append(moves.sum_rows(partial))

    proxy_grad = moves.sum_shares(shares, row_grads[:-1]).reshape(shard_tiles * TILE, D // dp)
    row_loss = jnp.concatenate(losses, axis=0).reshape(-1)
    grad_flat = jnp.concatenate([total.finish() for total in row_grads], axis=0).reshape(blocks * BR, D)
    radial = jnp.sum(unit_exact * grad_flat, axis=1, keepdims=True)
    embed_grad = ((grad_flat - unit_exact * radial) * inverse_norm).astype(jnp.bfloat16)
    return (row_loss, embed_grad, proxy_grad)


def solution(mesh):
    placed = (
        P(("dp", "cls"), None),
        P("cls", None),
        P(("dp", "cls"), None),
        P(("dp", "cls")),
        P(("dp", "cls")),
    )
    dp, groups = mesh.shape["dp"], mesh.shape["cls"]
    if (dp, groups) == (4, 2 * PIECES):
        moves, sizes = Neighbours(2, dp), [4, 4]
    else:
        chunks = max(1, groups // 8)
        moves, sizes = Groups(groups, dp), [8 // chunks] * chunks
    return jax.shard_map(
        functools.partial(per_device, moves, sizes),
        mesh=mesh,
        in_specs=placed,
        out_specs=(P(("dp", "cls")), P(("dp", "cls"), None), P("cls", "dp")),
        check_vma=False,
    )
```

```python
import functools

import jax
import jax.numpy as jnp
import numpy as np
from jax import lax
from jax.experimental import pallas as pl
from jax.experimental.pallas import tpu as pltpu
from jax.sharding import PartitionSpec as P

D = 512
TILE = 128
BR = 128
K = 8
PAIRS_PER_STEP = 4
FIELD = 128
PIECES = 4
VMEM_BYTES = 60 * 1024 * 1024
SPARE_BYTES = 4 * 1024 * 1024

logit_scale = 4.0
epsilon = 1e-06
unused_logit = -1e30

SMEM = pl.BlockSpec(memory_space=pltpu.SMEM)
VMEM = pl.BlockSpec(memory_space=pltpu.VMEM)
ANY = pl.BlockSpec(memory_space=pl.ANY)


def run_copies(jobs, sems, first=0):
    copies = [
        pltpu.make_async_copy(source, target, sems.at[first + index])
        for index, (source, target) in enumerate(jobs)
    ]
    for copy in copies:
        copy.start()
    return copies


def row_places(meta_ref, refs, blocks):
    size = blocks // PIECES
    if len(refs) > 1:
        return [(ref, piece * size) for piece, ref in enumerate(refs)]
    return [
        (refs[0].at[pl.ds(place * size, size)], (meta_ref[2] ^ place) * size)
        for place in range(PIECES)
    ]


def row_jobs(meta_ref, refs, rows_ref):
    return [
        (ref, rows_ref.at[pl.ds(start, ref.shape[0])])
        for ref, start in row_places(meta_ref, refs, rows_ref.shape[0])
    ]


def store_rows(meta_ref, rows_acc, out_ref, grad_refs, sems):
    blocks = out_ref.shape[0]
    out_ref[...] = rows_acc[:blocks].astype(out_ref.dtype)
    return run_copies(
        [
            (out_ref.at[pl.ds(start, ref.shape[0])], ref)
            for ref, start in row_places(meta_ref, grad_refs, blocks)
        ],
        sems,
    )


def aligned(refs, row, turned):
    parts = [ref[row] for ref in refs]
    if not turned:
        return parts
    size = parts[0].shape[0] // PIECES
    return [
        jnp.concatenate(
            [part[(piece ^ away) * size:((piece ^ away) + 1) * size] for piece in range(PIECES)]
        )
        for away, part in enumerate(parts)
    ]


def table_jobs(meta_ref, table_refs, table_ref):
    core = meta_ref[1] % 2
    jobs = [(table_refs[0], table_ref.at[pl.ds(0, table_refs[0].shape[0])])]
    if len(table_refs) > 1:
        half = table_refs[1].shape[0]
        jobs.append((table_refs[1], table_ref.at[pl.ds((2 + core) * half, half)]))
        jobs.append((table_refs[2], table_ref.at[pl.ds((3 - core) * half, half)]))
    return jobs


def transposed_logits(tile, rows):
    return logit_scale * lax.dot_general(
        tile, rows, (((1,), (1,)), ((), ())), preferred_element_type=jnp.float32
    )


def decode(code):
    return code // (2 * FIELD), (code // 2) % FIELD, (code % 2) == 1


def score_kernel(n_rows, n_tables, blocks, tiles, codes_ref, meta_ref, hit_ref, *refs):
    row_refs, refs = refs[:n_rows], refs[n_rows:]
    table_refs, refs = refs[:n_tables], refs[n_tables:]
    stats_ref, rows_ref, table_ref, lse_ref, pos_ref, sems = refs
    row_copies = run_copies(row_jobs(meta_ref, row_refs, rows_ref), sems)
    table_copies = run_copies(table_jobs(meta_ref, table_refs, table_ref), sems, PIECES)
    lse_ref[...] = jnp.full(lse_ref.shape, unused_logit, jnp.float32)
    pos_ref[...] = jnp.zeros(pos_ref.shape, jnp.float32)
    class_at = lax.broadcasted_iota(jnp.int32, (TILE, BR), 0)
    for copy in row_copies:
        copy.wait()

    def normalise(block, carry):
        exact = rows_ref[block].astype(jnp.float32)
        norm = lax.rsqrt(jnp.sum(exact * exact, axis=1, keepdims=True) + epsilon)
        rows_ref[block] = (exact * norm).astype(jnp.bfloat16)
        return carry

    lax.fori_loop(0, blocks, normalise, 0)
    for copy in table_copies:
        copy.wait()

    def step(index, carry):
        held = []
        for lane in range(PAIRS_PER_STEP):
            block, tile, first = decode(codes_ref[index * PAIRS_PER_STEP + lane])
            source = jnp.minimum(block, blocks - 1)
            logits = transposed_logits(
                table_ref[jnp.minimum(tile, tiles - 1)], rows_ref[source]
            )
            peak = jnp.max(logits, axis=0, keepdims=True)
            total = jnp.sum(jnp.exp(logits - peak), axis=0, keepdims=True)
            hit = class_at == hit_ref[pl.ds(source, 1), :]
            positive = jnp.sum(jnp.where(hit, logits, 0.0), axis=0, keepdims=True)
            held.append((block, peak + jnp.log(total), jnp.where(first, positive, 0.0)))
        for block, lse, positive in held:
            before = lse_ref[pl.ds(block, 1), :]
            top = jnp.maximum(before, lse)
            lse_ref[pl.ds(block, 1), :] = top + jnp.log(
                jnp.exp(before - top) + jnp.exp(lse - top)
            )
            pos_ref[pl.ds(block, 1), :] += positive
        return carry

    lax.fori_loop(0, pl.cdiv(meta_ref[0], PAIRS_PER_STEP), step, 0)
    stats_ref[0] = lse_ref[:blocks, :]
    stats_ref[1] = pos_ref[:blocks, :]


def make_totals(stat_refs, turned, total_ref, loss_ref):
    lse = aligned(stat_refs, 0, turned)
    top = functools.reduce(jnp.maximum, lse)
    total = top + jnp.log(sum(jnp.exp(part - top) for part in lse))
    total_ref[...] = total
    loss_ref[...] = total - sum(aligned(stat_refs, 1, turned))


def pair_score(code, blocks, tiles, rows_ref, table_ref, hit_ref, total_ref, class_at):
    block, tile, first = decode(code)
    source = jnp.minimum(block, blocks - 1)
    table_at = jnp.minimum(tile, tiles - 1)
    logits = transposed_logits(table_ref[table_at], rows_ref[source])
    share = jnp.exp(logits - total_ref[pl.ds(source, 1), :])
    wanted = jnp.where(first, hit_ref[pl.ds(source, 1), :], -1)
    hit = (class_at == wanted).astype(jnp.float32)
    return (logit_scale * (share - hit)).astype(jnp.bfloat16)


def row_terms(score, tile):
    return lax.dot_general(
        score, tile, (((0,), (0,)), ((), ())), preferred_element_type=jnp.float32
    )


def grad_kernel(
    n_grads, n_tables, n_stats, turned, blocks, tiles, codes_ref, meta_ref, hit_ref, *refs
):
    stat_refs, refs = refs[:n_stats], refs[n_stats:]
    unit_ref, refs = refs[0], refs[1:]
    table_refs, refs = refs[:n_tables], refs[n_tables:]
    grad_refs, refs = refs[:n_grads], refs[n_grads:]
    scores_ref, loss_ref, rows_ref, table_ref, total_ref, rows_acc, out_ref, sems = refs
    copies = run_copies(
        [(unit_ref, rows_ref)] + table_jobs(meta_ref, table_refs, table_ref), sems, PIECES
    )
    rows_acc[...] = jnp.zeros(rows_acc.shape, jnp.float32)
    make_totals(stat_refs, turned, total_ref, loss_ref)
    class_at = lax.broadcasted_iota(jnp.int32, (TILE, BR), 0)
    for copy in copies:
        copy.wait()

    def step(index, carry):
        held = []
        for lane in range(PAIRS_PER_STEP):
            pair = index * PAIRS_PER_STEP + lane
            score = pair_score(
                codes_ref[pair], blocks, tiles, rows_ref, table_ref, hit_ref, total_ref, class_at
            )
            scores_ref[pair] = score
            held.append(score)
        for lane, score in enumerate(held):
            block, tile, _ = decode(codes_ref[index * PAIRS_PER_STEP + lane])
            rows_acc[block] += row_terms(score, table_ref[jnp.minimum(tile, tiles - 1)])
        return carry

    lax.fori_loop(0, pl.cdiv(meta_ref[0], PAIRS_PER_STEP), step, 0)
    for copy in store_rows(meta_ref, rows_acc, out_ref, grad_refs, sems):
        copy.wait()


def last_kernel(sizes, n_grads, n_tables, n_stats, turned, n_shares, tiles, *refs):
    chunks, blocks = len(sizes), sizes[-1]
    codes_refs, refs = refs[:chunks], refs[chunks:]
    meta_refs, refs = refs[:chunks], refs[chunks:]
    hit_ref, refs = refs[0], refs[1:]
    stat_refs, refs = refs[:n_stats], refs[n_stats:]
    scores_refs, refs = refs[:chunks - 1], refs[chunks - 1:]
    unit_refs, refs = refs[:chunks], refs[chunks:]
    table_refs, refs = refs[:n_tables], refs[n_tables:]
    grad_refs, refs = refs[:n_grads], refs[n_grads:]
    share_refs, refs = refs[:n_shares], refs[n_shares:]
    loss_ref, refs = refs[0], refs[1:]
    rows_ref, early_ref, held_ref, table_ref, total_ref, rows_acc, out_ref, *refs = refs
    tiles_acc, sems, early_sems, row_sems = refs
    codes_ref, meta_ref = codes_refs[-1], meta_refs[-1]
    copies = run_copies(
        [(unit_refs[-1], rows_ref)] + table_jobs(meta_ref, table_refs, table_ref), sems
    )


    def fetch(chunk):
        early = early_ref.at[pl.ds(0, sizes[chunk])]
        return run_copies(
            [(unit_refs[chunk], early), (scores_refs[chunk], held_ref)], early_sems
        )

    early = fetch(0) if chunks > 1 else []
    rows_acc[...] = jnp.zeros(rows_acc.shape, jnp.float32)
    tiles_acc[...] = jnp.zeros(tiles_acc.shape, jnp.float32)
    make_totals(stat_refs, turned, total_ref, loss_ref)
    class_at = lax.broadcasted_iota(jnp.int32, (TILE, BR), 0)
    for copy in copies:
        copy.wait()

    def step(index, carry):
        held = [
            pair_score(
                codes_ref[index * PAIRS_PER_STEP + lane], blocks, tiles, rows_ref, table_ref,
                hit_ref, total_ref, class_at,
            )
            for lane in range(PAIRS_PER_STEP)
        ]
        for lane, score in enumerate(held):
            block, tile, _ = decode(codes_ref[index * PAIRS_PER_STEP + lane])
            rows_acc[block] += row_terms(score, table_ref[jnp.minimum(tile, tiles - 1)])
            tiles_acc[tile] += jnp.dot(
                score, rows_ref[jnp.minimum(block, blocks - 1)],
                preferred_element_type=jnp.float32,
            )
        return carry

    lax.fori_loop(0, pl.cdiv(meta_ref[0], PAIRS_PER_STEP), step, 0)
    stored = store_rows(meta_ref, rows_acc, out_ref, grad_refs, row_sems)
    for chunk in range(chunks - 1):
        for copy in early if chunk == 0 else fetch(chunk):
            copy.wait()

        def early_step(index, carry, chunk=chunk):
            for lane in range(PAIRS_PER_STEP):
                pair = index * PAIRS_PER_STEP + lane
                block, tile, _ = decode(codes_refs[chunk][pair])
                tiles_acc[tile] += jnp.dot(
                    held_ref[pair],
                    early_ref[jnp.minimum(block, sizes[chunk] - 1)],
                    preferred_element_type=jnp.float32,
                )
            return carry

        lax.fori_loop(0, pl.cdiv(meta_refs[chunk][0], PAIRS_PER_STEP), early_step, 0)
    if n_shares == 1:
        share_refs[0][...] = tiles_acc[:tiles].astype(jnp.bfloat16)
    else:
        part = meta_ref[1]
        shard, width = share_refs[0].shape[2], share_refs[0].shape[-1]
        for core, ref in enumerate(share_refs):
            for y in range(ref.shape[1]):
                start = pl.multiple_of(((2 * y + core) ^ part) * width, width)
                for x in range(ref.shape[0]):
                    ref[x, y] = tiles_acc[
                        pl.ds(x * shard, shard), :, pl.ds(start, width)
                    ].astype(jnp.bfloat16)
    for copy in stored:
        copy.wait()


def kernel_cost(blocks):
    return pl.CostEstimate(flops=blocks * BR * D, bytes_accessed=blocks * BR * D, transcendentals=0)


def limit(*scratch):
    total = 0
    for shape, dtype in scratch:
        total += int(np.prod(shape)) * jnp.dtype(dtype).itemsize
    return pltpu.CompilerParams(vmem_limit_bytes=min(VMEM_BYTES, total + SPARE_BYTES))


def rows_of(blocks):
    return (blocks, BR, D), jnp.bfloat16


def score(blocks, codes, meta, hit, rows, tables):
    tiles = sum(table.shape[0] for table in tables)
    table_room = ((tiles, TILE, D), jnp.bfloat16)
    return pl.pallas_call(
        functools.partial(score_kernel, len(rows), len(tables), blocks, tiles),
        out_shape=(
            jax.ShapeDtypeStruct((2, blocks, BR), jnp.float32),
            jax.ShapeDtypeStruct(*rows_of(blocks)),
        ),
        in_specs=[SMEM, SMEM, VMEM] + [ANY] * (len(rows) + len(tables)),
        out_specs=(VMEM, VMEM),
        scratch_shapes=[
            pltpu.VMEM(*table_room),
            pltpu.VMEM((blocks + 8, BR), jnp.float32),
            pltpu.VMEM((blocks + 8, BR), jnp.float32),
            pltpu.SemaphoreType.DMA((PIECES + len(tables),)),
        ],
        cost_estimate=kernel_cost(blocks),
        compiler_params=limit(rows_of(blocks), table_room),
    )(codes, meta, hit, *rows, *tables)


def grads(blocks, codes, meta, hit, stats, turned, unit, tables, shapes):
    tiles = sum(table.shape[0] for table in tables)
    table_room = ((tiles, TILE, D), jnp.bfloat16)
    acc_room = ((blocks + 1, BR, D), jnp.float32)
    scores = ((codes.shape[0], TILE, BR), jnp.bfloat16)
    outs = pl.pallas_call(
        functools.partial(
            grad_kernel, len(shapes), len(tables), len(stats), turned, blocks, tiles
        ),
        out_shape=(
            *(jax.ShapeDtypeStruct(shape, jnp.bfloat16) for shape in shapes),
            jax.ShapeDtypeStruct(*scores),
            jax.ShapeDtypeStruct((blocks, BR), jnp.float32),
        ),
        in_specs=[SMEM, SMEM] + [VMEM] * (1 + len(stats)) + [ANY] * (1 + len(tables)),
        out_specs=(*[ANY] * len(shapes), VMEM, VMEM),
        scratch_shapes=[
            pltpu.VMEM(*rows_of(blocks)),
            pltpu.VMEM(*table_room),
            pltpu.VMEM((blocks, BR), jnp.float32),
            pltpu.VMEM(*acc_room),
            pltpu.VMEM(*rows_of(blocks)),
            pltpu.SemaphoreType.DMA((PIECES + 1 + len(tables),)),
        ],
        cost_estimate=kernel_cost(blocks),
        compiler_params=limit(rows_of(2 * blocks), table_room, acc_room, scores),
    )(codes, meta, hit, *stats, unit, *tables)
    return list(outs[:len(shapes)]), outs[len(shapes)], outs[-1]


def last_grads(codes, metas, hit, stats, turned, scores, units, tables, shapes, share_shapes):
    sizes = [unit.shape[0] for unit in units]
    tiles = sum(table.shape[0] for table in tables)
    chunks, blocks = len(sizes), sizes[-1]
    n_inputs = 2 * chunks - 1 + len(tables)
    table_room = ((tiles, TILE, D), jnp.bfloat16)
    acc_room = ((blocks + 1, BR, D), jnp.float32)
    tiles_room = ((tiles + 1, TILE, D), jnp.float32)
    early_room = rows_of(max(sizes[:-1], default=PIECES))
    kept = ((scores or codes)[0].shape[0], TILE, BR), jnp.bfloat16
    outs = pl.pallas_call(
        functools.partial(
            last_kernel, sizes, len(shapes), len(tables), len(stats), turned,
            len(share_shapes), tiles,
        ),
        out_shape=(
            *(jax.ShapeDtypeStruct(shape, jnp.bfloat16) for shape in shapes),
            *(jax.ShapeDtypeStruct(shape, jnp.bfloat16) for shape in share_shapes),
            jax.ShapeDtypeStruct((blocks, BR), jnp.float32),
        ),
        in_specs=[SMEM] * (2 * chunks) + [VMEM] * (1 + len(stats)) + [ANY] * n_inputs,
        out_specs=(*[ANY] * len(shapes), *[VMEM] * len(share_shapes), VMEM),
        scratch_shapes=[
            pltpu.VMEM(*rows_of(blocks)),
            pltpu.VMEM(*early_room),
            pltpu.VMEM(*kept),
            pltpu.VMEM(*table_room),
            pltpu.VMEM((blocks, BR), jnp.float32),
            pltpu.VMEM(*acc_room),
            pltpu.VMEM(*rows_of(blocks)),
            pltpu.VMEM(*tiles_room),
            pltpu.SemaphoreType.DMA((1 + len(tables),)),
            pltpu.SemaphoreType.DMA((2,)),
            pltpu.SemaphoreType.DMA((PIECES,)),
        ],
        cost_estimate=kernel_cost(sum(sizes)),
        compiler_params=limit(
            rows_of(2 * blocks), early_room, kept, table_room, table_room, acc_room, tiles_room
        ),
    )(*codes, *metas, hit, *stats, *scores, *units, *tables)
    cut = len(shapes)
    return list(outs[:cut]), list(outs[cut:-1]), outs[-1]


def add(first, second):
    return (first.astype(jnp.float32) + second.astype(jnp.float32)).astype(jnp.bfloat16)


class GroupSum:
    def __init__(self, part, groups):
        self.total = lax.psum_scatter(
            part, "cls", scatter_dimension=0, axis_index_groups=groups, tiled=True
        )

    def hold(self, others):
        self.total, others = lax.optimization_barrier((self.total, others))
        return others

    def finish(self):
        return self.total.astype(jnp.float32)


class PairSum:
    def __init__(self, moves, parts, passed):
        self.parts = parts
        self.near = moves.over_z(parts[1], 1)
        self.far = moves.over_z(add(passed, parts[2]), 2)

    def finish(self):
        return sum(part.astype(jnp.float32) for part in (self.parts[0], self.near, self.far))


class Neighbours:
    def __init__(self, nx, dp):
        self.nx, self.nz, self.dp, self.turned = nx, PIECES, dp, True
        self.z_groups = [[z * nx + x for z in range(PIECES)] for x in range(nx)]

    def over_z(self, value, away):
        pairs = [
            (z * self.nx + x, (z ^ away) * self.nx + x)
            for z in range(self.nz) for x in range(self.nx)
        ]
        return lax.ppermute(value, "cls", pairs)

    def over_x(self, value):
        return lax.ppermute(value, "cls", [(c, c ^ 1) for c in range(self.nx * self.nz)])

    def over_y(self, value):
        return lax.ppermute(value, "dp", [(d, d ^ 2) for d in range(self.dp)])

    def over_core(self, value):
        return lax.ppermute(value, "dp", [(d, d ^ 1) for d in range(self.dp)])

    def all_over_z(self, value):
        return [value] + [self.over_z(value, away) for away in range(1, self.nz)]

    def gather(self, needed, chunks, lists, table, core, prepare):
        def moves(first, lists, table, core):
            half = table.shape[0] // 2
            sent = lax.dynamic_slice_in_dim(table, core * half, half, axis=0)
            far, near, from_x = lax.optimization_barrier(
                (self.over_z(first, 2), self.over_z(first, 1), self.over_x(sent))
            )
            passed, from_core = self.over_z(far, 1), self.over_core(from_x)
            return (near, far, passed), (from_x, from_core), prepare(
                jnp.stack(self.all_over_z(lists))
            )

        first, second = chunks
        whole = lax.all_gather(second, "cls", axis_index_groups=self.z_groups, tiled=True)
        pieces, tables, prepared = self.together(needed, moves, first, lists, table, core)
        return [[first, *pieces], [whole]], [table, *tables], prepared

    def grad_shapes(self, size, last):
        return [(size, BR, D)] * PIECES if last else [(PIECES * size, BR, D)]

    def gather_stats(self, stats):
        return self.all_over_z(stats)

    def sum_rows(self, parts):
        return GroupSum(parts[0], self.z_groups)

    def together(self, needed, work, *operands):
        def no_work(*operands):
            return jax.tree.map(
                lambda out: jnp.zeros(out.shape, out.dtype), jax.eval_shape(work, *operands)
            )

        return lax.cond(needed, work, no_work, *operands)

    def first_moves(self, parts, shares):
        return self.over_z(parts[3], 1), self.over_core(shares[1])

    def sum_last(self, results, pending):
        parts, shares, loss, (passed, got) = results
        for total in pending:
            got = total.hold(got)
        return PairSum(self, parts, passed), self.sum_shares(shares[0], got), loss

    def order(self, place):
        return place

    def own(self, loss, place, size):
        return loss[:size]

    def share_shapes(self, shard_tiles):
        return [(self.nx, self.dp // 2, shard_tiles, TILE, D // self.dp)] * 2

    def sum_shares(self, kept, got):
        half = kept.shape[2] // 2
        x_sent = add(kept[1, :, :half], got[1, :, :half])
        y_sent = add(kept[:, 1, half:], got[:, 1, half:])
        x_got, y_got = lax.optimization_barrier((self.over_x(x_sent), self.over_y(y_sent)))
        x_kept = [add(add(kept[0, y, :half], got[0, y, :half]), x_got[y]) for y in range(2)]
        y_kept = [add(add(kept[x, 0, half:], got[x, 0, half:]), y_got[x]) for x in range(2)]
        low, high = lax.optimization_barrier((self.over_y(x_kept[1]), self.over_x(y_kept[1])))
        low = x_kept[0].astype(jnp.float32) + low.astype(jnp.float32)
        high = y_kept[0].astype(jnp.float32) + high.astype(jnp.float32)
        return jnp.concatenate([low, high], axis=0)


class Groups:
    def __init__(self, nz, dp):
        self.nx, self.nz, self.dp, self.turned = 1, nz, dp, False

    def gather(self, needed, chunks, lists, table, core, prepare):
        gathered = [[lax.all_gather(rows, "cls", tiled=True)] for rows in chunks]
        return gathered, [table], prepare(lax.all_gather(lists, "cls"))

    def grad_shapes(self, size, last):
        return [(self.nz * size, BR, D)]

    def gather_stats(self, stats):
        return list(lax.all_gather(stats, "cls"))

    def sum_rows(self, parts):
        return GroupSum(parts[0], None)

    def together(self, needed, work, *operands):
        return work(*operands)

    def first_moves(self, parts, shares):
        return ()

    def sum_last(self, results, pending):
        parts, shares, loss, _ = results
        return self.sum_rows(parts), self.sum_shares(shares), loss

    def order(self, place):
        return jnp.zeros_like(place)

    def own(self, loss, place, size):
        return lax.dynamic_slice_in_dim(loss, place * size, size, axis=0)

    def share_shapes(self, shard_tiles):
        return [(shard_tiles, TILE, D)]

    def sum_shares(self, shares):
        return lax.psum_scatter(
            shares[0], "dp", scatter_dimension=2, tiled=True
        ).astype(jnp.float32)


def pair_codes(lists, shard_tiles, nx, place, column, room):
    entry = lists[:, :K].reshape(-1)
    owner = entry // shard_tiles
    mine = (entry >= 0) & (owner // nx == place)
    local = jnp.where(owner % nx == column, 0, shard_tiles) + entry % shard_tiles
    counter = jnp.arange(entry.shape[0], dtype=jnp.int32)
    code = ((counter // K) * FIELD + local) * 2 + (counter % K == 0)
    rank = jnp.sum(
        jnp.where(mine[None, :] & (counter[None, :] < counter[:, None]), 1, 0), axis=1
    ).astype(jnp.int32)
    slots = jnp.arange(room, dtype=jnp.int32)
    chosen = mine[None, :] & (rank[None, :] == slots[:, None])
    padding = (lists.shape[0] * FIELD + nx * shard_tiles) * 2
    codes = padding + jnp.sum(jnp.where(chosen, code[None, :] - padding, 0), axis=1)
    return codes.astype(jnp.int32), jnp.sum(mine.astype(jnp.int32))


def per_device(moves, sizes, embeddings, proxies, hard_tiles, tile_count, labels):
    nx, nz, dp = moves.nx, moves.nz, moves.dp
    blocks = hard_tiles.shape[0]
    shard_tiles = proxies.shape[0] // TILE
    me, part = lax.axis_index("cls"), lax.axis_index("dp")
    place, column = me // nx, me % nx

    emb_exact = embeddings.astype(jnp.float32)
    inverse_norm = lax.rsqrt(jnp.sum(emb_exact * emb_exact, axis=1, keepdims=True) + epsilon)
    unit_exact = emb_exact * inverse_norm
    row_blocks = embeddings.reshape(blocks, BR, D)

    position = labels.reshape(blocks, BR) - hard_tiles[:, 0:1] * TILE
    entries = jnp.arange(K, dtype=jnp.int32)
    used = jnp.where(entries[None, :] < tile_count[:, None], hard_tiles, -1)
    starts = [sum(sizes[:chunk]) for chunk in range(len(sizes))]
    spots = [slice(start, start + size) for start, size in zip(starts, sizes)]
    held = [nz * size for size in sizes]
    last = len(sizes) - 1
    needed = tile_count[0] > 0

    def prepare(lists):
        prepared = []
        for spot, blocks_held in zip(spots, held):
            room = min(blocks_held * K, nz * (blocks * K // (nx * nz)) * nx)
            room = -(-room // PAIRS_PER_STEP) * PAIRS_PER_STEP
            chunk_lists = lists[:, spot].reshape(blocks_held, K + BR)
            code, count = pair_codes(chunk_lists, shard_tiles, nx, place, column, room)
            meta = jnp.stack([count, part, moves.order(place)]).astype(jnp.int32)
            prepared.append((code, meta, chunk_lists[:, K:]))
        return prepared

    gathered, tables, prepared = moves.gather(
        needed,
        [row_blocks[spot] for spot in spots],
        jnp.concatenate([used, position], axis=1),
        proxies.reshape(shard_tiles, TILE, D),
        part % 2,
        prepare,
    )

    def early_work(gathered, tables, prepared):
        stats, units = [], []
        for rows, (code, meta, hit), blocks_held in zip(gathered, prepared, held):
            parts, unit = score(blocks_held, code, meta, hit, rows, tables)
            stats.append(moves.gather_stats(parts))
            units.append(unit)
        made = [
            grads(
                held[chunk], *prepared[chunk], stats[chunk], moves.turned, units[chunk], tables,
                moves.grad_shapes(sizes[chunk], False),
            )
            for chunk in range(last)
        ]
        return stats[-1], units, made

    def last_work(tables, prepared, stats, units, scores):
        codes, metas, hits = zip(*prepared)
        parts, shares, loss = last_grads(
            codes, metas, hits[-1], stats, moves.turned, scores, units, tables,
            moves.grad_shapes(sizes[-1], True), moves.share_shapes(shard_tiles),
        )
        return parts, shares, loss, moves.first_moves(parts, shares)

    stats, units, made = moves.together(needed, early_work, gathered, tables, prepared)
    row_grads = [moves.sum_rows(partial) for partial, _, _ in made]
    scores = [dscore for _, dscore, _ in made]
    losses = [moves.own(loss, place, size) for (_, _, loss), size in zip(made, sizes)]
    results = moves.together(needed, last_work, tables, prepared, stats, units, scores)
    last_sum, shares, loss = moves.sum_last(results, row_grads)
    row_grads.append(last_sum)
    losses.append(moves.own(loss, place, sizes[-1]))

    proxy_grad = shares.reshape(shard_tiles * TILE, D // dp)
    row_loss = jnp.concatenate(losses, axis=0).reshape(-1)
    grad_flat = jnp.concatenate([total.finish() for total in row_grads], axis=0)
    grad_flat = grad_flat.reshape(blocks * BR, D)
    radial = jnp.sum(unit_exact * grad_flat, axis=1, keepdims=True)
    embed_grad = ((grad_flat - unit_exact * radial) * inverse_norm).astype(jnp.bfloat16)
    return (row_loss, embed_grad, proxy_grad)


def solution(mesh):
    placed = (
        P(("dp", "cls"), None),
        P("cls", None),
        P(("dp", "cls"), None),
        P(("dp", "cls")),
        P(("dp", "cls")),
    )
    dp, groups = mesh.shape["dp"], mesh.shape["cls"]
    if (dp, groups) == (4, 2 * PIECES):
        moves, sizes = Neighbours(2, dp), [4, 4]
    else:
        chunks = max(1, groups // 8)
        moves, sizes = Groups(groups, dp), [8 // chunks] * chunks
    return jax.shard_map(
        functools.partial(per_device, moves, sizes),
        mesh=mesh,
        in_specs=placed,
        out_specs=(P(("dp", "cls")), P(("dp", "cls"), None), P("cls", "dp")),
        check_vma=False,
    )
```

```python
import functools

import jax
import jax.numpy as jnp
import numpy as np
from jax import lax
from jax.experimental import pallas as pl
from jax.experimental.pallas import tpu as pltpu
from jax.sharding import PartitionSpec as P

D = 512
TILE = 128
BR = 128
K = 8
PAIRS_PER_STEP = 4
FIELD = 128
PIECES = 4
VMEM_BYTES = 60 * 1024 * 1024
SPARE_BYTES = 4 * 1024 * 1024

logit_scale = 4.0
epsilon = 1e-06
unused_logit = -1e30

SMEM = pl.BlockSpec(memory_space=pltpu.SMEM)
VMEM = pl.BlockSpec(memory_space=pltpu.VMEM)
ANY = pl.BlockSpec(memory_space=pl.ANY)


def run_copies(jobs, sems, first=0):
    copies = [
        pltpu.make_async_copy(source, target, sems.at[first + index])
        for index, (source, target) in enumerate(jobs)
    ]
    for copy in copies:
        copy.start()
    return copies


def row_places(meta_ref, refs, blocks):
    size = blocks // PIECES
    if len(refs) > 1:
        return [(ref, piece * size) for piece, ref in enumerate(refs)]
    return [
        (refs[0].at[pl.ds(place * size, size)], (meta_ref[2] ^ place) * size)
        for place in range(PIECES)
    ]


def row_jobs(meta_ref, refs, rows_ref):
    return [
        (ref, rows_ref.at[pl.ds(start, ref.shape[0])])
        for ref, start in row_places(meta_ref, refs, rows_ref.shape[0])
    ]


def store_rows(meta_ref, rows_acc, out_ref, grad_refs, sems):
    blocks = out_ref.shape[0]
    out_ref[...] = rows_acc[:blocks].astype(out_ref.dtype)
    return run_copies(
        [
            (out_ref.at[pl.ds(start, ref.shape[0])], ref)
            for ref, start in row_places(meta_ref, grad_refs, blocks)
        ],
        sems,
    )


def aligned(refs, row, turned):
    parts = [ref[row] for ref in refs]
    if not turned:
        return parts
    size = parts[0].shape[0] // PIECES
    return [
        jnp.concatenate(
            [part[(piece ^ away) * size:((piece ^ away) + 1) * size] for piece in range(PIECES)]
        )
        for away, part in enumerate(parts)
    ]


def table_jobs(meta_ref, table_refs, table_ref):
    core = meta_ref[1] % 2
    jobs = [(table_refs[0], table_ref.at[pl.ds(0, table_refs[0].shape[0])])]
    if len(table_refs) > 1:
        half = table_refs[1].shape[0]
        jobs.append((table_refs[1], table_ref.at[pl.ds((2 + core) * half, half)]))
        jobs.append((table_refs[2], table_ref.at[pl.ds((3 - core) * half, half)]))
    return jobs


def transposed_logits(tile, rows):
    return logit_scale * lax.dot_general(
        tile, rows, (((1,), (1,)), ((), ())), preferred_element_type=jnp.float32
    )


def decode(code):
    return code // (2 * FIELD), (code // 2) % FIELD, (code % 2) == 1


def score_kernel(n_rows, n_tables, blocks, tiles, codes_ref, meta_ref, hit_ref, *refs):
    row_refs, refs = refs[:n_rows], refs[n_rows:]
    table_refs, refs = refs[:n_tables], refs[n_tables:]
    stats_ref, rows_ref, table_ref, lse_ref, pos_ref, sems = refs
    row_copies = run_copies(row_jobs(meta_ref, row_refs, rows_ref), sems)
    table_copies = run_copies(table_jobs(meta_ref, table_refs, table_ref), sems, PIECES)
    lse_ref[...] = jnp.full(lse_ref.shape, unused_logit, jnp.float32)
    pos_ref[...] = jnp.zeros(pos_ref.shape, jnp.float32)
    class_at = lax.broadcasted_iota(jnp.int32, (TILE, BR), 0)
    for copy in row_copies:
        copy.wait()

    def normalise(block, carry):
        exact = rows_ref[block].astype(jnp.float32)
        norm = lax.rsqrt(jnp.sum(exact * exact, axis=1, keepdims=True) + epsilon)
        rows_ref[block] = (exact * norm).astype(jnp.bfloat16)
        return carry

    lax.fori_loop(0, blocks, normalise, 0)
    for copy in table_copies:
        copy.wait()

    def step(index, carry):
        held = []
        for lane in range(PAIRS_PER_STEP):
            block, tile, first = decode(codes_ref[index * PAIRS_PER_STEP + lane])
            source = jnp.minimum(block, blocks - 1)
            logits = transposed_logits(
                table_ref[jnp.minimum(tile, tiles - 1)], rows_ref[source]
            )
            peak = jnp.max(logits, axis=0, keepdims=True)
            total = jnp.sum(jnp.exp(logits - peak), axis=0, keepdims=True)
            hit = class_at == hit_ref[pl.ds(source, 1), :]
            positive = jnp.sum(jnp.where(hit, logits, 0.0), axis=0, keepdims=True)
            held.append((block, peak + jnp.log(total), jnp.where(first, positive, 0.0)))
        for block, lse, positive in held:
            before = lse_ref[pl.ds(block, 1), :]
            top = jnp.maximum(before, lse)
            lse_ref[pl.ds(block, 1), :] = top + jnp.log(
                jnp.exp(before - top) + jnp.exp(lse - top)
            )
            pos_ref[pl.ds(block, 1), :] += positive
        return carry

    lax.fori_loop(0, pl.cdiv(meta_ref[0], PAIRS_PER_STEP), step, 0)
    stats_ref[0] = lse_ref[:blocks, :]
    stats_ref[1] = pos_ref[:blocks, :]


def make_totals(stat_refs, turned, total_ref, loss_ref):
    lse = aligned(stat_refs, 0, turned)
    top = functools.reduce(jnp.maximum, lse)
    total = top + jnp.log(sum(jnp.exp(part - top) for part in lse))
    total_ref[...] = total
    loss_ref[...] = total - sum(aligned(stat_refs, 1, turned))


def pair_score(code, blocks, tiles, rows_ref, table_ref, hit_ref, total_ref, class_at):
    block, tile, first = decode(code)
    source = jnp.minimum(block, blocks - 1)
    table_at = jnp.minimum(tile, tiles - 1)
    logits = transposed_logits(table_ref[table_at], rows_ref[source])
    share = jnp.exp(logits - total_ref[pl.ds(source, 1), :])
    wanted = jnp.where(first, hit_ref[pl.ds(source, 1), :], -1)
    hit = (class_at == wanted).astype(jnp.float32)
    return (logit_scale * (share - hit)).astype(jnp.bfloat16)


def row_terms(score, tile):
    return lax.dot_general(
        score, tile, (((0,), (0,)), ((), ())), preferred_element_type=jnp.float32
    )


def grad_kernel(
    n_grads, n_tables, n_stats, turned, blocks, tiles, codes_ref, meta_ref, hit_ref, *refs
):
    stat_refs, refs = refs[:n_stats], refs[n_stats:]
    unit_ref, refs = refs[0], refs[1:]
    table_refs, refs = refs[:n_tables], refs[n_tables:]
    grad_refs, refs = refs[:n_grads], refs[n_grads:]
    scores_ref, loss_ref, rows_ref, table_ref, total_ref, rows_acc, out_ref, sems = refs
    copies = run_copies(
        [(unit_ref, rows_ref)] + table_jobs(meta_ref, table_refs, table_ref), sems, PIECES
    )
    rows_acc[...] = jnp.zeros(rows_acc.shape, jnp.float32)
    make_totals(stat_refs, turned, total_ref, loss_ref)
    class_at = lax.broadcasted_iota(jnp.int32, (TILE, BR), 0)
    for copy in copies:
        copy.wait()

    def step(index, carry):
        held = []
        for lane in range(PAIRS_PER_STEP):
            pair = index * PAIRS_PER_STEP + lane
            score = pair_score(
                codes_ref[pair], blocks, tiles, rows_ref, table_ref, hit_ref, total_ref, class_at
            )
            scores_ref[pair] = score
            held.append(score)
        for lane, score in enumerate(held):
            block, tile, _ = decode(codes_ref[index * PAIRS_PER_STEP + lane])
            rows_acc[block] += row_terms(score, table_ref[jnp.minimum(tile, tiles - 1)])
        return carry

    lax.fori_loop(0, pl.cdiv(meta_ref[0], PAIRS_PER_STEP), step, 0)
    for copy in store_rows(meta_ref, rows_acc, out_ref, grad_refs, sems):
        copy.wait()


def last_kernel(sizes, n_grads, n_tables, n_stats, turned, n_shares, tiles, *refs):
    chunks, blocks = len(sizes), sizes[-1]
    codes_refs, refs = refs[:chunks], refs[chunks:]
    meta_refs, refs = refs[:chunks], refs[chunks:]
    hit_ref, refs = refs[0], refs[1:]
    stat_refs, refs = refs[:n_stats], refs[n_stats:]
    scores_refs, refs = refs[:chunks - 1], refs[chunks - 1:]
    unit_refs, refs = refs[:chunks], refs[chunks:]
    table_refs, refs = refs[:n_tables], refs[n_tables:]
    grad_refs, refs = refs[:n_grads], refs[n_grads:]
    share_refs, refs = refs[:n_shares], refs[n_shares:]
    loss_ref, refs = refs[0], refs[1:]
    rows_ref, early_ref, held_ref, table_ref, total_ref, rows_acc, out_ref, *refs = refs
    tiles_acc, sems, early_sems, row_sems = refs
    codes_ref, meta_ref = codes_refs[-1], meta_refs[-1]
    copies = run_copies(
        [(unit_refs[-1], rows_ref)] + table_jobs(meta_ref, table_refs, table_ref), sems
    )


    def fetch(chunk):
        early = early_ref.at[pl.ds(0, sizes[chunk])]
        return run_copies(
            [(unit_refs[chunk], early), (scores_refs[chunk], held_ref)], early_sems
        )

    early = fetch(0) if chunks > 1 else []
    rows_acc[...] = jnp.zeros(rows_acc.shape, jnp.float32)
    tiles_acc[...] = jnp.zeros(tiles_acc.shape, jnp.float32)
    make_totals(stat_refs, turned, total_ref, loss_ref)
    class_at = lax.broadcasted_iota(jnp.int32, (TILE, BR), 0)
    for copy in copies:
        copy.wait()

    def step(index, carry):
        held = [
            pair_score(
                codes_ref[index * PAIRS_PER_STEP + lane], blocks, tiles, rows_ref, table_ref,
                hit_ref, total_ref, class_at,
            )
            for lane in range(PAIRS_PER_STEP)
        ]
        for lane, score in enumerate(held):
            block, tile, _ = decode(codes_ref[index * PAIRS_PER_STEP + lane])
            rows_acc[block] += row_terms(score, table_ref[jnp.minimum(tile, tiles - 1)])
            tiles_acc[tile] += jnp.dot(
                score, rows_ref[jnp.minimum(block, blocks - 1)],
                preferred_element_type=jnp.float32,
            )
        return carry

    lax.fori_loop(0, pl.cdiv(meta_ref[0], PAIRS_PER_STEP), step, 0)
    stored = store_rows(meta_ref, rows_acc, out_ref, grad_refs, row_sems)
    for chunk in range(chunks - 1):
        for copy in early if chunk == 0 else fetch(chunk):
            copy.wait()

        def early_step(index, carry, chunk=chunk):
            for lane in range(PAIRS_PER_STEP):
                pair = index * PAIRS_PER_STEP + lane
                block, tile, _ = decode(codes_refs[chunk][pair])
                tiles_acc[tile] += jnp.dot(
                    held_ref[pair],
                    early_ref[jnp.minimum(block, sizes[chunk] - 1)],
                    preferred_element_type=jnp.float32,
                )
            return carry

        lax.fori_loop(0, pl.cdiv(meta_refs[chunk][0], PAIRS_PER_STEP), early_step, 0)
    if n_shares == 1:
        share_refs[0][...] = tiles_acc[:tiles].astype(jnp.bfloat16)
    else:
        part = meta_ref[1]
        shard, width = share_refs[0].shape[2], share_refs[0].shape[-1]
        for core, ref in enumerate(share_refs):
            for y in range(ref.shape[1]):
                start = pl.multiple_of(((2 * y + core) ^ part) * width, width)
                for x in range(ref.shape[0]):
                    ref[x, y] = tiles_acc[
                        pl.ds(x * shard, shard), :, pl.ds(start, width)
                    ].astype(jnp.bfloat16)
    for copy in stored:
        copy.wait()


def kernel_cost(blocks):
    return pl.CostEstimate(flops=blocks * BR * D, bytes_accessed=blocks * BR * D, transcendentals=0)


def limit(*scratch):
    total = 0
    for shape, dtype in scratch:
        total += int(np.prod(shape)) * jnp.dtype(dtype).itemsize
    return pltpu.CompilerParams(vmem_limit_bytes=min(VMEM_BYTES, total + SPARE_BYTES))


def rows_of(blocks):
    return (blocks, BR, D), jnp.bfloat16


def score(blocks, codes, meta, hit, rows, tables):
    tiles = sum(table.shape[0] for table in tables)
    table_room = ((tiles, TILE, D), jnp.bfloat16)
    return pl.pallas_call(
        functools.partial(score_kernel, len(rows), len(tables), blocks, tiles),
        out_shape=(
            jax.ShapeDtypeStruct((2, blocks, BR), jnp.float32),
            jax.ShapeDtypeStruct(*rows_of(blocks)),
        ),
        in_specs=[SMEM, SMEM, VMEM] + [ANY] * (len(rows) + len(tables)),
        out_specs=(VMEM, VMEM),
        scratch_shapes=[
            pltpu.VMEM(*table_room),
            pltpu.VMEM((blocks + 8, BR), jnp.float32),
            pltpu.VMEM((blocks + 8, BR), jnp.float32),
            pltpu.SemaphoreType.DMA((PIECES + len(tables),)),
        ],
        cost_estimate=kernel_cost(blocks),
        compiler_params=limit(rows_of(blocks), table_room),
    )(codes, meta, hit, *rows, *tables)


def grads(blocks, codes, meta, hit, stats, turned, unit, tables, shapes):
    tiles = sum(table.shape[0] for table in tables)
    table_room = ((tiles, TILE, D), jnp.bfloat16)
    acc_room = ((blocks + 1, BR, D), jnp.float32)
    scores = ((codes.shape[0], TILE, BR), jnp.bfloat16)
    outs = pl.pallas_call(
        functools.partial(
            grad_kernel, len(shapes), len(tables), len(stats), turned, blocks, tiles
        ),
        out_shape=(
            *(jax.ShapeDtypeStruct(shape, jnp.bfloat16) for shape in shapes),
            jax.ShapeDtypeStruct(*scores),
            jax.ShapeDtypeStruct((blocks, BR), jnp.float32),
        ),
        in_specs=[SMEM, SMEM] + [VMEM] * (1 + len(stats)) + [ANY] * (1 + len(tables)),
        out_specs=(*[ANY] * len(shapes), VMEM, VMEM),
        scratch_shapes=[
            pltpu.VMEM(*rows_of(blocks)),
            pltpu.VMEM(*table_room),
            pltpu.VMEM((blocks, BR), jnp.float32),
            pltpu.VMEM(*acc_room),
            pltpu.VMEM(*rows_of(blocks)),
            pltpu.SemaphoreType.DMA((PIECES + 1 + len(tables),)),
        ],
        cost_estimate=kernel_cost(blocks),
        compiler_params=limit(rows_of(2 * blocks), table_room, acc_room, scores),
    )(codes, meta, hit, *stats, unit, *tables)
    return list(outs[:len(shapes)]), outs[len(shapes)], outs[-1]


def last_grads(codes, metas, hit, stats, turned, scores, units, tables, shapes, share_shapes):
    sizes = [unit.shape[0] for unit in units]
    tiles = sum(table.shape[0] for table in tables)
    chunks, blocks = len(sizes), sizes[-1]
    n_inputs = 2 * chunks - 1 + len(tables)
    table_room = ((tiles, TILE, D), jnp.bfloat16)
    acc_room = ((blocks + 1, BR, D), jnp.float32)
    tiles_room = ((tiles + 1, TILE, D), jnp.float32)
    early_room = rows_of(max(sizes[:-1], default=PIECES))
    kept = ((scores or codes)[0].shape[0], TILE, BR), jnp.bfloat16
    outs = pl.pallas_call(
        functools.partial(
            last_kernel, sizes, len(shapes), len(tables), len(stats), turned,
            len(share_shapes), tiles,
        ),
        out_shape=(
            *(jax.ShapeDtypeStruct(shape, jnp.bfloat16) for shape in shapes),
            *(jax.ShapeDtypeStruct(shape, jnp.bfloat16) for shape in share_shapes),
            jax.ShapeDtypeStruct((blocks, BR), jnp.float32),
        ),
        in_specs=[SMEM] * (2 * chunks) + [VMEM] * (1 + len(stats)) + [ANY] * n_inputs,
        out_specs=(*[ANY] * len(shapes), *[VMEM] * len(share_shapes), VMEM),
        scratch_shapes=[
            pltpu.VMEM(*rows_of(blocks)),
            pltpu.VMEM(*early_room),
            pltpu.VMEM(*kept),
            pltpu.VMEM(*table_room),
            pltpu.VMEM((blocks, BR), jnp.float32),
            pltpu.VMEM(*acc_room),
            pltpu.VMEM(*rows_of(blocks)),
            pltpu.VMEM(*tiles_room),
            pltpu.SemaphoreType.DMA((1 + len(tables),)),
            pltpu.SemaphoreType.DMA((2,)),
            pltpu.SemaphoreType.DMA((PIECES,)),
        ],
        cost_estimate=kernel_cost(sum(sizes)),
        compiler_params=limit(
            rows_of(2 * blocks), early_room, kept, table_room, table_room, acc_room, tiles_room
        ),
    )(*codes, *metas, hit, *stats, *scores, *units, *tables)
    cut = len(shapes)
    return list(outs[:cut]), list(outs[cut:-1]), outs[-1]


def add(first, second):
    return (first.astype(jnp.float32) + second.astype(jnp.float32)).astype(jnp.bfloat16)


class GroupSum:
    def __init__(self, part, groups):
        self.total = lax.psum_scatter(
            part, "cls", scatter_dimension=0, axis_index_groups=groups, tiled=True
        )

    def hold(self, others):
        self.total, others = lax.optimization_barrier((self.total, others))
        return others

    def finish(self):
        return self.total.astype(jnp.float32)


class PairSum:
    def __init__(self, moves, parts, passed):
        self.parts = parts
        self.near = moves.over_z(parts[1], 1)
        self.far = moves.over_z(add(passed, parts[2]), 2)

    def finish(self):
        return sum(part.astype(jnp.float32) for part in (self.parts[0], self.near, self.far))


class Neighbours:
    def __init__(self, nx, dp):
        self.nx, self.nz, self.dp, self.turned = nx, PIECES, dp, True
        self.z_groups = [[z * nx + x for z in range(PIECES)] for x in range(nx)]

    def over_z(self, value, away):
        pairs = [
            (z * self.nx + x, (z ^ away) * self.nx + x)
            for z in range(self.nz) for x in range(self.nx)
        ]
        return lax.ppermute(value, "cls", pairs)

    def over_x(self, value):
        return lax.ppermute(value, "cls", [(c, c ^ 1) for c in range(self.nx * self.nz)])

    def over_y(self, value):
        return lax.ppermute(value, "dp", [(d, d ^ 2) for d in range(self.dp)])

    def over_core(self, value):
        return lax.ppermute(value, "dp", [(d, d ^ 1) for d in range(self.dp)])

    def all_over_z(self, value):
        return [value] + [self.over_z(value, away) for away in range(1, self.nz)]

    def gather(self, needed, chunks, lists, table, core, prepare):
        def moves(first, second, lists, table, core):
            half = table.shape[0] // 2
            sent = lax.dynamic_slice_in_dim(table, core * half, half, axis=0)
            far, near, from_x, second = lax.optimization_barrier(
                (self.over_z(first, 2), self.over_z(first, 1), self.over_x(sent), second)
            )
            passed, far_second = self.over_z(far, 1), self.over_z(second, 2)
            pieces = [first, near, far, passed], [second, far_second]
            return pieces, (from_x, self.over_core(from_x)), prepare(
                jnp.stack(self.all_over_z(lists))
            )

        gathered, tables, prepared = self.together(needed, moves, *chunks, lists, table, core)
        return gathered, [table, *tables], prepared

    def rest_of_rows(self, pieces, others):
        second, far = pieces
        near, passed, others = lax.optimization_barrier(
            (self.over_z(second, 1), self.over_z(far, 1), others)
        )
        return [second, near, far, passed], others

    def grad_shapes(self, size, last):
        return [(size, BR, D)] * PIECES if last else [(PIECES * size, BR, D)]

    def gather_stats(self, stats):
        return self.all_over_z(stats)

    def sum_rows(self, parts):
        return GroupSum(parts[0], self.z_groups)

    def together(self, needed, work, *operands):
        def no_work(*operands):
            return jax.tree.map(
                lambda out: jnp.zeros(out.shape, out.dtype), jax.eval_shape(work, *operands)
            )

        return lax.cond(needed, work, no_work, *operands)

    def first_moves(self, parts, shares):
        return self.over_z(parts[3], 1), self.over_core(shares[1])

    def sum_last(self, results, pending):
        parts, shares, loss, (passed, got) = results
        for total in pending:
            got = total.hold(got)
        return PairSum(self, parts, passed), self.sum_shares(shares[0], got), loss

    def order(self, place):
        return place

    def own(self, loss, place, size):
        return loss[:size]

    def share_shapes(self, shard_tiles):
        return [(self.nx, self.dp // 2, shard_tiles, TILE, D // self.dp)] * 2

    def sum_shares(self, kept, got):
        half = kept.shape[2] // 2
        x_sent = add(kept[1, :, :half], got[1, :, :half])
        y_sent = add(kept[:, 1, half:], got[:, 1, half:])
        x_got, y_got = lax.optimization_barrier((self.over_x(x_sent), self.over_y(y_sent)))
        x_kept = [add(add(kept[0, y, :half], got[0, y, :half]), x_got[y]) for y in range(2)]
        y_kept = [add(add(kept[x, 0, half:], got[x, 0, half:]), y_got[x]) for x in range(2)]
        low, high = lax.optimization_barrier((self.over_y(x_kept[1]), self.over_x(y_kept[1])))
        low = x_kept[0].astype(jnp.float32) + low.astype(jnp.float32)
        high = y_kept[0].astype(jnp.float32) + high.astype(jnp.float32)
        return jnp.concatenate([low, high], axis=0)


class Groups:
    def __init__(self, nz, dp):
        self.nx, self.nz, self.dp, self.turned = 1, nz, dp, False

    def gather(self, needed, chunks, lists, table, core, prepare):
        gathered = [[lax.all_gather(rows, "cls", tiled=True)] for rows in chunks]
        return gathered, [table], prepare(lax.all_gather(lists, "cls"))

    def rest_of_rows(self, pieces, others):
        return pieces, others

    def grad_shapes(self, size, last):
        return [(self.nz * size, BR, D)]

    def gather_stats(self, stats):
        return list(lax.all_gather(stats, "cls"))

    def sum_rows(self, parts):
        return GroupSum(parts[0], None)

    def together(self, needed, work, *operands):
        return work(*operands)

    def first_moves(self, parts, shares):
        return ()

    def sum_last(self, results, pending):
        parts, shares, loss, _ = results
        return self.sum_rows(parts), self.sum_shares(shares), loss

    def order(self, place):
        return jnp.zeros_like(place)

    def own(self, loss, place, size):
        return lax.dynamic_slice_in_dim(loss, place * size, size, axis=0)

    def share_shapes(self, shard_tiles):
        return [(shard_tiles, TILE, D)]

    def sum_shares(self, shares):
        return lax.psum_scatter(
            shares[0], "dp", scatter_dimension=2, tiled=True
        ).astype(jnp.float32)


def pair_codes(lists, shard_tiles, nx, place, column, room):
    entry = lists[:, :K].reshape(-1)
    owner = entry // shard_tiles
    mine = (entry >= 0) & (owner // nx == place)
    local = jnp.where(owner % nx == column, 0, shard_tiles) + entry % shard_tiles
    counter = jnp.arange(entry.shape[0], dtype=jnp.int32)
    code = ((counter // K) * FIELD + local) * 2 + (counter % K == 0)
    rank = jnp.sum(
        jnp.where(mine[None, :] & (counter[None, :] < counter[:, None]), 1, 0), axis=1
    ).astype(jnp.int32)
    slots = jnp.arange(room, dtype=jnp.int32)
    chosen = mine[None, :] & (rank[None, :] == slots[:, None])
    padding = (lists.shape[0] * FIELD + nx * shard_tiles) * 2
    codes = padding + jnp.sum(jnp.where(chosen, code[None, :] - padding, 0), axis=1)
    return codes.astype(jnp.int32), jnp.sum(mine.astype(jnp.int32))


def per_device(moves, sizes, embeddings, proxies, hard_tiles, tile_count, labels):
    nx, nz, dp = moves.nx, moves.nz, moves.dp
    blocks = hard_tiles.shape[0]
    shard_tiles = proxies.shape[0] // TILE
    me, part = lax.axis_index("cls"), lax.axis_index("dp")
    place, column = me // nx, me % nx

    emb_exact = embeddings.astype(jnp.float32)
    inverse_norm = lax.rsqrt(jnp.sum(emb_exact * emb_exact, axis=1, keepdims=True) + epsilon)
    unit_exact = emb_exact * inverse_norm
    row_blocks = embeddings.reshape(blocks, BR, D)

    position = labels.reshape(blocks, BR) - hard_tiles[:, 0:1] * TILE
    entries = jnp.arange(K, dtype=jnp.int32)
    used = jnp.where(entries[None, :] < tile_count[:, None], hard_tiles, -1)
    starts = [sum(sizes[:chunk]) for chunk in range(len(sizes))]
    spots = [slice(start, start + size) for start, size in zip(starts, sizes)]
    held = [nz * size for size in sizes]
    last = len(sizes) - 1
    needed = tile_count[0] > 0

    def prepare(lists):
        prepared = []
        for spot, blocks_held in zip(spots, held):
            room = min(blocks_held * K, nz * (blocks * K // (nx * nz)) * nx)
            room = -(-room // PAIRS_PER_STEP) * PAIRS_PER_STEP
            chunk_lists = lists[:, spot].reshape(blocks_held, K + BR)
            code, count = pair_codes(chunk_lists, shard_tiles, nx, place, column, room)
            meta = jnp.stack([count, part, moves.order(place)]).astype(jnp.int32)
            prepared.append((code, meta, chunk_lists[:, K:]))
        return prepared

    gathered, tables, prepared = moves.gather(
        needed,
        [row_blocks[spot] for spot in spots],
        jnp.concatenate([used, position], axis=1),
        proxies.reshape(shard_tiles, TILE, D),
        part % 2,
        prepare,
    )

    def scored(chunk, rows, tables, prepared):
        parts, unit = score(held[chunk], *prepared[chunk], rows, tables)
        return moves.gather_stats(parts), unit

    def early_work(gathered, tables, prepared):
        units, made, rows = [], [], gathered[-1]
        for chunk in range(last):
            stats, unit = scored(chunk, gathered[chunk], tables, prepared)
            if chunk == 0:
                rows, stats = moves.rest_of_rows(rows, stats)
            units.append(unit)
            made.append(grads(
                held[chunk], *prepared[chunk], stats, moves.turned, unit, tables,
                moves.grad_shapes(sizes[chunk], False),
            ))
        return rows, units, made

    def last_work(rows, tables, prepared, units, scores):
        codes, metas, hits = zip(*prepared)
        stats, unit = scored(last, rows, tables, prepared)
        parts, shares, loss = last_grads(
            codes, metas, hits[-1], stats, moves.turned, scores, units + [unit], tables,
            moves.grad_shapes(sizes[-1], True), moves.share_shapes(shard_tiles),
        )
        return parts, shares, loss, moves.first_moves(parts, shares)

    rows, units, made = moves.together(needed, early_work, gathered, tables, prepared)
    row_grads = [moves.sum_rows(partial) for partial, _, _ in made]
    scores = [dscore for _, dscore, _ in made]
    losses = [moves.own(loss, place, size) for (_, _, loss), size in zip(made, sizes)]
    results = moves.together(needed, last_work, rows, tables, prepared, units, scores)
    last_sum, shares, loss = moves.sum_last(results, row_grads)
    row_grads.append(last_sum)
    losses.append(moves.own(loss, place, sizes[-1]))

    proxy_grad = shares.reshape(shard_tiles * TILE, D // dp)
    row_loss = jnp.concatenate(losses, axis=0).reshape(-1)
    grad_flat = jnp.concatenate([total.finish() for total in row_grads], axis=0)
    grad_flat = grad_flat.reshape(blocks * BR, D)
    radial = jnp.sum(unit_exact * grad_flat, axis=1, keepdims=True)
    embed_grad = ((grad_flat - unit_exact * radial) * inverse_norm).astype(jnp.bfloat16)
    return (row_loss, embed_grad, proxy_grad)


def solution(mesh):
    placed = (
        P(("dp", "cls"), None),
        P("cls", None),
        P(("dp", "cls"), None),
        P(("dp", "cls")),
        P(("dp", "cls")),
    )
    dp, groups = mesh.shape["dp"], mesh.shape["cls"]
    if (dp, groups) == (4, 2 * PIECES):
        moves, sizes = Neighbours(2, dp), [5, 3]
    else:
        chunks = max(1, groups // 8)
        moves, sizes = Groups(groups, dp), [8 // chunks] * chunks
    return jax.shard_map(
        functools.partial(per_device, moves, sizes),
        mesh=mesh,
        in_specs=placed,
        out_specs=(P(("dp", "cls")), P(("dp", "cls"), None), P("cls", "dp")),
        check_vma=False,
    )
```

```python
import functools

import jax
import jax.numpy as jnp
import numpy as np
from jax import lax
from jax.experimental import pallas as pl
from jax.experimental.pallas import tpu as pltpu
from jax.sharding import PartitionSpec as P

D = 512
TILE = 128
BR = 128
K = 8
PAIRS_PER_STEP = 4
FIELD = 128
PIECES = 4
VMEM_BYTES = 60 * 1024 * 1024
SPARE_BYTES = 4 * 1024 * 1024

logit_scale = 4.0
epsilon = 1e-06
unused_logit = -1e30

SMEM = pl.BlockSpec(memory_space=pltpu.SMEM)
VMEM = pl.BlockSpec(memory_space=pltpu.VMEM)
ANY = pl.BlockSpec(memory_space=pl.ANY)


def run_copies(jobs, sems, first=0):
    copies = [
        pltpu.make_async_copy(source, target, sems.at[first + index])
        for index, (source, target) in enumerate(jobs)
    ]
    for copy in copies:
        copy.start()
    return copies


def row_places(meta_ref, refs, blocks):
    size = blocks // PIECES
    if len(refs) > 1:
        return [(ref, piece * size) for piece, ref in enumerate(refs)]
    return [
        (refs[0].at[pl.ds(place * size, size)], (meta_ref[2] ^ place) * size)
        for place in range(PIECES)
    ]


def row_jobs(meta_ref, refs, rows_ref):
    return [
        (ref, rows_ref.at[pl.ds(start, ref.shape[0])])
        for ref, start in row_places(meta_ref, refs, rows_ref.shape[0])
    ]


def store_rows(meta_ref, rows_acc, out_ref, grad_refs, sems):
    blocks = out_ref.shape[0]
    out_ref[...] = rows_acc[:blocks].astype(out_ref.dtype)
    return run_copies(
        [
            (out_ref.at[pl.ds(start, ref.shape[0])], ref)
            for ref, start in row_places(meta_ref, grad_refs, blocks)
        ],
        sems,
    )


def aligned(refs, row, turned):
    parts = [ref[row] for ref in refs]
    if not turned:
        return parts
    size = parts[0].shape[0] // PIECES
    return [
        jnp.concatenate(
            [part[(piece ^ away) * size:((piece ^ away) + 1) * size] for piece in range(PIECES)]
        )
        for away, part in enumerate(parts)
    ]


def table_jobs(meta_ref, table_refs, table_ref):
    core = meta_ref[1] % 2
    jobs = [(table_refs[0], table_ref.at[pl.ds(0, table_refs[0].shape[0])])]
    if len(table_refs) > 1:
        half = table_refs[1].shape[0]
        jobs.append((table_refs[1], table_ref.at[pl.ds((2 + core) * half, half)]))
        jobs.append((table_refs[2], table_ref.at[pl.ds((3 - core) * half, half)]))
    return jobs


def transposed_logits(tile, rows):
    return logit_scale * lax.dot_general(
        tile, rows, (((1,), (1,)), ((), ())), preferred_element_type=jnp.float32
    )


def decode(code):
    return code // (2 * FIELD), (code // 2) % FIELD, (code % 2) == 1


def score_kernel(n_rows, n_tables, blocks, tiles, codes_ref, meta_ref, hit_ref, *refs):
    row_refs, refs = refs[:n_rows], refs[n_rows:]
    table_refs, refs = refs[:n_tables], refs[n_tables:]
    stats_ref, rows_ref, table_ref, lse_ref, pos_ref, sems = refs
    row_copies = run_copies(row_jobs(meta_ref, row_refs, rows_ref), sems)
    table_copies = run_copies(table_jobs(meta_ref, table_refs, table_ref), sems, PIECES)
    lse_ref[...] = jnp.full(lse_ref.shape, unused_logit, jnp.float32)
    pos_ref[...] = jnp.zeros(pos_ref.shape, jnp.float32)
    class_at = lax.broadcasted_iota(jnp.int32, (TILE, BR), 0)
    for copy in row_copies:
        copy.wait()

    def normalise(block, carry):
        exact = rows_ref[block].astype(jnp.float32)
        norm = lax.rsqrt(jnp.sum(exact * exact, axis=1, keepdims=True) + epsilon)
        rows_ref[block] = (exact * norm).astype(jnp.bfloat16)
        return carry

    lax.fori_loop(0, blocks, normalise, 0)
    for copy in table_copies:
        copy.wait()

    def step(index, carry):
        held = []
        for lane in range(PAIRS_PER_STEP):
            block, tile, first = decode(codes_ref[index * PAIRS_PER_STEP + lane])
            source = jnp.minimum(block, blocks - 1)
            logits = transposed_logits(
                table_ref[jnp.minimum(tile, tiles - 1)], rows_ref[source]
            )
            peak = jnp.max(logits, axis=0, keepdims=True)
            total = jnp.sum(jnp.exp(logits - peak), axis=0, keepdims=True)
            hit = class_at == hit_ref[pl.ds(source, 1), :]
            positive = jnp.sum(jnp.where(hit, logits, 0.0), axis=0, keepdims=True)
            held.append((block, peak + jnp.log(total), jnp.where(first, positive, 0.0)))
        for block, lse, positive in held:
            before = lse_ref[pl.ds(block, 1), :]
            top = jnp.maximum(before, lse)
            lse_ref[pl.ds(block, 1), :] = top + jnp.log(
                jnp.exp(before - top) + jnp.exp(lse - top)
            )
            pos_ref[pl.ds(block, 1), :] += positive
        return carry

    lax.fori_loop(0, pl.cdiv(meta_ref[0], PAIRS_PER_STEP), step, 0)
    stats_ref[0] = lse_ref[:blocks, :]
    stats_ref[1] = pos_ref[:blocks, :]


def make_totals(stat_refs, turned, total_ref, loss_ref):
    lse = aligned(stat_refs, 0, turned)
    top = functools.reduce(jnp.maximum, lse)
    total = top + jnp.log(sum(jnp.exp(part - top) for part in lse))
    total_ref[...] = total
    loss_ref[...] = total - sum(aligned(stat_refs, 1, turned))


def pair_score(code, blocks, tiles, rows_ref, table_ref, hit_ref, total_ref, class_at):
    block, tile, first = decode(code)
    source = jnp.minimum(block, blocks - 1)
    table_at = jnp.minimum(tile, tiles - 1)
    logits = transposed_logits(table_ref[table_at], rows_ref[source])
    share = jnp.exp(logits - total_ref[pl.ds(source, 1), :])
    wanted = jnp.where(first, hit_ref[pl.ds(source, 1), :], -1)
    hit = (class_at == wanted).astype(jnp.float32)
    return (logit_scale * (share - hit)).astype(jnp.bfloat16)


def row_terms(score, tile):
    return lax.dot_general(
        score, tile, (((0,), (0,)), ((), ())), preferred_element_type=jnp.float32
    )


def grad_kernel(
    n_grads, n_tables, n_stats, turned, blocks, tiles, codes_ref, meta_ref, hit_ref, *refs
):
    stat_refs, refs = refs[:n_stats], refs[n_stats:]
    unit_ref, refs = refs[0], refs[1:]
    table_refs, refs = refs[:n_tables], refs[n_tables:]
    grad_refs, refs = refs[:n_grads], refs[n_grads:]
    scores_ref, loss_ref, rows_ref, table_ref, total_ref, rows_acc, out_ref, sems = refs
    copies = run_copies(
        [(unit_ref, rows_ref)] + table_jobs(meta_ref, table_refs, table_ref), sems, PIECES
    )
    rows_acc[...] = jnp.zeros(rows_acc.shape, jnp.float32)
    make_totals(stat_refs, turned, total_ref, loss_ref)
    class_at = lax.broadcasted_iota(jnp.int32, (TILE, BR), 0)
    for copy in copies:
        copy.wait()

    def step(index, carry):
        held = []
        for lane in range(PAIRS_PER_STEP):
            pair = index * PAIRS_PER_STEP + lane
            score = pair_score(
                codes_ref[pair], blocks, tiles, rows_ref, table_ref, hit_ref, total_ref, class_at
            )
            scores_ref[pair] = score
            held.append(score)
        for lane, score in enumerate(held):
            block, tile, _ = decode(codes_ref[index * PAIRS_PER_STEP + lane])
            rows_acc[block] += row_terms(score, table_ref[jnp.minimum(tile, tiles - 1)])
        return carry

    lax.fori_loop(0, pl.cdiv(meta_ref[0], PAIRS_PER_STEP), step, 0)
    for copy in store_rows(meta_ref, rows_acc, out_ref, grad_refs, sems):
        copy.wait()


def last_kernel(sizes, n_grads, n_tables, n_stats, turned, n_shares, tiles, *refs):
    chunks, blocks = len(sizes), sizes[-1]
    codes_refs, refs = refs[:chunks], refs[chunks:]
    meta_refs, refs = refs[:chunks], refs[chunks:]
    hit_ref, refs = refs[0], refs[1:]
    stat_refs, refs = refs[:n_stats], refs[n_stats:]
    scores_refs, refs = refs[:chunks - 1], refs[chunks - 1:]
    unit_refs, refs = refs[:chunks], refs[chunks:]
    table_refs, refs = refs[:n_tables], refs[n_tables:]
    grad_refs, refs = refs[:n_grads], refs[n_grads:]
    share_refs, refs = refs[:n_shares], refs[n_shares:]
    loss_ref, refs = refs[0], refs[1:]
    rows_ref, early_ref, held_ref, table_ref, total_ref, rows_acc, out_ref, *refs = refs
    tiles_acc, sems, early_sems, row_sems = refs
    codes_ref, meta_ref = codes_refs[-1], meta_refs[-1]
    copies = run_copies(
        [(unit_refs[-1], rows_ref)] + table_jobs(meta_ref, table_refs, table_ref), sems
    )


    def fetch(chunk):
        early = early_ref.at[pl.ds(0, sizes[chunk])]
        return run_copies(
            [(unit_refs[chunk], early), (scores_refs[chunk], held_ref)], early_sems
        )

    early = fetch(0) if chunks > 1 else []
    rows_acc[...] = jnp.zeros(rows_acc.shape, jnp.float32)
    tiles_acc[...] = jnp.zeros(tiles_acc.shape, jnp.float32)
    make_totals(stat_refs, turned, total_ref, loss_ref)
    class_at = lax.broadcasted_iota(jnp.int32, (TILE, BR), 0)
    for copy in copies:
        copy.wait()

    def step(index, carry):
        held = [
            pair_score(
                codes_ref[index * PAIRS_PER_STEP + lane], blocks, tiles, rows_ref, table_ref,
                hit_ref, total_ref, class_at,
            )
            for lane in range(PAIRS_PER_STEP)
        ]
        for lane, score in enumerate(held):
            block, tile, _ = decode(codes_ref[index * PAIRS_PER_STEP + lane])
            rows_acc[block] += row_terms(score, table_ref[jnp.minimum(tile, tiles - 1)])
            tiles_acc[tile] += jnp.dot(
                score, rows_ref[jnp.minimum(block, blocks - 1)],
                preferred_element_type=jnp.float32,
            )
        return carry

    lax.fori_loop(0, pl.cdiv(meta_ref[0], PAIRS_PER_STEP), step, 0)
    stored = store_rows(meta_ref, rows_acc, out_ref, grad_refs, row_sems)
    for chunk in range(chunks - 1):
        for copy in early if chunk == 0 else fetch(chunk):
            copy.wait()

        def early_step(index, carry, chunk=chunk):
            for lane in range(PAIRS_PER_STEP):
                pair = index * PAIRS_PER_STEP + lane
                block, tile, _ = decode(codes_refs[chunk][pair])
                tiles_acc[tile] += jnp.dot(
                    held_ref[pair],
                    early_ref[jnp.minimum(block, sizes[chunk] - 1)],
                    preferred_element_type=jnp.float32,
                )
            return carry

        lax.fori_loop(0, pl.cdiv(meta_refs[chunk][0], PAIRS_PER_STEP), early_step, 0)
    if n_shares == 1:
        share_refs[0][...] = tiles_acc[:tiles].astype(jnp.bfloat16)
    else:
        part = meta_ref[1]
        shard, width = share_refs[0].shape[2], share_refs[0].shape[-1]
        for core, ref in enumerate(share_refs):
            for y in range(ref.shape[1]):
                start = pl.multiple_of(((2 * y + core) ^ part) * width, width)
                for x in range(ref.shape[0]):
                    ref[x, y] = tiles_acc[
                        pl.ds(x * shard, shard), :, pl.ds(start, width)
                    ].astype(jnp.bfloat16)
    for copy in stored:
        copy.wait()


def kernel_cost(blocks):
    return pl.CostEstimate(flops=blocks * BR * D, bytes_accessed=blocks * BR * D, transcendentals=0)


def limit(*scratch):
    total = 0
    for shape, dtype in scratch:
        total += int(np.prod(shape)) * jnp.dtype(dtype).itemsize
    return pltpu.CompilerParams(vmem_limit_bytes=min(VMEM_BYTES, total + SPARE_BYTES))


def rows_of(blocks):
    return (blocks, BR, D), jnp.bfloat16


def score(blocks, codes, meta, hit, rows, tables):
    tiles = sum(table.shape[0] for table in tables)
    table_room = ((tiles, TILE, D), jnp.bfloat16)
    return pl.pallas_call(
        functools.partial(score_kernel, len(rows), len(tables), blocks, tiles),
        out_shape=(
            jax.ShapeDtypeStruct((2, blocks, BR), jnp.float32),
            jax.ShapeDtypeStruct(*rows_of(blocks)),
        ),
        in_specs=[SMEM, SMEM, VMEM] + [ANY] * (len(rows) + len(tables)),
        out_specs=(VMEM, VMEM),
        scratch_shapes=[
            pltpu.VMEM(*table_room),
            pltpu.VMEM((blocks + 8, BR), jnp.float32),
            pltpu.VMEM((blocks + 8, BR), jnp.float32),
            pltpu.SemaphoreType.DMA((PIECES + len(tables),)),
        ],
        cost_estimate=kernel_cost(blocks),
        compiler_params=limit(rows_of(blocks), table_room),
    )(codes, meta, hit, *rows, *tables)


def grads(blocks, codes, meta, hit, stats, turned, unit, tables, shapes):
    tiles = sum(table.shape[0] for table in tables)
    table_room = ((tiles, TILE, D), jnp.bfloat16)
    acc_room = ((blocks + 1, BR, D), jnp.float32)
    scores = ((codes.shape[0], TILE, BR), jnp.bfloat16)
    outs = pl.pallas_call(
        functools.partial(
            grad_kernel, len(shapes), len(tables), len(stats), turned, blocks, tiles
        ),
        out_shape=(
            *(jax.ShapeDtypeStruct(shape, jnp.bfloat16) for shape in shapes),
            jax.ShapeDtypeStruct(*scores),
            jax.ShapeDtypeStruct((blocks, BR), jnp.float32),
        ),
        in_specs=[SMEM, SMEM] + [VMEM] * (1 + len(stats)) + [ANY] * (1 + len(tables)),
        out_specs=(*[ANY] * len(shapes), VMEM, VMEM),
        scratch_shapes=[
            pltpu.VMEM(*rows_of(blocks)),
            pltpu.VMEM(*table_room),
            pltpu.VMEM((blocks, BR), jnp.float32),
            pltpu.VMEM(*acc_room),
            pltpu.VMEM(*rows_of(blocks)),
            pltpu.SemaphoreType.DMA((PIECES + 1 + len(tables),)),
        ],
        cost_estimate=kernel_cost(blocks),
        compiler_params=limit(rows_of(2 * blocks), table_room, acc_room, scores),
    )(codes, meta, hit, *stats, unit, *tables)
    return list(outs[:len(shapes)]), outs[len(shapes)], outs[-1]


def last_grads(codes, metas, hit, stats, turned, scores, units, tables, shapes, share_shapes):
    sizes = [unit.shape[0] for unit in units]
    tiles = sum(table.shape[0] for table in tables)
    chunks, blocks = len(sizes), sizes[-1]
    n_inputs = 2 * chunks - 1 + len(tables)
    table_room = ((tiles, TILE, D), jnp.bfloat16)
    acc_room = ((blocks + 1, BR, D), jnp.float32)
    tiles_room = ((tiles + 1, TILE, D), jnp.float32)
    early_room = rows_of(max(sizes[:-1], default=PIECES))
    kept = ((scores or codes)[0].shape[0], TILE, BR), jnp.bfloat16
    outs = pl.pallas_call(
        functools.partial(
            last_kernel, sizes, len(shapes), len(tables), len(stats), turned,
            len(share_shapes), tiles,
        ),
        out_shape=(
            *(jax.ShapeDtypeStruct(shape, jnp.bfloat16) for shape in shapes),
            *(jax.ShapeDtypeStruct(shape, jnp.bfloat16) for shape in share_shapes),
            jax.ShapeDtypeStruct((blocks, BR), jnp.float32),
        ),
        in_specs=[SMEM] * (2 * chunks) + [VMEM] * (1 + len(stats)) + [ANY] * n_inputs,
        out_specs=(*[ANY] * len(shapes), *[VMEM] * len(share_shapes), VMEM),
        scratch_shapes=[
            pltpu.VMEM(*rows_of(blocks)),
            pltpu.VMEM(*early_room),
            pltpu.VMEM(*kept),
            pltpu.VMEM(*table_room),
            pltpu.VMEM((blocks, BR), jnp.float32),
            pltpu.VMEM(*acc_room),
            pltpu.VMEM(*rows_of(blocks)),
            pltpu.VMEM(*tiles_room),
            pltpu.SemaphoreType.DMA((1 + len(tables),)),
            pltpu.SemaphoreType.DMA((2,)),
            pltpu.SemaphoreType.DMA((PIECES,)),
        ],
        cost_estimate=kernel_cost(sum(sizes)),
        compiler_params=limit(
            rows_of(2 * blocks), early_room, kept, table_room, table_room, acc_room, tiles_room
        ),
    )(*codes, *metas, hit, *stats, *scores, *units, *tables)
    cut = len(shapes)
    return list(outs[:cut]), list(outs[cut:-1]), outs[-1]


def add(first, second):
    return (first.astype(jnp.float32) + second.astype(jnp.float32)).astype(jnp.bfloat16)


class Neighbours:
    def __init__(self, nx, dp):
        self.nx, self.nz, self.dp, self.turned = nx, PIECES, dp, True

    def over_z(self, value, away):
        pairs = [
            (z * self.nx + x, (z ^ away) * self.nx + x)
            for z in range(self.nz) for x in range(self.nx)
        ]
        return lax.ppermute(value, "cls", pairs)

    def over_x(self, value):
        return lax.ppermute(value, "cls", [(c, c ^ 1) for c in range(self.nx * self.nz)])

    def over_y(self, value):
        return lax.ppermute(value, "dp", [(d, d ^ 2) for d in range(self.dp)])

    def over_core(self, value):
        return lax.ppermute(value, "dp", [(d, d ^ 1) for d in range(self.dp)])

    def all_over_z(self, value):
        return [value] + [self.over_z(value, away) for away in range(1, self.nz)]

    def gather(self, needed, chunks, lists, table, core, prepare):
        def moves(first, second, lists, table, core):
            half = table.shape[0] // 2
            sent = lax.dynamic_slice_in_dim(table, core * half, half, axis=0)
            far, near, from_x, second = lax.optimization_barrier(
                (self.over_z(first, 2), self.over_z(first, 1), self.over_x(sent), second)
            )
            passed, far_second = self.over_z(far, 1), self.over_z(second, 2)
            return (near, far, passed), far_second, (from_x, self.over_core(from_x)), prepare(
                jnp.stack(self.all_over_z(lists))
            )

        first, second = chunks
        pieces, far, tables, prepared = self.together(
            needed, moves, first, second, lists, table, core
        )
        return [[first, *pieces], [second, far]], [table, *tables], prepared

    def rest_of_rows(self, pieces, others):
        second, far = pieces
        passed = self.over_z(far, 1)
        near, others = lax.optimization_barrier((self.over_z(second, 1), others))
        return (near, passed), others

    def whole_rows(self, pieces, rest):
        (second, far), (near, passed) = pieces, rest
        return [second, near, far, passed]

    def grad_shapes(self, size):
        return [(size, BR, D)] * PIECES

    def gather_stats(self, stats):
        return self.all_over_z(stats)

    def order(self, place):
        return place

    def own(self, loss, place, size):
        return loss[:size]

    def early_return(self, early, others):
        parts, = early
        near, passed = self.over_z(parts[1], 1), self.over_z(parts[3], 1)
        passed, others = lax.optimization_barrier((passed, others))
        return (near, self.over_z(add(passed, parts[2]), 2)), others

    def early_sums(self, early, returned):
        return [sum(part.astype(jnp.float32) for part in (early[0][0], *returned))]

    def together(self, needed, work, *operands):
        def no_work(*operands):
            return jax.tree.map(
                lambda out: jnp.zeros(out.shape, out.dtype), jax.eval_shape(work, *operands)
            )

        return lax.cond(needed, work, no_work, *operands)

    def sum_last(self, parts, shares):
        kept, sent = shares
        passed, got = self.over_z(parts[3], 1), self.over_core(sent)
        near = self.over_z(parts[1], 1)
        half = kept.shape[2] // 2
        x_sent = add(kept[1, :, :half], got[1, :, :half])
        y_sent = add(kept[:, 1, half:], got[:, 1, half:])
        passed, _, _ = lax.optimization_barrier((passed, x_sent, y_sent))
        far = self.over_z(add(passed, parts[2]), 2)
        total = sum(part.astype(jnp.float32) for part in (parts[0], near, far))
        return total, self.sum_shares(kept, got, x_sent, y_sent)

    def share_shapes(self, shard_tiles):
        return [(self.nx, self.dp // 2, shard_tiles, TILE, D // self.dp)] * 2

    def sum_shares(self, kept, got, x_sent, y_sent):
        half = kept.shape[2] // 2
        x_got, y_got = lax.optimization_barrier((self.over_x(x_sent), self.over_y(y_sent)))
        x_kept = [add(add(kept[0, y, :half], got[0, y, :half]), x_got[y]) for y in range(2)]
        y_kept = [add(add(kept[x, 0, half:], got[x, 0, half:]), y_got[x]) for x in range(2)]
        low, high = lax.optimization_barrier((self.over_y(x_kept[1]), self.over_x(y_kept[1])))
        low = x_kept[0].astype(jnp.float32) + low.astype(jnp.float32)
        high = y_kept[0].astype(jnp.float32) + high.astype(jnp.float32)
        return jnp.concatenate([low, high], axis=0)


class Groups:
    def __init__(self, nz, dp):
        self.nx, self.nz, self.dp, self.turned = 1, nz, dp, False

    def gather(self, needed, chunks, lists, table, core, prepare):
        gathered = [[lax.all_gather(rows, "cls", tiled=True)] for rows in chunks]
        return gathered, [table], prepare(lax.all_gather(lists, "cls"))

    def rest_of_rows(self, pieces, others):
        return (), others

    def whole_rows(self, pieces, rest):
        return pieces

    def grad_shapes(self, size):
        return [(self.nz * size, BR, D)]

    def gather_stats(self, stats):
        return list(lax.all_gather(stats, "cls"))

    def order(self, place):
        return jnp.zeros_like(place)

    def own(self, loss, place, size):
        return lax.dynamic_slice_in_dim(loss, place * size, size, axis=0)

    def total(self, part):
        return lax.psum_scatter(
            part, "cls", scatter_dimension=0, tiled=True
        ).astype(jnp.float32)

    def early_return(self, early, others):
        return [self.total(part) for part, in early], others

    def early_sums(self, early, returned):
        return returned

    def together(self, needed, work, *operands):
        return work(*operands)

    def sum_last(self, parts, shares):
        return self.total(parts[0]), self.sum_shares(shares)

    def share_shapes(self, shard_tiles):
        return [(shard_tiles, TILE, D)]

    def sum_shares(self, shares):
        return lax.psum_scatter(
            shares[0], "dp", scatter_dimension=2, tiled=True
        ).astype(jnp.float32)


def pair_codes(lists, shard_tiles, nx, place, column, room):
    entry = lists[:, :K].reshape(-1)
    owner = entry // shard_tiles
    mine = (entry >= 0) & (owner // nx == place)
    local = jnp.where(owner % nx == column, 0, shard_tiles) + entry % shard_tiles
    counter = jnp.arange(entry.shape[0], dtype=jnp.int32)
    code = ((counter // K) * FIELD + local) * 2 + (counter % K == 0)
    rank = jnp.sum(
        jnp.where(mine[None, :] & (counter[None, :] < counter[:, None]), 1, 0), axis=1
    ).astype(jnp.int32)
    slots = jnp.arange(room, dtype=jnp.int32)
    chosen = mine[None, :] & (rank[None, :] == slots[:, None])
    padding = (lists.shape[0] * FIELD + nx * shard_tiles) * 2
    codes = padding + jnp.sum(jnp.where(chosen, code[None, :] - padding, 0), axis=1)
    return codes.astype(jnp.int32), jnp.sum(mine.astype(jnp.int32))


def per_device(moves, sizes, embeddings, proxies, hard_tiles, tile_count, labels):
    nx, nz, dp = moves.nx, moves.nz, moves.dp
    blocks = hard_tiles.shape[0]
    shard_tiles = proxies.shape[0] // TILE
    me, part = lax.axis_index("cls"), lax.axis_index("dp")
    place, column = me // nx, me % nx

    row_blocks = embeddings.reshape(blocks, BR, D)

    position = labels.reshape(blocks, BR) - hard_tiles[:, 0:1] * TILE
    entries = jnp.arange(K, dtype=jnp.int32)
    used = jnp.where(entries[None, :] < tile_count[:, None], hard_tiles, -1)
    starts = [sum(sizes[:chunk]) for chunk in range(len(sizes))]
    spots = [slice(start, start + size) for start, size in zip(starts, sizes)]
    held = [nz * size for size in sizes]
    last = len(sizes) - 1
    needed = tile_count[0] > 0

    def prepare(lists):
        prepared = []
        for spot, blocks_held in zip(spots, held):
            room = min(blocks_held * K, nz * (blocks * K // (nx * nz)) * nx)
            room = -(-room // PAIRS_PER_STEP) * PAIRS_PER_STEP
            chunk_lists = lists[:, spot].reshape(blocks_held, K + BR)
            code, count = pair_codes(chunk_lists, shard_tiles, nx, place, column, room)
            meta = jnp.stack([count, part, moves.order(place)]).astype(jnp.int32)
            prepared.append((code, meta, chunk_lists[:, K:]))
        return prepared

    gathered, tables, prepared = moves.gather(
        needed,
        [row_blocks[spot] for spot in spots],
        jnp.concatenate([used, position], axis=1),
        proxies.reshape(shard_tiles, TILE, D),
        part % 2,
        prepare,
    )

    def scored(chunk, rows, tables, prepared):
        parts, unit = score(held[chunk], *prepared[chunk], rows, tables)
        return moves.gather_stats(parts), unit

    def early_work(gathered, tables, prepared):
        units, made, rest = [], [], ()
        for chunk in range(last):
            stats, unit = scored(chunk, gathered[chunk], tables, prepared)
            if chunk == 0:
                rest, stats = moves.rest_of_rows(gathered[-1], stats)
            units.append(unit)
            made.append(grads(
                held[chunk], *prepared[chunk], stats, moves.turned, unit, tables,
                moves.grad_shapes(sizes[chunk]),
            ))
        return rest, units, made

    def last_work(rows, tables, prepared, units, scores, early):
        codes, metas, hits = zip(*prepared)
        stats, unit = scored(last, rows, tables, prepared)
        returned, stats = moves.early_return(early, stats)
        return returned, last_grads(
            codes, metas, hits[-1], stats, moves.turned, scores, units + [unit], tables,
            moves.grad_shapes(sizes[-1]), moves.share_shapes(shard_tiles),
        )

    rest, units, made = moves.together(needed, early_work, gathered, tables, prepared)
    rows = moves.whole_rows(gathered[-1], rest)
    early, scores, losses = zip(*made)
    returned, (parts, shares, loss) = moves.together(
        needed, last_work, rows, tables, prepared, units, list(scores), early
    )
    total, shares = moves.sum_last(parts, shares)
    row_grads = moves.early_sums(early, returned) + [total]
    losses = [
        moves.own(part, place, size) for part, size in zip((*losses, loss), sizes)
    ]

    embeddings, units = lax.optimization_barrier((embeddings, units))
    emb_exact = embeddings.astype(jnp.float32)
    inverse_norm = lax.rsqrt(jnp.sum(emb_exact * emb_exact, axis=1, keepdims=True) + epsilon)
    unit_exact = emb_exact * inverse_norm
    proxy_grad = shares.reshape(shard_tiles * TILE, D // dp)
    row_loss = jnp.concatenate(losses, axis=0).reshape(-1)
    grad_flat = jnp.concatenate(row_grads, axis=0)
    grad_flat = grad_flat.reshape(blocks * BR, D)
    radial = jnp.sum(unit_exact * grad_flat, axis=1, keepdims=True)
    embed_grad = ((grad_flat - unit_exact * radial) * inverse_norm).astype(jnp.bfloat16)
    return (row_loss, embed_grad, proxy_grad)


def solution(mesh):
    placed = (
        P(("dp", "cls"), None),
        P("cls", None),
        P(("dp", "cls"), None),
        P(("dp", "cls")),
        P(("dp", "cls")),
    )
    dp, groups = mesh.shape["dp"], mesh.shape["cls"]
    if (dp, groups) == (4, 2 * PIECES):
        moves, sizes = Neighbours(2, dp), [4, 4]
    else:
        chunks = max(1, groups // 8)
        moves, sizes = Groups(groups, dp), [8 // chunks] * chunks
    return jax.shard_map(
        functools.partial(per_device, moves, sizes),
        mesh=mesh,
        in_specs=placed,
        out_specs=(P(("dp", "cls")), P(("dp", "cls"), None), P("cls", "dp")),
        check_vma=False,
    )
```

```python
import functools

import jax
import jax.numpy as jnp
import numpy as np
from jax import lax
from jax.experimental import pallas as pl
from jax.experimental.pallas import tpu as pltpu
from jax.sharding import PartitionSpec as P

D = 512
TILE = 128
BR = 128
K = 8
PAIRS_PER_STEP = 4
FIELD = 128
PIECES = 4
VMEM_BYTES = 60 * 1024 * 1024
SPARE_BYTES = 4 * 1024 * 1024

logit_scale = 4.0
epsilon = 1e-06
unused_logit = -1e30

SMEM = pl.BlockSpec(memory_space=pltpu.SMEM)
VMEM = pl.BlockSpec(memory_space=pltpu.VMEM)
ANY = pl.BlockSpec(memory_space=pl.ANY)


def run_copies(jobs, sems, first=0):
    copies = [
        pltpu.make_async_copy(source, target, sems.at[first + index])
        for index, (source, target) in enumerate(jobs)
    ]
    for copy in copies:
        copy.start()
    return copies


def row_places(meta_ref, refs, blocks):
    size = blocks // PIECES
    if len(refs) > 1:
        return [(ref, piece * size) for piece, ref in enumerate(refs)]
    return [
        (refs[0].at[pl.ds(place * size, size)], (meta_ref[2] ^ place) * size)
        for place in range(PIECES)
    ]


def row_jobs(meta_ref, refs, rows_ref):
    return [
        (ref, rows_ref.at[pl.ds(start, ref.shape[0])])
        for ref, start in row_places(meta_ref, refs, rows_ref.shape[0])
    ]


def store_rows(meta_ref, rows_acc, out_ref, grad_refs, sems):
    blocks = out_ref.shape[0]
    out_ref[...] = rows_acc[:blocks].astype(out_ref.dtype)
    return run_copies(
        [
            (out_ref.at[pl.ds(start, ref.shape[0])], ref)
            for ref, start in row_places(meta_ref, grad_refs, blocks)
        ],
        sems,
    )


def aligned(refs, row, turned):
    parts = [ref[row] for ref in refs]
    if not turned:
        return parts
    size = parts[0].shape[0] // PIECES
    return [
        jnp.concatenate(
            [part[(piece ^ away) * size:((piece ^ away) + 1) * size] for piece in range(PIECES)]
        )
        for away, part in enumerate(parts)
    ]


def table_jobs(meta_ref, table_refs, table_ref):
    core = meta_ref[1] % 2
    jobs = [(table_refs[0], table_ref.at[pl.ds(0, table_refs[0].shape[0])])]
    if len(table_refs) > 1:
        half = table_refs[1].shape[0]
        jobs.append((table_refs[1], table_ref.at[pl.ds((2 + core) * half, half)]))
        jobs.append((table_refs[2], table_ref.at[pl.ds((3 - core) * half, half)]))
    return jobs


def transposed_logits(tile, rows):
    return logit_scale * lax.dot_general(
        tile, rows, (((1,), (1,)), ((), ())), preferred_element_type=jnp.float32
    )


def decode(code):
    return code // (2 * FIELD), (code // 2) % FIELD, (code % 2) == 1


def score_kernel(n_rows, n_tables, blocks, tiles, codes_ref, meta_ref, hit_ref, *refs):
    row_refs, refs = refs[:n_rows], refs[n_rows:]
    table_refs, refs = refs[:n_tables], refs[n_tables:]
    stats_ref, rows_ref, table_ref, lse_ref, pos_ref, sems = refs
    row_copies = run_copies(row_jobs(meta_ref, row_refs, rows_ref), sems)
    table_copies = run_copies(table_jobs(meta_ref, table_refs, table_ref), sems, PIECES)
    lse_ref[...] = jnp.full(lse_ref.shape, unused_logit, jnp.float32)
    pos_ref[...] = jnp.zeros(pos_ref.shape, jnp.float32)
    class_at = lax.broadcasted_iota(jnp.int32, (TILE, BR), 0)
    for copy in row_copies:
        copy.wait()

    def normalise(block, carry):
        exact = rows_ref[block].astype(jnp.float32)
        norm = lax.rsqrt(jnp.sum(exact * exact, axis=1, keepdims=True) + epsilon)
        rows_ref[block] = (exact * norm).astype(jnp.bfloat16)
        return carry

    lax.fori_loop(0, blocks, normalise, 0)
    for copy in table_copies:
        copy.wait()

    def step(index, carry):
        held = []
        for lane in range(PAIRS_PER_STEP):
            block, tile, first = decode(codes_ref[index * PAIRS_PER_STEP + lane])
            source = jnp.minimum(block, blocks - 1)
            logits = transposed_logits(
                table_ref[jnp.minimum(tile, tiles - 1)], rows_ref[source]
            )
            peak = jnp.max(logits, axis=0, keepdims=True)
            total = jnp.sum(jnp.exp(logits - peak), axis=0, keepdims=True)
            hit = class_at == hit_ref[pl.ds(source, 1), :]
            positive = jnp.sum(jnp.where(hit, logits, 0.0), axis=0, keepdims=True)
            held.append((block, peak + jnp.log(total), jnp.where(first, positive, 0.0)))
        for block, lse, positive in held:
            before = lse_ref[pl.ds(block, 1), :]
            top = jnp.maximum(before, lse)
            lse_ref[pl.ds(block, 1), :] = top + jnp.log(
                jnp.exp(before - top) + jnp.exp(lse - top)
            )
            pos_ref[pl.ds(block, 1), :] += positive
        return carry

    lax.fori_loop(0, pl.cdiv(meta_ref[0], PAIRS_PER_STEP), step, 0)
    stats_ref[0] = lse_ref[:blocks, :]
    stats_ref[1] = pos_ref[:blocks, :]


def make_totals(stat_refs, turned, total_ref, loss_ref):
    lse = aligned(stat_refs, 0, turned)
    top = functools.reduce(jnp.maximum, lse)
    total = top + jnp.log(sum(jnp.exp(part - top) for part in lse))
    total_ref[...] = total
    loss_ref[...] = total - sum(aligned(stat_refs, 1, turned))


def pair_score(code, blocks, tiles, rows_ref, table_ref, hit_ref, total_ref, class_at):
    block, tile, first = decode(code)
    source = jnp.minimum(block, blocks - 1)
    table_at = jnp.minimum(tile, tiles - 1)
    logits = transposed_logits(table_ref[table_at], rows_ref[source])
    share = jnp.exp(logits - total_ref[pl.ds(source, 1), :])
    wanted = jnp.where(first, hit_ref[pl.ds(source, 1), :], -1)
    hit = (class_at == wanted).astype(jnp.float32)
    return (logit_scale * (share - hit)).astype(jnp.bfloat16)


def row_terms(score, tile):
    return lax.dot_general(
        score, tile, (((0,), (0,)), ((), ())), preferred_element_type=jnp.float32
    )


def grad_kernel(
    n_grads, n_tables, n_stats, turned, blocks, tiles, codes_ref, meta_ref, hit_ref, *refs
):
    stat_refs, refs = refs[:n_stats], refs[n_stats:]
    unit_ref, refs = refs[0], refs[1:]
    table_refs, refs = refs[:n_tables], refs[n_tables:]
    grad_refs, refs = refs[:n_grads], refs[n_grads:]
    scores_ref, loss_ref, rows_ref, table_ref, total_ref, rows_acc, out_ref, sems = refs
    copies = run_copies(
        [(unit_ref, rows_ref)] + table_jobs(meta_ref, table_refs, table_ref), sems, PIECES
    )
    rows_acc[...] = jnp.zeros(rows_acc.shape, jnp.float32)
    make_totals(stat_refs, turned, total_ref, loss_ref)
    class_at = lax.broadcasted_iota(jnp.int32, (TILE, BR), 0)
    for copy in copies:
        copy.wait()

    def step(index, carry):
        held = []
        for lane in range(PAIRS_PER_STEP):
            pair = index * PAIRS_PER_STEP + lane
            score = pair_score(
                codes_ref[pair], blocks, tiles, rows_ref, table_ref, hit_ref, total_ref, class_at
            )
            scores_ref[pair] = score
            held.append(score)
        for lane, score in enumerate(held):
            block, tile, _ = decode(codes_ref[index * PAIRS_PER_STEP + lane])
            rows_acc[block] += row_terms(score, table_ref[jnp.minimum(tile, tiles - 1)])
        return carry

    lax.fori_loop(0, pl.cdiv(meta_ref[0], PAIRS_PER_STEP), step, 0)
    for copy in store_rows(meta_ref, rows_acc, out_ref, grad_refs, sems):
        copy.wait()


def last_kernel(sizes, n_grads, n_tables, n_stats, turned, n_shares, tiles, *refs):
    chunks, blocks = len(sizes), sizes[-1]
    codes_refs, refs = refs[:chunks], refs[chunks:]
    meta_refs, refs = refs[:chunks], refs[chunks:]
    hit_ref, refs = refs[0], refs[1:]
    stat_refs, refs = refs[:n_stats], refs[n_stats:]
    scores_refs, refs = refs[:chunks - 1], refs[chunks - 1:]
    unit_refs, refs = refs[:chunks], refs[chunks:]
    table_refs, refs = refs[:n_tables], refs[n_tables:]
    grad_refs, refs = refs[:n_grads], refs[n_grads:]
    share_refs, refs = refs[:n_shares], refs[n_shares:]
    loss_ref, refs = refs[0], refs[1:]
    rows_ref, early_ref, held_ref, table_ref, total_ref, rows_acc, out_ref, *refs = refs
    tiles_acc, sems, early_sems, row_sems = refs
    codes_ref, meta_ref = codes_refs[-1], meta_refs[-1]
    copies = run_copies(
        [(unit_refs[-1], rows_ref)] + table_jobs(meta_ref, table_refs, table_ref), sems
    )


    def fetch(chunk):
        early = early_ref.at[pl.ds(0, sizes[chunk])]
        return run_copies(
            [(unit_refs[chunk], early), (scores_refs[chunk], held_ref)], early_sems
        )

    early = fetch(0) if chunks > 1 else []
    rows_acc[...] = jnp.zeros(rows_acc.shape, jnp.float32)
    tiles_acc[...] = jnp.zeros(tiles_acc.shape, jnp.float32)
    make_totals(stat_refs, turned, total_ref, loss_ref)
    class_at = lax.broadcasted_iota(jnp.int32, (TILE, BR), 0)
    for copy in copies:
        copy.wait()

    def step(index, carry):
        held = [
            pair_score(
                codes_ref[index * PAIRS_PER_STEP + lane], blocks, tiles, rows_ref, table_ref,
                hit_ref, total_ref, class_at,
            )
            for lane in range(PAIRS_PER_STEP)
        ]
        for lane, score in enumerate(held):
            block, tile, _ = decode(codes_ref[index * PAIRS_PER_STEP + lane])
            rows_acc[block] += row_terms(score, table_ref[jnp.minimum(tile, tiles - 1)])
            tiles_acc[tile] += jnp.dot(
                score, rows_ref[jnp.minimum(block, blocks - 1)],
                preferred_element_type=jnp.float32,
            )
        return carry

    lax.fori_loop(0, pl.cdiv(meta_ref[0], PAIRS_PER_STEP), step, 0)
    stored = store_rows(meta_ref, rows_acc, out_ref, grad_refs, row_sems)
    for chunk in range(chunks - 1):
        for copy in early if chunk == 0 else fetch(chunk):
            copy.wait()

        def early_step(index, carry, chunk=chunk):
            for lane in range(PAIRS_PER_STEP):
                pair = index * PAIRS_PER_STEP + lane
                block, tile, _ = decode(codes_refs[chunk][pair])
                tiles_acc[tile] += jnp.dot(
                    held_ref[pair],
                    early_ref[jnp.minimum(block, sizes[chunk] - 1)],
                    preferred_element_type=jnp.float32,
                )
            return carry

        lax.fori_loop(0, pl.cdiv(meta_refs[chunk][0], PAIRS_PER_STEP), early_step, 0)
    if n_shares == 1:
        share_refs[0][...] = tiles_acc[:tiles].astype(jnp.bfloat16)
    else:
        part = meta_ref[1]
        shard, width = share_refs[0].shape[2], share_refs[0].shape[-1]
        for core, ref in enumerate(share_refs):
            for y in range(ref.shape[1]):
                start = pl.multiple_of(((2 * y + core) ^ part) * width, width)
                for x in range(ref.shape[0]):
                    ref[x, y] = tiles_acc[
                        pl.ds(x * shard, shard), :, pl.ds(start, width)
                    ].astype(jnp.bfloat16)
    for copy in stored:
        copy.wait()


def kernel_cost(blocks):
    return pl.CostEstimate(flops=blocks * BR * D, bytes_accessed=blocks * BR * D, transcendentals=0)


def limit(*scratch):
    total = 0
    for shape, dtype in scratch:
        total += int(np.prod(shape)) * jnp.dtype(dtype).itemsize
    return pltpu.CompilerParams(vmem_limit_bytes=min(VMEM_BYTES, total + SPARE_BYTES))


def rows_of(blocks):
    return (blocks, BR, D), jnp.bfloat16


def score(blocks, codes, meta, hit, rows, tables):
    tiles = sum(table.shape[0] for table in tables)
    table_room = ((tiles, TILE, D), jnp.bfloat16)
    return pl.pallas_call(
        functools.partial(score_kernel, len(rows), len(tables), blocks, tiles),
        out_shape=(
            jax.ShapeDtypeStruct((2, blocks, BR), jnp.float32),
            jax.ShapeDtypeStruct(*rows_of(blocks)),
        ),
        in_specs=[SMEM, SMEM, VMEM] + [ANY] * (len(rows) + len(tables)),
        out_specs=(VMEM, VMEM),
        scratch_shapes=[
            pltpu.VMEM(*table_room),
            pltpu.VMEM((blocks + 8, BR), jnp.float32),
            pltpu.VMEM((blocks + 8, BR), jnp.float32),
            pltpu.SemaphoreType.DMA((PIECES + len(tables),)),
        ],
        cost_estimate=kernel_cost(blocks),
        compiler_params=limit(rows_of(blocks), table_room),
    )(codes, meta, hit, *rows, *tables)


def grads(blocks, codes, meta, hit, stats, turned, unit, tables, shapes):
    tiles = sum(table.shape[0] for table in tables)
    table_room = ((tiles, TILE, D), jnp.bfloat16)
    acc_room = ((blocks + 1, BR, D), jnp.float32)
    scores = ((codes.shape[0], TILE, BR), jnp.bfloat16)
    outs = pl.pallas_call(
        functools.partial(
            grad_kernel, len(shapes), len(tables), len(stats), turned, blocks, tiles
        ),
        out_shape=(
            *(jax.ShapeDtypeStruct(shape, jnp.bfloat16) for shape in shapes),
            jax.ShapeDtypeStruct(*scores),
            jax.ShapeDtypeStruct((blocks, BR), jnp.float32),
        ),
        in_specs=[SMEM, SMEM] + [VMEM] * (1 + len(stats)) + [ANY] * (1 + len(tables)),
        out_specs=(*[ANY] * len(shapes), VMEM, VMEM),
        scratch_shapes=[
            pltpu.VMEM(*rows_of(blocks)),
            pltpu.VMEM(*table_room),
            pltpu.VMEM((blocks, BR), jnp.float32),
            pltpu.VMEM(*acc_room),
            pltpu.VMEM(*rows_of(blocks)),
            pltpu.SemaphoreType.DMA((PIECES + 1 + len(tables),)),
        ],
        cost_estimate=kernel_cost(blocks),
        compiler_params=limit(rows_of(2 * blocks), table_room, acc_room, scores),
    )(codes, meta, hit, *stats, unit, *tables)
    return list(outs[:len(shapes)]), outs[len(shapes)], outs[-1]


def last_grads(codes, metas, hit, stats, turned, scores, units, tables, shapes, share_shapes):
    sizes = [unit.shape[0] for unit in units]
    tiles = sum(table.shape[0] for table in tables)
    chunks, blocks = len(sizes), sizes[-1]
    n_inputs = 2 * chunks - 1 + len(tables)
    table_room = ((tiles, TILE, D), jnp.bfloat16)
    acc_room = ((blocks + 1, BR, D), jnp.float32)
    tiles_room = ((tiles + 1, TILE, D), jnp.float32)
    early_room = rows_of(max(sizes[:-1], default=PIECES))
    kept = ((scores or codes)[0].shape[0], TILE, BR), jnp.bfloat16
    outs = pl.pallas_call(
        functools.partial(
            last_kernel, sizes, len(shapes), len(tables), len(stats), turned,
            len(share_shapes), tiles,
        ),
        out_shape=(
            *(jax.ShapeDtypeStruct(shape, jnp.bfloat16) for shape in shapes),
            *(jax.ShapeDtypeStruct(shape, jnp.bfloat16) for shape in share_shapes),
            jax.ShapeDtypeStruct((blocks, BR), jnp.float32),
        ),
        in_specs=[SMEM] * (2 * chunks) + [VMEM] * (1 + len(stats)) + [ANY] * n_inputs,
        out_specs=(*[ANY] * len(shapes), *[VMEM] * len(share_shapes), VMEM),
        scratch_shapes=[
            pltpu.VMEM(*rows_of(blocks)),
            pltpu.VMEM(*early_room),
            pltpu.VMEM(*kept),
            pltpu.VMEM(*table_room),
            pltpu.VMEM((blocks, BR), jnp.float32),
            pltpu.VMEM(*acc_room),
            pltpu.VMEM(*rows_of(blocks)),
            pltpu.VMEM(*tiles_room),
            pltpu.SemaphoreType.DMA((1 + len(tables),)),
            pltpu.SemaphoreType.DMA((2,)),
            pltpu.SemaphoreType.DMA((PIECES,)),
        ],
        cost_estimate=kernel_cost(sum(sizes)),
        compiler_params=limit(
            rows_of(2 * blocks), early_room, kept, table_room, table_room, acc_room, tiles_room
        ),
    )(*codes, *metas, hit, *stats, *scores, *units, *tables)
    cut = len(shapes)
    return list(outs[:cut]), list(outs[cut:-1]), outs[-1]


def add(first, second):
    return (first.astype(jnp.float32) + second.astype(jnp.float32)).astype(jnp.bfloat16)


class Neighbours:
    def __init__(self, nx, dp):
        self.nx, self.nz, self.dp, self.turned = nx, PIECES, dp, True

    def over_z(self, value, away):
        pairs = [
            (z * self.nx + x, (z ^ away) * self.nx + x)
            for z in range(self.nz) for x in range(self.nx)
        ]
        return lax.ppermute(value, "cls", pairs)

    def over_x(self, value):
        return lax.ppermute(value, "cls", [(c, c ^ 1) for c in range(self.nx * self.nz)])

    def over_y(self, value):
        return lax.ppermute(value, "dp", [(d, d ^ 2) for d in range(self.dp)])

    def over_core(self, value):
        return lax.ppermute(value, "dp", [(d, d ^ 1) for d in range(self.dp)])

    def all_over_z(self, value):
        return [value] + [self.over_z(value, away) for away in range(1, self.nz)]

    def gather(self, needed, chunks, lists, table, core, prepare):
        def moves(first, lists, table, core):
            half = table.shape[0] // 2
            sent = lax.dynamic_slice_in_dim(table, core * half, half, axis=0)
            far, near, from_x = lax.optimization_barrier(
                (self.over_z(first, 2), self.over_z(first, 1), self.over_x(sent))
            )
            return (near, far, self.over_z(far, 1)), (from_x, self.over_core(from_x)), prepare(
                jnp.stack(self.all_over_z(lists))
            )

        first, second = chunks
        pieces, tables, prepared = self.together(needed, moves, first, lists, table, core)
        return [[first, *pieces], [second]], [table, *tables], prepared

    def rest_of_rows(self, pieces, others):
        second, = pieces
        far, near, others = lax.optimization_barrier(
            (self.over_z(second, 2), self.over_z(second, 1), others)
        )
        return (near, far, self.over_z(far, 1)), others

    def whole_rows(self, pieces, rest):
        return [*pieces, *rest]

    def grad_shapes(self, size):
        return [(size, BR, D)] * PIECES

    def gather_stats(self, stats):
        return self.all_over_z(stats)

    def order(self, place):
        return place

    def own(self, loss, place, size):
        return loss[:size]

    def early_return(self, early, others):
        parts, = early
        near, passed = self.over_z(parts[1], 1), self.over_z(parts[3], 1)
        passed, others = lax.optimization_barrier((passed, others))
        return (near, self.over_z(add(passed, parts[2]), 2)), others

    def early_sums(self, early, returned):
        return [sum(part.astype(jnp.float32) for part in (early[0][0], *returned))]

    def together(self, needed, work, *operands):
        def no_work(*operands):
            return jax.tree.map(
                lambda out: jnp.zeros(out.shape, out.dtype), jax.eval_shape(work, *operands)
            )

        return lax.cond(needed, work, no_work, *operands)

    def sum_last(self, parts, shares):
        kept, sent = shares
        passed, got = self.over_z(parts[3], 1), self.over_core(sent)
        near = self.over_z(parts[1], 1)
        half = kept.shape[2] // 2
        x_sent = add(kept[1, :, :half], got[1, :, :half])
        y_sent = add(kept[:, 1, half:], got[:, 1, half:])
        passed, _, _ = lax.optimization_barrier((passed, x_sent, y_sent))
        far = self.over_z(add(passed, parts[2]), 2)
        total = sum(part.astype(jnp.float32) for part in (parts[0], near, far))
        return total, self.sum_shares(kept, got, x_sent, y_sent)

    def share_shapes(self, shard_tiles):
        return [(self.nx, self.dp // 2, shard_tiles, TILE, D // self.dp)] * 2

    def sum_shares(self, kept, got, x_sent, y_sent):
        half = kept.shape[2] // 2
        x_got, y_got = lax.optimization_barrier((self.over_x(x_sent), self.over_y(y_sent)))
        x_kept = [add(add(kept[0, y, :half], got[0, y, :half]), x_got[y]) for y in range(2)]
        y_kept = [add(add(kept[x, 0, half:], got[x, 0, half:]), y_got[x]) for x in range(2)]
        low, high = lax.optimization_barrier((self.over_y(x_kept[1]), self.over_x(y_kept[1])))
        low = x_kept[0].astype(jnp.float32) + low.astype(jnp.float32)
        high = y_kept[0].astype(jnp.float32) + high.astype(jnp.float32)
        return jnp.concatenate([low, high], axis=0)


class Groups:
    def __init__(self, nz, dp):
        self.nx, self.nz, self.dp, self.turned = 1, nz, dp, False

    def gather(self, needed, chunks, lists, table, core, prepare):
        gathered = [[lax.all_gather(rows, "cls", tiled=True)] for rows in chunks]
        return gathered, [table], prepare(lax.all_gather(lists, "cls"))

    def rest_of_rows(self, pieces, others):
        return (), others

    def whole_rows(self, pieces, rest):
        return pieces

    def grad_shapes(self, size):
        return [(self.nz * size, BR, D)]

    def gather_stats(self, stats):
        return list(lax.all_gather(stats, "cls"))

    def order(self, place):
        return jnp.zeros_like(place)

    def own(self, loss, place, size):
        return lax.dynamic_slice_in_dim(loss, place * size, size, axis=0)

    def total(self, part):
        return lax.psum_scatter(
            part, "cls", scatter_dimension=0, tiled=True
        ).astype(jnp.float32)

    def early_return(self, early, others):
        return [self.total(part) for part, in early], others

    def early_sums(self, early, returned):
        return returned

    def together(self, needed, work, *operands):
        return work(*operands)

    def sum_last(self, parts, shares):
        return self.total(parts[0]), self.sum_shares(shares)

    def share_shapes(self, shard_tiles):
        return [(shard_tiles, TILE, D)]

    def sum_shares(self, shares):
        return lax.psum_scatter(
            shares[0], "dp", scatter_dimension=2, tiled=True
        ).astype(jnp.float32)


def pair_codes(lists, shard_tiles, nx, place, column, room):
    entry = lists[:, :K].reshape(-1)
    owner = entry // shard_tiles
    mine = (entry >= 0) & (owner // nx == place)
    local = jnp.where(owner % nx == column, 0, shard_tiles) + entry % shard_tiles
    counter = jnp.arange(entry.shape[0], dtype=jnp.int32)
    code = ((counter // K) * FIELD + local) * 2 + (counter % K == 0)
    rank = jnp.sum(
        jnp.where(mine[None, :] & (counter[None, :] < counter[:, None]), 1, 0), axis=1
    ).astype(jnp.int32)
    slots = jnp.arange(room, dtype=jnp.int32)
    chosen = mine[None, :] & (rank[None, :] == slots[:, None])
    padding = (lists.shape[0] * FIELD + nx * shard_tiles) * 2
    codes = padding + jnp.sum(jnp.where(chosen, code[None, :] - padding, 0), axis=1)
    return codes.astype(jnp.int32), jnp.sum(mine.astype(jnp.int32))


def per_device(moves, sizes, embeddings, proxies, hard_tiles, tile_count, labels):
    nx, nz, dp = moves.nx, moves.nz, moves.dp
    blocks = hard_tiles.shape[0]
    shard_tiles = proxies.shape[0] // TILE
    me, part = lax.axis_index("cls"), lax.axis_index("dp")
    place, column = me // nx, me % nx

    row_blocks = embeddings.reshape(blocks, BR, D)

    position = labels.reshape(blocks, BR) - hard_tiles[:, 0:1] * TILE
    entries = jnp.arange(K, dtype=jnp.int32)
    used = jnp.where(entries[None, :] < tile_count[:, None], hard_tiles, -1)
    starts = [sum(sizes[:chunk]) for chunk in range(len(sizes))]
    spots = [slice(start, start + size) for start, size in zip(starts, sizes)]
    held = [nz * size for size in sizes]
    last = len(sizes) - 1
    needed = tile_count[0] > 0

    def prepare(lists):
        prepared = []
        for spot, blocks_held in zip(spots, held):
            room = min(blocks_held * K, nz * (blocks * K // (nx * nz)) * nx)
            room = -(-room // PAIRS_PER_STEP) * PAIRS_PER_STEP
            chunk_lists = lists[:, spot].reshape(blocks_held, K + BR)
            code, count = pair_codes(chunk_lists, shard_tiles, nx, place, column, room)
            meta = jnp.stack([count, part, moves.order(place)]).astype(jnp.int32)
            prepared.append((code, meta, chunk_lists[:, K:]))
        return prepared

    gathered, tables, prepared = moves.gather(
        needed,
        [row_blocks[spot] for spot in spots],
        jnp.concatenate([used, position], axis=1),
        proxies.reshape(shard_tiles, TILE, D),
        part % 2,
        prepare,
    )

    def scored(chunk, rows, tables, prepared):
        parts, unit = score(held[chunk], *prepared[chunk], rows, tables)
        return moves.gather_stats(parts), unit

    def early_work(gathered, tables, prepared):
        units, made, rest = [], [], ()
        for chunk in range(last):
            stats, unit = scored(chunk, gathered[chunk], tables, prepared)
            if chunk == 0:
                rest, stats = moves.rest_of_rows(gathered[-1], stats)
            units.append(unit)
            made.append(grads(
                held[chunk], *prepared[chunk], stats, moves.turned, unit, tables,
                moves.grad_shapes(sizes[chunk]),
            ))
        return rest, units, made

    def last_work(rows, tables, prepared, units, scores, early):
        codes, metas, hits = zip(*prepared)
        stats, unit = scored(last, rows, tables, prepared)
        returned, stats = moves.early_return(early, stats)
        return returned, last_grads(
            codes, metas, hits[-1], stats, moves.turned, scores, units + [unit], tables,
            moves.grad_shapes(sizes[-1]), moves.share_shapes(shard_tiles),
        )

    rest, units, made = moves.together(needed, early_work, gathered, tables, prepared)
    rows = moves.whole_rows(gathered[-1], rest)
    early, scores, losses = zip(*made)
    returned, (parts, shares, loss) = moves.together(
        needed, last_work, rows, tables, prepared, units, list(scores), early
    )
    total, shares = moves.sum_last(parts, shares)
    row_grads = moves.early_sums(early, returned) + [total]
    losses = [
        moves.own(part, place, size) for part, size in zip((*losses, loss), sizes)
    ]

    embeddings, units = lax.optimization_barrier((embeddings, units))
    emb_exact = embeddings.astype(jnp.float32)
    inverse_norm = lax.rsqrt(jnp.sum(emb_exact * emb_exact, axis=1, keepdims=True) + epsilon)
    unit_exact = emb_exact * inverse_norm
    proxy_grad = shares.reshape(shard_tiles * TILE, D // dp)
    row_loss = jnp.concatenate(losses, axis=0).reshape(-1)
    grad_flat = jnp.concatenate(row_grads, axis=0)
    grad_flat = grad_flat.reshape(blocks * BR, D)
    radial = jnp.sum(unit_exact * grad_flat, axis=1, keepdims=True)
    embed_grad = ((grad_flat - unit_exact * radial) * inverse_norm).astype(jnp.bfloat16)
    return (row_loss, embed_grad, proxy_grad)


def solution(mesh):
    placed = (
        P(("dp", "cls"), None),
        P("cls", None),
        P(("dp", "cls"), None),
        P(("dp", "cls")),
        P(("dp", "cls")),
    )
    dp, groups = mesh.shape["dp"], mesh.shape["cls"]
    if (dp, groups) == (4, 2 * PIECES):
        moves, sizes = Neighbours(2, dp), [4, 4]
    else:
        chunks = max(1, groups // 8)
        moves, sizes = Groups(groups, dp), [8 // chunks] * chunks
    return jax.shard_map(
        functools.partial(per_device, moves, sizes),
        mesh=mesh,
        in_specs=placed,
        out_specs=(P(("dp", "cls")), P(("dp", "cls"), None), P("cls", "dp")),
        check_vma=False,
    )
```

```python
import functools

import jax
import jax.numpy as jnp
import numpy as np
from jax import lax
from jax.experimental import pallas as pl
from jax.experimental.pallas import tpu as pltpu
from jax.sharding import PartitionSpec as P

D = 512
TILE = 128
BR = 128
K = 8
PAIRS_PER_STEP = 4
FIELD = 128
PIECES = 4
VMEM_BYTES = 60 * 1024 * 1024
SPARE_BYTES = 4 * 1024 * 1024

logit_scale = 4.0
epsilon = 1e-06
unused_logit = -1e30

SMEM = pl.BlockSpec(memory_space=pltpu.SMEM)
VMEM = pl.BlockSpec(memory_space=pltpu.VMEM)
ANY = pl.BlockSpec(memory_space=pl.ANY)


def run_copies(jobs, sems, first=0):
    copies = [
        pltpu.make_async_copy(source, target, sems.at[first + index])
        for index, (source, target) in enumerate(jobs)
    ]
    for copy in copies:
        copy.start()
    return copies


def row_places(meta_ref, refs, blocks):
    size = blocks // PIECES
    if len(refs) > 1:
        return [(ref, piece * size) for piece, ref in enumerate(refs)]
    return [
        (refs[0].at[pl.ds(place * size, size)], (meta_ref[2] ^ place) * size)
        for place in range(PIECES)
    ]


def row_jobs(meta_ref, refs, rows_ref):
    return [
        (ref, rows_ref.at[pl.ds(start, ref.shape[0])])
        for ref, start in row_places(meta_ref, refs, rows_ref.shape[0])
    ]


def store_rows(meta_ref, rows_acc, out_ref, grad_refs, sems):
    blocks = out_ref.shape[0]
    out_ref[...] = rows_acc[:blocks].astype(out_ref.dtype)
    return run_copies(
        [
            (out_ref.at[pl.ds(start, ref.shape[0])], ref)
            for ref, start in row_places(meta_ref, grad_refs, blocks)
        ],
        sems,
    )


def aligned(refs, row, turned):
    parts = [ref[row] for ref in refs]
    if not turned:
        return parts
    size = parts[0].shape[0] // PIECES
    return [
        jnp.concatenate(
            [part[(piece ^ away) * size:((piece ^ away) + 1) * size] for piece in range(PIECES)]
        )
        for away, part in enumerate(parts)
    ]


def table_jobs(meta_ref, table_refs, table_ref):
    core = meta_ref[1] % 2
    jobs = [(table_refs[0], table_ref.at[pl.ds(0, table_refs[0].shape[0])])]
    if len(table_refs) > 1:
        half = table_refs[1].shape[0]
        jobs.append((table_refs[1], table_ref.at[pl.ds((2 + core) * half, half)]))
        jobs.append((table_refs[2], table_ref.at[pl.ds((3 - core) * half, half)]))
    return jobs


def transposed_logits(tile, rows):
    return logit_scale * lax.dot_general(
        tile, rows, (((1,), (1,)), ((), ())), preferred_element_type=jnp.float32
    )


def decode(code):
    return code // (2 * FIELD), (code // 2) % FIELD, (code % 2) == 1


def score_kernel(n_rows, n_tables, blocks, tiles, codes_ref, meta_ref, hit_ref, *refs):
    row_refs, refs = refs[:n_rows], refs[n_rows:]
    table_refs, refs = refs[:n_tables], refs[n_tables:]
    stats_ref, rows_ref, table_ref, lse_ref, pos_ref, sems = refs
    row_copies = run_copies(row_jobs(meta_ref, row_refs, rows_ref), sems)
    table_copies = run_copies(table_jobs(meta_ref, table_refs, table_ref), sems, PIECES)
    lse_ref[...] = jnp.full(lse_ref.shape, unused_logit, jnp.float32)
    pos_ref[...] = jnp.zeros(pos_ref.shape, jnp.float32)
    class_at = lax.broadcasted_iota(jnp.int32, (TILE, BR), 0)
    for copy in row_copies:
        copy.wait()

    def normalise(block, carry):
        exact = rows_ref[block].astype(jnp.float32)
        norm = lax.rsqrt(jnp.sum(exact * exact, axis=1, keepdims=True) + epsilon)
        rows_ref[block] = (exact * norm).astype(jnp.bfloat16)
        return carry

    lax.fori_loop(0, blocks, normalise, 0)
    for copy in table_copies:
        copy.wait()

    def step(index, carry):
        held = []
        for lane in range(PAIRS_PER_STEP):
            block, tile, first = decode(codes_ref[index * PAIRS_PER_STEP + lane])
            source = jnp.minimum(block, blocks - 1)
            logits = transposed_logits(
                table_ref[jnp.minimum(tile, tiles - 1)], rows_ref[source]
            )
            peak = jnp.max(logits, axis=0, keepdims=True)
            total = jnp.sum(jnp.exp(logits - peak), axis=0, keepdims=True)
            hit = class_at == hit_ref[pl.ds(source, 1), :]
            positive = jnp.sum(jnp.where(hit, logits, 0.0), axis=0, keepdims=True)
            held.append((block, peak + jnp.log(total), jnp.where(first, positive, 0.0)))
        for block, lse, positive in held:
            before = lse_ref[pl.ds(block, 1), :]
            top = jnp.maximum(before, lse)
            lse_ref[pl.ds(block, 1), :] = top + jnp.log(
                jnp.exp(before - top) + jnp.exp(lse - top)
            )
            pos_ref[pl.ds(block, 1), :] += positive
        return carry

    lax.fori_loop(0, pl.cdiv(meta_ref[0], PAIRS_PER_STEP), step, 0)
    stats_ref[0] = lse_ref[:blocks, :]
    stats_ref[1] = pos_ref[:blocks, :]


def make_totals(stat_refs, turned, total_ref, loss_ref):
    lse = aligned(stat_refs, 0, turned)
    top = functools.reduce(jnp.maximum, lse)
    total = top + jnp.log(sum(jnp.exp(part - top) for part in lse))
    total_ref[...] = total
    loss_ref[...] = total - sum(aligned(stat_refs, 1, turned))


def pair_score(code, blocks, tiles, rows_ref, table_ref, hit_ref, total_ref, class_at):
    block, tile, first = decode(code)
    source = jnp.minimum(block, blocks - 1)
    table_at = jnp.minimum(tile, tiles - 1)
    logits = transposed_logits(table_ref[table_at], rows_ref[source])
    share = jnp.exp(logits - total_ref[pl.ds(source, 1), :])
    wanted = jnp.where(first, hit_ref[pl.ds(source, 1), :], -1)
    hit = (class_at == wanted).astype(jnp.float32)
    return (logit_scale * (share - hit)).astype(jnp.bfloat16)


def row_terms(score, tile):
    return lax.dot_general(
        score, tile, (((0,), (0,)), ((), ())), preferred_element_type=jnp.float32
    )


def grad_kernel(
    n_grads, n_tables, n_stats, turned, blocks, tiles, codes_ref, meta_ref, hit_ref, *refs
):
    stat_refs, refs = refs[:n_stats], refs[n_stats:]
    unit_ref, refs = refs[0], refs[1:]
    table_refs, refs = refs[:n_tables], refs[n_tables:]
    grad_refs, refs = refs[:n_grads], refs[n_grads:]
    scores_ref, loss_ref, rows_ref, table_ref, total_ref, rows_acc, out_ref, sems = refs
    copies = run_copies(
        [(unit_ref, rows_ref)] + table_jobs(meta_ref, table_refs, table_ref), sems, PIECES
    )
    rows_acc[...] = jnp.zeros(rows_acc.shape, jnp.float32)
    make_totals(stat_refs, turned, total_ref, loss_ref)
    class_at = lax.broadcasted_iota(jnp.int32, (TILE, BR), 0)
    for copy in copies:
        copy.wait()

    def step(index, carry):
        held = []
        for lane in range(PAIRS_PER_STEP):
            pair = index * PAIRS_PER_STEP + lane
            score = pair_score(
                codes_ref[pair], blocks, tiles, rows_ref, table_ref, hit_ref, total_ref, class_at
            )
            scores_ref[pair] = score
            held.append(score)
        for lane, score in enumerate(held):
            block, tile, _ = decode(codes_ref[index * PAIRS_PER_STEP + lane])
            rows_acc[block] += row_terms(score, table_ref[jnp.minimum(tile, tiles - 1)])
        return carry

    lax.fori_loop(0, pl.cdiv(meta_ref[0], PAIRS_PER_STEP), step, 0)
    for copy in store_rows(meta_ref, rows_acc, out_ref, grad_refs, sems):
        copy.wait()


def last_kernel(sizes, n_grads, n_tables, n_stats, turned, n_shares, tiles, *refs):
    chunks, blocks = len(sizes), sizes[-1]
    codes_refs, refs = refs[:chunks], refs[chunks:]
    meta_refs, refs = refs[:chunks], refs[chunks:]
    hit_ref, refs = refs[0], refs[1:]
    stat_refs, refs = refs[:n_stats], refs[n_stats:]
    scores_refs, refs = refs[:chunks - 1], refs[chunks - 1:]
    unit_refs, refs = refs[:chunks], refs[chunks:]
    table_refs, refs = refs[:n_tables], refs[n_tables:]
    grad_refs, refs = refs[:n_grads], refs[n_grads:]
    share_refs, refs = refs[:n_shares], refs[n_shares:]
    loss_ref, refs = refs[0], refs[1:]
    rows_ref, early_ref, held_ref, table_ref, total_ref, rows_acc, out_ref, *refs = refs
    tiles_acc, sems, early_sems, row_sems = refs
    codes_ref, meta_ref = codes_refs[-1], meta_refs[-1]
    copies = run_copies(
        [(unit_refs[-1], rows_ref)] + table_jobs(meta_ref, table_refs, table_ref), sems
    )


    def fetch(chunk):
        early = early_ref.at[pl.ds(0, sizes[chunk])]
        return run_copies(
            [(unit_refs[chunk], early), (scores_refs[chunk], held_ref)], early_sems
        )

    early = fetch(0) if chunks > 1 else []
    rows_acc[...] = jnp.zeros(rows_acc.shape, jnp.float32)
    tiles_acc[...] = jnp.zeros(tiles_acc.shape, jnp.float32)
    make_totals(stat_refs, turned, total_ref, loss_ref)
    class_at = lax.broadcasted_iota(jnp.int32, (TILE, BR), 0)
    for copy in copies:
        copy.wait()

    def step(index, carry):
        held = [
            pair_score(
                codes_ref[index * PAIRS_PER_STEP + lane], blocks, tiles, rows_ref, table_ref,
                hit_ref, total_ref, class_at,
            )
            for lane in range(PAIRS_PER_STEP)
        ]
        for lane, score in enumerate(held):
            block, tile, _ = decode(codes_ref[index * PAIRS_PER_STEP + lane])
            rows_acc[block] += row_terms(score, table_ref[jnp.minimum(tile, tiles - 1)])
            tiles_acc[tile] += jnp.dot(
                score, rows_ref[jnp.minimum(block, blocks - 1)],
                preferred_element_type=jnp.float32,
            )
        return carry

    lax.fori_loop(0, pl.cdiv(meta_ref[0], PAIRS_PER_STEP), step, 0)
    stored = store_rows(meta_ref, rows_acc, out_ref, grad_refs, row_sems)
    for chunk in range(chunks - 1):
        for copy in early if chunk == 0 else fetch(chunk):
            copy.wait()

        def early_step(index, carry, chunk=chunk):
            for lane in range(PAIRS_PER_STEP):
                pair = index * PAIRS_PER_STEP + lane
                block, tile, _ = decode(codes_refs[chunk][pair])
                tiles_acc[tile] += jnp.dot(
                    held_ref[pair],
                    early_ref[jnp.minimum(block, sizes[chunk] - 1)],
                    preferred_element_type=jnp.float32,
                )
            return carry

        lax.fori_loop(0, pl.cdiv(meta_refs[chunk][0], PAIRS_PER_STEP), early_step, 0)
    if n_shares == 1:
        share_refs[0][...] = tiles_acc[:tiles].astype(jnp.bfloat16)
    else:
        part = meta_ref[1]
        shard, width = share_refs[0].shape[2], share_refs[0].shape[-1]
        for core, ref in enumerate(share_refs):
            for y in range(ref.shape[1]):
                start = pl.multiple_of(((2 * y + core) ^ part) * width, width)
                for x in range(ref.shape[0]):
                    ref[x, y] = tiles_acc[
                        pl.ds(x * shard, shard), :, pl.ds(start, width)
                    ].astype(jnp.bfloat16)
    for copy in stored:
        copy.wait()


def kernel_cost(blocks):
    return pl.CostEstimate(flops=blocks * BR * D, bytes_accessed=blocks * BR * D, transcendentals=0)


def limit(*scratch):
    total = 0
    for shape, dtype in scratch:
        total += int(np.prod(shape)) * jnp.dtype(dtype).itemsize
    return pltpu.CompilerParams(vmem_limit_bytes=min(VMEM_BYTES, total + SPARE_BYTES))


def rows_of(blocks):
    return (blocks, BR, D), jnp.bfloat16


def score(blocks, codes, meta, hit, rows, tables):
    tiles = sum(table.shape[0] for table in tables)
    table_room = ((tiles, TILE, D), jnp.bfloat16)
    return pl.pallas_call(
        functools.partial(score_kernel, len(rows), len(tables), blocks, tiles),
        out_shape=(
            jax.ShapeDtypeStruct((2, blocks, BR), jnp.float32),
            jax.ShapeDtypeStruct(*rows_of(blocks)),
        ),
        in_specs=[SMEM, SMEM, VMEM] + [ANY] * (len(rows) + len(tables)),
        out_specs=(VMEM, VMEM),
        scratch_shapes=[
            pltpu.VMEM(*table_room),
            pltpu.VMEM((blocks + 8, BR), jnp.float32),
            pltpu.VMEM((blocks + 8, BR), jnp.float32),
            pltpu.SemaphoreType.DMA((PIECES + len(tables),)),
        ],
        cost_estimate=kernel_cost(blocks),
        compiler_params=limit(rows_of(blocks), table_room),
    )(codes, meta, hit, *rows, *tables)


def grads(blocks, codes, meta, hit, stats, turned, unit, tables, shapes):
    tiles = sum(table.shape[0] for table in tables)
    table_room = ((tiles, TILE, D), jnp.bfloat16)
    acc_room = ((blocks + 1, BR, D), jnp.float32)
    scores = ((codes.shape[0], TILE, BR), jnp.bfloat16)
    outs = pl.pallas_call(
        functools.partial(
            grad_kernel, len(shapes), len(tables), len(stats), turned, blocks, tiles
        ),
        out_shape=(
            *(jax.ShapeDtypeStruct(shape, jnp.bfloat16) for shape in shapes),
            jax.ShapeDtypeStruct(*scores),
            jax.ShapeDtypeStruct((blocks, BR), jnp.float32),
        ),
        in_specs=[SMEM, SMEM] + [VMEM] * (1 + len(stats)) + [ANY] * (1 + len(tables)),
        out_specs=(*[ANY] * len(shapes), VMEM, VMEM),
        scratch_shapes=[
            pltpu.VMEM(*rows_of(blocks)),
            pltpu.VMEM(*table_room),
            pltpu.VMEM((blocks, BR), jnp.float32),
            pltpu.VMEM(*acc_room),
            pltpu.VMEM(*rows_of(blocks)),
            pltpu.SemaphoreType.DMA((PIECES + 1 + len(tables),)),
        ],
        cost_estimate=kernel_cost(blocks),
        compiler_params=limit(rows_of(2 * blocks), table_room, acc_room, scores),
    )(codes, meta, hit, *stats, unit, *tables)
    return list(outs[:len(shapes)]), outs[len(shapes)], outs[-1]


def last_grads(codes, metas, hit, stats, turned, scores, units, tables, shapes, share_shapes):
    sizes = [unit.shape[0] for unit in units]
    tiles = sum(table.shape[0] for table in tables)
    chunks, blocks = len(sizes), sizes[-1]
    n_inputs = 2 * chunks - 1 + len(tables)
    table_room = ((tiles, TILE, D), jnp.bfloat16)
    acc_room = ((blocks + 1, BR, D), jnp.float32)
    tiles_room = ((tiles + 1, TILE, D), jnp.float32)
    early_room = rows_of(max(sizes[:-1], default=PIECES))
    kept = ((scores or codes)[0].shape[0], TILE, BR), jnp.bfloat16
    outs = pl.pallas_call(
        functools.partial(
            last_kernel, sizes, len(shapes), len(tables), len(stats), turned,
            len(share_shapes), tiles,
        ),
        out_shape=(
            *(jax.ShapeDtypeStruct(shape, jnp.bfloat16) for shape in shapes),
            *(jax.ShapeDtypeStruct(shape, jnp.bfloat16) for shape in share_shapes),
            jax.ShapeDtypeStruct((blocks, BR), jnp.float32),
        ),
        in_specs=[SMEM] * (2 * chunks) + [VMEM] * (1 + len(stats)) + [ANY] * n_inputs,
        out_specs=(*[ANY] * len(shapes), *[VMEM] * len(share_shapes), VMEM),
        scratch_shapes=[
            pltpu.VMEM(*rows_of(blocks)),
            pltpu.VMEM(*early_room),
            pltpu.VMEM(*kept),
            pltpu.VMEM(*table_room),
            pltpu.VMEM((blocks, BR), jnp.float32),
            pltpu.VMEM(*acc_room),
            pltpu.VMEM(*rows_of(blocks)),
            pltpu.VMEM(*tiles_room),
            pltpu.SemaphoreType.DMA((1 + len(tables),)),
            pltpu.SemaphoreType.DMA((2,)),
            pltpu.SemaphoreType.DMA((PIECES,)),
        ],
        cost_estimate=kernel_cost(sum(sizes)),
        compiler_params=limit(
            rows_of(2 * blocks), early_room, kept, table_room, table_room, acc_room, tiles_room
        ),
    )(*codes, *metas, hit, *stats, *scores, *units, *tables)
    cut = len(shapes)
    return list(outs[:cut]), list(outs[cut:-1]), outs[-1]


def add(first, second):
    return (first.astype(jnp.float32) + second.astype(jnp.float32)).astype(jnp.bfloat16)


class Neighbours:
    def __init__(self, nx, dp):
        self.nx, self.nz, self.dp, self.turned = nx, PIECES, dp, True

    def over_z(self, value, away):
        pairs = [
            (z * self.nx + x, (z ^ away) * self.nx + x)
            for z in range(self.nz) for x in range(self.nx)
        ]
        return lax.ppermute(value, "cls", pairs)

    def over_x(self, value):
        return lax.ppermute(value, "cls", [(c, c ^ 1) for c in range(self.nx * self.nz)])

    def over_y(self, value):
        return lax.ppermute(value, "dp", [(d, d ^ 2) for d in range(self.dp)])

    def over_core(self, value):
        return lax.ppermute(value, "dp", [(d, d ^ 1) for d in range(self.dp)])

    def all_over_z(self, value):
        return [value] + [self.over_z(value, away) for away in range(1, self.nz)]

    def gather(self, needed, chunks, lists, table, core, prepare):
        def moves(first, lists, table, core):
            half = table.shape[0] // 2
            sent = lax.dynamic_slice_in_dim(table, core * half, half, axis=0)
            far, near, from_x = lax.optimization_barrier(
                (self.over_z(first, 2), self.over_z(first, 1), self.over_x(sent))
            )
            return (near, far, self.over_z(far, 1)), (from_x, self.over_core(from_x)), prepare(
                jnp.stack(self.all_over_z(lists))
            )

        first, second = chunks
        pieces, tables, prepared = self.together(needed, moves, first, lists, table, core)
        return [[first, *pieces], [second]], [table, *tables], prepared

    def rest_of_rows(self, pieces, others):
        second, = pieces
        far, near, others = lax.optimization_barrier(
            (self.over_z(second, 2), self.over_z(second, 1), others)
        )
        return (near, far, self.over_z(far, 1)), others

    def whole_rows(self, pieces, rest):
        return [*pieces, *rest]

    def grad_shapes(self, size):
        return [(size, BR, D)] * PIECES

    def gather_stats(self, stats):
        return self.all_over_z(stats)

    def order(self, place):
        return place

    def own(self, loss, place, size):
        return loss[:size]

    def early_return(self, early, others):
        parts, = early
        near, passed = self.over_z(parts[1], 1), self.over_z(parts[3], 1)
        passed, others = lax.optimization_barrier((passed, others))
        return (near, self.over_z(add(passed, parts[2]), 2)), others

    def early_sums(self, early, returned):
        return [sum(part.astype(jnp.float32) for part in (early[0][0], *returned))]

    def together(self, needed, work, *operands):
        def no_work(*operands):
            return jax.tree.map(
                lambda out: jnp.zeros(out.shape, out.dtype), jax.eval_shape(work, *operands)
            )

        return lax.cond(needed, work, no_work, *operands)

    def sum_last(self, parts, shares):
        kept, sent = shares
        passed, got = self.over_z(parts[3], 1), self.over_core(sent)
        near = self.over_z(parts[1], 1)
        half = kept.shape[2] // 2
        x_sent = add(kept[1, :, :half], got[1, :, :half])
        y_sent = add(kept[:, 1, half:], got[:, 1, half:])
        passed, _, _ = lax.optimization_barrier((passed, x_sent, y_sent))
        far = self.over_z(add(passed, parts[2]), 2)
        near, far, shares = self.sum_shares(near, far, kept, got, x_sent, y_sent)
        return sum(part.astype(jnp.float32) for part in (parts[0], near, far)), shares

    def share_shapes(self, shard_tiles):
        return [(self.nx, self.dp // 2, shard_tiles, TILE, D // self.dp)] * 2

    def sum_shares(self, near, far, kept, got, x_sent, y_sent):
        half = kept.shape[2] // 2
        x_got, y_got = lax.optimization_barrier((self.over_x(x_sent), self.over_y(y_sent)))
        x_kept = [add(add(kept[0, y, :half], got[0, y, :half]), x_got[y]) for y in range(2)]
        y_kept = [add(add(kept[x, 0, half:], got[x, 0, half:]), y_got[x]) for x in range(2)]
        near, far, low, high = lax.optimization_barrier(
            (near, far, self.over_y(x_kept[1]), self.over_x(y_kept[1]))
        )
        low = x_kept[0].astype(jnp.float32) + low.astype(jnp.float32)
        high = y_kept[0].astype(jnp.float32) + high.astype(jnp.float32)
        return near, far, jnp.concatenate([low, high], axis=0)


class Groups:
    def __init__(self, nz, dp):
        self.nx, self.nz, self.dp, self.turned = 1, nz, dp, False

    def gather(self, needed, chunks, lists, table, core, prepare):
        gathered = [[lax.all_gather(rows, "cls", tiled=True)] for rows in chunks]
        return gathered, [table], prepare(lax.all_gather(lists, "cls"))

    def rest_of_rows(self, pieces, others):
        return (), others

    def whole_rows(self, pieces, rest):
        return pieces

    def grad_shapes(self, size):
        return [(self.nz * size, BR, D)]

    def gather_stats(self, stats):
        return list(lax.all_gather(stats, "cls"))

    def order(self, place):
        return jnp.zeros_like(place)

    def own(self, loss, place, size):
        return lax.dynamic_slice_in_dim(loss, place * size, size, axis=0)

    def total(self, part):
        return lax.psum_scatter(
            part, "cls", scatter_dimension=0, tiled=True
        ).astype(jnp.float32)

    def early_return(self, early, others):
        return [self.total(part) for part, in early], others

    def early_sums(self, early, returned):
        return returned

    def together(self, needed, work, *operands):
        return work(*operands)

    def sum_last(self, parts, shares):
        return self.total(parts[0]), self.sum_shares(shares)

    def share_shapes(self, shard_tiles):
        return [(shard_tiles, TILE, D)]

    def sum_shares(self, shares):
        return lax.psum_scatter(
            shares[0], "dp", scatter_dimension=2, tiled=True
        ).astype(jnp.float32)


def pair_codes(lists, shard_tiles, nx, place, column, room):
    entry = lists[:, :K].reshape(-1)
    owner = entry // shard_tiles
    mine = (entry >= 0) & (owner // nx == place)
    local = jnp.where(owner % nx == column, 0, shard_tiles) + entry % shard_tiles
    counter = jnp.arange(entry.shape[0], dtype=jnp.int32)
    code = ((counter // K) * FIELD + local) * 2 + (counter % K == 0)
    rank = jnp.sum(
        jnp.where(mine[None, :] & (counter[None, :] < counter[:, None]), 1, 0), axis=1
    ).astype(jnp.int32)
    slots = jnp.arange(room, dtype=jnp.int32)
    chosen = mine[None, :] & (rank[None, :] == slots[:, None])
    padding = (lists.shape[0] * FIELD + nx * shard_tiles) * 2
    codes = padding + jnp.sum(jnp.where(chosen, code[None, :] - padding, 0), axis=1)
    return codes.astype(jnp.int32), jnp.sum(mine.astype(jnp.int32))


def per_device(moves, sizes, embeddings, proxies, hard_tiles, tile_count, labels):
    nx, nz, dp = moves.nx, moves.nz, moves.dp
    blocks = hard_tiles.shape[0]
    shard_tiles = proxies.shape[0] // TILE
    me, part = lax.axis_index("cls"), lax.axis_index("dp")
    place, column = me // nx, me % nx

    row_blocks = embeddings.reshape(blocks, BR, D)

    position = labels.reshape(blocks, BR) - hard_tiles[:, 0:1] * TILE
    entries = jnp.arange(K, dtype=jnp.int32)
    used = jnp.where(entries[None, :] < tile_count[:, None], hard_tiles, -1)
    starts = [sum(sizes[:chunk]) for chunk in range(len(sizes))]
    spots = [slice(start, start + size) for start, size in zip(starts, sizes)]
    held = [nz * size for size in sizes]
    last = len(sizes) - 1
    needed = tile_count[0] > 0

    def prepare(lists):
        prepared = []
        for spot, blocks_held in zip(spots, held):
            room = min(blocks_held * K, nz * (blocks * K // (nx * nz)) * nx)
            room = -(-room // PAIRS_PER_STEP) * PAIRS_PER_STEP
            chunk_lists = lists[:, spot].reshape(blocks_held, K + BR)
            code, count = pair_codes(chunk_lists, shard_tiles, nx, place, column, room)
            meta = jnp.stack([count, part, moves.order(place)]).astype(jnp.int32)
            prepared.append((code, meta, chunk_lists[:, K:]))
        return prepared

    gathered, tables, prepared = moves.gather(
        needed,
        [row_blocks[spot] for spot in spots],
        jnp.concatenate([used, position], axis=1),
        proxies.reshape(shard_tiles, TILE, D),
        part % 2,
        prepare,
    )

    def scored(chunk, rows, tables, prepared):
        parts, unit = score(held[chunk], *prepared[chunk], rows, tables)
        return moves.gather_stats(parts), unit

    def early_work(gathered, tables, prepared):
        units, made, rest = [], [], ()
        for chunk in range(last):
            stats, unit = scored(chunk, gathered[chunk], tables, prepared)
            if chunk == 0:
                rest, stats = moves.rest_of_rows(gathered[-1], stats)
            units.append(unit)
            made.append(grads(
                held[chunk], *prepared[chunk], stats, moves.turned, unit, tables,
                moves.grad_shapes(sizes[chunk]),
            ))
        return rest, units, made

    def last_work(rows, tables, prepared, units, scores, early):
        codes, metas, hits = zip(*prepared)
        stats, unit = scored(last, rows, tables, prepared)
        returned, stats = moves.early_return(early, stats)
        return returned, last_grads(
            codes, metas, hits[-1], stats, moves.turned, scores, units + [unit], tables,
            moves.grad_shapes(sizes[-1]), moves.share_shapes(shard_tiles),
        )

    rest, units, made = moves.together(needed, early_work, gathered, tables, prepared)
    rows = moves.whole_rows(gathered[-1], rest)
    early, scores, losses = zip(*made)
    returned, (parts, shares, loss) = moves.together(
        needed, last_work, rows, tables, prepared, units, list(scores), early
    )
    total, shares = moves.sum_last(parts, shares)
    row_grads = moves.early_sums(early, returned) + [total]
    losses = [
        moves.own(part, place, size) for part, size in zip((*losses, loss), sizes)
    ]

    embeddings, units = lax.optimization_barrier((embeddings, units))
    emb_exact = embeddings.astype(jnp.float32)
    inverse_norm = lax.rsqrt(jnp.sum(emb_exact * emb_exact, axis=1, keepdims=True) + epsilon)
    unit_exact = emb_exact * inverse_norm
    proxy_grad = shares.reshape(shard_tiles * TILE, D // dp)
    row_loss = jnp.concatenate(losses, axis=0).reshape(-1)
    grad_flat = jnp.concatenate(row_grads, axis=0)
    grad_flat = grad_flat.reshape(blocks * BR, D)
    radial = jnp.sum(unit_exact * grad_flat, axis=1, keepdims=True)
    embed_grad = ((grad_flat - unit_exact * radial) * inverse_norm).astype(jnp.bfloat16)
    return (row_loss, embed_grad, proxy_grad)


def solution(mesh):
    placed = (
        P(("dp", "cls"), None),
        P("cls", None),
        P(("dp", "cls"), None),
        P(("dp", "cls")),
        P(("dp", "cls")),
    )
    dp, groups = mesh.shape["dp"], mesh.shape["cls"]
    if (dp, groups) == (4, 2 * PIECES):
        moves, sizes = Neighbours(2, dp), [4, 4]
    else:
        chunks = max(1, groups // 8)
        moves, sizes = Groups(groups, dp), [8 // chunks] * chunks
    return jax.shard_map(
        functools.partial(per_device, moves, sizes),
        mesh=mesh,
        in_specs=placed,
        out_specs=(P(("dp", "cls")), P(("dp", "cls"), None), P("cls", "dp")),
        check_vma=False,
    )
```

```python
import functools

import jax
import jax.numpy as jnp
import numpy as np
from jax import lax
from jax.experimental import pallas as pl
from jax.experimental.pallas import tpu as pltpu
from jax.sharding import PartitionSpec as P

D = 512
TILE = 128
BR = 128
K = 8
PAIRS_PER_STEP = 4
FIELD = 128
PIECES = 4
VMEM_BYTES = 60 * 1024 * 1024
SPARE_BYTES = 4 * 1024 * 1024

logit_scale = 4.0
epsilon = 1e-06
unused_logit = -1e30

SMEM = pl.BlockSpec(memory_space=pltpu.SMEM)
VMEM = pl.BlockSpec(memory_space=pltpu.VMEM)
ANY = pl.BlockSpec(memory_space=pl.ANY)


def run_copies(jobs, sems, first=0):
    copies = [
        pltpu.make_async_copy(source, target, sems.at[first + index])
        for index, (source, target) in enumerate(jobs)
    ]
    for copy in copies:
        copy.start()
    return copies


def row_places(meta_ref, refs, blocks):
    size = blocks // PIECES
    if len(refs) > 1:
        return [(ref, piece * size) for piece, ref in enumerate(refs)]
    return [
        (refs[0].at[pl.ds(place * size, size)], (meta_ref[2] ^ place) * size)
        for place in range(PIECES)
    ]


def row_jobs(meta_ref, refs, rows_ref):
    return [
        (ref, rows_ref.at[pl.ds(start, ref.shape[0])])
        for ref, start in row_places(meta_ref, refs, rows_ref.shape[0])
    ]


def store_rows(meta_ref, rows_acc, out_ref, grad_refs, sems):
    blocks = out_ref.shape[0]
    out_ref[...] = rows_acc[:blocks].astype(out_ref.dtype)
    return run_copies(
        [
            (out_ref.at[pl.ds(start, ref.shape[0])], ref)
            for ref, start in row_places(meta_ref, grad_refs, blocks)
        ],
        sems,
    )


def aligned(refs, row, turned):
    parts = [ref[row] for ref in refs]
    if not turned:
        return parts
    size = parts[0].shape[0] // PIECES
    return [
        jnp.concatenate(
            [part[(piece ^ away) * size:((piece ^ away) + 1) * size] for piece in range(PIECES)]
        )
        for away, part in enumerate(parts)
    ]


def table_jobs(meta_ref, table_refs, table_ref):
    core = meta_ref[1] % 2
    jobs = [(table_refs[0], table_ref.at[pl.ds(0, table_refs[0].shape[0])])]
    if len(table_refs) > 1:
        half = table_refs[1].shape[0]
        jobs.append((table_refs[1], table_ref.at[pl.ds((2 + core) * half, half)]))
        jobs.append((table_refs[2], table_ref.at[pl.ds((3 - core) * half, half)]))
    return jobs


def transposed_logits(tile, rows):
    return logit_scale * lax.dot_general(
        tile, rows, (((1,), (1,)), ((), ())), preferred_element_type=jnp.float32
    )


def decode(code):
    return code // (2 * FIELD), (code // 2) % FIELD, (code % 2) == 1


def score_kernel(n_rows, n_tables, blocks, tiles, codes_ref, meta_ref, hit_ref, *refs):
    row_refs, refs = refs[:n_rows], refs[n_rows:]
    table_refs, refs = refs[:n_tables], refs[n_tables:]
    stats_ref, rows_ref, table_ref, lse_ref, pos_ref, sems = refs
    row_copies = run_copies(row_jobs(meta_ref, row_refs, rows_ref), sems)
    table_copies = run_copies(table_jobs(meta_ref, table_refs, table_ref), sems, PIECES)
    lse_ref[...] = jnp.full(lse_ref.shape, unused_logit, jnp.float32)
    pos_ref[...] = jnp.zeros(pos_ref.shape, jnp.float32)
    class_at = lax.broadcasted_iota(jnp.int32, (TILE, BR), 0)
    for copy in row_copies:
        copy.wait()

    def normalise(block, carry):
        exact = rows_ref[block].astype(jnp.float32)
        norm = lax.rsqrt(jnp.sum(exact * exact, axis=1, keepdims=True) + epsilon)
        rows_ref[block] = (exact * norm).astype(jnp.bfloat16)
        return carry

    lax.fori_loop(0, blocks, normalise, 0)
    for copy in table_copies:
        copy.wait()

    def step(index, carry):
        held = []
        for lane in range(PAIRS_PER_STEP):
            block, tile, first = decode(codes_ref[index * PAIRS_PER_STEP + lane])
            source = jnp.minimum(block, blocks - 1)
            logits = transposed_logits(
                table_ref[jnp.minimum(tile, tiles - 1)], rows_ref[source]
            )
            peak = jnp.max(logits, axis=0, keepdims=True)
            total = jnp.sum(jnp.exp(logits - peak), axis=0, keepdims=True)
            hit = class_at == hit_ref[pl.ds(source, 1), :]
            positive = jnp.sum(jnp.where(hit, logits, 0.0), axis=0, keepdims=True)
            held.append((block, peak + jnp.log(total), jnp.where(first, positive, 0.0)))
        for block, lse, positive in held:
            before = lse_ref[pl.ds(block, 1), :]
            top = jnp.maximum(before, lse)
            lse_ref[pl.ds(block, 1), :] = top + jnp.log(
                jnp.exp(before - top) + jnp.exp(lse - top)
            )
            pos_ref[pl.ds(block, 1), :] += positive
        return carry

    lax.fori_loop(0, pl.cdiv(meta_ref[0], PAIRS_PER_STEP), step, 0)
    stats_ref[0] = lse_ref[:blocks, :]
    stats_ref[1] = pos_ref[:blocks, :]


def make_totals(stat_refs, turned, total_ref, loss_ref):
    lse = aligned(stat_refs, 0, turned)
    top = functools.reduce(jnp.maximum, lse)
    total = top + jnp.log(sum(jnp.exp(part - top) for part in lse))
    total_ref[...] = total
    loss_ref[...] = total - sum(aligned(stat_refs, 1, turned))


def pair_score(code, blocks, tiles, rows_ref, table_ref, hit_ref, total_ref, class_at):
    block, tile, first = decode(code)
    source = jnp.minimum(block, blocks - 1)
    table_at = jnp.minimum(tile, tiles - 1)
    logits = transposed_logits(table_ref[table_at], rows_ref[source])
    share = jnp.exp(logits - total_ref[pl.ds(source, 1), :])
    wanted = jnp.where(first, hit_ref[pl.ds(source, 1), :], -1)
    hit = (class_at == wanted).astype(jnp.float32)
    return (logit_scale * (share - hit)).astype(jnp.bfloat16)


def row_terms(score, tile):
    return lax.dot_general(
        score, tile, (((0,), (0,)), ((), ())), preferred_element_type=jnp.float32
    )


def grad_kernel(
    n_grads, n_tables, n_stats, turned, blocks, tiles, codes_ref, meta_ref, hit_ref, *refs
):
    stat_refs, refs = refs[:n_stats], refs[n_stats:]
    unit_ref, refs = refs[0], refs[1:]
    table_refs, refs = refs[:n_tables], refs[n_tables:]
    grad_refs, refs = refs[:n_grads], refs[n_grads:]
    scores_ref, loss_ref, rows_ref, table_ref, total_ref, rows_acc, out_ref, sems = refs
    copies = run_copies(
        [(unit_ref, rows_ref)] + table_jobs(meta_ref, table_refs, table_ref), sems, PIECES
    )
    rows_acc[...] = jnp.zeros(rows_acc.shape, jnp.float32)
    make_totals(stat_refs, turned, total_ref, loss_ref)
    class_at = lax.broadcasted_iota(jnp.int32, (TILE, BR), 0)
    for copy in copies:
        copy.wait()

    def step(index, carry):
        held = []
        for lane in range(PAIRS_PER_STEP):
            pair = index * PAIRS_PER_STEP + lane
            score = pair_score(
                codes_ref[pair], blocks, tiles, rows_ref, table_ref, hit_ref, total_ref, class_at
            )
            scores_ref[pair] = score
            held.append(score)
        for lane, score in enumerate(held):
            block, tile, _ = decode(codes_ref[index * PAIRS_PER_STEP + lane])
            rows_acc[block] += row_terms(score, table_ref[jnp.minimum(tile, tiles - 1)])
        return carry

    lax.fori_loop(0, pl.cdiv(meta_ref[0], PAIRS_PER_STEP), step, 0)
    for copy in store_rows(meta_ref, rows_acc, out_ref, grad_refs, sems):
        copy.wait()


def last_kernel(sizes, n_grads, n_tables, n_stats, turned, n_shares, tiles, *refs):
    chunks, blocks = len(sizes), sizes[-1]
    codes_refs, refs = refs[:chunks], refs[chunks:]
    meta_refs, refs = refs[:chunks], refs[chunks:]
    hit_ref, refs = refs[0], refs[1:]
    stat_refs, refs = refs[:n_stats], refs[n_stats:]
    scores_refs, refs = refs[:chunks - 1], refs[chunks - 1:]
    unit_refs, refs = refs[:chunks], refs[chunks:]
    table_refs, refs = refs[:n_tables], refs[n_tables:]
    grad_refs, refs = refs[:n_grads], refs[n_grads:]
    share_refs, refs = refs[:n_shares], refs[n_shares:]
    loss_ref, refs = refs[0], refs[1:]
    rows_ref, early_ref, held_ref, table_ref, total_ref, rows_acc, out_ref, *refs = refs
    tiles_acc, sems, early_sems, row_sems = refs
    codes_ref, meta_ref = codes_refs[-1], meta_refs[-1]
    copies = run_copies(
        [(unit_refs[-1], rows_ref)] + table_jobs(meta_ref, table_refs, table_ref), sems
    )


    def fetch(chunk):
        early = early_ref.at[pl.ds(0, sizes[chunk])]
        return run_copies(
            [(unit_refs[chunk], early), (scores_refs[chunk], held_ref)], early_sems
        )

    early = fetch(0) if chunks > 1 else []
    rows_acc[...] = jnp.zeros(rows_acc.shape, jnp.float32)
    tiles_acc[...] = jnp.zeros(tiles_acc.shape, jnp.float32)
    make_totals(stat_refs, turned, total_ref, loss_ref)
    class_at = lax.broadcasted_iota(jnp.int32, (TILE, BR), 0)
    for copy in copies:
        copy.wait()

    def step(index, carry):
        held = [
            pair_score(
                codes_ref[index * PAIRS_PER_STEP + lane], blocks, tiles, rows_ref, table_ref,
                hit_ref, total_ref, class_at,
            )
            for lane in range(PAIRS_PER_STEP)
        ]
        for lane, score in enumerate(held):
            block, tile, _ = decode(codes_ref[index * PAIRS_PER_STEP + lane])
            rows_acc[block] += row_terms(score, table_ref[jnp.minimum(tile, tiles - 1)])
            tiles_acc[tile] += jnp.dot(
                score, rows_ref[jnp.minimum(block, blocks - 1)],
                preferred_element_type=jnp.float32,
            )
        return carry

    lax.fori_loop(0, pl.cdiv(meta_ref[0], PAIRS_PER_STEP), step, 0)
    stored = store_rows(meta_ref, rows_acc, out_ref, grad_refs, row_sems)
    for chunk in range(chunks - 1):
        for copy in early if chunk == 0 else fetch(chunk):
            copy.wait()

        def early_step(index, carry, chunk=chunk):
            for lane in range(PAIRS_PER_STEP):
                pair = index * PAIRS_PER_STEP + lane
                block, tile, _ = decode(codes_refs[chunk][pair])
                tiles_acc[tile] += jnp.dot(
                    held_ref[pair],
                    early_ref[jnp.minimum(block, sizes[chunk] - 1)],
                    preferred_element_type=jnp.float32,
                )
            return carry

        lax.fori_loop(0, pl.cdiv(meta_refs[chunk][0], PAIRS_PER_STEP), early_step, 0)
    if n_shares == 1:
        share_refs[0][...] = tiles_acc[:tiles].astype(jnp.bfloat16)
    else:
        part = meta_ref[1]
        shard, width = share_refs[0].shape[2], share_refs[0].shape[-1]
        for core, ref in enumerate(share_refs):
            for y in range(ref.shape[1]):
                start = pl.multiple_of(((2 * y + core) ^ part) * width, width)
                for x in range(ref.shape[0]):
                    ref[x, y] = tiles_acc[
                        pl.ds(x * shard, shard), :, pl.ds(start, width)
                    ].astype(jnp.bfloat16)
    for copy in stored:
        copy.wait()


def kernel_cost(blocks):
    return pl.CostEstimate(flops=blocks * BR * D, bytes_accessed=blocks * BR * D, transcendentals=0)


def limit(*scratch):
    total = 0
    for shape, dtype in scratch:
        total += int(np.prod(shape)) * jnp.dtype(dtype).itemsize
    return pltpu.CompilerParams(vmem_limit_bytes=min(VMEM_BYTES, total + SPARE_BYTES))


def rows_of(blocks):
    return (blocks, BR, D), jnp.bfloat16


def score(blocks, codes, meta, hit, rows, tables):
    tiles = sum(table.shape[0] for table in tables)
    table_room = ((tiles, TILE, D), jnp.bfloat16)
    return pl.pallas_call(
        functools.partial(score_kernel, len(rows), len(tables), blocks, tiles),
        out_shape=(
            jax.ShapeDtypeStruct((2, blocks, BR), jnp.float32),
            jax.ShapeDtypeStruct(*rows_of(blocks)),
        ),
        in_specs=[SMEM, SMEM, VMEM] + [ANY] * (len(rows) + len(tables)),
        out_specs=(VMEM, VMEM),
        scratch_shapes=[
            pltpu.VMEM(*table_room),
            pltpu.VMEM((blocks + 8, BR), jnp.float32),
            pltpu.VMEM((blocks + 8, BR), jnp.float32),
            pltpu.SemaphoreType.DMA((PIECES + len(tables),)),
        ],
        cost_estimate=kernel_cost(blocks),
        compiler_params=limit(rows_of(blocks), table_room),
    )(codes, meta, hit, *rows, *tables)


def grads(blocks, codes, meta, hit, stats, turned, unit, tables, shapes):
    tiles = sum(table.shape[0] for table in tables)
    table_room = ((tiles, TILE, D), jnp.bfloat16)
    acc_room = ((blocks + 1, BR, D), jnp.float32)
    scores = ((codes.shape[0], TILE, BR), jnp.bfloat16)
    outs = pl.pallas_call(
        functools.partial(
            grad_kernel, len(shapes), len(tables), len(stats), turned, blocks, tiles
        ),
        out_shape=(
            *(jax.ShapeDtypeStruct(shape, jnp.bfloat16) for shape in shapes),
            jax.ShapeDtypeStruct(*scores),
            jax.ShapeDtypeStruct((blocks, BR), jnp.float32),
        ),
        in_specs=[SMEM, SMEM] + [VMEM] * (1 + len(stats)) + [ANY] * (1 + len(tables)),
        out_specs=(*[ANY] * len(shapes), VMEM, VMEM),
        scratch_shapes=[
            pltpu.VMEM(*rows_of(blocks)),
            pltpu.VMEM(*table_room),
            pltpu.VMEM((blocks, BR), jnp.float32),
            pltpu.VMEM(*acc_room),
            pltpu.VMEM(*rows_of(blocks)),
            pltpu.SemaphoreType.DMA((PIECES + 1 + len(tables),)),
        ],
        cost_estimate=kernel_cost(blocks),
        compiler_params=limit(rows_of(2 * blocks), table_room, acc_room, scores),
    )(codes, meta, hit, *stats, unit, *tables)
    return list(outs[:len(shapes)]), outs[len(shapes)], outs[-1]


def last_grads(codes, metas, hit, stats, turned, scores, units, tables, shapes, share_shapes):
    sizes = [unit.shape[0] for unit in units]
    tiles = sum(table.shape[0] for table in tables)
    chunks, blocks = len(sizes), sizes[-1]
    n_inputs = 2 * chunks - 1 + len(tables)
    table_room = ((tiles, TILE, D), jnp.bfloat16)
    acc_room = ((blocks + 1, BR, D), jnp.float32)
    tiles_room = ((tiles + 1, TILE, D), jnp.float32)
    early_room = rows_of(max(sizes[:-1], default=PIECES))
    kept = ((scores or codes)[0].shape[0], TILE, BR), jnp.bfloat16
    outs = pl.pallas_call(
        functools.partial(
            last_kernel, sizes, len(shapes), len(tables), len(stats), turned,
            len(share_shapes), tiles,
        ),
        out_shape=(
            *(jax.ShapeDtypeStruct(shape, jnp.bfloat16) for shape in shapes),
            *(jax.ShapeDtypeStruct(shape, jnp.bfloat16) for shape in share_shapes),
            jax.ShapeDtypeStruct((blocks, BR), jnp.float32),
        ),
        in_specs=[SMEM] * (2 * chunks) + [VMEM] * (1 + len(stats)) + [ANY] * n_inputs,
        out_specs=(*[ANY] * len(shapes), *[VMEM] * len(share_shapes), VMEM),
        scratch_shapes=[
            pltpu.VMEM(*rows_of(blocks)),
            pltpu.VMEM(*early_room),
            pltpu.VMEM(*kept),
            pltpu.VMEM(*table_room),
            pltpu.VMEM((blocks, BR), jnp.float32),
            pltpu.VMEM(*acc_room),
            pltpu.VMEM(*rows_of(blocks)),
            pltpu.VMEM(*tiles_room),
            pltpu.SemaphoreType.DMA((1 + len(tables),)),
            pltpu.SemaphoreType.DMA((2,)),
            pltpu.SemaphoreType.DMA((PIECES,)),
        ],
        cost_estimate=kernel_cost(sum(sizes)),
        compiler_params=limit(
            rows_of(2 * blocks), early_room, kept, table_room, table_room, acc_room, tiles_room
        ),
    )(*codes, *metas, hit, *stats, *scores, *units, *tables)
    cut = len(shapes)
    return list(outs[:cut]), list(outs[cut:-1]), outs[-1]


def add(first, second):
    return (first.astype(jnp.float32) + second.astype(jnp.float32)).astype(jnp.bfloat16)


class Neighbours:
    def __init__(self, nx, dp):
        self.nx, self.nz, self.dp, self.turned = nx, PIECES, dp, True

    def over_z(self, value, away):
        pairs = [
            (z * self.nx + x, (z ^ away) * self.nx + x)
            for z in range(self.nz) for x in range(self.nx)
        ]
        return lax.ppermute(value, "cls", pairs)

    def over_x(self, value):
        return lax.ppermute(value, "cls", [(c, c ^ 1) for c in range(self.nx * self.nz)])

    def over_y(self, value):
        return lax.ppermute(value, "dp", [(d, d ^ 2) for d in range(self.dp)])

    def over_core(self, value):
        return lax.ppermute(value, "dp", [(d, d ^ 1) for d in range(self.dp)])

    def all_over_z(self, value):
        return [value] + [self.over_z(value, away) for away in range(1, self.nz)]

    def gather(self, needed, chunks, lists, table, core, prepare):
        def moves(first, lists, table, core):
            half = table.shape[0] // 2
            sent = lax.dynamic_slice_in_dim(table, core * half, half, axis=0)
            from_x = self.over_x(sent)
            far, near = lax.optimization_barrier((self.over_z(first, 2), self.over_z(first, 1)))
            return (near, far, self.over_z(far, 1)), from_x, prepare(
                jnp.stack(self.all_over_z(lists))
            )

        first, second = chunks
        pieces, from_x, prepared = self.together(needed, moves, first, lists, table, core)
        return [[first, *pieces], [second]], [table, from_x], prepared

    def all_tables(self, tables):
        return [*tables, self.over_core(tables[-1])]

    def rest_of_rows(self, pieces, others):
        second, = pieces
        far, near, others = lax.optimization_barrier(
            (self.over_z(second, 2), self.over_z(second, 1), others)
        )
        return (near, far, self.over_z(far, 1)), others

    def whole_rows(self, pieces, rest):
        return [*pieces, *rest]

    def grad_shapes(self, size):
        return [(size, BR, D)] * PIECES

    def gather_stats(self, stats):
        return self.all_over_z(stats)

    def order(self, place):
        return place

    def own(self, loss, place, size):
        return loss[:size]

    def early_return(self, early, others):
        parts, = early
        near, passed = self.over_z(parts[1], 1), self.over_z(parts[3], 1)
        passed, others = lax.optimization_barrier((passed, others))
        return (near, self.over_z(add(passed, parts[2]), 2)), others

    def early_sums(self, early, returned):
        return [sum(part.astype(jnp.float32) for part in (early[0][0], *returned))]

    def together(self, needed, work, *operands):
        def no_work(*operands):
            return jax.tree.map(
                lambda out: jnp.zeros(out.shape, out.dtype), jax.eval_shape(work, *operands)
            )

        return lax.cond(needed, work, no_work, *operands)

    def sum_last(self, parts, shares):
        kept, sent = shares
        passed, got = self.over_z(parts[3], 1), self.over_core(sent)
        near = self.over_z(parts[1], 1)
        half = kept.shape[2] // 2
        x_sent = add(kept[1, :, :half], got[1, :, :half])
        y_sent = add(kept[:, 1, half:], got[:, 1, half:])
        passed, _, _ = lax.optimization_barrier((passed, x_sent, y_sent))
        far = self.over_z(add(passed, parts[2]), 2)
        near, far, shares = self.sum_shares(near, far, kept, got, x_sent, y_sent)
        return sum(part.astype(jnp.float32) for part in (parts[0], near, far)), shares

    def share_shapes(self, shard_tiles):
        return [(self.nx, self.dp // 2, shard_tiles, TILE, D // self.dp)] * 2

    def sum_shares(self, near, far, kept, got, x_sent, y_sent):
        half = kept.shape[2] // 2
        x_got, y_got = lax.optimization_barrier((self.over_x(x_sent), self.over_y(y_sent)))
        x_kept = [add(add(kept[0, y, :half], got[0, y, :half]), x_got[y]) for y in range(2)]
        y_kept = [add(add(kept[x, 0, half:], got[x, 0, half:]), y_got[x]) for x in range(2)]
        near, far, low, high = lax.optimization_barrier(
            (near, far, self.over_y(x_kept[1]), self.over_x(y_kept[1]))
        )
        low = x_kept[0].astype(jnp.float32) + low.astype(jnp.float32)
        high = y_kept[0].astype(jnp.float32) + high.astype(jnp.float32)
        return near, far, jnp.concatenate([low, high], axis=0)


class Groups:
    def __init__(self, nz, dp):
        self.nx, self.nz, self.dp, self.turned = 1, nz, dp, False

    def gather(self, needed, chunks, lists, table, core, prepare):
        gathered = [[lax.all_gather(rows, "cls", tiled=True)] for rows in chunks]
        return gathered, [table], prepare(lax.all_gather(lists, "cls"))

    def all_tables(self, tables):
        return tables

    def rest_of_rows(self, pieces, others):
        return (), others

    def whole_rows(self, pieces, rest):
        return pieces

    def grad_shapes(self, size):
        return [(self.nz * size, BR, D)]

    def gather_stats(self, stats):
        return list(lax.all_gather(stats, "cls"))

    def order(self, place):
        return jnp.zeros_like(place)

    def own(self, loss, place, size):
        return lax.dynamic_slice_in_dim(loss, place * size, size, axis=0)

    def total(self, part):
        return lax.psum_scatter(
            part, "cls", scatter_dimension=0, tiled=True
        ).astype(jnp.float32)

    def early_return(self, early, others):
        return [self.total(part) for part, in early], others

    def early_sums(self, early, returned):
        return returned

    def together(self, needed, work, *operands):
        return work(*operands)

    def sum_last(self, parts, shares):
        return self.total(parts[0]), self.sum_shares(shares)

    def share_shapes(self, shard_tiles):
        return [(shard_tiles, TILE, D)]

    def sum_shares(self, shares):
        return lax.psum_scatter(
            shares[0], "dp", scatter_dimension=2, tiled=True
        ).astype(jnp.float32)


def pair_codes(lists, shard_tiles, nx, place, column, room):
    entry = lists[:, :K].reshape(-1)
    owner = entry // shard_tiles
    mine = (entry >= 0) & (owner // nx == place)
    local = jnp.where(owner % nx == column, 0, shard_tiles) + entry % shard_tiles
    counter = jnp.arange(entry.shape[0], dtype=jnp.int32)
    code = ((counter // K) * FIELD + local) * 2 + (counter % K == 0)
    rank = jnp.sum(
        jnp.where(mine[None, :] & (counter[None, :] < counter[:, None]), 1, 0), axis=1
    ).astype(jnp.int32)
    slots = jnp.arange(room, dtype=jnp.int32)
    chosen = mine[None, :] & (rank[None, :] == slots[:, None])
    padding = (lists.shape[0] * FIELD + nx * shard_tiles) * 2
    codes = padding + jnp.sum(jnp.where(chosen, code[None, :] - padding, 0), axis=1)
    return codes.astype(jnp.int32), jnp.sum(mine.astype(jnp.int32))


def per_device(moves, sizes, embeddings, proxies, hard_tiles, tile_count, labels):
    nx, nz, dp = moves.nx, moves.nz, moves.dp
    blocks = hard_tiles.shape[0]
    shard_tiles = proxies.shape[0] // TILE
    me, part = lax.axis_index("cls"), lax.axis_index("dp")
    place, column = me // nx, me % nx

    row_blocks = embeddings.reshape(blocks, BR, D)

    position = labels.reshape(blocks, BR) - hard_tiles[:, 0:1] * TILE
    entries = jnp.arange(K, dtype=jnp.int32)
    used = jnp.where(entries[None, :] < tile_count[:, None], hard_tiles, -1)
    starts = [sum(sizes[:chunk]) for chunk in range(len(sizes))]
    spots = [slice(start, start + size) for start, size in zip(starts, sizes)]
    held = [nz * size for size in sizes]
    last = len(sizes) - 1
    needed = tile_count[0] > 0

    def prepare(lists):
        prepared = []
        for spot, blocks_held in zip(spots, held):
            room = min(blocks_held * K, nz * (blocks * K // (nx * nz)) * nx)
            room = -(-room // PAIRS_PER_STEP) * PAIRS_PER_STEP
            chunk_lists = lists[:, spot].reshape(blocks_held, K + BR)
            code, count = pair_codes(chunk_lists, shard_tiles, nx, place, column, room)
            meta = jnp.stack([count, part, moves.order(place)]).astype(jnp.int32)
            prepared.append((code, meta, chunk_lists[:, K:]))
        return prepared

    gathered, tables, prepared = moves.gather(
        needed,
        [row_blocks[spot] for spot in spots],
        jnp.concatenate([used, position], axis=1),
        proxies.reshape(shard_tiles, TILE, D),
        part % 2,
        prepare,
    )

    def scored(chunk, rows, tables, prepared):
        parts, unit = score(held[chunk], *prepared[chunk], rows, tables)
        return moves.gather_stats(parts), unit

    def early_work(gathered, own_tables, prepared):
        units, made, rest = [], [], ()
        tables = moves.all_tables(own_tables)
        for chunk in range(last):
            stats, unit = scored(chunk, gathered[chunk], tables, prepared)
            if chunk == 0:
                rest, stats = moves.rest_of_rows(gathered[-1], stats)
            units.append(unit)
            made.append(grads(
                held[chunk], *prepared[chunk], stats, moves.turned, unit, tables,
                moves.grad_shapes(sizes[chunk]),
            ))
        return rest, tables[len(own_tables):], units, made

    def last_work(rows, tables, prepared, units, scores, early):
        codes, metas, hits = zip(*prepared)
        stats, unit = scored(last, rows, tables, prepared)
        returned, stats = moves.early_return(early, stats)
        return returned, last_grads(
            codes, metas, hits[-1], stats, moves.turned, scores, units + [unit], tables,
            moves.grad_shapes(sizes[-1]), moves.share_shapes(shard_tiles),
        )

    rest, more, units, made = moves.together(needed, early_work, gathered, tables, prepared)
    tables = [*tables, *more]
    rows = moves.whole_rows(gathered[-1], rest)
    early, scores, losses = zip(*made)
    returned, (parts, shares, loss) = moves.together(
        needed, last_work, rows, tables, prepared, units, list(scores), early
    )
    total, shares = moves.sum_last(parts, shares)
    row_grads = moves.early_sums(early, returned) + [total]
    losses = [
        moves.own(part, place, size) for part, size in zip((*losses, loss), sizes)
    ]

    embeddings, units = lax.optimization_barrier((embeddings, units))
    emb_exact = embeddings.astype(jnp.float32)
    inverse_norm = lax.rsqrt(jnp.sum(emb_exact * emb_exact, axis=1, keepdims=True) + epsilon)
    unit_exact = emb_exact * inverse_norm
    proxy_grad = shares.reshape(shard_tiles * TILE, D // dp)
    row_loss = jnp.concatenate(losses, axis=0).reshape(-1)
    embed_grad = []
    for spot, grad_rows in zip(spots, row_grads):
        span = slice(spot.start * BR, spot.stop * BR)
        exact, norm = unit_exact[span], inverse_norm[span]
        grad_rows = grad_rows.reshape(-1, D)
        radial = jnp.sum(exact * grad_rows, axis=1, keepdims=True)
        embed_grad.append(((grad_rows - exact * radial) * norm).astype(jnp.bfloat16))
    embed_grad = jnp.concatenate(embed_grad, axis=0)
    return (row_loss, embed_grad, proxy_grad)


def solution(mesh):
    placed = (
        P(("dp", "cls"), None),
        P("cls", None),
        P(("dp", "cls"), None),
        P(("dp", "cls")),
        P(("dp", "cls")),
    )
    dp, groups = mesh.shape["dp"], mesh.shape["cls"]
    if (dp, groups) == (4, 2 * PIECES):
        moves, sizes = Neighbours(2, dp), [4, 4]
    else:
        chunks = max(1, groups // 8)
        moves, sizes = Groups(groups, dp), [8 // chunks] * chunks
    return jax.shard_map(
        functools.partial(per_device, moves, sizes),
        mesh=mesh,
        in_specs=placed,
        out_specs=(P(("dp", "cls")), P(("dp", "cls"), None), P("cls", "dp")),
        check_vma=False,
    )
```

```python
import functools

import jax
import jax.numpy as jnp
import numpy as np
from jax import lax
from jax.experimental import pallas as pl
from jax.experimental.pallas import tpu as pltpu
from jax.sharding import PartitionSpec as P

D = 512
TILE = 128
BR = 128
K = 8
PAIRS_PER_STEP = 4
FIELD = 128
PIECES = 4
VMEM_BYTES = 60 * 1024 * 1024
SPARE_BYTES = 4 * 1024 * 1024

logit_scale = 4.0
epsilon = 1e-06
unused_logit = -1e30

SMEM = pl.BlockSpec(memory_space=pltpu.SMEM)
VMEM = pl.BlockSpec(memory_space=pltpu.VMEM)
ANY = pl.BlockSpec(memory_space=pl.ANY)


def run_copies(jobs, sems, first=0):
    copies = [
        pltpu.make_async_copy(source, target, sems.at[first + index])
        for index, (source, target) in enumerate(jobs)
    ]
    for copy in copies:
        copy.start()
    return copies


def row_places(meta_ref, refs, blocks):
    size = blocks // PIECES
    if len(refs) > 1:
        return [(ref, piece * size) for piece, ref in enumerate(refs)]
    return [
        (refs[0].at[pl.ds(place * size, size)], (meta_ref[2] ^ place) * size)
        for place in range(PIECES)
    ]


def row_jobs(meta_ref, refs, rows_ref):
    return [
        (ref, rows_ref.at[pl.ds(start, ref.shape[0])])
        for ref, start in row_places(meta_ref, refs, rows_ref.shape[0])
    ]


def store_rows(meta_ref, rows_acc, out_ref, grad_refs, sems):
    blocks = out_ref.shape[0]
    out_ref[...] = rows_acc[:blocks].astype(out_ref.dtype)
    return run_copies(
        [
            (out_ref.at[pl.ds(start, ref.shape[0])], ref)
            for ref, start in row_places(meta_ref, grad_refs, blocks)
        ],
        sems,
    )


def aligned(refs, row, turned):
    parts = [ref[row] for ref in refs]
    if not turned:
        return parts
    size = parts[0].shape[0] // PIECES
    return [
        jnp.concatenate(
            [part[(piece ^ away) * size:((piece ^ away) + 1) * size] for piece in range(PIECES)]
        )
        for away, part in enumerate(parts)
    ]


def table_jobs(meta_ref, table_refs, table_ref):
    core = meta_ref[1] % 2
    jobs = [(table_refs[0], table_ref.at[pl.ds(0, table_refs[0].shape[0])])]
    if len(table_refs) > 1:
        half = table_refs[1].shape[0]
        jobs.append((table_refs[1], table_ref.at[pl.ds((2 + core) * half, half)]))
        jobs.append((table_refs[2], table_ref.at[pl.ds((3 - core) * half, half)]))
    return jobs


def transposed_logits(tile, rows):
    return logit_scale * lax.dot_general(
        tile, rows, (((1,), (1,)), ((), ())), preferred_element_type=jnp.float32
    )


def decode(code):
    return code // (2 * FIELD), (code // 2) % FIELD, (code % 2) == 1


def score_kernel(n_rows, n_tables, blocks, tiles, codes_ref, meta_ref, hit_ref, *refs):
    row_refs, refs = refs[:n_rows], refs[n_rows:]
    table_refs, refs = refs[:n_tables], refs[n_tables:]
    stats_ref, rows_ref, table_ref, lse_ref, pos_ref, sems = refs
    row_copies = run_copies(row_jobs(meta_ref, row_refs, rows_ref), sems)
    table_copies = run_copies(table_jobs(meta_ref, table_refs, table_ref), sems, PIECES)
    lse_ref[...] = jnp.full(lse_ref.shape, unused_logit, jnp.float32)
    pos_ref[...] = jnp.zeros(pos_ref.shape, jnp.float32)
    class_at = lax.broadcasted_iota(jnp.int32, (TILE, BR), 0)
    for copy in row_copies:
        copy.wait()

    def normalise(block, carry):
        exact = rows_ref[block].astype(jnp.float32)
        norm = lax.rsqrt(jnp.sum(exact * exact, axis=1, keepdims=True) + epsilon)
        rows_ref[block] = (exact * norm).astype(jnp.bfloat16)
        return carry

    lax.fori_loop(0, blocks, normalise, 0)
    for copy in table_copies:
        copy.wait()

    def step(index, carry):
        held = []
        for lane in range(PAIRS_PER_STEP):
            block, tile, first = decode(codes_ref[index * PAIRS_PER_STEP + lane])
            source = jnp.minimum(block, blocks - 1)
            logits = transposed_logits(
                table_ref[jnp.minimum(tile, tiles - 1)], rows_ref[source]
            )
            peak = jnp.max(logits, axis=0, keepdims=True)
            total = jnp.sum(jnp.exp(logits - peak), axis=0, keepdims=True)
            hit = class_at == hit_ref[pl.ds(source, 1), :]
            positive = jnp.sum(jnp.where(hit, logits, 0.0), axis=0, keepdims=True)
            held.append((block, peak + jnp.log(total), jnp.where(first, positive, 0.0)))
        for block, lse, positive in held:
            before = lse_ref[pl.ds(block, 1), :]
            top = jnp.maximum(before, lse)
            lse_ref[pl.ds(block, 1), :] = top + jnp.log(
                jnp.exp(before - top) + jnp.exp(lse - top)
            )
            pos_ref[pl.ds(block, 1), :] += positive
        return carry

    lax.fori_loop(0, pl.cdiv(meta_ref[0], PAIRS_PER_STEP), step, 0)
    stats_ref[0] = lse_ref[:blocks, :]
    stats_ref[1] = pos_ref[:blocks, :]


def make_totals(stat_refs, turned, total_ref, loss_ref):
    lse = aligned(stat_refs, 0, turned)
    top = functools.reduce(jnp.maximum, lse)
    total = top + jnp.log(sum(jnp.exp(part - top) for part in lse))
    total_ref[...] = total
    loss_ref[...] = total - sum(aligned(stat_refs, 1, turned))


def pair_score(code, blocks, tiles, rows_ref, table_ref, hit_ref, total_ref, class_at):
    block, tile, first = decode(code)
    source = jnp.minimum(block, blocks - 1)
    table_at = jnp.minimum(tile, tiles - 1)
    logits = transposed_logits(table_ref[table_at], rows_ref[source])
    share = jnp.exp(logits - total_ref[pl.ds(source, 1), :])
    wanted = jnp.where(first, hit_ref[pl.ds(source, 1), :], -1)
    hit = (class_at == wanted).astype(jnp.float32)
    return (logit_scale * (share - hit)).astype(jnp.bfloat16)


def row_terms(score, tile):
    return lax.dot_general(
        score, tile, (((0,), (0,)), ((), ())), preferred_element_type=jnp.float32
    )


def grad_kernel(
    n_grads, n_tables, n_stats, turned, blocks, tiles, codes_ref, meta_ref, hit_ref, *refs
):
    stat_refs, refs = refs[:n_stats], refs[n_stats:]
    unit_ref, refs = refs[0], refs[1:]
    table_refs, refs = refs[:n_tables], refs[n_tables:]
    grad_refs, refs = refs[:n_grads], refs[n_grads:]
    scores_ref, loss_ref, rows_ref, table_ref, total_ref, rows_acc, out_ref, sems = refs
    copies = run_copies(
        [(unit_ref, rows_ref)] + table_jobs(meta_ref, table_refs, table_ref), sems, PIECES
    )
    rows_acc[...] = jnp.zeros(rows_acc.shape, jnp.float32)
    make_totals(stat_refs, turned, total_ref, loss_ref)
    class_at = lax.broadcasted_iota(jnp.int32, (TILE, BR), 0)
    for copy in copies:
        copy.wait()

    def step(index, carry):
        held = []
        for lane in range(PAIRS_PER_STEP):
            pair = index * PAIRS_PER_STEP + lane
            score = pair_score(
                codes_ref[pair], blocks, tiles, rows_ref, table_ref, hit_ref, total_ref, class_at
            )
            scores_ref[pair] = score
            held.append(score)
        for lane, score in enumerate(held):
            block, tile, _ = decode(codes_ref[index * PAIRS_PER_STEP + lane])
            rows_acc[block] += row_terms(score, table_ref[jnp.minimum(tile, tiles - 1)])
        return carry

    lax.fori_loop(0, pl.cdiv(meta_ref[0], PAIRS_PER_STEP), step, 0)
    for copy in store_rows(meta_ref, rows_acc, out_ref, grad_refs, sems):
        copy.wait()


def last_kernel(sizes, n_grads, n_tables, n_stats, turned, n_shares, tiles, *refs):
    chunks, blocks = len(sizes), sizes[-1]
    codes_refs, refs = refs[:chunks], refs[chunks:]
    meta_refs, refs = refs[:chunks], refs[chunks:]
    hit_ref, refs = refs[0], refs[1:]
    stat_refs, refs = refs[:n_stats], refs[n_stats:]
    scores_refs, refs = refs[:chunks - 1], refs[chunks - 1:]
    unit_refs, refs = refs[:chunks], refs[chunks:]
    table_refs, refs = refs[:n_tables], refs[n_tables:]
    grad_refs, refs = refs[:n_grads], refs[n_grads:]
    share_refs, refs = refs[:n_shares], refs[n_shares:]
    loss_ref, refs = refs[0], refs[1:]
    rows_ref, early_ref, held_ref, table_ref, total_ref, rows_acc, out_ref, *refs = refs
    tiles_acc, sems, early_sems, row_sems = refs
    codes_ref, meta_ref = codes_refs[-1], meta_refs[-1]
    copies = run_copies(
        [(unit_refs[-1], rows_ref)] + table_jobs(meta_ref, table_refs, table_ref), sems
    )


    def fetch(chunk):
        early = early_ref.at[pl.ds(0, sizes[chunk])]
        return run_copies(
            [(unit_refs[chunk], early), (scores_refs[chunk], held_ref)], early_sems
        )

    early = fetch(0) if chunks > 1 else []
    rows_acc[...] = jnp.zeros(rows_acc.shape, jnp.float32)
    tiles_acc[...] = jnp.zeros(tiles_acc.shape, jnp.float32)
    make_totals(stat_refs, turned, total_ref, loss_ref)
    class_at = lax.broadcasted_iota(jnp.int32, (TILE, BR), 0)
    for copy in copies:
        copy.wait()

    def step(index, carry):
        held = [
            pair_score(
                codes_ref[index * PAIRS_PER_STEP + lane], blocks, tiles, rows_ref, table_ref,
                hit_ref, total_ref, class_at,
            )
            for lane in range(PAIRS_PER_STEP)
        ]
        for lane, score in enumerate(held):
            block, tile, _ = decode(codes_ref[index * PAIRS_PER_STEP + lane])
            rows_acc[block] += row_terms(score, table_ref[jnp.minimum(tile, tiles - 1)])
            tiles_acc[tile] += jnp.dot(
                score, rows_ref[jnp.minimum(block, blocks - 1)],
                preferred_element_type=jnp.float32,
            )
        return carry

    lax.fori_loop(0, pl.cdiv(meta_ref[0], PAIRS_PER_STEP), step, 0)
    stored = store_rows(meta_ref, rows_acc, out_ref, grad_refs, row_sems)
    for chunk in range(chunks - 1):
        for copy in early if chunk == 0 else fetch(chunk):
            copy.wait()

        def early_step(index, carry, chunk=chunk):
            for lane in range(PAIRS_PER_STEP):
                pair = index * PAIRS_PER_STEP + lane
                block, tile, _ = decode(codes_refs[chunk][pair])
                tiles_acc[tile] += jnp.dot(
                    held_ref[pair],
                    early_ref[jnp.minimum(block, sizes[chunk] - 1)],
                    preferred_element_type=jnp.float32,
                )
            return carry

        lax.fori_loop(0, pl.cdiv(meta_refs[chunk][0], PAIRS_PER_STEP), early_step, 0)
    if n_shares == 1:
        share_refs[0][...] = tiles_acc[:tiles].astype(jnp.bfloat16)
    else:
        part = meta_ref[1]
        shard, width = share_refs[0].shape[2], share_refs[0].shape[-1]
        for core, ref in enumerate(share_refs):
            for y in range(ref.shape[1]):
                start = pl.multiple_of(((2 * y + core) ^ part) * width, width)
                for x in range(ref.shape[0]):
                    ref[x, y] = tiles_acc[
                        pl.ds(x * shard, shard), :, pl.ds(start, width)
                    ].astype(jnp.bfloat16)
    for copy in stored:
        copy.wait()


def kernel_cost(blocks):
    return pl.CostEstimate(flops=blocks * BR * D, bytes_accessed=blocks * BR * D, transcendentals=0)


def limit(*scratch):
    total = 0
    for shape, dtype in scratch:
        total += int(np.prod(shape)) * jnp.dtype(dtype).itemsize
    return pltpu.CompilerParams(vmem_limit_bytes=min(VMEM_BYTES, total + SPARE_BYTES))


def rows_of(blocks):
    return (blocks, BR, D), jnp.bfloat16


def score(blocks, codes, meta, hit, rows, tables):
    tiles = sum(table.shape[0] for table in tables)
    table_room = ((tiles, TILE, D), jnp.bfloat16)
    return pl.pallas_call(
        functools.partial(score_kernel, len(rows), len(tables), blocks, tiles),
        out_shape=(
            jax.ShapeDtypeStruct((2, blocks, BR), jnp.float32),
            jax.ShapeDtypeStruct(*rows_of(blocks)),
        ),
        in_specs=[SMEM, SMEM, VMEM] + [ANY] * (len(rows) + len(tables)),
        out_specs=(VMEM, VMEM),
        scratch_shapes=[
            pltpu.VMEM(*table_room),
            pltpu.VMEM((blocks + 8, BR), jnp.float32),
            pltpu.VMEM((blocks + 8, BR), jnp.float32),
            pltpu.SemaphoreType.DMA((PIECES + len(tables),)),
        ],
        cost_estimate=kernel_cost(blocks),
        compiler_params=limit(rows_of(blocks), table_room),
    )(codes, meta, hit, *rows, *tables)


def grads(blocks, codes, meta, hit, stats, turned, unit, tables, shapes):
    tiles = sum(table.shape[0] for table in tables)
    table_room = ((tiles, TILE, D), jnp.bfloat16)
    acc_room = ((blocks + 1, BR, D), jnp.float32)
    scores = ((codes.shape[0], TILE, BR), jnp.bfloat16)
    outs = pl.pallas_call(
        functools.partial(
            grad_kernel, len(shapes), len(tables), len(stats), turned, blocks, tiles
        ),
        out_shape=(
            *(jax.ShapeDtypeStruct(shape, jnp.bfloat16) for shape in shapes),
            jax.ShapeDtypeStruct(*scores),
            jax.ShapeDtypeStruct((blocks, BR), jnp.float32),
        ),
        in_specs=[SMEM, SMEM] + [VMEM] * (1 + len(stats)) + [ANY] * (1 + len(tables)),
        out_specs=(*[ANY] * len(shapes), VMEM, VMEM),
        scratch_shapes=[
            pltpu.VMEM(*rows_of(blocks)),
            pltpu.VMEM(*table_room),
            pltpu.VMEM((blocks, BR), jnp.float32),
            pltpu.VMEM(*acc_room),
            pltpu.VMEM(*rows_of(blocks)),
            pltpu.SemaphoreType.DMA((PIECES + 1 + len(tables),)),
        ],
        cost_estimate=kernel_cost(blocks),
        compiler_params=limit(rows_of(2 * blocks), table_room, acc_room, scores),
    )(codes, meta, hit, *stats, unit, *tables)
    return list(outs[:len(shapes)]), outs[len(shapes)], outs[-1]


def last_grads(codes, metas, hit, stats, turned, scores, units, tables, shapes, share_shapes):
    sizes = [unit.shape[0] for unit in units]
    tiles = sum(table.shape[0] for table in tables)
    chunks, blocks = len(sizes), sizes[-1]
    n_inputs = 2 * chunks - 1 + len(tables)
    table_room = ((tiles, TILE, D), jnp.bfloat16)
    acc_room = ((blocks + 1, BR, D), jnp.float32)
    tiles_room = ((tiles + 1, TILE, D), jnp.float32)
    early_room = rows_of(max(sizes[:-1], default=PIECES))
    kept = ((scores or codes)[0].shape[0], TILE, BR), jnp.bfloat16
    outs = pl.pallas_call(
        functools.partial(
            last_kernel, sizes, len(shapes), len(tables), len(stats), turned,
            len(share_shapes), tiles,
        ),
        out_shape=(
            *(jax.ShapeDtypeStruct(shape, jnp.bfloat16) for shape in shapes),
            *(jax.ShapeDtypeStruct(shape, jnp.bfloat16) for shape in share_shapes),
            jax.ShapeDtypeStruct((blocks, BR), jnp.float32),
        ),
        in_specs=[SMEM] * (2 * chunks) + [VMEM] * (1 + len(stats)) + [ANY] * n_inputs,
        out_specs=(*[ANY] * len(shapes), *[VMEM] * len(share_shapes), VMEM),
        scratch_shapes=[
            pltpu.VMEM(*rows_of(blocks)),
            pltpu.VMEM(*early_room),
            pltpu.VMEM(*kept),
            pltpu.VMEM(*table_room),
            pltpu.VMEM((blocks, BR), jnp.float32),
            pltpu.VMEM(*acc_room),
            pltpu.VMEM(*rows_of(blocks)),
            pltpu.VMEM(*tiles_room),
            pltpu.SemaphoreType.DMA((1 + len(tables),)),
            pltpu.SemaphoreType.DMA((2,)),
            pltpu.SemaphoreType.DMA((PIECES,)),
        ],
        cost_estimate=kernel_cost(sum(sizes)),
        compiler_params=limit(
            rows_of(2 * blocks), early_room, kept, table_room, table_room, acc_room, tiles_room
        ),
    )(*codes, *metas, hit, *stats, *scores, *units, *tables)
    cut = len(shapes)
    return list(outs[:cut]), list(outs[cut:-1]), outs[-1]


def add(first, second):
    return (first.astype(jnp.float32) + second.astype(jnp.float32)).astype(jnp.bfloat16)


class Neighbours:
    def __init__(self, nx, dp):
        self.nx, self.nz, self.dp, self.turned = nx, PIECES, dp, True

    def over_z(self, value, away):
        pairs = [
            (z * self.nx + x, (z ^ away) * self.nx + x)
            for z in range(self.nz) for x in range(self.nx)
        ]
        return lax.ppermute(value, "cls", pairs)

    def over_x(self, value):
        return lax.ppermute(value, "cls", [(c, c ^ 1) for c in range(self.nx * self.nz)])

    def over_y(self, value):
        return lax.ppermute(value, "dp", [(d, d ^ 2) for d in range(self.dp)])

    def over_core(self, value):
        return lax.ppermute(value, "dp", [(d, d ^ 1) for d in range(self.dp)])

    def all_over_z(self, value):
        return [value] + [self.over_z(value, away) for away in range(1, self.nz)]

    def gather(self, needed, chunks, lists, table, core, prepare):
        def moves(first, lists, table, core):
            half = table.shape[0] // 2
            sent = lax.dynamic_slice_in_dim(table, core * half, half, axis=0)
            from_x = self.over_x(sent)
            far, near = lax.optimization_barrier((self.over_z(first, 2), self.over_z(first, 1)))
            return (near, far, self.over_z(far, 1)), from_x, prepare(
                jnp.stack(self.all_over_z(lists))
            )

        first, second = chunks
        pieces, from_x, prepared = self.together(needed, moves, first, lists, table, core)
        return [[first, *pieces], [second]], [table, from_x], prepared

    def all_tables(self, tables):
        return [*tables, self.over_core(tables[-1])]

    def rest_of_rows(self, pieces, others):
        second, = pieces
        far, near, others = lax.optimization_barrier(
            (self.over_z(second, 2), self.over_z(second, 1), others)
        )
        return (near, far, self.over_z(far, 1)), others

    def whole_rows(self, pieces, rest):
        return [*pieces, *rest]

    def grad_shapes(self, size):
        return [(size, BR, D)] * PIECES

    def gather_stats(self, stats):
        return self.all_over_z(stats)

    def order(self, place):
        return place

    def own(self, loss, place, size):
        return loss[:size]

    def early_return(self, early, others):
        parts, = early
        near, passed = self.over_z(parts[1], 1), self.over_z(parts[3], 1)
        passed, others = lax.optimization_barrier((passed, others))
        return (near, self.over_z(add(passed, parts[2]), 2)), others

    def early_sums(self, early, returned):
        return [sum(part.astype(jnp.float32) for part in (early[0], *returned))]

    def together(self, needed, work, *operands):
        def no_work(*operands):
            return jax.tree.map(
                lambda out: jnp.zeros(out.shape, out.dtype), jax.eval_shape(work, *operands)
            )

        return lax.cond(needed, work, no_work, *operands)

    def sum_last(self, parts, shares):
        kept, sent = shares
        passed, got = self.over_z(parts[3], 1), self.over_core(sent)
        near = self.over_z(parts[1], 1)
        half = kept.shape[2] // 2
        x_sent = add(kept[1, :, :half], got[1, :, :half])
        y_sent = add(kept[:, 1, half:], got[:, 1, half:])
        passed, _, _ = lax.optimization_barrier((passed, x_sent, y_sent))
        far = self.over_z(add(passed, parts[2]), 2)
        near, far, shares = self.sum_shares(near, far, kept, got, x_sent, y_sent)
        return sum(part.astype(jnp.float32) for part in (parts[0], near, far)), shares

    def share_shapes(self, shard_tiles):
        return [(self.nx, self.dp // 2, shard_tiles, TILE, D // self.dp)] * 2

    def sum_shares(self, near, far, kept, got, x_sent, y_sent):
        half = kept.shape[2] // 2
        x_got, y_got = lax.optimization_barrier((self.over_x(x_sent), self.over_y(y_sent)))
        x_kept = [add(add(kept[0, y, :half], got[0, y, :half]), x_got[y]) for y in range(2)]
        y_kept = [add(add(kept[x, 0, half:], got[x, 0, half:]), y_got[x]) for x in range(2)]
        low, high = self.over_y(x_kept[1]), self.over_x(y_kept[1])
        near, far, _, _ = lax.optimization_barrier((near, far, low, high))
        low = x_kept[0].astype(jnp.float32) + low.astype(jnp.float32)
        high = y_kept[0].astype(jnp.float32) + high.astype(jnp.float32)
        return near, far, jnp.concatenate([low, high], axis=0)


class Groups:
    def __init__(self, nz, dp):
        self.nx, self.nz, self.dp, self.turned = 1, nz, dp, False

    def gather(self, needed, chunks, lists, table, core, prepare):
        gathered = [[lax.all_gather(rows, "cls", tiled=True)] for rows in chunks]
        return gathered, [table], prepare(lax.all_gather(lists, "cls"))

    def all_tables(self, tables):
        return tables

    def rest_of_rows(self, pieces, others):
        return (), others

    def whole_rows(self, pieces, rest):
        return pieces

    def grad_shapes(self, size):
        return [(self.nz * size, BR, D)]

    def gather_stats(self, stats):
        return list(lax.all_gather(stats, "cls"))

    def order(self, place):
        return jnp.zeros_like(place)

    def own(self, loss, place, size):
        return lax.dynamic_slice_in_dim(loss, place * size, size, axis=0)

    def total(self, part):
        return lax.psum_scatter(
            part, "cls", scatter_dimension=0, tiled=True
        ).astype(jnp.float32)

    def early_return(self, early, others):
        return [self.total(part) for part, in early], others

    def early_sums(self, early, returned):
        return returned

    def together(self, needed, work, *operands):
        return work(*operands)

    def sum_last(self, parts, shares):
        return self.total(parts[0]), self.sum_shares(shares)

    def share_shapes(self, shard_tiles):
        return [(shard_tiles, TILE, D)]

    def sum_shares(self, shares):
        return lax.psum_scatter(
            shares[0], "dp", scatter_dimension=2, tiled=True
        ).astype(jnp.float32)


def pair_codes(lists, shard_tiles, nx, place, column, room):
    entry = lists[:, :K].reshape(-1)
    owner = entry // shard_tiles
    mine = (entry >= 0) & (owner // nx == place)
    local = jnp.where(owner % nx == column, 0, shard_tiles) + entry % shard_tiles
    counter = jnp.arange(entry.shape[0], dtype=jnp.int32)
    code = ((counter // K) * FIELD + local) * 2 + (counter % K == 0)
    rank = jnp.sum(
        jnp.where(mine[None, :] & (counter[None, :] < counter[:, None]), 1, 0), axis=1
    ).astype(jnp.int32)
    slots = jnp.arange(room, dtype=jnp.int32)
    chosen = mine[None, :] & (rank[None, :] == slots[:, None])
    padding = (lists.shape[0] * FIELD + nx * shard_tiles) * 2
    codes = padding + jnp.sum(jnp.where(chosen, code[None, :] - padding, 0), axis=1)
    return codes.astype(jnp.int32), jnp.sum(mine.astype(jnp.int32))


def per_device(moves, sizes, embeddings, proxies, hard_tiles, tile_count, labels):
    nx, nz, dp = moves.nx, moves.nz, moves.dp
    blocks = hard_tiles.shape[0]
    shard_tiles = proxies.shape[0] // TILE
    me, part = lax.axis_index("cls"), lax.axis_index("dp")
    place, column = me // nx, me % nx

    row_blocks = embeddings.reshape(blocks, BR, D)

    position = labels.reshape(blocks, BR) - hard_tiles[:, 0:1] * TILE
    entries = jnp.arange(K, dtype=jnp.int32)
    used = jnp.where(entries[None, :] < tile_count[:, None], hard_tiles, -1)
    starts = [sum(sizes[:chunk]) for chunk in range(len(sizes))]
    spots = [slice(start, start + size) for start, size in zip(starts, sizes)]
    held = [nz * size for size in sizes]
    last = len(sizes) - 1
    needed = tile_count[0] > 0

    def prepare(lists):
        prepared = []
        for spot, blocks_held in zip(spots, held):
            room = min(blocks_held * K, nz * (blocks * K // (nx * nz)) * nx)
            room = -(-room // PAIRS_PER_STEP) * PAIRS_PER_STEP
            chunk_lists = lists[:, spot].reshape(blocks_held, K + BR)
            code, count = pair_codes(chunk_lists, shard_tiles, nx, place, column, room)
            meta = jnp.stack([count, part, moves.order(place)]).astype(jnp.int32)
            prepared.append((code, meta, chunk_lists[:, K:]))
        return prepared

    gathered, tables, prepared = moves.gather(
        needed,
        [row_blocks[spot] for spot in spots],
        jnp.concatenate([used, position], axis=1),
        proxies.reshape(shard_tiles, TILE, D),
        part % 2,
        prepare,
    )

    def scored(chunk, rows, tables, prepared):
        parts, unit = score(held[chunk], *prepared[chunk], rows, tables)
        return moves.gather_stats(parts), unit

    def early_work(gathered, own_tables, prepared):
        units, made, rest = [], [], ()
        tables = moves.all_tables(own_tables)
        for chunk in range(last):
            stats, unit = scored(chunk, gathered[chunk], tables, prepared)
            if chunk == 0:
                rest, stats = moves.rest_of_rows(gathered[-1], stats)
            units.append(unit)
            made.append(grads(
                held[chunk], *prepared[chunk], stats, moves.turned, unit, tables,
                moves.grad_shapes(sizes[chunk]),
            ))
        return rest, tables[len(own_tables):], units, made

    def last_work(rows, tables, prepared, units, scores, early):
        codes, metas, hits = zip(*prepared)
        stats, unit = scored(last, rows, tables, prepared)
        returned, stats = moves.early_return(early, stats)
        return returned, last_grads(
            codes, metas, hits[-1], stats, moves.turned, scores, units + [unit], tables,
            moves.grad_shapes(sizes[-1]), moves.share_shapes(shard_tiles),
        )

    def work(gathered, tables, prepared):
        rest, more, units, made = early_work(gathered, tables, prepared)
        early, scores, losses = zip(*made)
        returned, (parts, shares, loss) = last_work(
            moves.whole_rows(gathered[-1], rest), [*tables, *more], prepared, units,
            list(scores), early,
        )
        return [part[0] for part in early], returned, parts, shares, [*losses, loss]

    early, returned, parts, shares, losses = moves.together(
        needed, work, gathered, tables, prepared
    )
    total, shares = moves.sum_last(parts, shares)
    row_grads = moves.early_sums(early, returned) + [total]
    losses = [
        moves.own(part, place, size) for part, size in zip(losses, sizes)
    ]

    embeddings, losses = lax.optimization_barrier((embeddings, losses))
    emb_exact = embeddings.astype(jnp.float32)
    inverse_norm = lax.rsqrt(jnp.sum(emb_exact * emb_exact, axis=1, keepdims=True) + epsilon)
    unit_exact = emb_exact * inverse_norm
    proxy_grad = shares.reshape(shard_tiles * TILE, D // dp)
    row_loss = jnp.concatenate(losses, axis=0).reshape(-1)
    embed_grad = []
    for spot, grad_rows in zip(spots, row_grads):
        span = slice(spot.start * BR, spot.stop * BR)
        exact, norm = unit_exact[span], inverse_norm[span]
        grad_rows = grad_rows.reshape(-1, D)
        radial = jnp.sum(exact * grad_rows, axis=1, keepdims=True)
        embed_grad.append(((grad_rows - exact * radial) * norm).astype(jnp.bfloat16))
    embed_grad = jnp.concatenate(embed_grad, axis=0)
    return (row_loss, embed_grad, proxy_grad)


def solution(mesh):
    placed = (
        P(("dp", "cls"), None),
        P("cls", None),
        P(("dp", "cls"), None),
        P(("dp", "cls")),
        P(("dp", "cls")),
    )
    dp, groups = mesh.shape["dp"], mesh.shape["cls"]
    if (dp, groups) == (4, 2 * PIECES):
        moves, sizes = Neighbours(2, dp), [4, 4]
    else:
        chunks = max(1, groups // 8)
        moves, sizes = Groups(groups, dp), [8 // chunks] * chunks
    return jax.shard_map(
        functools.partial(per_device, moves, sizes),
        mesh=mesh,
        in_specs=placed,
        out_specs=(P(("dp", "cls")), P(("dp", "cls"), None), P("cls", "dp")),
        check_vma=False,
    )
```

```python
import functools

import jax
import jax.numpy as jnp
import numpy as np
from jax import lax
from jax.experimental import pallas as pl
from jax.experimental.pallas import tpu as pltpu
from jax.sharding import PartitionSpec as P

D = 512
TILE = 128
BR = 128
K = 8
PAIRS_PER_STEP = 4
FIELD = 128
PIECES = 4
VMEM_BYTES = 60 * 1024 * 1024
SPARE_BYTES = 4 * 1024 * 1024

logit_scale = 4.0
epsilon = 1e-06
unused_logit = -1e30

SMEM = pl.BlockSpec(memory_space=pltpu.SMEM)
VMEM = pl.BlockSpec(memory_space=pltpu.VMEM)
ANY = pl.BlockSpec(memory_space=pl.ANY)


def run_copies(jobs, sems, first=0):
    copies = [
        pltpu.make_async_copy(source, target, sems.at[first + index])
        for index, (source, target) in enumerate(jobs)
    ]
    for copy in copies:
        copy.start()
    return copies


def row_places(meta_ref, refs, blocks):
    size = blocks // PIECES
    if len(refs) > 1:
        return [(ref, piece * size) for piece, ref in enumerate(refs)]
    return [
        (refs[0].at[pl.ds(place * size, size)], (meta_ref[2] ^ place) * size)
        for place in range(PIECES)
    ]


def row_jobs(meta_ref, refs, rows_ref):
    return [
        (ref, rows_ref.at[pl.ds(start, ref.shape[0])])
        for ref, start in row_places(meta_ref, refs, rows_ref.shape[0])
    ]


def store_rows(meta_ref, rows_acc, out_ref, grad_refs, sems):
    blocks = out_ref.shape[0]
    out_ref[...] = rows_acc[:blocks].astype(out_ref.dtype)
    return run_copies(
        [
            (out_ref.at[pl.ds(start, ref.shape[0])], ref)
            for ref, start in row_places(meta_ref, grad_refs, blocks)
        ],
        sems,
    )


def aligned(refs, row, turned):
    parts = [ref[row] for ref in refs]
    if not turned:
        return parts
    size = parts[0].shape[0] // PIECES
    return [
        jnp.concatenate(
            [part[(piece ^ away) * size:((piece ^ away) + 1) * size] for piece in range(PIECES)]
        )
        for away, part in enumerate(parts)
    ]


def table_jobs(meta_ref, table_refs, table_ref):
    core = meta_ref[1] % 2
    jobs = [(table_refs[0], table_ref.at[pl.ds(0, table_refs[0].shape[0])])]
    if len(table_refs) > 1:
        half = table_refs[1].shape[0]
        jobs.append((table_refs[1], table_ref.at[pl.ds((2 + core) * half, half)]))
        jobs.append((table_refs[2], table_ref.at[pl.ds((3 - core) * half, half)]))
    return jobs


def transposed_logits(tile, rows):
    return logit_scale * lax.dot_general(
        tile, rows, (((1,), (1,)), ((), ())), preferred_element_type=jnp.float32
    )


def decode(code):
    return code // (2 * FIELD), (code // 2) % FIELD, (code % 2) == 1


def score_kernel(n_rows, n_tables, blocks, tiles, codes_ref, meta_ref, hit_ref, *refs):
    row_refs, refs = refs[:n_rows], refs[n_rows:]
    table_refs, refs = refs[:n_tables], refs[n_tables:]
    stats_ref, rows_ref, table_ref, lse_ref, pos_ref, sems = refs
    row_copies = run_copies(row_jobs(meta_ref, row_refs, rows_ref), sems)
    table_copies = run_copies(table_jobs(meta_ref, table_refs, table_ref), sems, PIECES)
    lse_ref[...] = jnp.full(lse_ref.shape, unused_logit, jnp.float32)
    pos_ref[...] = jnp.zeros(pos_ref.shape, jnp.float32)
    class_at = lax.broadcasted_iota(jnp.int32, (TILE, BR), 0)
    for copy in row_copies:
        copy.wait()

    def normalise(block, carry):
        exact = rows_ref[block].astype(jnp.float32)
        norm = lax.rsqrt(jnp.sum(exact * exact, axis=1, keepdims=True) + epsilon)
        rows_ref[block] = (exact * norm).astype(jnp.bfloat16)
        return carry

    lax.fori_loop(0, blocks, normalise, 0)
    for copy in table_copies:
        copy.wait()

    def step(index, carry):
        held = []
        for lane in range(PAIRS_PER_STEP):
            block, tile, first = decode(codes_ref[index * PAIRS_PER_STEP + lane])
            source = jnp.minimum(block, blocks - 1)
            logits = transposed_logits(
                table_ref[jnp.minimum(tile, tiles - 1)], rows_ref[source]
            )
            peak = jnp.max(logits, axis=0, keepdims=True)
            total = jnp.sum(jnp.exp(logits - peak), axis=0, keepdims=True)
            hit = class_at == hit_ref[pl.ds(source, 1), :]
            positive = jnp.sum(jnp.where(hit, logits, 0.0), axis=0, keepdims=True)
            held.append((block, peak + jnp.log(total), jnp.where(first, positive, 0.0)))
        for block, lse, positive in held:
            before = lse_ref[pl.ds(block, 1), :]
            top = jnp.maximum(before, lse)
            lse_ref[pl.ds(block, 1), :] = top + jnp.log(
                jnp.exp(before - top) + jnp.exp(lse - top)
            )
            pos_ref[pl.ds(block, 1), :] += positive
        return carry

    lax.fori_loop(0, pl.cdiv(meta_ref[0], PAIRS_PER_STEP), step, 0)
    stats_ref[0] = lse_ref[:blocks, :]
    stats_ref[1] = pos_ref[:blocks, :]


def make_totals(stat_refs, turned, total_ref, loss_ref):
    lse = aligned(stat_refs, 0, turned)
    top = functools.reduce(jnp.maximum, lse)
    total = top + jnp.log(sum(jnp.exp(part - top) for part in lse))
    total_ref[...] = total
    loss_ref[...] = total - sum(aligned(stat_refs, 1, turned))


def pair_score(code, blocks, tiles, rows_ref, table_ref, hit_ref, total_ref, class_at):
    block, tile, first = decode(code)
    source = jnp.minimum(block, blocks - 1)
    table_at = jnp.minimum(tile, tiles - 1)
    logits = transposed_logits(table_ref[table_at], rows_ref[source])
    share = jnp.exp(logits - total_ref[pl.ds(source, 1), :])
    wanted = jnp.where(first, hit_ref[pl.ds(source, 1), :], -1)
    hit = (class_at == wanted).astype(jnp.float32)
    return (logit_scale * (share - hit)).astype(jnp.bfloat16)


def row_terms(score, tile):
    return lax.dot_general(
        score, tile, (((0,), (0,)), ((), ())), preferred_element_type=jnp.float32
    )


def grad_kernel(
    n_grads, n_tables, n_stats, turned, blocks, tiles, codes_ref, meta_ref, hit_ref, *refs
):
    stat_refs, refs = refs[:n_stats], refs[n_stats:]
    unit_ref, refs = refs[0], refs[1:]
    table_refs, refs = refs[:n_tables], refs[n_tables:]
    grad_refs, refs = refs[:n_grads], refs[n_grads:]
    scores_ref, loss_ref, rows_ref, table_ref, total_ref, rows_acc, out_ref, sems = refs
    copies = run_copies(
        [(unit_ref, rows_ref)] + table_jobs(meta_ref, table_refs, table_ref), sems, PIECES
    )
    rows_acc[...] = jnp.zeros(rows_acc.shape, jnp.float32)
    make_totals(stat_refs, turned, total_ref, loss_ref)
    class_at = lax.broadcasted_iota(jnp.int32, (TILE, BR), 0)
    for copy in copies:
        copy.wait()

    def step(index, carry):
        held = []
        for lane in range(PAIRS_PER_STEP):
            pair = index * PAIRS_PER_STEP + lane
            score = pair_score(
                codes_ref[pair], blocks, tiles, rows_ref, table_ref, hit_ref, total_ref, class_at
            )
            scores_ref[pair] = score
            held.append(score)
        for lane, score in enumerate(held):
            block, tile, _ = decode(codes_ref[index * PAIRS_PER_STEP + lane])
            rows_acc[block] += row_terms(score, table_ref[jnp.minimum(tile, tiles - 1)])
        return carry

    lax.fori_loop(0, pl.cdiv(meta_ref[0], PAIRS_PER_STEP), step, 0)
    for copy in store_rows(meta_ref, rows_acc, out_ref, grad_refs, sems):
        copy.wait()


def last_kernel(sizes, n_grads, n_tables, n_stats, turned, n_shares, tiles, *refs):
    chunks, blocks = len(sizes), sizes[-1]
    codes_refs, refs = refs[:chunks], refs[chunks:]
    meta_refs, refs = refs[:chunks], refs[chunks:]
    hit_ref, refs = refs[0], refs[1:]
    stat_refs, refs = refs[:n_stats], refs[n_stats:]
    scores_refs, refs = refs[:chunks - 1], refs[chunks - 1:]
    unit_refs, refs = refs[:chunks], refs[chunks:]
    table_refs, refs = refs[:n_tables], refs[n_tables:]
    grad_refs, refs = refs[:n_grads], refs[n_grads:]
    share_refs, refs = refs[:n_shares], refs[n_shares:]
    loss_ref, refs = refs[0], refs[1:]
    rows_ref, early_ref, held_ref, table_ref, total_ref, rows_acc, out_ref, *refs = refs
    tiles_acc, sems, early_sems, row_sems = refs
    codes_ref, meta_ref = codes_refs[-1], meta_refs[-1]
    copies = run_copies(
        [(unit_refs[-1], rows_ref)] + table_jobs(meta_ref, table_refs, table_ref), sems
    )


    def fetch(chunk):
        early = early_ref.at[pl.ds(0, sizes[chunk])]
        return run_copies(
            [(unit_refs[chunk], early), (scores_refs[chunk], held_ref)], early_sems
        )

    early = fetch(0) if chunks > 1 else []
    rows_acc[...] = jnp.zeros(rows_acc.shape, jnp.float32)
    tiles_acc[...] = jnp.zeros(tiles_acc.shape, jnp.float32)
    make_totals(stat_refs, turned, total_ref, loss_ref)
    class_at = lax.broadcasted_iota(jnp.int32, (TILE, BR), 0)
    for copy in copies:
        copy.wait()

    def step(index, carry):
        held = [
            pair_score(
                codes_ref[index * PAIRS_PER_STEP + lane], blocks, tiles, rows_ref, table_ref,
                hit_ref, total_ref, class_at,
            )
            for lane in range(PAIRS_PER_STEP)
        ]
        for lane, score in enumerate(held):
            block, tile, _ = decode(codes_ref[index * PAIRS_PER_STEP + lane])
            rows_acc[block] += row_terms(score, table_ref[jnp.minimum(tile, tiles - 1)])
            tiles_acc[tile] += jnp.dot(
                score, rows_ref[jnp.minimum(block, blocks - 1)],
                preferred_element_type=jnp.float32,
            )
        return carry

    lax.fori_loop(0, pl.cdiv(meta_ref[0], PAIRS_PER_STEP), step, 0)
    stored = store_rows(meta_ref, rows_acc, out_ref, grad_refs, row_sems)
    for chunk in range(chunks - 1):
        for copy in early if chunk == 0 else fetch(chunk):
            copy.wait()

        def early_step(index, carry, chunk=chunk):
            for lane in range(PAIRS_PER_STEP):
                pair = index * PAIRS_PER_STEP + lane
                block, tile, _ = decode(codes_refs[chunk][pair])
                tiles_acc[tile] += jnp.dot(
                    held_ref[pair],
                    early_ref[jnp.minimum(block, sizes[chunk] - 1)],
                    preferred_element_type=jnp.float32,
                )
            return carry

        lax.fori_loop(0, pl.cdiv(meta_refs[chunk][0], PAIRS_PER_STEP), early_step, 0)
    if n_shares == 1:
        share_refs[0][...] = tiles_acc[:tiles].astype(jnp.bfloat16)
    else:
        part = meta_ref[1]
        shard, width = share_refs[0].shape[2], share_refs[0].shape[-1]
        for core, ref in enumerate(share_refs):
            for y in range(ref.shape[1]):
                start = pl.multiple_of(((2 * y + core) ^ part) * width, width)
                for x in range(ref.shape[0]):
                    ref[x, y] = tiles_acc[
                        pl.ds(x * shard, shard), :, pl.ds(start, width)
                    ].astype(jnp.bfloat16)
    for copy in stored:
        copy.wait()


def kernel_cost(blocks):
    return pl.CostEstimate(flops=blocks * BR * D, bytes_accessed=blocks * BR * D, transcendentals=0)


def limit(*scratch):
    total = 0
    for shape, dtype in scratch:
        total += int(np.prod(shape)) * jnp.dtype(dtype).itemsize
    return pltpu.CompilerParams(vmem_limit_bytes=min(VMEM_BYTES, total + SPARE_BYTES))


def rows_of(blocks):
    return (blocks, BR, D), jnp.bfloat16


def score(blocks, codes, meta, hit, rows, tables):
    tiles = sum(table.shape[0] for table in tables)
    table_room = ((tiles, TILE, D), jnp.bfloat16)
    return pl.pallas_call(
        functools.partial(score_kernel, len(rows), len(tables), blocks, tiles),
        out_shape=(
            jax.ShapeDtypeStruct((2, blocks, BR), jnp.float32),
            jax.ShapeDtypeStruct(*rows_of(blocks)),
        ),
        in_specs=[SMEM, SMEM, VMEM] + [ANY] * (len(rows) + len(tables)),
        out_specs=(VMEM, VMEM),
        scratch_shapes=[
            pltpu.VMEM(*table_room),
            pltpu.VMEM((blocks + 8, BR), jnp.float32),
            pltpu.VMEM((blocks + 8, BR), jnp.float32),
            pltpu.SemaphoreType.DMA((PIECES + len(tables),)),
        ],
        cost_estimate=kernel_cost(blocks),
        compiler_params=limit(rows_of(blocks), table_room),
    )(codes, meta, hit, *rows, *tables)


def grads(blocks, codes, meta, hit, stats, turned, unit, tables, shapes):
    tiles = sum(table.shape[0] for table in tables)
    table_room = ((tiles, TILE, D), jnp.bfloat16)
    acc_room = ((blocks + 1, BR, D), jnp.float32)
    scores = ((codes.shape[0], TILE, BR), jnp.bfloat16)
    outs = pl.pallas_call(
        functools.partial(
            grad_kernel, len(shapes), len(tables), len(stats), turned, blocks, tiles
        ),
        out_shape=(
            *(jax.ShapeDtypeStruct(shape, jnp.bfloat16) for shape in shapes),
            jax.ShapeDtypeStruct(*scores),
            jax.ShapeDtypeStruct((blocks, BR), jnp.float32),
        ),
        in_specs=[SMEM, SMEM] + [VMEM] * (1 + len(stats)) + [ANY] * (1 + len(tables)),
        out_specs=(*[ANY] * len(shapes), VMEM, VMEM),
        scratch_shapes=[
            pltpu.VMEM(*rows_of(blocks)),
            pltpu.VMEM(*table_room),
            pltpu.VMEM((blocks, BR), jnp.float32),
            pltpu.VMEM(*acc_room),
            pltpu.VMEM(*rows_of(blocks)),
            pltpu.SemaphoreType.DMA((PIECES + 1 + len(tables),)),
        ],
        cost_estimate=kernel_cost(blocks),
        compiler_params=limit(rows_of(2 * blocks), table_room, acc_room, scores),
    )(codes, meta, hit, *stats, unit, *tables)
    return list(outs[:len(shapes)]), outs[len(shapes)], outs[-1]


def last_grads(codes, metas, hit, stats, turned, scores, units, tables, shapes, share_shapes):
    sizes = [unit.shape[0] for unit in units]
    tiles = sum(table.shape[0] for table in tables)
    chunks, blocks = len(sizes), sizes[-1]
    n_inputs = 2 * chunks - 1 + len(tables)
    table_room = ((tiles, TILE, D), jnp.bfloat16)
    acc_room = ((blocks + 1, BR, D), jnp.float32)
    tiles_room = ((tiles + 1, TILE, D), jnp.float32)
    early_room = rows_of(max(sizes[:-1], default=PIECES))
    kept = ((scores or codes)[0].shape[0], TILE, BR), jnp.bfloat16
    outs = pl.pallas_call(
        functools.partial(
            last_kernel, sizes, len(shapes), len(tables), len(stats), turned,
            len(share_shapes), tiles,
        ),
        out_shape=(
            *(jax.ShapeDtypeStruct(shape, jnp.bfloat16) for shape in shapes),
            *(jax.ShapeDtypeStruct(shape, jnp.bfloat16) for shape in share_shapes),
            jax.ShapeDtypeStruct((blocks, BR), jnp.float32),
        ),
        in_specs=[SMEM] * (2 * chunks) + [VMEM] * (1 + len(stats)) + [ANY] * n_inputs,
        out_specs=(*[ANY] * len(shapes), *[VMEM] * len(share_shapes), VMEM),
        scratch_shapes=[
            pltpu.VMEM(*rows_of(blocks)),
            pltpu.VMEM(*early_room),
            pltpu.VMEM(*kept),
            pltpu.VMEM(*table_room),
            pltpu.VMEM((blocks, BR), jnp.float32),
            pltpu.VMEM(*acc_room),
            pltpu.VMEM(*rows_of(blocks)),
            pltpu.VMEM(*tiles_room),
            pltpu.SemaphoreType.DMA((1 + len(tables),)),
            pltpu.SemaphoreType.DMA((2,)),
            pltpu.SemaphoreType.DMA((PIECES,)),
        ],
        cost_estimate=kernel_cost(sum(sizes)),
        compiler_params=limit(
            rows_of(2 * blocks), early_room, kept, table_room, table_room, acc_room, tiles_room
        ),
    )(*codes, *metas, hit, *stats, *scores, *units, *tables)
    cut = len(shapes)
    return list(outs[:cut]), list(outs[cut:-1]), outs[-1]


def add(first, second):
    return (first.astype(jnp.float32) + second.astype(jnp.float32)).astype(jnp.bfloat16)


class Neighbours:
    def __init__(self, nx, dp):
        self.nx, self.nz, self.dp, self.turned = nx, PIECES, dp, True

    def over_z(self, value, away):
        pairs = [
            (z * self.nx + x, (z ^ away) * self.nx + x)
            for z in range(self.nz) for x in range(self.nx)
        ]
        return lax.ppermute(value, "cls", pairs)

    def over_x(self, value):
        return lax.ppermute(value, "cls", [(c, c ^ 1) for c in range(self.nx * self.nz)])

    def over_y(self, value):
        return lax.ppermute(value, "dp", [(d, d ^ 2) for d in range(self.dp)])

    def over_core(self, value):
        return lax.ppermute(value, "dp", [(d, d ^ 1) for d in range(self.dp)])

    def all_over_z(self, value):
        return [value] + [self.over_z(value, away) for away in range(1, self.nz)]

    def gather(self, needed, rows, spots, lists, table, core, prepare):
        def moves(rows, lists, table, core):
            first = rows[:size]
            half = table.shape[0] // 2
            sent = lax.dynamic_slice_in_dim(table, core * half, half, axis=0)
            from_x = self.over_x(sent)
            far, near = lax.optimization_barrier((self.over_z(first, 2), self.over_z(first, 1)))
            return (near, far, self.over_z(far, 1)), from_x, prepare(
                jnp.stack(self.all_over_z(lists))
            )

        size = spots[0].stop
        pieces, from_x, prepared = self.together(needed, moves, rows, lists, table, core)
        return [[rows[spots[0]], *pieces], [rows[spots[1]]]], [table, from_x], prepared

    def all_tables(self, tables):
        return [*tables, self.over_core(tables[-1])]

    def rest_of_rows(self, pieces, others):
        second, = pieces
        far, near, others = lax.optimization_barrier(
            (self.over_z(second, 2), self.over_z(second, 1), others)
        )
        return (near, far, self.over_z(far, 1)), others

    def whole_rows(self, pieces, rest):
        return [*pieces, *rest]

    def grad_shapes(self, size):
        return [(size, BR, D)] * PIECES

    def gather_stats(self, stats):
        return self.all_over_z(stats)

    def order(self, place):
        return place

    def own(self, loss, place, size):
        return loss[:size]

    def early_return(self, early, others):
        parts, = early
        near, passed = self.over_z(parts[1], 1), self.over_z(parts[3], 1)
        passed, others = lax.optimization_barrier((passed, others))
        return (near, self.over_z(add(passed, parts[2]), 2)), others

    def early_sums(self, early, returned):
        return [sum(part.astype(jnp.float32) for part in (early[0][0], *returned))]

    def together(self, needed, work, *operands):
        def no_work(*operands):
            return jax.tree.map(
                lambda out: jnp.zeros(out.shape, out.dtype), jax.eval_shape(work, *operands)
            )

        return lax.cond(needed, work, no_work, *operands)

    def sum_last(self, parts, shares):
        kept, sent = shares
        passed, got = self.over_z(parts[3], 1), self.over_core(sent)
        near = self.over_z(parts[1], 1)
        half = kept.shape[2] // 2
        x_sent = add(kept[1, :, :half], got[1, :, :half])
        y_sent = add(kept[:, 1, half:], got[:, 1, half:])
        passed, _, _ = lax.optimization_barrier((passed, x_sent, y_sent))
        far = self.over_z(add(passed, parts[2]), 2)
        near, far, shares = self.sum_shares(near, far, kept, got, x_sent, y_sent)
        return sum(part.astype(jnp.float32) for part in (parts[0], near, far)), shares

    def share_shapes(self, shard_tiles):
        return [(self.nx, self.dp // 2, shard_tiles, TILE, D // self.dp)] * 2

    def sum_shares(self, near, far, kept, got, x_sent, y_sent):
        half = kept.shape[2] // 2
        x_got, y_got = lax.optimization_barrier((self.over_x(x_sent), self.over_y(y_sent)))
        x_kept = [add(add(kept[0, y, :half], got[0, y, :half]), x_got[y]) for y in range(2)]
        y_kept = [add(add(kept[x, 0, half:], got[x, 0, half:]), y_got[x]) for x in range(2)]
        near, far, low, high = lax.optimization_barrier(
            (near, far, self.over_y(x_kept[1]), self.over_x(y_kept[1]))
        )
        low = x_kept[0].astype(jnp.float32) + low.astype(jnp.float32)
        high = y_kept[0].astype(jnp.float32) + high.astype(jnp.float32)
        return near, far, jnp.concatenate([low, high], axis=0)


class Groups:
    def __init__(self, nz, dp):
        self.nx, self.nz, self.dp, self.turned = 1, nz, dp, False

    def gather(self, needed, rows, spots, lists, table, core, prepare):
        gathered = [[lax.all_gather(rows[spot], "cls", tiled=True)] for spot in spots]
        return gathered, [table], prepare(lax.all_gather(lists, "cls"))

    def all_tables(self, tables):
        return tables

    def rest_of_rows(self, pieces, others):
        return (), others

    def whole_rows(self, pieces, rest):
        return pieces

    def grad_shapes(self, size):
        return [(self.nz * size, BR, D)]

    def gather_stats(self, stats):
        return list(lax.all_gather(stats, "cls"))

    def order(self, place):
        return jnp.zeros_like(place)

    def own(self, loss, place, size):
        return lax.dynamic_slice_in_dim(loss, place * size, size, axis=0)

    def total(self, part):
        return lax.psum_scatter(
            part, "cls", scatter_dimension=0, tiled=True
        ).astype(jnp.float32)

    def early_return(self, early, others):
        return [self.total(part) for part, in early], others

    def early_sums(self, early, returned):
        return returned

    def together(self, needed, work, *operands):
        return work(*operands)

    def sum_last(self, parts, shares):
        return self.total(parts[0]), self.sum_shares(shares)

    def share_shapes(self, shard_tiles):
        return [(shard_tiles, TILE, D)]

    def sum_shares(self, shares):
        return lax.psum_scatter(
            shares[0], "dp", scatter_dimension=2, tiled=True
        ).astype(jnp.float32)


def pair_codes(lists, shard_tiles, nx, place, column, room):
    entry = lists[:, :K].reshape(-1)
    owner = entry // shard_tiles
    mine = (entry >= 0) & (owner // nx == place)
    local = jnp.where(owner % nx == column, 0, shard_tiles) + entry % shard_tiles
    counter = jnp.arange(entry.shape[0], dtype=jnp.int32)
    code = ((counter // K) * FIELD + local) * 2 + (counter % K == 0)
    rank = jnp.sum(
        jnp.where(mine[None, :] & (counter[None, :] < counter[:, None]), 1, 0), axis=1
    ).astype(jnp.int32)
    slots = jnp.arange(room, dtype=jnp.int32)
    chosen = mine[None, :] & (rank[None, :] == slots[:, None])
    padding = (lists.shape[0] * FIELD + nx * shard_tiles) * 2
    codes = padding + jnp.sum(jnp.where(chosen, code[None, :] - padding, 0), axis=1)
    return codes.astype(jnp.int32), jnp.sum(mine.astype(jnp.int32))


def per_device(moves, sizes, embeddings, proxies, hard_tiles, tile_count, labels):
    nx, nz, dp = moves.nx, moves.nz, moves.dp
    blocks = hard_tiles.shape[0]
    shard_tiles = proxies.shape[0] // TILE
    me, part = lax.axis_index("cls"), lax.axis_index("dp")
    place, column = me // nx, me % nx

    row_blocks = embeddings.reshape(blocks, BR, D)

    position = labels.reshape(blocks, BR) - hard_tiles[:, 0:1] * TILE
    entries = jnp.arange(K, dtype=jnp.int32)
    used = jnp.where(entries[None, :] < tile_count[:, None], hard_tiles, -1)
    starts = [sum(sizes[:chunk]) for chunk in range(len(sizes))]
    spots = [slice(start, start + size) for start, size in zip(starts, sizes)]
    held = [nz * size for size in sizes]
    last = len(sizes) - 1
    needed = tile_count[0] > 0

    def prepare(lists):
        prepared = []
        for spot, blocks_held in zip(spots, held):
            room = min(blocks_held * K, nz * (blocks * K // (nx * nz)) * nx)
            room = -(-room // PAIRS_PER_STEP) * PAIRS_PER_STEP
            chunk_lists = lists[:, spot].reshape(blocks_held, K + BR)
            code, count = pair_codes(chunk_lists, shard_tiles, nx, place, column, room)
            meta = jnp.stack([count, part, moves.order(place)]).astype(jnp.int32)
            prepared.append((code, meta, chunk_lists[:, K:]))
        return prepared

    gathered, tables, prepared = moves.gather(
        needed,
        row_blocks,
        spots,
        jnp.concatenate([used, position], axis=1),
        proxies.reshape(shard_tiles, TILE, D),
        part % 2,
        prepare,
    )

    def scored(chunk, rows, tables, prepared):
        parts, unit = score(held[chunk], *prepared[chunk], rows, tables)
        return moves.gather_stats(parts), unit

    def early_work(gathered, own_tables, prepared):
        units, made, rest = [], [], ()
        tables = moves.all_tables(own_tables)
        for chunk in range(last):
            stats, unit = scored(chunk, gathered[chunk], tables, prepared)
            if chunk == 0:
                rest, stats = moves.rest_of_rows(gathered[-1], stats)
            units.append(unit)
            made.append(grads(
                held[chunk], *prepared[chunk], stats, moves.turned, unit, tables,
                moves.grad_shapes(sizes[chunk]),
            ))
        return rest, tables[len(own_tables):], units, made

    def last_work(rows, tables, prepared, units, scores, early):
        codes, metas, hits = zip(*prepared)
        stats, unit = scored(last, rows, tables, prepared)
        returned, stats = moves.early_return(early, stats)
        return returned, last_grads(
            codes, metas, hits[-1], stats, moves.turned, scores, units + [unit], tables,
            moves.grad_shapes(sizes[-1]), moves.share_shapes(shard_tiles),
        )

    rest, more, units, made = moves.together(needed, early_work, gathered, tables, prepared)
    tables = [*tables, *more]
    rows = moves.whole_rows(gathered[-1], rest)
    early, scores, losses = zip(*made)
    returned, (parts, shares, loss) = moves.together(
        needed, last_work, rows, tables, prepared, units, list(scores), early
    )
    total, shares = moves.sum_last(parts, shares)
    row_grads = moves.early_sums(early, returned) + [total]
    losses = [
        moves.own(part, place, size) for part, size in zip((*losses, loss), sizes)
    ]

    embeddings, units = lax.optimization_barrier((embeddings, units))
    emb_exact = embeddings.astype(jnp.float32)
    inverse_norm = lax.rsqrt(jnp.sum(emb_exact * emb_exact, axis=1, keepdims=True) + epsilon)
    unit_exact = emb_exact * inverse_norm
    proxy_grad = shares.reshape(shard_tiles * TILE, D // dp)
    row_loss = jnp.concatenate(losses, axis=0).reshape(-1)
    embed_grad = jnp.zeros((blocks * BR, D), jnp.bfloat16)
    for spot, grad_rows in zip(spots, row_grads):
        span = slice(spot.start * BR, spot.stop * BR)
        exact, norm = unit_exact[span], inverse_norm[span]
        grad_rows = grad_rows.reshape(-1, D)
        radial = jnp.sum(exact * grad_rows, axis=1, keepdims=True)
        grad_rows = ((grad_rows - exact * radial) * norm).astype(jnp.bfloat16)
        embed_grad = lax.dynamic_update_slice_in_dim(embed_grad, grad_rows, span.start, axis=0)
    return (row_loss, embed_grad, proxy_grad)


def solution(mesh):
    placed = (
        P(("dp", "cls"), None),
        P("cls", None),
        P(("dp", "cls"), None),
        P(("dp", "cls")),
        P(("dp", "cls")),
    )
    dp, groups = mesh.shape["dp"], mesh.shape["cls"]
    if (dp, groups) == (4, 2 * PIECES):
        moves, sizes = Neighbours(2, dp), [4, 4]
    else:
        chunks = max(1, groups // 8)
        moves, sizes = Groups(groups, dp), [8 // chunks] * chunks
    return jax.shard_map(
        functools.partial(per_device, moves, sizes),
        mesh=mesh,
        in_specs=placed,
        out_specs=(P(("dp", "cls")), P(("dp", "cls"), None), P("cls", "dp")),
        check_vma=False,
    )
```

```python
import functools

import jax
import jax.numpy as jnp
import numpy as np
from jax import lax
from jax.experimental import pallas as pl
from jax.experimental.pallas import tpu as pltpu
from jax.sharding import PartitionSpec as P

D = 512
TILE = 128
BR = 128
K = 8
PAIRS_PER_STEP = 4
FIELD = 128
PIECES = 4
VMEM_BYTES = 60 * 1024 * 1024
SPARE_BYTES = 4 * 1024 * 1024

logit_scale = 4.0
epsilon = 1e-06
unused_logit = -1e30

SMEM = pl.BlockSpec(memory_space=pltpu.SMEM)
VMEM = pl.BlockSpec(memory_space=pltpu.VMEM)
ANY = pl.BlockSpec(memory_space=pl.ANY)


def run_copies(jobs, sems, first=0):
    copies = [
        pltpu.make_async_copy(source, target, sems.at[first + index])
        for index, (source, target) in enumerate(jobs)
    ]
    for copy in copies:
        copy.start()
    return copies


def row_places(meta_ref, refs, blocks):
    size = blocks // PIECES
    if len(refs) > 1:
        return [(ref, piece * size) for piece, ref in enumerate(refs)]
    return [
        (refs[0].at[pl.ds(place * size, size)], (meta_ref[2] ^ place) * size)
        for place in range(PIECES)
    ]


def row_jobs(meta_ref, refs, rows_ref):
    return [
        (ref, rows_ref.at[pl.ds(start, ref.shape[0])])
        for ref, start in row_places(meta_ref, refs, rows_ref.shape[0])
    ]


def store_rows(meta_ref, rows_acc, out_ref, grad_refs, sems):
    blocks = out_ref.shape[0]
    out_ref[...] = rows_acc[:blocks].astype(out_ref.dtype)
    return run_copies(
        [
            (out_ref.at[pl.ds(start, ref.shape[0])], ref)
            for ref, start in row_places(meta_ref, grad_refs, blocks)
        ],
        sems,
    )


def aligned(refs, row, turned):
    parts = [ref[row] for ref in refs]
    if not turned:
        return parts
    size = parts[0].shape[0] // PIECES
    return [
        jnp.concatenate(
            [part[(piece ^ away) * size:((piece ^ away) + 1) * size] for piece in range(PIECES)]
        )
        for away, part in enumerate(parts)
    ]


def table_jobs(meta_ref, table_refs, table_ref):
    core = meta_ref[1] % 2
    jobs = [(table_refs[0], table_ref.at[pl.ds(0, table_refs[0].shape[0])])]
    if len(table_refs) > 1:
        half = table_refs[1].shape[0]
        jobs.append((table_refs[1], table_ref.at[pl.ds((2 + core) * half, half)]))
        jobs.append((table_refs[2], table_ref.at[pl.ds((3 - core) * half, half)]))
    return jobs


def transposed_logits(tile, rows):
    return logit_scale * lax.dot_general(
        tile, rows, (((1,), (1,)), ((), ())), preferred_element_type=jnp.float32
    )


def decode(code):
    return code // (2 * FIELD), (code // 2) % FIELD, (code % 2) == 1


def score_kernel(n_rows, n_tables, blocks, tiles, codes_ref, meta_ref, hit_ref, *refs):
    row_refs, refs = refs[:n_rows], refs[n_rows:]
    table_refs, refs = refs[:n_tables], refs[n_tables:]
    stats_ref, rows_ref, table_ref, lse_ref, pos_ref, sems = refs
    row_copies = run_copies(row_jobs(meta_ref, row_refs, rows_ref), sems)
    table_copies = run_copies(table_jobs(meta_ref, table_refs, table_ref), sems, PIECES)
    lse_ref[...] = jnp.full(lse_ref.shape, unused_logit, jnp.float32)
    pos_ref[...] = jnp.zeros(pos_ref.shape, jnp.float32)
    class_at = lax.broadcasted_iota(jnp.int32, (TILE, BR), 0)
    for copy in row_copies:
        copy.wait()

    def normalise(block, carry):
        exact = rows_ref[block].astype(jnp.float32)
        norm = lax.rsqrt(jnp.sum(exact * exact, axis=1, keepdims=True) + epsilon)
        rows_ref[block] = (exact * norm).astype(jnp.bfloat16)
        return carry

    lax.fori_loop(0, blocks, normalise, 0)
    for copy in table_copies:
        copy.wait()

    def step(index, carry):
        held = []
        for lane in range(PAIRS_PER_STEP):
            block, tile, first = decode(codes_ref[index * PAIRS_PER_STEP + lane])
            source = jnp.minimum(block, blocks - 1)
            logits = transposed_logits(
                table_ref[jnp.minimum(tile, tiles - 1)], rows_ref[source]
            )
            peak = jnp.max(logits, axis=0, keepdims=True)
            total = jnp.sum(jnp.exp(logits - peak), axis=0, keepdims=True)
            hit = class_at == hit_ref[pl.ds(source, 1), :]
            positive = jnp.sum(jnp.where(hit, logits, 0.0), axis=0, keepdims=True)
            held.append((block, peak + jnp.log(total), jnp.where(first, positive, 0.0)))
        for block, lse, positive in held:
            before = lse_ref[pl.ds(block, 1), :]
            top = jnp.maximum(before, lse)
            lse_ref[pl.ds(block, 1), :] = top + jnp.log(
                jnp.exp(before - top) + jnp.exp(lse - top)
            )
            pos_ref[pl.ds(block, 1), :] += positive
        return carry

    lax.fori_loop(0, pl.cdiv(meta_ref[0], PAIRS_PER_STEP), step, 0)
    stats_ref[0] = lse_ref[:blocks, :]
    stats_ref[1] = pos_ref[:blocks, :]


def make_totals(stat_refs, turned, total_ref, loss_ref):
    lse = aligned(stat_refs, 0, turned)
    top = functools.reduce(jnp.maximum, lse)
    total = top + jnp.log(sum(jnp.exp(part - top) for part in lse))
    total_ref[...] = total
    loss_ref[...] = total - sum(aligned(stat_refs, 1, turned))


def pair_score(code, blocks, tiles, rows_ref, table_ref, hit_ref, total_ref, class_at):
    block, tile, first = decode(code)
    source = jnp.minimum(block, blocks - 1)
    table_at = jnp.minimum(tile, tiles - 1)
    logits = transposed_logits(table_ref[table_at], rows_ref[source])
    share = jnp.exp(logits - total_ref[pl.ds(source, 1), :])
    wanted = jnp.where(first, hit_ref[pl.ds(source, 1), :], -1)
    hit = (class_at == wanted).astype(jnp.float32)
    return (logit_scale * (share - hit)).astype(jnp.bfloat16)


def row_terms(score, tile):
    return lax.dot_general(
        score, tile, (((0,), (0,)), ((), ())), preferred_element_type=jnp.float32
    )


def grad_kernel(
    n_grads, n_tables, n_stats, turned, blocks, tiles, codes_ref, meta_ref, hit_ref, *refs
):
    stat_refs, refs = refs[:n_stats], refs[n_stats:]
    unit_ref, refs = refs[0], refs[1:]
    table_refs, refs = refs[:n_tables], refs[n_tables:]
    grad_refs, refs = refs[:n_grads], refs[n_grads:]
    scores_ref, loss_ref, rows_ref, table_ref, total_ref, rows_acc, out_ref, sems = refs
    copies = run_copies(
        [(unit_ref, rows_ref)] + table_jobs(meta_ref, table_refs, table_ref), sems, PIECES
    )
    rows_acc[...] = jnp.zeros(rows_acc.shape, jnp.float32)
    make_totals(stat_refs, turned, total_ref, loss_ref)
    class_at = lax.broadcasted_iota(jnp.int32, (TILE, BR), 0)
    for copy in copies:
        copy.wait()

    def step(index, carry):
        held = []
        for lane in range(PAIRS_PER_STEP):
            pair = index * PAIRS_PER_STEP + lane
            score = pair_score(
                codes_ref[pair], blocks, tiles, rows_ref, table_ref, hit_ref, total_ref, class_at
            )
            scores_ref[pair] = score
            held.append(score)
        for lane, score in enumerate(held):
            block, tile, _ = decode(codes_ref[index * PAIRS_PER_STEP + lane])
            rows_acc[block] += row_terms(score, table_ref[jnp.minimum(tile, tiles - 1)])
        return carry

    lax.fori_loop(0, pl.cdiv(meta_ref[0], PAIRS_PER_STEP), step, 0)
    for copy in store_rows(meta_ref, rows_acc, out_ref, grad_refs, sems):
        copy.wait()


def last_kernel(sizes, n_grads, n_tables, n_stats, turned, n_shares, tiles, *refs):
    chunks, blocks = len(sizes), sizes[-1]
    codes_refs, refs = refs[:chunks], refs[chunks:]
    meta_refs, refs = refs[:chunks], refs[chunks:]
    hit_ref, refs = refs[0], refs[1:]
    stat_refs, refs = refs[:n_stats], refs[n_stats:]
    scores_refs, refs = refs[:chunks - 1], refs[chunks - 1:]
    unit_refs, refs = refs[:chunks], refs[chunks:]
    table_refs, refs = refs[:n_tables], refs[n_tables:]
    grad_refs, refs = refs[:n_grads], refs[n_grads:]
    share_refs, refs = refs[:n_shares], refs[n_shares:]
    loss_ref, refs = refs[0], refs[1:]
    rows_ref, early_ref, held_ref, table_ref, total_ref, rows_acc, out_ref, *refs = refs
    tiles_acc, sems, early_sems, row_sems = refs
    codes_ref, meta_ref = codes_refs[-1], meta_refs[-1]
    copies = run_copies(
        [(unit_refs[-1], rows_ref)] + table_jobs(meta_ref, table_refs, table_ref), sems
    )


    def fetch(chunk):
        early = early_ref.at[pl.ds(0, sizes[chunk])]
        return run_copies(
            [(unit_refs[chunk], early), (scores_refs[chunk], held_ref)], early_sems
        )

    early = fetch(0) if chunks > 1 else []
    rows_acc[...] = jnp.zeros(rows_acc.shape, jnp.float32)
    tiles_acc[...] = jnp.zeros(tiles_acc.shape, jnp.float32)
    make_totals(stat_refs, turned, total_ref, loss_ref)
    class_at = lax.broadcasted_iota(jnp.int32, (TILE, BR), 0)
    for copy in copies:
        copy.wait()

    def step(index, carry):
        held = [
            pair_score(
                codes_ref[index * PAIRS_PER_STEP + lane], blocks, tiles, rows_ref, table_ref,
                hit_ref, total_ref, class_at,
            )
            for lane in range(PAIRS_PER_STEP)
        ]
        for lane, score in enumerate(held):
            block, tile, _ = decode(codes_ref[index * PAIRS_PER_STEP + lane])
            rows_acc[block] += row_terms(score, table_ref[jnp.minimum(tile, tiles - 1)])
            tiles_acc[tile] += jnp.dot(
                score, rows_ref[jnp.minimum(block, blocks - 1)],
                preferred_element_type=jnp.float32,
            )
        return carry

    lax.fori_loop(0, pl.cdiv(meta_ref[0], PAIRS_PER_STEP), step, 0)
    stored = store_rows(meta_ref, rows_acc, out_ref, grad_refs, row_sems)
    for chunk in range(chunks - 1):
        for copy in early if chunk == 0 else fetch(chunk):
            copy.wait()

        def early_step(index, carry, chunk=chunk):
            for lane in range(PAIRS_PER_STEP):
                pair = index * PAIRS_PER_STEP + lane
                block, tile, _ = decode(codes_refs[chunk][pair])
                tiles_acc[tile] += jnp.dot(
                    held_ref[pair],
                    early_ref[jnp.minimum(block, sizes[chunk] - 1)],
                    preferred_element_type=jnp.float32,
                )
            return carry

        lax.fori_loop(0, pl.cdiv(meta_refs[chunk][0], PAIRS_PER_STEP), early_step, 0)
    if n_shares == 1:
        share_refs[0][...] = tiles_acc[:tiles].astype(jnp.bfloat16)
    else:
        part = meta_ref[1]
        shard, width = share_refs[0].shape[2], share_refs[0].shape[-1]
        for core, ref in enumerate(share_refs):
            for y in range(ref.shape[1]):
                start = pl.multiple_of(((2 * y + core) ^ part) * width, width)
                for x in range(ref.shape[0]):
                    ref[x, y] = tiles_acc[
                        pl.ds(x * shard, shard), :, pl.ds(start, width)
                    ].astype(jnp.bfloat16)
    for copy in stored:
        copy.wait()


def kernel_cost(blocks):
    return pl.CostEstimate(flops=blocks * BR * D, bytes_accessed=blocks * BR * D, transcendentals=0)


def limit(*scratch):
    total = 0
    for shape, dtype in scratch:
        total += int(np.prod(shape)) * jnp.dtype(dtype).itemsize
    return pltpu.CompilerParams(vmem_limit_bytes=min(VMEM_BYTES, total + SPARE_BYTES))


def rows_of(blocks):
    return (blocks, BR, D), jnp.bfloat16


def score(blocks, codes, meta, hit, rows, tables):
    tiles = sum(table.shape[0] for table in tables)
    table_room = ((tiles, TILE, D), jnp.bfloat16)
    return pl.pallas_call(
        functools.partial(score_kernel, len(rows), len(tables), blocks, tiles),
        out_shape=(
            jax.ShapeDtypeStruct((2, blocks, BR), jnp.float32),
            jax.ShapeDtypeStruct(*rows_of(blocks)),
        ),
        in_specs=[SMEM, SMEM, VMEM] + [ANY] * (len(rows) + len(tables)),
        out_specs=(VMEM, VMEM),
        scratch_shapes=[
            pltpu.VMEM(*table_room),
            pltpu.VMEM((blocks + 8, BR), jnp.float32),
            pltpu.VMEM((blocks + 8, BR), jnp.float32),
            pltpu.SemaphoreType.DMA((PIECES + len(tables),)),
        ],
        cost_estimate=kernel_cost(blocks),
        compiler_params=limit(rows_of(blocks), table_room),
    )(codes, meta, hit, *rows, *tables)


def grads(blocks, codes, meta, hit, stats, turned, unit, tables, shapes):
    tiles = sum(table.shape[0] for table in tables)
    table_room = ((tiles, TILE, D), jnp.bfloat16)
    acc_room = ((blocks + 1, BR, D), jnp.float32)
    scores = ((codes.shape[0], TILE, BR), jnp.bfloat16)
    outs = pl.pallas_call(
        functools.partial(
            grad_kernel, len(shapes), len(tables), len(stats), turned, blocks, tiles
        ),
        out_shape=(
            *(jax.ShapeDtypeStruct(shape, jnp.bfloat16) for shape in shapes),
            jax.ShapeDtypeStruct(*scores),
            jax.ShapeDtypeStruct((blocks, BR), jnp.float32),
        ),
        in_specs=[SMEM, SMEM] + [VMEM] * (1 + len(stats)) + [ANY] * (1 + len(tables)),
        out_specs=(*[ANY] * len(shapes), VMEM, VMEM),
        scratch_shapes=[
            pltpu.VMEM(*rows_of(blocks)),
            pltpu.VMEM(*table_room),
            pltpu.VMEM((blocks, BR), jnp.float32),
            pltpu.VMEM(*acc_room),
            pltpu.VMEM(*rows_of(blocks)),
            pltpu.SemaphoreType.DMA((PIECES + 1 + len(tables),)),
        ],
        cost_estimate=kernel_cost(blocks),
        compiler_params=limit(rows_of(2 * blocks), table_room, acc_room, scores),
    )(codes, meta, hit, *stats, unit, *tables)
    return list(outs[:len(shapes)]), outs[len(shapes)], outs[-1]


def last_grads(codes, metas, hit, stats, turned, scores, units, tables, shapes, share_shapes):
    sizes = [unit.shape[0] for unit in units]
    tiles = sum(table.shape[0] for table in tables)
    chunks, blocks = len(sizes), sizes[-1]
    n_inputs = 2 * chunks - 1 + len(tables)
    table_room = ((tiles, TILE, D), jnp.bfloat16)
    acc_room = ((blocks + 1, BR, D), jnp.float32)
    tiles_room = ((tiles + 1, TILE, D), jnp.float32)
    early_room = rows_of(max(sizes[:-1], default=PIECES))
    kept = ((scores or codes)[0].shape[0], TILE, BR), jnp.bfloat16
    outs = pl.pallas_call(
        functools.partial(
            last_kernel, sizes, len(shapes), len(tables), len(stats), turned,
            len(share_shapes), tiles,
        ),
        out_shape=(
            *(jax.ShapeDtypeStruct(shape, jnp.bfloat16) for shape in shapes),
            *(jax.ShapeDtypeStruct(shape, jnp.bfloat16) for shape in share_shapes),
            jax.ShapeDtypeStruct((blocks, BR), jnp.float32),
        ),
        in_specs=[SMEM] * (2 * chunks) + [VMEM] * (1 + len(stats)) + [ANY] * n_inputs,
        out_specs=(*[ANY] * len(shapes), *[VMEM] * len(share_shapes), VMEM),
        scratch_shapes=[
            pltpu.VMEM(*rows_of(blocks)),
            pltpu.VMEM(*early_room),
            pltpu.VMEM(*kept),
            pltpu.VMEM(*table_room),
            pltpu.VMEM((blocks, BR), jnp.float32),
            pltpu.VMEM(*acc_room),
            pltpu.VMEM(*rows_of(blocks)),
            pltpu.VMEM(*tiles_room),
            pltpu.SemaphoreType.DMA((1 + len(tables),)),
            pltpu.SemaphoreType.DMA((2,)),
            pltpu.SemaphoreType.DMA((PIECES,)),
        ],
        cost_estimate=kernel_cost(sum(sizes)),
        compiler_params=limit(
            rows_of(2 * blocks), early_room, kept, table_room, table_room, acc_room, tiles_room
        ),
    )(*codes, *metas, hit, *stats, *scores, *units, *tables)
    cut = len(shapes)
    return list(outs[:cut]), list(outs[cut:-1]), outs[-1]


def add(first, second):
    return (first.astype(jnp.float32) + second.astype(jnp.float32)).astype(jnp.bfloat16)


class Neighbours:
    def __init__(self, nx, dp):
        self.nx, self.nz, self.dp, self.turned = nx, PIECES, dp, True

    def over_z(self, value, away):
        pairs = [
            (z * self.nx + x, (z ^ away) * self.nx + x)
            for z in range(self.nz) for x in range(self.nx)
        ]
        return lax.ppermute(value, "cls", pairs)

    def over_x(self, value):
        return lax.ppermute(value, "cls", [(c, c ^ 1) for c in range(self.nx * self.nz)])

    def over_y(self, value):
        return lax.ppermute(value, "dp", [(d, d ^ 2) for d in range(self.dp)])

    def over_core(self, value):
        return lax.ppermute(value, "dp", [(d, d ^ 1) for d in range(self.dp)])

    def all_over_z(self, value):
        return [value] + [self.over_z(value, away) for away in range(1, self.nz)]

    def gather(self, needed, chunks, lists, table, core, prepare):
        def moves(first, lists, table, core):
            half = table.shape[0] // 2
            sent = lax.dynamic_slice_in_dim(table, core * half, half, axis=0)
            from_x = self.over_x(sent)
            far, near = lax.optimization_barrier((self.over_z(first, 2), self.over_z(first, 1)))
            return (near, far, self.over_z(far, 1)), from_x, prepare(
                jnp.stack(self.all_over_z(lists))
            )

        first, second = chunks
        pieces, from_x, prepared = self.together(needed, moves, first, lists, table, core)
        return [[first, *pieces], [second]], [table, from_x], prepared

    def all_tables(self, tables):
        return [*tables, self.over_core(tables[-1])]

    def rest_of_rows(self, pieces, others):
        second, = pieces
        far, near, others = lax.optimization_barrier(
            (self.over_z(second, 2), self.over_z(second, 1), others)
        )
        return (near, far, self.over_z(far, 1)), others

    def whole_rows(self, pieces, rest):
        return [*pieces, *rest]

    def grad_shapes(self, size):
        return [(size, BR, D)] * PIECES

    def gather_stats(self, stats):
        return self.all_over_z(stats)

    def order(self, place):
        return place

    def own(self, loss, place, size):
        return loss[:size]

    def early_return(self, early, others):
        parts, = early
        near, passed = self.over_z(parts[1], 1), self.over_z(parts[3], 1)
        passed, others = lax.optimization_barrier((passed, others))
        return (near, self.over_z(add(passed, parts[2]), 2)), others

    def early_sums(self, early, returned):
        return [sum(part.astype(jnp.float32) for part in (early[0], *returned))]

    def together(self, needed, work, *operands):
        def no_work(*operands):
            return jax.tree.map(
                lambda out: jnp.zeros(out.shape, out.dtype), jax.eval_shape(work, *operands)
            )

        return lax.cond(needed, work, no_work, *operands)

    def sum_last(self, parts, shares):
        kept, sent = shares
        passed, got = self.over_z(parts[3], 1), self.over_core(sent)
        half = kept.shape[2] // 2
        x_sent = add(kept[1, :, :half], got[1, :, :half])
        y_sent = add(kept[:, 1, half:], got[:, 1, half:])
        passed, near, _, _ = lax.optimization_barrier((passed, parts[1], x_sent, y_sent))
        near = self.over_z(near, 1)
        far = self.over_z(add(passed, parts[2]), 2)
        near, far, shares = self.sum_shares(near, far, kept, got, x_sent, y_sent)
        return sum(part.astype(jnp.float32) for part in (parts[0], near, far)), shares

    def share_shapes(self, shard_tiles):
        return [(self.nx, self.dp // 2, shard_tiles, TILE, D // self.dp)] * 2

    def sum_shares(self, near, far, kept, got, x_sent, y_sent):
        half = kept.shape[2] // 2
        x_got, y_got = lax.optimization_barrier((self.over_x(x_sent), self.over_y(y_sent)))
        x_kept = [add(add(kept[0, y, :half], got[0, y, :half]), x_got[y]) for y in range(2)]
        y_kept = [add(add(kept[x, 0, half:], got[x, 0, half:]), y_got[x]) for x in range(2)]
        low, high = self.over_y(x_kept[1]), self.over_x(y_kept[1])
        near, far, _, _ = lax.optimization_barrier((near, far, low, high))
        low = x_kept[0].astype(jnp.float32) + low.astype(jnp.float32)
        high = y_kept[0].astype(jnp.float32) + high.astype(jnp.float32)
        return near, far, jnp.concatenate([low, high], axis=0)


class Groups:
    def __init__(self, nz, dp):
        self.nx, self.nz, self.dp, self.turned = 1, nz, dp, False

    def gather(self, needed, chunks, lists, table, core, prepare):
        gathered = [[lax.all_gather(rows, "cls", tiled=True)] for rows in chunks]
        return gathered, [table], prepare(lax.all_gather(lists, "cls"))

    def all_tables(self, tables):
        return tables

    def rest_of_rows(self, pieces, others):
        return (), others

    def whole_rows(self, pieces, rest):
        return pieces

    def grad_shapes(self, size):
        return [(self.nz * size, BR, D)]

    def gather_stats(self, stats):
        return list(lax.all_gather(stats, "cls"))

    def order(self, place):
        return jnp.zeros_like(place)

    def own(self, loss, place, size):
        return lax.dynamic_slice_in_dim(loss, place * size, size, axis=0)

    def total(self, part):
        return lax.psum_scatter(
            part, "cls", scatter_dimension=0, tiled=True
        ).astype(jnp.float32)

    def early_return(self, early, others):
        return [self.total(part) for part, in early], others

    def early_sums(self, early, returned):
        return returned

    def together(self, needed, work, *operands):
        return work(*operands)

    def sum_last(self, parts, shares):
        return self.total(parts[0]), self.sum_shares(shares)

    def share_shapes(self, shard_tiles):
        return [(shard_tiles, TILE, D)]

    def sum_shares(self, shares):
        return lax.psum_scatter(
            shares[0], "dp", scatter_dimension=2, tiled=True
        ).astype(jnp.float32)


def pair_codes(lists, shard_tiles, nx, place, column, room):
    entry = lists[:, :K].reshape(-1)
    owner = entry // shard_tiles
    mine = (entry >= 0) & (owner // nx == place)
    local = jnp.where(owner % nx == column, 0, shard_tiles) + entry % shard_tiles
    counter = jnp.arange(entry.shape[0], dtype=jnp.int32)
    code = ((counter // K) * FIELD + local) * 2 + (counter % K == 0)
    rank = jnp.sum(
        jnp.where(mine[None, :] & (counter[None, :] < counter[:, None]), 1, 0), axis=1
    ).astype(jnp.int32)
    slots = jnp.arange(room, dtype=jnp.int32)
    chosen = mine[None, :] & (rank[None, :] == slots[:, None])
    padding = (lists.shape[0] * FIELD + nx * shard_tiles) * 2
    codes = padding + jnp.sum(jnp.where(chosen, code[None, :] - padding, 0), axis=1)
    return codes.astype(jnp.int32), jnp.sum(mine.astype(jnp.int32))


def per_device(moves, sizes, embeddings, proxies, hard_tiles, tile_count, labels):
    nx, nz, dp = moves.nx, moves.nz, moves.dp
    blocks = hard_tiles.shape[0]
    shard_tiles = proxies.shape[0] // TILE
    me, part = lax.axis_index("cls"), lax.axis_index("dp")
    place, column = me // nx, me % nx

    row_blocks = embeddings.reshape(blocks, BR, D)

    position = labels.reshape(blocks, BR) - hard_tiles[:, 0:1] * TILE
    entries = jnp.arange(K, dtype=jnp.int32)
    used = jnp.where(entries[None, :] < tile_count[:, None], hard_tiles, -1)
    starts = [sum(sizes[:chunk]) for chunk in range(len(sizes))]
    spots = [slice(start, start + size) for start, size in zip(starts, sizes)]
    held = [nz * size for size in sizes]
    last = len(sizes) - 1
    needed = tile_count[0] > 0

    def prepare(lists):
        prepared = []
        for spot, blocks_held in zip(spots, held):
            room = min(blocks_held * K, nz * (blocks * K // (nx * nz)) * nx)
            room = -(-room // PAIRS_PER_STEP) * PAIRS_PER_STEP
            chunk_lists = lists[:, spot].reshape(blocks_held, K + BR)
            code, count = pair_codes(chunk_lists, shard_tiles, nx, place, column, room)
            meta = jnp.stack([count, part, moves.order(place)]).astype(jnp.int32)
            prepared.append((code, meta, chunk_lists[:, K:]))
        return prepared

    gathered, tables, prepared = moves.gather(
        needed,
        [row_blocks[spot] for spot in spots],
        jnp.concatenate([used, position], axis=1),
        proxies.reshape(shard_tiles, TILE, D),
        part % 2,
        prepare,
    )

    def scored(chunk, rows, tables, prepared):
        parts, unit = score(held[chunk], *prepared[chunk], rows, tables)
        return moves.gather_stats(parts), unit

    def early_work(gathered, own_tables, prepared):
        units, made, rest = [], [], ()
        tables = moves.all_tables(own_tables)
        for chunk in range(last):
            stats, unit = scored(chunk, gathered[chunk], tables, prepared)
            if chunk == 0:
                rest, stats = moves.rest_of_rows(gathered[-1], stats)
            units.append(unit)
            made.append(grads(
                held[chunk], *prepared[chunk], stats, moves.turned, unit, tables,
                moves.grad_shapes(sizes[chunk]),
            ))
        return rest, tables[len(own_tables):], units, made

    def last_work(rows, tables, prepared, units, scores, early):
        codes, metas, hits = zip(*prepared)
        stats, unit = scored(last, rows, tables, prepared)
        returned, stats = moves.early_return(early, stats)
        return returned, last_grads(
            codes, metas, hits[-1], stats, moves.turned, scores, units + [unit], tables,
            moves.grad_shapes(sizes[-1]), moves.share_shapes(shard_tiles),
        )

    def work(gathered, tables, prepared):
        rest, more, units, made = early_work(gathered, tables, prepared)
        early, scores, losses = zip(*made)
        returned, (parts, shares, loss) = last_work(
            moves.whole_rows(gathered[-1], rest), [*tables, *more], prepared, units,
            list(scores), early,
        )
        return [part[0] for part in early], returned, parts, shares, [*losses, loss]

    early, returned, parts, shares, losses = moves.together(
        needed, work, gathered, tables, prepared
    )
    total, shares = moves.sum_last(parts, shares)
    row_grads = moves.early_sums(early, returned) + [total]
    losses = [
        moves.own(part, place, size) for part, size in zip(losses, sizes)
    ]

    embeddings, losses = lax.optimization_barrier((embeddings, losses))
    emb_exact = embeddings.astype(jnp.float32)
    inverse_norm = lax.rsqrt(jnp.sum(emb_exact * emb_exact, axis=1, keepdims=True) + epsilon)
    unit_exact = emb_exact * inverse_norm
    proxy_grad = shares.reshape(shard_tiles * TILE, D // dp)
    row_loss = jnp.concatenate(losses, axis=0).reshape(-1)
    embed_grad = []
    for spot, grad_rows in zip(spots, row_grads):
        span = slice(spot.start * BR, spot.stop * BR)
        exact, norm = unit_exact[span], inverse_norm[span]
        grad_rows = grad_rows.reshape(-1, D)
        radial = jnp.sum(exact * grad_rows, axis=1, keepdims=True)
        embed_grad.append(((grad_rows - exact * radial) * norm).astype(jnp.bfloat16))
    embed_grad = jnp.concatenate(embed_grad, axis=0)
    return (row_loss, embed_grad, proxy_grad)


def solution(mesh):
    placed = (
        P(("dp", "cls"), None),
        P("cls", None),
        P(("dp", "cls"), None),
        P(("dp", "cls")),
        P(("dp", "cls")),
    )
    dp, groups = mesh.shape["dp"], mesh.shape["cls"]
    if (dp, groups) == (4, 2 * PIECES):
        moves, sizes = Neighbours(2, dp), [4, 4]
    else:
        chunks = max(1, groups // 8)
        moves, sizes = Groups(groups, dp), [8 // chunks] * chunks
    return jax.shard_map(
        functools.partial(per_device, moves, sizes),
        mesh=mesh,
        in_specs=placed,
        out_specs=(P(("dp", "cls")), P(("dp", "cls"), None), P("cls", "dp")),
        check_vma=False,
    )
```

```python
import functools

import jax
import jax.numpy as jnp
import numpy as np
from jax import lax
from jax.experimental import pallas as pl
from jax.experimental.pallas import tpu as pltpu
from jax.sharding import PartitionSpec as P

D = 512
TILE = 128
BR = 128
K = 8
PAIRS_PER_STEP = 4
FIELD = 128
PIECES = 4
VMEM_BYTES = 60 * 1024 * 1024
SPARE_BYTES = 4 * 1024 * 1024

logit_scale = 4.0
epsilon = 1e-06
unused_logit = -1e30

SMEM = pl.BlockSpec(memory_space=pltpu.SMEM)
VMEM = pl.BlockSpec(memory_space=pltpu.VMEM)
ANY = pl.BlockSpec(memory_space=pl.ANY)


def run_copies(jobs, sems, first=0):
    copies = [
        pltpu.make_async_copy(source, target, sems.at[first + index])
        for index, (source, target) in enumerate(jobs)
    ]
    for copy in copies:
        copy.start()
    return copies


def row_places(meta_ref, refs, blocks):
    size = blocks // PIECES
    if len(refs) > 1:
        return [(ref, piece * size) for piece, ref in enumerate(refs)]
    return [
        (refs[0].at[pl.ds(place * size, size)], (meta_ref[2] ^ place) * size)
        for place in range(PIECES)
    ]


def row_jobs(meta_ref, refs, rows_ref):
    return [
        (ref, rows_ref.at[pl.ds(start, ref.shape[0])])
        for ref, start in row_places(meta_ref, refs, rows_ref.shape[0])
    ]


def store_rows(meta_ref, rows_acc, out_ref, grad_refs, sems):
    blocks = out_ref.shape[0]
    out_ref[...] = rows_acc[:blocks].astype(out_ref.dtype)
    return run_copies(
        [
            (out_ref.at[pl.ds(start, ref.shape[0])], ref)
            for ref, start in row_places(meta_ref, grad_refs, blocks)
        ],
        sems,
    )


def aligned(refs, row, turned):
    parts = [ref[row] for ref in refs]
    if not turned:
        return parts
    size = parts[0].shape[0] // PIECES
    return [
        jnp.concatenate(
            [part[(piece ^ away) * size:((piece ^ away) + 1) * size] for piece in range(PIECES)]
        )
        for away, part in enumerate(parts)
    ]


def table_jobs(meta_ref, table_refs, table_ref):
    core = meta_ref[1] % 2
    jobs = [(table_refs[0], table_ref.at[pl.ds(0, table_refs[0].shape[0])])]
    if len(table_refs) > 1:
        half = table_refs[1].shape[0]
        jobs.append((table_refs[1], table_ref.at[pl.ds((2 + core) * half, half)]))
        jobs.append((table_refs[2], table_ref.at[pl.ds((3 - core) * half, half)]))
    return jobs


def transposed_logits(tile, rows):
    return logit_scale * lax.dot_general(
        tile, rows, (((1,), (1,)), ((), ())), preferred_element_type=jnp.float32
    )


def decode(code):
    return code // (2 * FIELD), (code // 2) % FIELD, (code % 2) == 1


def score_kernel(n_rows, n_tables, blocks, tiles, codes_ref, meta_ref, hit_ref, *refs):
    row_refs, refs = refs[:n_rows], refs[n_rows:]
    table_refs, refs = refs[:n_tables], refs[n_tables:]
    stats_ref, rows_ref, table_ref, lse_ref, pos_ref, sems = refs
    row_copies = run_copies(row_jobs(meta_ref, row_refs, rows_ref), sems)
    table_copies = run_copies(table_jobs(meta_ref, table_refs, table_ref), sems, PIECES)
    lse_ref[...] = jnp.full(lse_ref.shape, unused_logit, jnp.float32)
    pos_ref[...] = jnp.zeros(pos_ref.shape, jnp.float32)
    class_at = lax.broadcasted_iota(jnp.int32, (TILE, BR), 0)
    for copy in row_copies:
        copy.wait()

    def normalise(block, carry):
        exact = rows_ref[block].astype(jnp.float32)
        norm = lax.rsqrt(jnp.sum(exact * exact, axis=1, keepdims=True) + epsilon)
        rows_ref[block] = (exact * norm).astype(jnp.bfloat16)
        return carry

    lax.fori_loop(0, blocks, normalise, 0)
    for copy in table_copies:
        copy.wait()

    def step(index, carry):
        held = []
        for lane in range(PAIRS_PER_STEP):
            block, tile, first = decode(codes_ref[index * PAIRS_PER_STEP + lane])
            source = jnp.minimum(block, blocks - 1)
            logits = transposed_logits(
                table_ref[jnp.minimum(tile, tiles - 1)], rows_ref[source]
            )
            peak = jnp.max(logits, axis=0, keepdims=True)
            total = jnp.sum(jnp.exp(logits - peak), axis=0, keepdims=True)
            hit = class_at == hit_ref[pl.ds(source, 1), :]
            positive = jnp.sum(jnp.where(hit, logits, 0.0), axis=0, keepdims=True)
            held.append((block, peak + jnp.log(total), jnp.where(first, positive, 0.0)))
        for block, lse, positive in held:
            before = lse_ref[pl.ds(block, 1), :]
            top = jnp.maximum(before, lse)
            lse_ref[pl.ds(block, 1), :] = top + jnp.log(
                jnp.exp(before - top) + jnp.exp(lse - top)
            )
            pos_ref[pl.ds(block, 1), :] += positive
        return carry

    lax.fori_loop(0, pl.cdiv(meta_ref[0], PAIRS_PER_STEP), step, 0)
    stats_ref[0] = lse_ref[:blocks, :]
    stats_ref[1] = pos_ref[:blocks, :]


def make_totals(stat_refs, turned, total_ref, loss_ref):
    lse = aligned(stat_refs, 0, turned)
    top = functools.reduce(jnp.maximum, lse)
    total = top + jnp.log(sum(jnp.exp(part - top) for part in lse))
    total_ref[...] = total
    loss_ref[...] = total - sum(aligned(stat_refs, 1, turned))


def pair_score(code, blocks, tiles, rows_ref, table_ref, hit_ref, total_ref, class_at):
    block, tile, first = decode(code)
    source = jnp.minimum(block, blocks - 1)
    table_at = jnp.minimum(tile, tiles - 1)
    logits = transposed_logits(table_ref[table_at], rows_ref[source])
    share = jnp.exp(logits - total_ref[pl.ds(source, 1), :])
    wanted = jnp.where(first, hit_ref[pl.ds(source, 1), :], -1)
    hit = (class_at == wanted).astype(jnp.float32)
    return (logit_scale * (share - hit)).astype(jnp.bfloat16)


def row_terms(score, tile):
    return lax.dot_general(
        score, tile, (((0,), (0,)), ((), ())), preferred_element_type=jnp.float32
    )


def grad_kernel(
    n_grads, n_tables, n_stats, turned, blocks, tiles, codes_ref, meta_ref, hit_ref, *refs
):
    stat_refs, refs = refs[:n_stats], refs[n_stats:]
    unit_ref, refs = refs[0], refs[1:]
    table_refs, refs = refs[:n_tables], refs[n_tables:]
    grad_refs, refs = refs[:n_grads], refs[n_grads:]
    scores_ref, loss_ref, rows_ref, table_ref, total_ref, rows_acc, out_ref, sems = refs
    copies = run_copies(
        [(unit_ref, rows_ref)] + table_jobs(meta_ref, table_refs, table_ref), sems, PIECES
    )
    rows_acc[...] = jnp.zeros(rows_acc.shape, jnp.float32)
    make_totals(stat_refs, turned, total_ref, loss_ref)
    class_at = lax.broadcasted_iota(jnp.int32, (TILE, BR), 0)
    for copy in copies:
        copy.wait()

    def step(index, carry):
        held = []
        for lane in range(PAIRS_PER_STEP):
            pair = index * PAIRS_PER_STEP + lane
            score = pair_score(
                codes_ref[pair], blocks, tiles, rows_ref, table_ref, hit_ref, total_ref, class_at
            )
            scores_ref[pair] = score
            held.append(score)
        for lane, score in enumerate(held):
            block, tile, _ = decode(codes_ref[index * PAIRS_PER_STEP + lane])
            rows_acc[block] += row_terms(score, table_ref[jnp.minimum(tile, tiles - 1)])
        return carry

    lax.fori_loop(0, pl.cdiv(meta_ref[0], PAIRS_PER_STEP), step, 0)
    for copy in store_rows(meta_ref, rows_acc, out_ref, grad_refs, sems):
        copy.wait()


def last_kernel(sizes, n_grads, n_tables, n_stats, turned, n_shares, tiles, *refs):
    chunks, blocks = len(sizes), sizes[-1]
    codes_refs, refs = refs[:chunks], refs[chunks:]
    meta_refs, refs = refs[:chunks], refs[chunks:]
    hit_ref, refs = refs[0], refs[1:]
    stat_refs, refs = refs[:n_stats], refs[n_stats:]
    scores_refs, refs = refs[:chunks - 1], refs[chunks - 1:]
    unit_refs, refs = refs[:chunks], refs[chunks:]
    table_refs, refs = refs[:n_tables], refs[n_tables:]
    grad_refs, refs = refs[:n_grads], refs[n_grads:]
    share_refs, refs = refs[:n_shares], refs[n_shares:]
    loss_ref, refs = refs[0], refs[1:]
    rows_ref, early_ref, held_ref, table_ref, total_ref, rows_acc, out_ref, *refs = refs
    tiles_acc, sems, early_sems, row_sems = refs
    codes_ref, meta_ref = codes_refs[-1], meta_refs[-1]
    copies = run_copies(
        [(unit_refs[-1], rows_ref)] + table_jobs(meta_ref, table_refs, table_ref), sems
    )


    def fetch(chunk):
        early = early_ref.at[pl.ds(0, sizes[chunk])]
        return run_copies(
            [(unit_refs[chunk], early), (scores_refs[chunk], held_ref)], early_sems
        )

    early = fetch(0) if chunks > 1 else []
    rows_acc[...] = jnp.zeros(rows_acc.shape, jnp.float32)
    tiles_acc[...] = jnp.zeros(tiles_acc.shape, jnp.float32)
    make_totals(stat_refs, turned, total_ref, loss_ref)
    class_at = lax.broadcasted_iota(jnp.int32, (TILE, BR), 0)
    for copy in copies:
        copy.wait()

    def step(index, carry):
        held = [
            pair_score(
                codes_ref[index * PAIRS_PER_STEP + lane], blocks, tiles, rows_ref, table_ref,
                hit_ref, total_ref, class_at,
            )
            for lane in range(PAIRS_PER_STEP)
        ]
        for lane, score in enumerate(held):
            block, tile, _ = decode(codes_ref[index * PAIRS_PER_STEP + lane])
            rows_acc[block] += row_terms(score, table_ref[jnp.minimum(tile, tiles - 1)])
            tiles_acc[tile] += jnp.dot(
                score, rows_ref[jnp.minimum(block, blocks - 1)],
                preferred_element_type=jnp.float32,
            )
        return carry

    lax.fori_loop(0, pl.cdiv(meta_ref[0], PAIRS_PER_STEP), step, 0)
    stored = store_rows(meta_ref, rows_acc, out_ref, grad_refs, row_sems)
    for chunk in range(chunks - 1):
        for copy in early if chunk == 0 else fetch(chunk):
            copy.wait()

        def early_step(index, carry, chunk=chunk):
            for lane in range(PAIRS_PER_STEP):
                pair = index * PAIRS_PER_STEP + lane
                block, tile, _ = decode(codes_refs[chunk][pair])
                tiles_acc[tile] += jnp.dot(
                    held_ref[pair],
                    early_ref[jnp.minimum(block, sizes[chunk] - 1)],
                    preferred_element_type=jnp.float32,
                )
            return carry

        lax.fori_loop(0, pl.cdiv(meta_refs[chunk][0], PAIRS_PER_STEP), early_step, 0)
    if n_shares == 1:
        share_refs[0][...] = tiles_acc[:tiles].astype(jnp.bfloat16)
    else:
        part = meta_ref[1]
        shard, width = share_refs[0].shape[2], share_refs[0].shape[-1]
        for core, ref in enumerate(share_refs):
            for y in range(ref.shape[1]):
                start = pl.multiple_of(((2 * y + core) ^ part) * width, width)
                for x in range(ref.shape[0]):
                    ref[x, y] = tiles_acc[
                        pl.ds(x * shard, shard), :, pl.ds(start, width)
                    ].astype(jnp.bfloat16)
    for copy in stored:
        copy.wait()


def kernel_cost(blocks):
    return pl.CostEstimate(flops=blocks * BR * D, bytes_accessed=blocks * BR * D, transcendentals=0)


def limit(*scratch):
    total = 0
    for shape, dtype in scratch:
        total += int(np.prod(shape)) * jnp.dtype(dtype).itemsize
    return pltpu.CompilerParams(vmem_limit_bytes=min(VMEM_BYTES, total + SPARE_BYTES))


def rows_of(blocks):
    return (blocks, BR, D), jnp.bfloat16


def score(blocks, codes, meta, hit, rows, tables):
    tiles = sum(table.shape[0] for table in tables)
    table_room = ((tiles, TILE, D), jnp.bfloat16)
    return pl.pallas_call(
        functools.partial(score_kernel, len(rows), len(tables), blocks, tiles),
        out_shape=(
            jax.ShapeDtypeStruct((2, blocks, BR), jnp.float32),
            jax.ShapeDtypeStruct(*rows_of(blocks)),
        ),
        in_specs=[SMEM, SMEM, VMEM] + [ANY] * (len(rows) + len(tables)),
        out_specs=(VMEM, VMEM),
        scratch_shapes=[
            pltpu.VMEM(*table_room),
            pltpu.VMEM((blocks + 8, BR), jnp.float32),
            pltpu.VMEM((blocks + 8, BR), jnp.float32),
            pltpu.SemaphoreType.DMA((PIECES + len(tables),)),
        ],
        cost_estimate=kernel_cost(blocks),
        compiler_params=limit(rows_of(blocks), table_room),
    )(codes, meta, hit, *rows, *tables)


def grads(blocks, codes, meta, hit, stats, turned, unit, tables, shapes):
    tiles = sum(table.shape[0] for table in tables)
    table_room = ((tiles, TILE, D), jnp.bfloat16)
    acc_room = ((blocks + 1, BR, D), jnp.float32)
    scores = ((codes.shape[0], TILE, BR), jnp.bfloat16)
    outs = pl.pallas_call(
        functools.partial(
            grad_kernel, len(shapes), len(tables), len(stats), turned, blocks, tiles
        ),
        out_shape=(
            *(jax.ShapeDtypeStruct(shape, jnp.bfloat16) for shape in shapes),
            jax.ShapeDtypeStruct(*scores),
            jax.ShapeDtypeStruct((blocks, BR), jnp.float32),
        ),
        in_specs=[SMEM, SMEM] + [VMEM] * (1 + len(stats)) + [ANY] * (1 + len(tables)),
        out_specs=(*[ANY] * len(shapes), VMEM, VMEM),
        scratch_shapes=[
            pltpu.VMEM(*rows_of(blocks)),
            pltpu.VMEM(*table_room),
            pltpu.VMEM((blocks, BR), jnp.float32),
            pltpu.VMEM(*acc_room),
            pltpu.VMEM(*rows_of(blocks)),
            pltpu.SemaphoreType.DMA((PIECES + 1 + len(tables),)),
        ],
        cost_estimate=kernel_cost(blocks),
        compiler_params=limit(rows_of(2 * blocks), table_room, acc_room, scores),
    )(codes, meta, hit, *stats, unit, *tables)
    return list(outs[:len(shapes)]), outs[len(shapes)], outs[-1]


def last_grads(codes, metas, hit, stats, turned, scores, units, tables, shapes, share_shapes):
    sizes = [unit.shape[0] for unit in units]
    tiles = sum(table.shape[0] for table in tables)
    chunks, blocks = len(sizes), sizes[-1]
    n_inputs = 2 * chunks - 1 + len(tables)
    table_room = ((tiles, TILE, D), jnp.bfloat16)
    acc_room = ((blocks + 1, BR, D), jnp.float32)
    tiles_room = ((tiles + 1, TILE, D), jnp.float32)
    early_room = rows_of(max(sizes[:-1], default=PIECES))
    kept = ((scores or codes)[0].shape[0], TILE, BR), jnp.bfloat16
    outs = pl.pallas_call(
        functools.partial(
            last_kernel, sizes, len(shapes), len(tables), len(stats), turned,
            len(share_shapes), tiles,
        ),
        out_shape=(
            *(jax.ShapeDtypeStruct(shape, jnp.bfloat16) for shape in shapes),
            *(jax.ShapeDtypeStruct(shape, jnp.bfloat16) for shape in share_shapes),
            jax.ShapeDtypeStruct((blocks, BR), jnp.float32),
        ),
        in_specs=[SMEM] * (2 * chunks) + [VMEM] * (1 + len(stats)) + [ANY] * n_inputs,
        out_specs=(*[ANY] * len(shapes), *[VMEM] * len(share_shapes), VMEM),
        scratch_shapes=[
            pltpu.VMEM(*rows_of(blocks)),
            pltpu.VMEM(*early_room),
            pltpu.VMEM(*kept),
            pltpu.VMEM(*table_room),
            pltpu.VMEM((blocks, BR), jnp.float32),
            pltpu.VMEM(*acc_room),
            pltpu.VMEM(*rows_of(blocks)),
            pltpu.VMEM(*tiles_room),
            pltpu.SemaphoreType.DMA((1 + len(tables),)),
            pltpu.SemaphoreType.DMA((2,)),
            pltpu.SemaphoreType.DMA((PIECES,)),
        ],
        cost_estimate=kernel_cost(sum(sizes)),
        compiler_params=limit(
            rows_of(2 * blocks), early_room, kept, table_room, table_room, acc_room, tiles_room
        ),
    )(*codes, *metas, hit, *stats, *scores, *units, *tables)
    cut = len(shapes)
    return list(outs[:cut]), list(outs[cut:-1]), outs[-1]


def add(first, second):
    return (first.astype(jnp.float32) + second.astype(jnp.float32)).astype(jnp.bfloat16)


class Neighbours:
    def __init__(self, nx, dp):
        self.nx, self.nz, self.dp, self.turned = nx, PIECES, dp, True

    def over_z(self, value, away):
        pairs = [
            (z * self.nx + x, (z ^ away) * self.nx + x)
            for z in range(self.nz) for x in range(self.nx)
        ]
        return lax.ppermute(value, "cls", pairs)

    def over_x(self, value):
        return lax.ppermute(value, "cls", [(c, c ^ 1) for c in range(self.nx * self.nz)])

    def over_y(self, value):
        return lax.ppermute(value, "dp", [(d, d ^ 2) for d in range(self.dp)])

    def over_core(self, value):
        return lax.ppermute(value, "dp", [(d, d ^ 1) for d in range(self.dp)])

    def all_over_z(self, value):
        return [value] + [self.over_z(value, away) for away in range(1, self.nz)]

    def gather(self, needed, chunks, lists, table, core, prepare):
        def moves(first, lists, table, core):
            half = table.shape[0] // 2
            sent = lax.dynamic_slice_in_dim(table, core * half, half, axis=0)
            from_x = self.over_x(sent)
            far, near = lax.optimization_barrier((self.over_z(first, 2), self.over_z(first, 1)))
            return (near, far, self.over_z(far, 1)), from_x, prepare(
                jnp.stack(self.all_over_z(lists))
            )

        first, second = chunks
        pieces, from_x, prepared = self.together(needed, moves, first, lists, table, core)
        return [[first, *pieces], [second]], [table, from_x], prepared

    def all_tables(self, tables):
        return [*tables, self.over_core(tables[-1])]

    def rest_of_rows(self, pieces, others):
        second, = pieces
        far, near, others = lax.optimization_barrier(
            (self.over_z(second, 2), self.over_z(second, 1), others)
        )
        return (near, far, self.over_z(far, 1)), others

    def whole_rows(self, pieces, rest):
        return [*pieces, *rest]

    def grad_shapes(self, size):
        return [(size, BR, D)] * PIECES

    def gather_stats(self, stats):
        return self.all_over_z(stats)

    def order(self, place):
        return place

    def own(self, loss, place, size):
        return loss[:size]

    def early_return(self, early, others):
        parts, = early
        near, passed = self.over_z(parts[1], 1), self.over_z(parts[3], 1)
        passed, others = lax.optimization_barrier((passed, others))
        return (near, self.over_z(add(passed, parts[2]), 2)), others

    def early_sums(self, early, returned):
        return [sum(part.astype(jnp.float32) for part in (early[0], *returned))]

    def together(self, needed, work, *operands):
        def no_work(*operands):
            return jax.tree.map(
                lambda out: jnp.zeros(out.shape, out.dtype), jax.eval_shape(work, *operands)
            )

        return lax.cond(needed, work, no_work, *operands)

    def sum_last(self, parts, shares, early):
        kept, sent = shares
        passed, got = self.over_z(parts[3], 1), self.over_core(sent)
        half = kept.shape[2] // 2
        x_sent = add(kept[1, :, :half], got[1, :, :half])
        y_sent = add(kept[:, 1, half:], got[:, 1, half:])
        passed, near, early, _, _ = lax.optimization_barrier(
            (passed, parts[1], early, x_sent, y_sent)
        )
        near = self.over_z(near, 1)
        far = self.over_z(add(passed, parts[2]), 2)
        near, far, shares = self.sum_shares(near, far, kept, got, x_sent, y_sent)
        return sum(part.astype(jnp.float32) for part in (parts[0], near, far)), shares, early

    def share_shapes(self, shard_tiles):
        return [(self.nx, self.dp // 2, shard_tiles, TILE, D // self.dp)] * 2

    def sum_shares(self, near, far, kept, got, x_sent, y_sent):
        half = kept.shape[2] // 2
        x_got, y_got = lax.optimization_barrier((self.over_x(x_sent), self.over_y(y_sent)))
        x_kept = [add(add(kept[0, y, :half], got[0, y, :half]), x_got[y]) for y in range(2)]
        y_kept = [add(add(kept[x, 0, half:], got[x, 0, half:]), y_got[x]) for x in range(2)]
        low, high = self.over_y(x_kept[1]), self.over_x(y_kept[1])
        near, far, _, _ = lax.optimization_barrier((near, far, low, high))
        low = x_kept[0].astype(jnp.float32) + low.astype(jnp.float32)
        high = y_kept[0].astype(jnp.float32) + high.astype(jnp.float32)
        return near, far, jnp.concatenate([low, high], axis=0)


class Groups:
    def __init__(self, nz, dp):
        self.nx, self.nz, self.dp, self.turned = 1, nz, dp, False

    def gather(self, needed, chunks, lists, table, core, prepare):
        gathered = [[lax.all_gather(rows, "cls", tiled=True)] for rows in chunks]
        return gathered, [table], prepare(lax.all_gather(lists, "cls"))

    def all_tables(self, tables):
        return tables

    def rest_of_rows(self, pieces, others):
        return (), others

    def whole_rows(self, pieces, rest):
        return pieces

    def grad_shapes(self, size):
        return [(self.nz * size, BR, D)]

    def gather_stats(self, stats):
        return list(lax.all_gather(stats, "cls"))

    def order(self, place):
        return jnp.zeros_like(place)

    def own(self, loss, place, size):
        return lax.dynamic_slice_in_dim(loss, place * size, size, axis=0)

    def total(self, part):
        return lax.psum_scatter(
            part, "cls", scatter_dimension=0, tiled=True
        ).astype(jnp.float32)

    def early_return(self, early, others):
        return [self.total(part) for part, in early], others

    def early_sums(self, early, returned):
        return returned

    def together(self, needed, work, *operands):
        return work(*operands)

    def sum_last(self, parts, shares, early):
        return self.total(parts[0]), self.sum_shares(shares), early

    def share_shapes(self, shard_tiles):
        return [(shard_tiles, TILE, D)]

    def sum_shares(self, shares):
        return lax.psum_scatter(
            shares[0], "dp", scatter_dimension=2, tiled=True
        ).astype(jnp.float32)


def pair_codes(lists, shard_tiles, nx, place, column, room):
    entry = lists[:, :K].reshape(-1)
    owner = entry // shard_tiles
    mine = (entry >= 0) & (owner // nx == place)
    local = jnp.where(owner % nx == column, 0, shard_tiles) + entry % shard_tiles
    counter = jnp.arange(entry.shape[0], dtype=jnp.int32)
    code = ((counter // K) * FIELD + local) * 2 + (counter % K == 0)
    rank = jnp.sum(
        jnp.where(mine[None, :] & (counter[None, :] < counter[:, None]), 1, 0), axis=1
    ).astype(jnp.int32)
    slots = jnp.arange(room, dtype=jnp.int32)
    chosen = mine[None, :] & (rank[None, :] == slots[:, None])
    padding = (lists.shape[0] * FIELD + nx * shard_tiles) * 2
    codes = padding + jnp.sum(jnp.where(chosen, code[None, :] - padding, 0), axis=1)
    return codes.astype(jnp.int32), jnp.sum(mine.astype(jnp.int32))


def per_device(moves, sizes, embeddings, proxies, hard_tiles, tile_count, labels):
    nx, nz, dp = moves.nx, moves.nz, moves.dp
    blocks = hard_tiles.shape[0]
    shard_tiles = proxies.shape[0] // TILE
    me, part = lax.axis_index("cls"), lax.axis_index("dp")
    place, column = me // nx, me % nx

    row_blocks = embeddings.reshape(blocks, BR, D)

    position = labels.reshape(blocks, BR) - hard_tiles[:, 0:1] * TILE
    entries = jnp.arange(K, dtype=jnp.int32)
    used = jnp.where(entries[None, :] < tile_count[:, None], hard_tiles, -1)
    starts = [sum(sizes[:chunk]) for chunk in range(len(sizes))]
    spots = [slice(start, start + size) for start, size in zip(starts, sizes)]
    held = [nz * size for size in sizes]
    last = len(sizes) - 1
    needed = tile_count[0] > 0

    def prepare(lists):
        prepared = []
        for spot, blocks_held in zip(spots, held):
            room = min(blocks_held * K, nz * (blocks * K // (nx * nz)) * nx)
            room = -(-room // PAIRS_PER_STEP) * PAIRS_PER_STEP
            chunk_lists = lists[:, spot].reshape(blocks_held, K + BR)
            code, count = pair_codes(chunk_lists, shard_tiles, nx, place, column, room)
            meta = jnp.stack([count, part, moves.order(place)]).astype(jnp.int32)
            prepared.append((code, meta, chunk_lists[:, K:]))
        return prepared

    gathered, tables, prepared = moves.gather(
        needed,
        [row_blocks[spot] for spot in spots],
        jnp.concatenate([used, position], axis=1),
        proxies.reshape(shard_tiles, TILE, D),
        part % 2,
        prepare,
    )

    def scored(chunk, rows, tables, prepared):
        parts, unit = score(held[chunk], *prepared[chunk], rows, tables)
        return moves.gather_stats(parts), unit

    def early_work(gathered, own_tables, prepared):
        units, made, rest = [], [], ()
        tables = moves.all_tables(own_tables)
        for chunk in range(last):
            stats, unit = scored(chunk, gathered[chunk], tables, prepared)
            if chunk == 0:
                rest, stats = moves.rest_of_rows(gathered[-1], stats)
            units.append(unit)
            made.append(grads(
                held[chunk], *prepared[chunk], stats, moves.turned, unit, tables,
                moves.grad_shapes(sizes[chunk]),
            ))
        return rest, tables[len(own_tables):], units, made

    def last_work(rows, tables, prepared, units, scores, early):
        codes, metas, hits = zip(*prepared)
        stats, unit = scored(last, rows, tables, prepared)
        returned, stats = moves.early_return(early, stats)
        return returned, last_grads(
            codes, metas, hits[-1], stats, moves.turned, scores, units + [unit], tables,
            moves.grad_shapes(sizes[-1]), moves.share_shapes(shard_tiles),
        )

    def work(gathered, tables, prepared):
        rest, more, units, made = early_work(gathered, tables, prepared)
        early, scores, losses = zip(*made)
        returned, (parts, shares, loss) = last_work(
            moves.whole_rows(gathered[-1], rest), [*tables, *more], prepared, units,
            list(scores), early,
        )
        return [part[0] for part in early], returned, parts, shares, [*losses, loss]

    early, returned, parts, shares, losses = moves.together(
        needed, work, gathered, tables, prepared
    )
    total, shares, (early, returned) = moves.sum_last(parts, shares, (early, returned))
    row_grads = moves.early_sums(early, returned) + [total]
    losses = [
        moves.own(part, place, size) for part, size in zip(losses, sizes)
    ]

    embeddings, losses = lax.optimization_barrier((embeddings, losses))
    emb_exact = embeddings.astype(jnp.float32)
    inverse_norm = lax.rsqrt(jnp.sum(emb_exact * emb_exact, axis=1, keepdims=True) + epsilon)
    unit_exact = emb_exact * inverse_norm
    proxy_grad = shares.reshape(shard_tiles * TILE, D // dp)
    row_loss = jnp.concatenate(losses, axis=0).reshape(-1)
    embed_grad = []
    for spot, grad_rows in zip(spots, row_grads):
        span = slice(spot.start * BR, spot.stop * BR)
        exact, norm = unit_exact[span], inverse_norm[span]
        grad_rows = grad_rows.reshape(-1, D)
        radial = jnp.sum(exact * grad_rows, axis=1, keepdims=True)
        embed_grad.append(((grad_rows - exact * radial) * norm).astype(jnp.bfloat16))
    embed_grad = jnp.concatenate(embed_grad, axis=0)
    return (row_loss, embed_grad, proxy_grad)


def solution(mesh):
    placed = (
        P(("dp", "cls"), None),
        P("cls", None),
        P(("dp", "cls"), None),
        P(("dp", "cls")),
        P(("dp", "cls")),
    )
    dp, groups = mesh.shape["dp"], mesh.shape["cls"]
    if (dp, groups) == (4, 2 * PIECES):
        moves, sizes = Neighbours(2, dp), [4, 4]
    else:
        chunks = max(1, groups // 8)
        moves, sizes = Groups(groups, dp), [8 // chunks] * chunks
    return jax.shard_map(
        functools.partial(per_device, moves, sizes),
        mesh=mesh,
        in_specs=placed,
        out_specs=(P(("dp", "cls")), P(("dp", "cls"), None), P("cls", "dp")),
        check_vma=False,
    )
```

```python
import functools

import jax
import jax.numpy as jnp
import numpy as np
from jax import lax
from jax.experimental import pallas as pl
from jax.experimental.pallas import tpu as pltpu
from jax.sharding import PartitionSpec as P

D = 512
TILE = 128
BR = 128
K = 8
PAIRS_PER_STEP = 4
FIELD = 128
PIECES = 4
VMEM_BYTES = 60 * 1024 * 1024
SPARE_BYTES = 4 * 1024 * 1024

logit_scale = 4.0
epsilon = 1e-06
unused_logit = -1e30

SMEM = pl.BlockSpec(memory_space=pltpu.SMEM)
VMEM = pl.BlockSpec(memory_space=pltpu.VMEM)
ANY = pl.BlockSpec(memory_space=pl.ANY)


def run_copies(jobs, sems, first=0):
    copies = [
        pltpu.make_async_copy(source, target, sems.at[first + index])
        for index, (source, target) in enumerate(jobs)
    ]
    for copy in copies:
        copy.start()
    return copies


def row_places(meta_ref, refs, blocks):
    size = blocks // PIECES
    if len(refs) > 1:
        return [(ref, piece * size) for piece, ref in enumerate(refs)]
    return [
        (refs[0].at[pl.ds(place * size, size)], (meta_ref[2] ^ place) * size)
        for place in range(PIECES)
    ]


def row_jobs(meta_ref, refs, rows_ref):
    return [
        (ref, rows_ref.at[pl.ds(start, ref.shape[0])])
        for ref, start in row_places(meta_ref, refs, rows_ref.shape[0])
    ]


def store_rows(meta_ref, rows_acc, out_ref, grad_refs, sems):
    blocks = out_ref.shape[0]
    out_ref[...] = rows_acc[:blocks].astype(out_ref.dtype)
    return run_copies(
        [
            (out_ref.at[pl.ds(start, ref.shape[0])], ref)
            for ref, start in row_places(meta_ref, grad_refs, blocks)
        ],
        sems,
    )


def aligned(refs, row, turned):
    parts = [ref[row] for ref in refs]
    if not turned:
        return parts
    size = parts[0].shape[0] // PIECES
    return [
        jnp.concatenate(
            [part[(piece ^ away) * size:((piece ^ away) + 1) * size] for piece in range(PIECES)]
        )
        for away, part in enumerate(parts)
    ]


def table_jobs(meta_ref, table_refs, table_ref):
    core = meta_ref[1] % 2
    jobs = [(table_refs[0], table_ref.at[pl.ds(0, table_refs[0].shape[0])])]
    if len(table_refs) > 1:
        half = table_refs[1].shape[0]
        jobs.append((table_refs[1], table_ref.at[pl.ds((2 + core) * half, half)]))
        jobs.append((table_refs[2], table_ref.at[pl.ds((3 - core) * half, half)]))
    return jobs


def transposed_logits(tile, rows):
    return logit_scale * lax.dot_general(
        tile, rows, (((1,), (1,)), ((), ())), preferred_element_type=jnp.float32
    )


def decode(code):
    return code // (2 * FIELD), (code // 2) % FIELD, (code % 2) == 1


def score_kernel(n_rows, n_tables, blocks, tiles, codes_ref, meta_ref, hit_ref, *refs):
    row_refs, refs = refs[:n_rows], refs[n_rows:]
    table_refs, refs = refs[:n_tables], refs[n_tables:]
    stats_ref, rows_ref, table_ref, lse_ref, pos_ref, sems = refs
    row_copies = run_copies(row_jobs(meta_ref, row_refs, rows_ref), sems)
    table_copies = run_copies(table_jobs(meta_ref, table_refs, table_ref), sems, PIECES)
    lse_ref[...] = jnp.full(lse_ref.shape, unused_logit, jnp.float32)
    pos_ref[...] = jnp.zeros(pos_ref.shape, jnp.float32)
    class_at = lax.broadcasted_iota(jnp.int32, (TILE, BR), 0)
    for copy in row_copies:
        copy.wait()

    def normalise(block, carry):
        exact = rows_ref[block].astype(jnp.float32)
        norm = lax.rsqrt(jnp.sum(exact * exact, axis=1, keepdims=True) + epsilon)
        rows_ref[block] = (exact * norm).astype(jnp.bfloat16)
        return carry

    lax.fori_loop(0, blocks, normalise, 0)
    for copy in table_copies:
        copy.wait()

    def step(index, carry):
        held = []
        for lane in range(PAIRS_PER_STEP):
            block, tile, first = decode(codes_ref[index * PAIRS_PER_STEP + lane])
            source = jnp.minimum(block, blocks - 1)
            logits = transposed_logits(
                table_ref[jnp.minimum(tile, tiles - 1)], rows_ref[source]
            )
            peak = jnp.max(logits, axis=0, keepdims=True)
            total = jnp.sum(jnp.exp(logits - peak), axis=0, keepdims=True)
            hit = class_at == hit_ref[pl.ds(source, 1), :]
            positive = jnp.sum(jnp.where(hit, logits, 0.0), axis=0, keepdims=True)
            held.append((block, peak + jnp.log(total), jnp.where(first, positive, 0.0)))
        for block, lse, positive in held:
            before = lse_ref[pl.ds(block, 1), :]
            top = jnp.maximum(before, lse)
            lse_ref[pl.ds(block, 1), :] = top + jnp.log(
                jnp.exp(before - top) + jnp.exp(lse - top)
            )
            pos_ref[pl.ds(block, 1), :] += positive
        return carry

    lax.fori_loop(0, pl.cdiv(meta_ref[0], PAIRS_PER_STEP), step, 0)
    stats_ref[0] = lse_ref[:blocks, :]
    stats_ref[1] = pos_ref[:blocks, :]


def make_totals(stat_refs, turned, total_ref, loss_ref):
    lse = aligned(stat_refs, 0, turned)
    top = functools.reduce(jnp.maximum, lse)
    total = top + jnp.log(sum(jnp.exp(part - top) for part in lse))
    total_ref[...] = total
    loss_ref[...] = total - sum(aligned(stat_refs, 1, turned))


def pair_score(code, blocks, tiles, rows_ref, table_ref, hit_ref, total_ref, class_at):
    block, tile, first = decode(code)
    source = jnp.minimum(block, blocks - 1)
    table_at = jnp.minimum(tile, tiles - 1)
    logits = transposed_logits(table_ref[table_at], rows_ref[source])
    share = jnp.exp(logits - total_ref[pl.ds(source, 1), :])
    wanted = jnp.where(first, hit_ref[pl.ds(source, 1), :], -1)
    hit = (class_at == wanted).astype(jnp.float32)
    return (logit_scale * (share - hit)).astype(jnp.bfloat16)


def row_terms(score, tile):
    return lax.dot_general(
        score, tile, (((0,), (0,)), ((), ())), preferred_element_type=jnp.float32
    )


def grad_kernel(
    n_grads, n_tables, n_stats, turned, blocks, tiles, codes_ref, meta_ref, hit_ref, *refs
):
    stat_refs, refs = refs[:n_stats], refs[n_stats:]
    unit_ref, refs = refs[0], refs[1:]
    table_refs, refs = refs[:n_tables], refs[n_tables:]
    grad_refs, refs = refs[:n_grads], refs[n_grads:]
    scores_ref, loss_ref, rows_ref, table_ref, total_ref, rows_acc, out_ref, sems = refs
    copies = run_copies(
        [(unit_ref, rows_ref)] + table_jobs(meta_ref, table_refs, table_ref), sems, PIECES
    )
    rows_acc[...] = jnp.zeros(rows_acc.shape, jnp.float32)
    make_totals(stat_refs, turned, total_ref, loss_ref)
    class_at = lax.broadcasted_iota(jnp.int32, (TILE, BR), 0)
    for copy in copies:
        copy.wait()

    def step(index, carry):
        held = []
        for lane in range(PAIRS_PER_STEP):
            pair = index * PAIRS_PER_STEP + lane
            score = pair_score(
                codes_ref[pair], blocks, tiles, rows_ref, table_ref, hit_ref, total_ref, class_at
            )
            scores_ref[pair] = score
            held.append(score)
        for lane, score in enumerate(held):
            block, tile, _ = decode(codes_ref[index * PAIRS_PER_STEP + lane])
            rows_acc[block] += row_terms(score, table_ref[jnp.minimum(tile, tiles - 1)])
        return carry

    lax.fori_loop(0, pl.cdiv(meta_ref[0], PAIRS_PER_STEP), step, 0)
    for copy in store_rows(meta_ref, rows_acc, out_ref, grad_refs, sems):
        copy.wait()


def last_kernel(sizes, n_grads, n_tables, n_stats, turned, n_shares, tiles, *refs):
    chunks, blocks = len(sizes), sizes[-1]
    codes_refs, refs = refs[:chunks], refs[chunks:]
    meta_refs, refs = refs[:chunks], refs[chunks:]
    hit_ref, refs = refs[0], refs[1:]
    stat_refs, refs = refs[:n_stats], refs[n_stats:]
    scores_refs, refs = refs[:chunks - 1], refs[chunks - 1:]
    unit_refs, refs = refs[:chunks], refs[chunks:]
    table_refs, refs = refs[:n_tables], refs[n_tables:]
    grad_refs, refs = refs[:n_grads], refs[n_grads:]
    share_refs, refs = refs[:n_shares], refs[n_shares:]
    loss_ref, refs = refs[0], refs[1:]
    rows_ref, early_ref, held_ref, table_ref, total_ref, rows_acc, out_ref, *refs = refs
    tiles_acc, sems, early_sems, row_sems = refs
    codes_ref, meta_ref = codes_refs[-1], meta_refs[-1]
    copies = run_copies(
        [(unit_refs[-1], rows_ref)] + table_jobs(meta_ref, table_refs, table_ref), sems
    )


    def fetch(chunk):
        early = early_ref.at[pl.ds(0, sizes[chunk])]
        return run_copies(
            [(unit_refs[chunk], early), (scores_refs[chunk], held_ref)], early_sems
        )

    early = fetch(0) if chunks > 1 else []
    rows_acc[...] = jnp.zeros(rows_acc.shape, jnp.float32)
    tiles_acc[...] = jnp.zeros(tiles_acc.shape, jnp.float32)
    make_totals(stat_refs, turned, total_ref, loss_ref)
    class_at = lax.broadcasted_iota(jnp.int32, (TILE, BR), 0)
    for copy in copies:
        copy.wait()

    def step(index, carry):
        held = [
            pair_score(
                codes_ref[index * PAIRS_PER_STEP + lane], blocks, tiles, rows_ref, table_ref,
                hit_ref, total_ref, class_at,
            )
            for lane in range(PAIRS_PER_STEP)
        ]
        for lane, score in enumerate(held):
            block, tile, _ = decode(codes_ref[index * PAIRS_PER_STEP + lane])
            rows_acc[block] += row_terms(score, table_ref[jnp.minimum(tile, tiles - 1)])
            tiles_acc[tile] += jnp.dot(
                score, rows_ref[jnp.minimum(block, blocks - 1)],
                preferred_element_type=jnp.float32,
            )
        return carry

    lax.fori_loop(0, pl.cdiv(meta_ref[0], PAIRS_PER_STEP), step, 0)
    stored = store_rows(meta_ref, rows_acc, out_ref, grad_refs, row_sems)
    for chunk in range(chunks - 1):
        for copy in early if chunk == 0 else fetch(chunk):
            copy.wait()

        def early_step(index, carry, chunk=chunk):
            for lane in range(PAIRS_PER_STEP):
                pair = index * PAIRS_PER_STEP + lane
                block, tile, _ = decode(codes_refs[chunk][pair])
                tiles_acc[tile] += jnp.dot(
                    held_ref[pair],
                    early_ref[jnp.minimum(block, sizes[chunk] - 1)],
                    preferred_element_type=jnp.float32,
                )
            return carry

        lax.fori_loop(0, pl.cdiv(meta_refs[chunk][0], PAIRS_PER_STEP), early_step, 0)
    if n_shares == 1:
        share_refs[0][...] = tiles_acc[:tiles].astype(jnp.bfloat16)
    else:
        part = meta_ref[1]
        shard, width = share_refs[0].shape[2], share_refs[0].shape[-1]
        for core, ref in enumerate(share_refs):
            for y in range(ref.shape[1]):
                start = pl.multiple_of(((2 * y + core) ^ part) * width, width)
                for x in range(ref.shape[0]):
                    ref[x, y] = tiles_acc[
                        pl.ds(x * shard, shard), :, pl.ds(start, width)
                    ].astype(jnp.bfloat16)
    for copy in stored:
        copy.wait()


def kernel_cost(blocks):
    return pl.CostEstimate(flops=blocks * BR * D, bytes_accessed=blocks * BR * D, transcendentals=0)


def limit(*scratch):
    total = 0
    for shape, dtype in scratch:
        total += int(np.prod(shape)) * jnp.dtype(dtype).itemsize
    return pltpu.CompilerParams(vmem_limit_bytes=min(VMEM_BYTES, total + SPARE_BYTES))


def rows_of(blocks):
    return (blocks, BR, D), jnp.bfloat16


def score(blocks, codes, meta, hit, rows, tables):
    tiles = sum(table.shape[0] for table in tables)
    table_room = ((tiles, TILE, D), jnp.bfloat16)
    return pl.pallas_call(
        functools.partial(score_kernel, len(rows), len(tables), blocks, tiles),
        out_shape=(
            jax.ShapeDtypeStruct((2, blocks, BR), jnp.float32),
            jax.ShapeDtypeStruct(*rows_of(blocks)),
        ),
        in_specs=[SMEM, SMEM, VMEM] + [ANY] * (len(rows) + len(tables)),
        out_specs=(VMEM, VMEM),
        scratch_shapes=[
            pltpu.VMEM(*table_room),
            pltpu.VMEM((blocks + 8, BR), jnp.float32),
            pltpu.VMEM((blocks + 8, BR), jnp.float32),
            pltpu.SemaphoreType.DMA((PIECES + len(tables),)),
        ],
        cost_estimate=kernel_cost(blocks),
        compiler_params=limit(rows_of(blocks), table_room),
    )(codes, meta, hit, *rows, *tables)


def grads(blocks, codes, meta, hit, stats, turned, unit, tables, shapes):
    tiles = sum(table.shape[0] for table in tables)
    table_room = ((tiles, TILE, D), jnp.bfloat16)
    acc_room = ((blocks + 1, BR, D), jnp.float32)
    scores = ((codes.shape[0], TILE, BR), jnp.bfloat16)
    outs = pl.pallas_call(
        functools.partial(
            grad_kernel, len(shapes), len(tables), len(stats), turned, blocks, tiles
        ),
        out_shape=(
            *(jax.ShapeDtypeStruct(shape, jnp.bfloat16) for shape in shapes),
            jax.ShapeDtypeStruct(*scores),
            jax.ShapeDtypeStruct((blocks, BR), jnp.float32),
        ),
        in_specs=[SMEM, SMEM] + [VMEM] * (1 + len(stats)) + [ANY] * (1 + len(tables)),
        out_specs=(*[ANY] * len(shapes), VMEM, VMEM),
        scratch_shapes=[
            pltpu.VMEM(*rows_of(blocks)),
            pltpu.VMEM(*table_room),
            pltpu.VMEM((blocks, BR), jnp.float32),
            pltpu.VMEM(*acc_room),
            pltpu.VMEM(*rows_of(blocks)),
            pltpu.SemaphoreType.DMA((PIECES + 1 + len(tables),)),
        ],
        cost_estimate=kernel_cost(blocks),
        compiler_params=limit(rows_of(2 * blocks), table_room, acc_room, scores),
    )(codes, meta, hit, *stats, unit, *tables)
    return list(outs[:len(shapes)]), outs[len(shapes)], outs[-1]


def last_grads(codes, metas, hit, stats, turned, scores, units, tables, shapes, share_shapes):
    sizes = [unit.shape[0] for unit in units]
    tiles = sum(table.shape[0] for table in tables)
    chunks, blocks = len(sizes), sizes[-1]
    n_inputs = 2 * chunks - 1 + len(tables)
    table_room = ((tiles, TILE, D), jnp.bfloat16)
    acc_room = ((blocks + 1, BR, D), jnp.float32)
    tiles_room = ((tiles + 1, TILE, D), jnp.float32)
    early_room = rows_of(max(sizes[:-1], default=PIECES))
    kept = ((scores or codes)[0].shape[0], TILE, BR), jnp.bfloat16
    outs = pl.pallas_call(
        functools.partial(
            last_kernel, sizes, len(shapes), len(tables), len(stats), turned,
            len(share_shapes), tiles,
        ),
        out_shape=(
            *(jax.ShapeDtypeStruct(shape, jnp.bfloat16) for shape in shapes),
            *(jax.ShapeDtypeStruct(shape, jnp.bfloat16) for shape in share_shapes),
            jax.ShapeDtypeStruct((blocks, BR), jnp.float32),
        ),
        in_specs=[SMEM] * (2 * chunks) + [VMEM] * (1 + len(stats)) + [ANY] * n_inputs,
        out_specs=(*[ANY] * len(shapes), *[VMEM] * len(share_shapes), VMEM),
        scratch_shapes=[
            pltpu.VMEM(*rows_of(blocks)),
            pltpu.VMEM(*early_room),
            pltpu.VMEM(*kept),
            pltpu.VMEM(*table_room),
            pltpu.VMEM((blocks, BR), jnp.float32),
            pltpu.VMEM(*acc_room),
            pltpu.VMEM(*rows_of(blocks)),
            pltpu.VMEM(*tiles_room),
            pltpu.SemaphoreType.DMA((1 + len(tables),)),
            pltpu.SemaphoreType.DMA((2,)),
            pltpu.SemaphoreType.DMA((PIECES,)),
        ],
        cost_estimate=kernel_cost(sum(sizes)),
        compiler_params=limit(
            rows_of(2 * blocks), early_room, kept, table_room, table_room, acc_room, tiles_room
        ),
    )(*codes, *metas, hit, *stats, *scores, *units, *tables)
    cut = len(shapes)
    return list(outs[:cut]), list(outs[cut:-1]), outs[-1]


def add(first, second):
    return (first.astype(jnp.float32) + second.astype(jnp.float32)).astype(jnp.bfloat16)


class Neighbours:
    def __init__(self, nx, dp):
        self.nx, self.nz, self.dp, self.turned = nx, PIECES, dp, True

    def over_z(self, value, away):
        pairs = [
            (z * self.nx + x, (z ^ away) * self.nx + x)
            for z in range(self.nz) for x in range(self.nx)
        ]
        return lax.ppermute(value, "cls", pairs)

    def over_x(self, value):
        return lax.ppermute(value, "cls", [(c, c ^ 1) for c in range(self.nx * self.nz)])

    def over_y(self, value):
        return lax.ppermute(value, "dp", [(d, d ^ 2) for d in range(self.dp)])

    def over_core(self, value):
        return lax.ppermute(value, "dp", [(d, d ^ 1) for d in range(self.dp)])

    def all_over_z(self, value):
        return [value] + [self.over_z(value, away) for away in range(1, self.nz)]

    def gather(self, needed, chunks, lists, table, core, prepare):
        def moves(first, lists, table, core):
            half = table.shape[0] // 2
            sent = lax.dynamic_slice_in_dim(table, core * half, half, axis=0)
            from_x = self.over_x(sent)
            far, near = lax.optimization_barrier((self.over_z(first, 2), self.over_z(first, 1)))
            return (near, far, self.over_z(far, 1)), from_x, prepare(
                jnp.stack(self.all_over_z(lists))
            )

        first, second = chunks
        pieces, from_x, prepared = self.together(needed, moves, first, lists, table, core)
        return [[first, *pieces], [second]], [table, from_x], prepared

    def all_tables(self, tables):
        return [*tables, self.over_core(tables[-1])]

    def rest_of_rows(self, pieces, others):
        second, = pieces
        far, near, others = lax.optimization_barrier(
            (self.over_z(second, 2), self.over_z(second, 1), others)
        )
        return (near, far, self.over_z(far, 1)), others

    def whole_rows(self, pieces, rest):
        return [*pieces, *rest]

    def grad_shapes(self, size):
        return [(size, BR, D)] * PIECES

    def gather_stats(self, stats):
        return self.all_over_z(stats)

    def order(self, place):
        return place

    def own(self, loss, place, size):
        return loss[:size]

    def early_return(self, early, others):
        parts, = early
        near, passed = self.over_z(parts[1], 1), self.over_z(parts[3], 1)
        passed, others = lax.optimization_barrier((passed, others))
        return (near, self.over_z(add(passed, parts[2]), 2)), others

    def early_sums(self, early, returned):
        return [sum(part.astype(jnp.float32) for part in (early[0], *returned))]

    def together(self, needed, work, *operands):
        def no_work(*operands):
            return jax.tree.map(
                lambda out: jnp.zeros(out.shape, out.dtype), jax.eval_shape(work, *operands)
            )

        return lax.cond(needed, work, no_work, *operands)

    def sum_last(self, parts, shares, early):
        kept, sent = shares
        passed, got = self.over_z(parts[3], 1), self.over_core(sent)
        half = kept.shape[2] // 2
        x_sent = add(kept[1, :, :half], got[1, :, :half])
        y_sent = add(kept[:, 1, half:], got[:, 1, half:])
        passed, near, early, _, _ = lax.optimization_barrier(
            (passed, parts[1], early, x_sent, y_sent)
        )
        near = self.over_z(near, 1)
        far = self.over_z(add(passed, parts[2]), 2)
        near, far, shares = self.sum_shares(near, far, kept, got, x_sent, y_sent)
        return sum(part.astype(jnp.float32) for part in (parts[0], near, far)), shares, early

    def share_shapes(self, shard_tiles):
        return [(self.nx, self.dp // 2, shard_tiles, TILE, D // self.dp)] * 2

    def sum_shares(self, near, far, kept, got, x_sent, y_sent):
        half = kept.shape[2] // 2
        x_got, y_got = lax.optimization_barrier((self.over_x(x_sent), self.over_y(y_sent)))
        x_kept = [add(add(kept[0, y, :half], got[0, y, :half]), x_got[y]) for y in range(2)]
        y_kept = [add(add(kept[x, 0, half:], got[x, 0, half:]), y_got[x]) for x in range(2)]
        low, high = self.over_y(x_kept[1]), self.over_x(y_kept[1])
        near, far, _, _ = lax.optimization_barrier((near, far, low, high))
        low = x_kept[0].astype(jnp.float32) + low.astype(jnp.float32)
        high = y_kept[0].astype(jnp.float32) + high.astype(jnp.float32)
        return near, far, jnp.concatenate([low, high], axis=0)


class Groups:
    def __init__(self, nz, dp):
        self.nx, self.nz, self.dp, self.turned = 1, nz, dp, False

    def gather(self, needed, chunks, lists, table, core, prepare):
        gathered = [[lax.all_gather(rows, "cls", tiled=True)] for rows in chunks]
        return gathered, [table], prepare(lax.all_gather(lists, "cls"))

    def all_tables(self, tables):
        return tables

    def rest_of_rows(self, pieces, others):
        return (), others

    def whole_rows(self, pieces, rest):
        return pieces

    def grad_shapes(self, size):
        return [(self.nz * size, BR, D)]

    def gather_stats(self, stats):
        return list(lax.all_gather(stats, "cls"))

    def order(self, place):
        return jnp.zeros_like(place)

    def own(self, loss, place, size):
        return lax.dynamic_slice_in_dim(loss, place * size, size, axis=0)

    def total(self, part):
        return lax.psum_scatter(
            part, "cls", scatter_dimension=0, tiled=True
        ).astype(jnp.float32)

    def early_return(self, early, others):
        return [self.total(part) for part, in early], others

    def early_sums(self, early, returned):
        return returned

    def together(self, needed, work, *operands):
        return work(*operands)

    def sum_last(self, parts, shares, early):
        return self.total(parts[0]), self.sum_shares(shares), early

    def share_shapes(self, shard_tiles):
        return [(shard_tiles, TILE, D)]

    def sum_shares(self, shares):
        return lax.psum_scatter(
            shares[0], "dp", scatter_dimension=2, tiled=True
        ).astype(jnp.float32)


def pair_codes(lists, shard_tiles, nx, place, column, room):
    entry = lists[:, :K].reshape(-1)
    owner = entry // shard_tiles
    mine = (entry >= 0) & (owner // nx == place)
    local = jnp.where(owner % nx == column, 0, shard_tiles) + entry % shard_tiles
    counter = jnp.arange(entry.shape[0], dtype=jnp.int32)
    code = ((counter // K) * FIELD + local) * 2 + (counter % K == 0)
    rank = jnp.sum(
        jnp.where(mine[None, :] & (counter[None, :] < counter[:, None]), 1, 0), axis=1
    ).astype(jnp.int32)
    slots = jnp.arange(room, dtype=jnp.int32)
    chosen = mine[None, :] & (rank[None, :] == slots[:, None])
    padding = (lists.shape[0] * FIELD + nx * shard_tiles) * 2
    codes = padding + jnp.sum(jnp.where(chosen, code[None, :] - padding, 0), axis=1)
    return codes.astype(jnp.int32), jnp.sum(mine.astype(jnp.int32))


def per_device(moves, sizes, embeddings, proxies, hard_tiles, tile_count, labels):
    nx, nz, dp = moves.nx, moves.nz, moves.dp
    blocks = hard_tiles.shape[0]
    shard_tiles = proxies.shape[0] // TILE
    me, part = lax.axis_index("cls"), lax.axis_index("dp")
    place, column = me // nx, me % nx

    row_blocks = embeddings.reshape(blocks, BR, D)

    position = labels.reshape(blocks, BR) - hard_tiles[:, 0:1] * TILE
    entries = jnp.arange(K, dtype=jnp.int32)
    used = jnp.where(entries[None, :] < tile_count[:, None], hard_tiles, -1)
    starts = [sum(sizes[:chunk]) for chunk in range(len(sizes))]
    spots = [slice(start, start + size) for start, size in zip(starts, sizes)]
    held = [nz * size for size in sizes]
    last = len(sizes) - 1
    needed = tile_count[0] > 0

    def prepare(lists):
        prepared = []
        for spot, blocks_held in zip(spots, held):
            room = min(blocks_held * K, nz * (blocks * K // (nx * nz)) * nx)
            room = -(-room // PAIRS_PER_STEP) * PAIRS_PER_STEP
            chunk_lists = lists[:, spot].reshape(blocks_held, K + BR)
            code, count = pair_codes(chunk_lists, shard_tiles, nx, place, column, room)
            meta = jnp.stack([count, part, moves.order(place)]).astype(jnp.int32)
            prepared.append((code, meta, chunk_lists[:, K:]))
        return prepared

    gathered, tables, prepared = moves.gather(
        needed,
        lax.optimization_barrier([row_blocks[spot] for spot in spots]),
        jnp.concatenate([used, position], axis=1),
        proxies.reshape(shard_tiles, TILE, D),
        part % 2,
        prepare,
    )

    def scored(chunk, rows, tables, prepared):
        parts, unit = score(held[chunk], *prepared[chunk], rows, tables)
        return moves.gather_stats(parts), unit

    def early_work(gathered, own_tables, prepared):
        units, made, rest = [], [], ()
        tables = moves.all_tables(own_tables)
        for chunk in range(last):
            stats, unit = scored(chunk, gathered[chunk], tables, prepared)
            if chunk == 0:
                rest, stats = moves.rest_of_rows(gathered[-1], stats)
            units.append(unit)
            made.append(grads(
                held[chunk], *prepared[chunk], stats, moves.turned, unit, tables,
                moves.grad_shapes(sizes[chunk]),
            ))
        return rest, tables[len(own_tables):], units, made

    def last_work(rows, tables, prepared, units, scores, early):
        codes, metas, hits = zip(*prepared)
        stats, unit = scored(last, rows, tables, prepared)
        returned, stats = moves.early_return(early, stats)
        return returned, last_grads(
            codes, metas, hits[-1], stats, moves.turned, scores, units + [unit], tables,
            moves.grad_shapes(sizes[-1]), moves.share_shapes(shard_tiles),
        )

    def work(gathered, tables, prepared):
        rest, more, units, made = early_work(gathered, tables, prepared)
        early, scores, losses = zip(*made)
        returned, (parts, shares, loss) = last_work(
            moves.whole_rows(gathered[-1], rest), [*tables, *more], prepared, units,
            list(scores), early,
        )
        return [part[0] for part in early], returned, parts, shares, [*losses, loss]

    early, returned, parts, shares, losses = moves.together(
        needed, work, gathered, tables, prepared
    )
    total, shares, (early, returned) = moves.sum_last(parts, shares, (early, returned))
    row_grads = moves.early_sums(early, returned) + [total]
    losses = [
        moves.own(part, place, size) for part, size in zip(losses, sizes)
    ]

    embeddings, losses = lax.optimization_barrier((embeddings, losses))
    emb_exact = embeddings.astype(jnp.float32)
    inverse_norm = lax.rsqrt(jnp.sum(emb_exact * emb_exact, axis=1, keepdims=True) + epsilon)
    unit_exact = emb_exact * inverse_norm
    proxy_grad = shares.reshape(shard_tiles * TILE, D // dp)
    row_loss = jnp.concatenate(losses, axis=0).reshape(-1)
    embed_grad = []
    for spot, grad_rows in zip(spots, row_grads):
        span = slice(spot.start * BR, spot.stop * BR)
        exact, norm = unit_exact[span], inverse_norm[span]
        grad_rows = grad_rows.reshape(-1, D)
        radial = jnp.sum(exact * grad_rows, axis=1, keepdims=True)
        embed_grad.append(((grad_rows - exact * radial) * norm).astype(jnp.bfloat16))
    embed_grad = jnp.concatenate(embed_grad, axis=0)
    return (row_loss, embed_grad, proxy_grad)


def solution(mesh):
    placed = (
        P(("dp", "cls"), None),
        P("cls", None),
        P(("dp", "cls"), None),
        P(("dp", "cls")),
        P(("dp", "cls")),
    )
    dp, groups = mesh.shape["dp"], mesh.shape["cls"]
    if (dp, groups) == (4, 2 * PIECES):
        moves, sizes = Neighbours(2, dp), [4, 4]
    else:
        chunks = max(1, groups // 8)
        moves, sizes = Groups(groups, dp), [8 // chunks] * chunks
    return jax.shard_map(
        functools.partial(per_device, moves, sizes),
        mesh=mesh,
        in_specs=placed,
        out_specs=(P(("dp", "cls")), P(("dp", "cls"), None), P("cls", "dp")),
        check_vma=False,
    )
```
